32 devices in a mesh: groups: 2 (over x), ctx: 16 (over z, y, core).
Axes of the slice: x: 2, y: 2, z: 4, core: 2. Of those that a mesh axis runs over, the one named last changes fastest.
Arguments:
- q_heads: bfloat16 [4096, 12288], P(('groups', 'ctx')), parts along dimension 0, may hold values from -12 to 12
- kv_latent: bfloat16 [4096, 576], P(('groups', 'ctx')), parts along dimension 0, may hold values from -12 to 12
- latent_gain: float32 [512], replicated, may hold values from 0.1 to 1.9
- w_up: bfloat16 [512, 16384], P('ctx'), may hold values from -0.25 to 0.25
- page_ranks: int32 [4096, 1], P(('groups', 'ctx')), parts along dimension 0, may hold values from 0 to 15; in each aligned block of 128 rows (0 to 127, 128 to 255, ...) at most 16 rows name the same one
- lengths: int32 [16], P('groups'), parts along dimension 0, may hold values from 1 to 1024, 2048 in all
Outputs:
- attn_out: bfloat16 [4096, 8192], P(('groups', 'ctx')), parts along dimension 0
- decode_cache: bfloat16 [8192, 576], P(('groups', 'ctx')), parts along dimension 0
The draws below stay inside these ranges and needn't reach their ends.
There are 2 independent parts, one for each index of `groups`. The reference program is written for one: setup_inputs(seed, part) draws one part's arguments, and reference() takes and returns one part's arrays. A program takes and returns all parts, laid end to end along the dimension named above; an argument that names none is the same for every part. Nothing has to cross between parts.
Inputs may be any that keep to these rules, and one draw needn't show every extreme that they name: `page_ranks`: the 128 positions of one device name one decode rank at most 16 times. The 8 lengths add up to 2048; the longest is 1024.
All inputs are finite; a program needn't handle non-finite values.
Results may differ from the reference program's by a relative error of at most 0.012.
The reference program's roundings to bfloat16 on the way (of `cache_rows`, `query_rope`, `expanded` and `weights`) count: a program that leaves them out, or rounds other values in their place, can miss the bound.
Values may be sent and summed in bfloat16 or wider, within the bound.
No kernel may reach another device: no remote copies, remote signals or barrier semaphores. Data moves between devices by JAX's collectives and lax.ppermute only.
A program may use at most 128 MiB of HBM per device.

```python
import math
import jax
import jax.numpy as jnp
import numpy as np
from jax import lax

H = 64
NOPE = 128
ROPE = 64
VDIM = 128
LAT = 512
REACH = 3
REQS = 8
TOK_DEV = 128
TOKENS = 2048
MOST = 1024
CAP = 16
N_CTX = 16


def draw_kv_latent(key, part):
    own_key = jax.random.fold_in(key, 3)
    base = jnp.clip(jax.random.normal(own_key, (TOKENS, LAT + ROPE), jnp.float32), -12.0, 12.0)
    return base.astype(jnp.bfloat16)


def draw_q_heads(key, part):
    own_key = jax.random.fold_in(key, 5)
    base = jnp.clip(jax.random.normal(own_key, (TOKENS, H, NOPE + ROPE), jnp.float32), -12.0, 12.0)
    return base.reshape(TOKENS, H * (NOPE + ROPE)).astype(jnp.bfloat16)


def block_scale(stream_key, extent, pieces, low, high):
    def one(axis_at, shards_of):
        steps = jax.random.uniform(jax.random.fold_in(jax.random.fold_in(stream_key, 6), axis_at), (shards_of,), jnp.float32, low / len(pieces), high / len(pieces))
        return jnp.repeat(jnp.exp(steps), extent[axis_at] // shards_of).reshape((-1,) + (1,) * (len(extent) - axis_at - 1))

    factor_of = one(*pieces[0])
    for cut in pieces[1:]:
        factor_of = factor_of * one(*cut)
    return factor_of


def length_profile(count, total, limit, slope):
    weights = [(1 << 20) // math.isqrt(rank ** slope) + 1 for rank in range(2, count + 1)]
    rest, counts = total - limit - (count - 1), [1] * (count - 1)
    while rest > 0:
        candidates = [i for i in range(count - 1) if counts[i] < limit]
        pool, budget = sum([weights[i] for i in candidates]), rest
        for i in candidates:
            addition = min(limit - counts[i], max(1, budget * weights[i] // pool), rest)
            counts[i] = counts[i] + addition
            rest = rest - addition
    return np.array([limit] + counts)


def uneven(key, number_of, total, limit, slope):
    if number_of == 2:
        one = jax.random.randint(key, (), max(1, total - limit), min(limit, total - 1) + 1)
        return jnp.stack([one, total - one])
    sizes = jnp.asarray(length_profile(number_of, total, limit, slope), jnp.int32)
    couples = (number_of - 1) // 2
    source_of, sink = sizes[1:1 + 2 * couples:2], sizes[2:2 + 2 * couples:2]
    room = jnp.minimum(source_of - 1, limit - sink)
    passed = jax.random.randint(jax.random.fold_in(key, 1), (couples,), 0, 1 << 20) % (room + 1)
    sizes = sizes.at[1:1 + 2 * couples:2].set(source_of - passed).at[2:2 + 2 * couples:2].set(sink + passed)
    return sizes[jax.random.permutation(jax.random.fold_in(key, 2), number_of)]


def deal_out(rng, own, number, rows, amount, top, reach, lean):
    order = jax.random.permutation(rng, amount)
    packed, ordinary = shares(amount, rows * top, reach, lean, True), shares(amount, rows * top, reach, lean, False)
    places = jnp.arange(amount)

    def named(sizes, rotation):
        used = int((sizes > 0).sum())
        fixed = max(1, used // 4)
        moved = fixed + (places - fixed + rotation * (used - fixed)) % max(1, amount - fixed)
        return jnp.zeros((amount,), jnp.int32).at[order[jnp.where(places < fixed, places, moved)]].set(jnp.asarray(sizes, jnp.int32))

    sizes = jnp.where(number % 4 == 0, named(packed, number // 4), named(ordinary, number - number // 4 - 1))
    mixed = jax.random.permutation(jax.random.fold_in(own, 3), amount)
    donor, taker = mixed[0:amount // 2 * 2:2], mixed[1:amount // 2 * 2:2]
    room = jnp.minimum(sizes[donor] - 1, reach - sizes[taker]) // 2
    room = jnp.where((donor == order[0]) | (taker == order[0]) | (sizes[taker] == 0), 0, jnp.maximum(room, 0))
    moved = jax.random.randint(jax.random.fold_in(own, 4), (amount // 2,), 0, 1 << 20) % (room + 1)
    sizes = sizes.at[donor].add(-moved).at[taker].add(moved)
    labels = jnp.searchsorted(jnp.cumsum(sizes), jnp.arange(rows * top), side="right").astype(jnp.int32)
    grid = labels.reshape(top, rows).T
    grid = grid[jax.random.permutation(jax.random.fold_in(own, 1), rows)]
    rotation = jax.random.randint(jax.random.fold_in(own, 2), (rows, 1), 0, top)
    return jnp.take_along_axis(grid, (jnp.arange(top)[None, :] + rotation) % top, axis=1)


def shares(number_of, total, reach, slope, full):
    portions = [(1 << 20) // math.isqrt(rank ** slope) + 1 for rank in range(1, number_of + 1)]
    largest = reach if full else min(reach, max(-(-total // number_of), total * portions[0] // sum(portions)))
    least = 1 if total - largest >= number_of - 1 else 0
    holding, rest = [largest] + [least] * (number_of - 1), total - largest - least * (number_of - 1)
    while rest > 0:
        movable = [i for i in range(1, number_of) if holding[i] < largest] or [i for i in range(1, number_of) if holding[i] < reach]
        whole, left = sum([portions[i] for i in movable]), rest
        for i in movable:
            extra = min(reach - holding[i], max(1, left * portions[i] // whole), rest)
            holding[i] = holding[i] + extra
            rest = rest - extra
    return np.array(holding)


def gaussian(rng, dims, scale, bound, pieces=(), kind=jnp.bfloat16):
    drawn = scale * jax.random.normal(rng, dims, jnp.float32)
    if pieces:
        drawn = drawn * block_scale(rng, dims, pieces, -0.22, 0.18)
    return jnp.clip(drawn, -bound, bound).astype(kind)


def setup_inputs(seed: int = 0, part: int = 0) -> dict:
    arg_keys = jax.random.split(jax.random.key(seed), 7)
    own_keys = jax.random.split(jax.random.fold_in(arg_keys[6], part), 7)
    q_heads = draw_q_heads(jax.random.fold_in(jax.random.fold_in(arg_keys[6], part), 71), part)
    kv_latent = draw_kv_latent(jax.random.fold_in(jax.random.fold_in(arg_keys[6], part), 71), part)
    latent_gain = jnp.clip(1.0 + 0.18 * jax.random.normal(arg_keys[2], (LAT,), jnp.float32), 0.1, 1.9)
    w_up = gaussian(arg_keys[3], (LAT, H * (NOPE + VDIM)), LAT ** -0.5, 0.25, ((0, 16),))
    page_ranks_keys = jax.random.split(jax.random.fold_in(own_keys[4], 1), TOKENS // TOK_DEV)
    page_ranks_turns = jax.random.permutation(jax.random.fold_in(own_keys[4], 3), TOKENS // TOK_DEV)
    page_ranks = jax.vmap(lambda own, number: deal_out(jax.random.fold_in(own_keys[4], 2), own, number, TOK_DEV, N_CTX, 1, CAP, 2))(page_ranks_keys, page_ranks_turns).reshape((TOKENS, 1))
    lengths = uneven(own_keys[5], REQS, TOKENS, MOST, 2).astype(jnp.int32)
    return dict(q_heads=q_heads, kv_latent=kv_latent, latent_gain=latent_gain, w_up=w_up, page_ranks=page_ranks, lengths=lengths)


def locate(positions, starts):
    inside = positions[:, None] >= starts[None, :]
    request = lax.optimization_barrier(jnp.sum(inside.astype(jnp.int32), axis=1)).astype(jnp.int32)
    own_start = lax.optimization_barrier(jnp.max(jnp.where(inside, starts[None, :], 0), axis=1)).astype(jnp.int32)
    return (request, (positions - own_start).astype(jnp.int32))

def rope_tables(offset, width):
    half_width = width // 2
    frequency = jnp.exp(-jnp.arange(half_width, dtype=jnp.float32) * (2.0 * math.log(10000.0) / width))
    angles = offset.astype(jnp.float32)[:, None] * frequency[None, :]
    return (jnp.cos(angles), jnp.sin(angles))

def rotate(values, cosine, sine_table):
    half_width = values.shape[-1] // 2
    view_shape = (cosine.shape[0],) + (1,) * (values.ndim - 2) + (half_width,)
    cosine = cosine.reshape(view_shape)
    sine_table = sine_table.reshape(view_shape)
    front_half = values[..., :half_width]
    back_half = values[..., half_width:]
    return jnp.concatenate([front_half * cosine - back_half * sine_table, back_half * cosine + front_half * sine_table], axis=-1)

def cache_rows_of(kv_latent, latent_gain, cosine, sine_table):
    raw_values = kv_latent.astype(jnp.float32)
    latent_part = raw_values[:, :LAT]
    inverse_rms = lax.rsqrt(lax.optimization_barrier(jnp.mean(latent_part * latent_part, axis=1, keepdims=True)) + 1e-06)
    latent = latent_part * inverse_rms * latent_gain[None, :]
    key_rope = rotate(raw_values[:, LAT:], cosine, sine_table)
    return jnp.concatenate([latent, key_rope], axis=1).astype(jnp.bfloat16)

def attend(query_nope, query_rope, key_nope, key_rope, value_heads, allowed):
    softmax_scale = (query_nope.shape[-1] + query_rope.shape[-1]) ** (-0.5)
    scores = jnp.einsum('thd,uhd->htu', query_nope.astype(jnp.float32), key_nope.astype(jnp.float32))
    scores = scores + jnp.einsum('thr,ur->htu', query_rope.astype(jnp.float32), key_rope.astype(jnp.float32))
    scores = jnp.where(allowed[None], scores * softmax_scale, -1e+30)
    row_max = lax.optimization_barrier(jnp.max(scores, axis=2, keepdims=True))
    exponent = jnp.where(allowed[None], jnp.exp(scores - row_max), 0.0)
    totals = lax.optimization_barrier(jnp.sum(exponent, axis=2))
    weights = exponent.astype(jnp.bfloat16)
    mixed_values = jnp.einsum('htu,uhv->thv', weights.astype(jnp.float32), value_heads.astype(jnp.float32))
    return (mixed_values / jnp.transpose(totals)[:, :, None]).astype(jnp.bfloat16)

def reference(q_heads, kv_latent, latent_gain, w_up, page_ranks, lengths):
    positions = jnp.arange(TOKENS, dtype=jnp.int32)
    starts = (jnp.cumsum(lengths) - lengths).astype(jnp.int32)
    request, offset = locate(positions, starts)
    cosine, sine_table = rope_tables(offset, ROPE)
    cache_rows = cache_rows_of(kv_latent, latent_gain, cosine, sine_table)
    query = q_heads.reshape(TOKENS, H, NOPE + ROPE)
    query_nope = query[:, :, :NOPE]
    query_rope = rotate(query[:, :, NOPE:].astype(jnp.float32), cosine, sine_table).astype(jnp.bfloat16)

    def expand_block(block_rows):
        return jnp.dot(block_rows[:, :LAT], w_up, preferred_element_type=jnp.float32).astype(jnp.bfloat16)
    expanded = lax.map(expand_block, cache_rows.reshape(N_CTX, TOK_DEV, LAT + ROPE))
    expanded = expanded.reshape(TOKENS, H * (NOPE + VDIM))
    lead_rows = REACH * TOK_DEV
    window = lead_rows + TOK_DEV
    padded_rows = jnp.concatenate([jnp.zeros((lead_rows, LAT + ROPE), jnp.bfloat16), cache_rows], axis=0)
    padded_kv = jnp.concatenate([jnp.zeros((lead_rows, H * (NOPE + VDIM)), jnp.bfloat16), expanded], axis=0)
    padded_request = jnp.concatenate([jnp.full((lead_rows,), -1, jnp.int32), request], axis=0)

    def one_block(block_index):
        first_row = (block_index * TOK_DEV).astype(jnp.int32)
        key_rows = lax.dynamic_slice_in_dim(padded_rows, first_row, window, 0)
        key_kv = lax.dynamic_slice_in_dim(padded_kv, first_row, window, 0).reshape(window, H, NOPE + VDIM)
        key_request = lax.dynamic_slice_in_dim(padded_request, first_row, window, 0)
        query_request = lax.dynamic_slice_in_dim(request, first_row, TOK_DEV, 0)
        key_spots = first_row - lead_rows + jnp.arange(window, dtype=jnp.int32)
        query_spots = first_row + jnp.arange(TOK_DEV, dtype=jnp.int32)
        allowed = (key_spots[None, :] >= 0) & (key_spots[None, :] <= query_spots[:, None]) & (key_request[None, :] == query_request[:, None])
        block_nope = lax.dynamic_slice_in_dim(query_nope, first_row, TOK_DEV, 0)
        block_rope = lax.dynamic_slice_in_dim(query_rope, first_row, TOK_DEV, 0)
        return attend(block_nope, block_rope, key_kv[:, :, :NOPE], key_rows[:, LAT:], key_kv[:, :, NOPE:], allowed)
    attn_out = lax.map(one_block, jnp.arange(N_CTX, dtype=jnp.int32)).reshape(TOKENS, H * VDIM)
    dest_rank = page_ranks[:, 0]
    onehot = (dest_rank[:, None] == jnp.arange(N_CTX, dtype=jnp.int32)[None, :]).astype(jnp.int32)
    running = jnp.cumsum(onehot.reshape(N_CTX, TOK_DEV, N_CTX), axis=1).astype(jnp.int32).reshape(TOKENS, N_CTX)
    slot_index = lax.optimization_barrier(jnp.sum((running - 1) * onehot, axis=1)).astype(jnp.int32)
    target = (dest_rank * N_CTX + positions // TOK_DEV) * CAP + slot_index
    decode_cache = jnp.zeros((N_CTX * N_CTX * CAP, LAT + ROPE), jnp.bfloat16).at[target].set(cache_rows)
    return (attn_out, decode_cache)
```

```python
import functools
import math

import jax
import jax.numpy as jnp
import numpy as np
from jax import lax
from jax.experimental import pallas as pl
from jax.experimental.pallas import tpu as pltpu
from jax.sharding import PartitionSpec as P

H = 64
NOPE = 128
ROPE = 64
VDIM = 128
LAT = 512
REACH = 3
QUAD = 4
HQ = H // QUAD
CHUNKS = 2
HC = HQ // CHUNKS
ROW = LAT + ROPE
EXT = 640
VMEM_LIMIT = 48 * 1024 * 1024
SMEM = pltpu.SMEM
VMEM = pltpu.VMEM


def rows_kernel(slot_count, info, kv, gain, ranks, freq, rows_out, cos_out, sin_out, outgoing_out):
    tok = kv.shape[0]
    base = info[0] * tok
    spots = base + lax.broadcasted_iota(jnp.int32, (tok, 128), 0)
    lane = lax.broadcasted_iota(jnp.int32, (tok, 128), 1)
    begin = jnp.int32(0)
    own_start = jnp.zeros((tok, 128), jnp.int32)
    for r in range(info.shape[0] - 1):
        own_start = jnp.where(spots >= begin, begin, own_start)
        begin = begin + info[1 + r]
    offset = spots - own_start
    angles = offset.astype(jnp.float32) * freq[...]
    cosine = jnp.cos(angles)
    sine = jnp.where((lane & 32) == 0, -jnp.sin(angles), jnp.sin(angles))
    cos_out[...] = cosine
    sin_out[...] = sine
    raw = kv[...].astype(jnp.float32)
    latent = raw[:, :LAT]
    mean = jnp.sum(latent * latent, axis=1, keepdims=True) * (1.0 / LAT)
    latent = latent * lax.rsqrt(mean + 1e-06) * gain[...]
    key = raw[:, LAT:]
    swapped = jnp.concatenate([key[:, ROPE // 2 :], key[:, : ROPE // 2]], axis=1)
    turned = key * cosine[:, :ROPE] + swapped * sine[:, :ROPE]
    high = (offset >> 8).astype(jnp.float32)
    low = (offset & 255).astype(jnp.float32)
    meta = jnp.where(lane == 0, high, jnp.where(lane == 1, low, 0.0))
    tail = jnp.concatenate([turned, meta[:, :ROPE]], axis=1)
    rows_out[:, :LAT] = latent.astype(jnp.bfloat16)
    rows_out[:, LAT:] = tail.astype(jnp.bfloat16)

    rank_col = jnp.broadcast_to(ranks[...], (tok, tok)).astype(jnp.float32)
    rank_row = rank_col.T
    earlier = lax.broadcasted_iota(jnp.int32, (tok, tok), 0) < lax.broadcasted_iota(
        jnp.int32, (tok, tok), 1
    )
    same = jnp.where((rank_col == rank_row) & earlier, 1.0, 0.0)
    slot = jnp.sum(same, axis=0, keepdims=True)
    target = (rank_row[:1] * slot_count + slot).astype(jnp.int32)
    spots_out = lax.broadcasted_iota(jnp.int32, (outgoing_out.shape[0], tok), 0)
    selector = jnp.where(spots_out == target, 1.0, 0.0).astype(jnp.bfloat16)
    picked = jnp.dot(selector, rows_out[:, :ROW], preferred_element_type=jnp.float32)
    outgoing_out[...] = picked.astype(jnp.bfloat16)


def query_kernel(info, query, cosine, sine, *outs):
    tok = query.shape[0]
    lane = lax.broadcasted_iota(jnp.int32, (tok, 128), 1)
    low_half = lane < 64
    first_quarter = (lane & 32) == 0
    cos_table = cosine[...]
    sin_table = sine[...]
    for r in range(QUAD):
        first = (info[0] ^ r) * (HQ * (NOPE + ROPE))
        for pair in range(HQ // 2):
            out = outs[r * CHUNKS + pair // (HC // 2)]
            at = pair % (HC // 2)
            begin = pl.multiple_of(first + pair * 2 * (NOPE + ROPE), 128)
            both = query[:, pl.ds(begin, 2 * (NOPE + ROPE))]
            mid = both[:, 128:256].astype(jnp.float32)
            end = both[:, 256:384].astype(jnp.float32)
            turned = jnp.where(low_half, mid, end)
            odd_nope = pltpu.roll(jnp.where(low_half, end, mid), 64, 1)
            swapped = jnp.where(
                first_quarter, pltpu.roll(turned, 96, 1), pltpu.roll(turned, 32, 1)
            )
            turned = turned * cos_table + swapped * sin_table
            out[:, at * 256 : at * 256 + 128] = both[:, :128]
            out[:, at * 256 + 128 : at * 256 + 256] = odd_nope.astype(jnp.bfloat16)
            out[:, HC * NOPE + at * 128 : HC * NOPE + at * 128 + 128] = turned.astype(
                jnp.bfloat16
            )


def attend_kernel(info, own, other, weight, *refs):
    nope = refs[0:QUAD]
    rope = refs[QUAD : 2 * QUAD]
    outs = refs[2 * QUAD : 3 * QUAD]
    latent, rope_even, rope_odd, bias = refs[3 * QUAD :]
    tok = nope[0].shape[0]
    blocks = REACH + 2
    mine = info[0]
    partner = mine ^ 1
    scale = (NOPE + ROPE) ** (-0.5) * math.log2(math.e)

    @pl.when(pl.program_id(0) == 0)
    def _():
        has_last = (mine & 1) == 1
        starts = [mine, partner, mine - 2, partner - 2, (mine >> 1) * 2 - 3]
        blank = jnp.zeros((tok, ROPE), jnp.bfloat16)
        lane = lax.broadcasted_iota(jnp.int32, (tok, tok), 1)
        row = lax.broadcasted_iota(jnp.int32, (tok, tok), 0)
        for g in range(2):
            pieces = [
                own[g * tok : (g + 1) * tok],
                other[g * tok : (g + 1) * tok],
                own[(2 + g) * tok : (3 + g) * tok],
                other[(2 + g) * tok : (3 + g) * tok],
                jnp.where(
                    has_last,
                    own[(4 + g) * tok : (5 + g) * tok],
                    other[(4 + g) * tok : (5 + g) * tok],
                ),
            ]
            for b, piece in enumerate(pieces):
                here = slice(b * tok, (b + 1) * tok)
                latent[g, here] = piece[:, :LAT]
                turned = piece[:, LAT : LAT + ROPE]
                rope_even[g, here] = jnp.concatenate([turned, blank], axis=1)
                rope_odd[g, here] = jnp.concatenate([blank, turned], axis=1)
            for half in range(2):
                meta = pieces[half][:, LAT:].astype(jnp.float32)
                offset = (meta[:, ROPE : ROPE + 1] * 256.0 + meta[:, ROPE + 1 : ROPE + 2]).astype(
                    jnp.int32
                )
                spots = starts[half] * tok + row
                lowest = jnp.maximum(spots - offset, (starts[half] - REACH) * tok)
                for b in range(blocks):
                    keys = starts[b] * tok + lane
                    allowed = (keys >= lowest) & (keys <= spots)
                    bias[g, half * tok : (half + 1) * tok, b * tok : (b + 1) * tok] = jnp.where(
                        allowed, 0.0, -1e30
                    )

    for g in range(2):
        expanded = jnp.dot(latent[g], weight[...], preferred_element_type=jnp.float32).astype(
            jnp.bfloat16
        )
        query_rope = jnp.concatenate([rope[2 * g][...], rope[2 * g + 1][...]], axis=0)
        for b in range(2):
            at = slice(b * 128, (b + 1) * 128)
            key_rope = (rope_even, rope_odd)[b][g]
            key = jnp.concatenate([expanded[:, b * 256 : b * 256 + 128], key_rope], axis=1)
            value = expanded[:, b * 256 + 128 : b * 256 + 256]
            query = jnp.concatenate([nope[2 * g][:, at], nope[2 * g + 1][:, at]], axis=0)
            query = jnp.concatenate([query, query_rope], axis=1)
            scores = lax.dot_general(
                query, key, (((1,), (1,)), ((), ())), preferred_element_type=jnp.float32
            )
            scores = scores * scale + bias[g]
            largest = jnp.max(scores, axis=1, keepdims=True)
            expo = jnp.exp2(scores - largest)
            total = jnp.sum(expo, axis=1, keepdims=True)
            mixed = jnp.dot(expo.astype(jnp.bfloat16), value, preferred_element_type=jnp.float32)
            mixed = (mixed / total).astype(jnp.bfloat16)
            outs[2 * g][:, at] = mixed[:tok]
            outs[2 * g + 1][:, at] = mixed[tok:]


def gather_kernel(info, *refs):
    pieces, out, sems = refs[:-2], refs[-2], refs[-1]
    copies = []
    for i, piece in enumerate(pieces):
        r, j = i // CHUNKS, i % CHUNKS
        begin = (info[0] ^ r) * (HQ * VDIM) + j * HC * VDIM
        begin = pl.multiple_of(begin, 128)
        copies.append(
            pltpu.make_async_copy(piece, out.at[:, pl.ds(begin, HC * VDIM)], sems.at[i])
        )
    for copy in copies:
        copy.start()
    for copy in copies:
        copy.wait()


def shape(dims, kind=jnp.bfloat16):
    return jax.ShapeDtypeStruct(dims, kind)


def body(q_heads, kv_latent, latent_gain, w_up, page_ranks, lengths):
    tok = q_heads.shape[0]
    size = lax.axis_size("ctx")
    groups = lax.axis_size("groups")
    mine = lax.axis_index("ctx")
    quarter = lax.axis_index("groups") * 2 + mine % 2
    slot_count = max(2, 2 * tok // size)
    smem = pl.BlockSpec(memory_space=SMEM)
    whole = pl.BlockSpec(memory_space=VMEM)
    params = pltpu.CompilerParams(vmem_limit_bytes=VMEM_LIMIT)

    def quad_swap(array, r):
        dx, dc = r // 2, r % 2
        pairs = [
            (g * size + i, (g ^ dx) * size + (i ^ dc)) for g in range(groups) for i in range(size)
        ]
        return lax.ppermute(array, ("groups", "ctx"), pairs)

    def from_behind(array, by, odd_only):
        first = 1 if odd_only else 0
        step = 2 if odd_only else 1
        pairs = [(i, i + by) for i in range(first, size - by, step)]
        return lax.ppermute(array, "ctx", pairs)

    width = HQ * (NOPE + VDIM)
    keep = lax.dynamic_slice_in_dim(w_up, quarter * width, width, 1)
    give = lax.dynamic_slice_in_dim(w_up, (quarter ^ 1) * width, width, 1)
    got = quad_swap(give, 1)
    even = mine % 2 == 0
    pair_rows = jnp.concatenate(
        [jnp.where(even, keep, got), jnp.where(even, got, keep)], axis=0
    )
    same_core = [list(range(c, size, 2)) for c in range(2)]
    part = width // CHUNKS
    weights = [
        lax.all_gather(
            pair_rows[:, j * part : (j + 1) * part],
            "ctx",
            axis=0,
            tiled=True,
            axis_index_groups=same_core,
        )
        for j in range(CHUNKS)
    ]

    frequency = np.exp(-np.arange(ROPE // 2) * (2.0 * math.log(10000.0) / ROPE))
    frequency = jnp.asarray(np.tile(frequency, 4)[None, :], jnp.float32)
    info = jnp.concatenate([mine[None].astype(jnp.int32), lengths.astype(jnp.int32)])
    rows, cosine, sine, outgoing = pl.pallas_call(
        functools.partial(rows_kernel, slot_count),
        out_shape=(
            shape((tok, EXT)),
            shape((tok, 128), jnp.float32),
            shape((tok, 128), jnp.float32),
            shape((size * slot_count, ROW)),
        ),
        in_specs=[smem] + [whole] * 4,
        out_specs=[whole] * 4,
        compiler_params=params,
        name="rows",
    )(info, kv_latent, latent_gain[None, :], page_ranks, frequency)

    quarter_info = quarter[None].astype(jnp.int32)
    queries = pl.pallas_call(
        query_kernel,
        out_shape=[shape((tok, HC * (NOPE + ROPE)))] * (QUAD * CHUNKS),
        in_specs=[smem] + [whole] * 3,
        out_specs=[whole] * (QUAD * CHUNKS),
        compiler_params=params,
        name="queries",
    )(quarter_info, q_heads, cosine, sine)

    both_groups = jnp.concatenate([rows, quad_swap(rows, 2)], axis=0)
    behind = from_behind(both_groups, 2, False)
    far_behind = from_behind(both_groups, 4, True)
    own_rows = jnp.concatenate([both_groups, behind, far_behind], axis=0)
    other_rows = quad_swap(own_rows, 1)

    moved = [
        [
            queries[r * CHUNKS + j] if r == 0 else quad_swap(queries[r * CHUNKS + j], r)
            for r in range(QUAD)
        ]
        for j in range(CHUNKS)
    ]

    arrived = lax.all_to_all(
        outgoing.reshape(size, slot_count, ROW), "ctx", split_axis=0, concat_axis=0, tiled=True
    )
    decode_cache = arrived.reshape(size * slot_count, ROW)

    mine_info = mine[None].astype(jnp.int32)
    window = (REACH + 2) * tok
    flops = 2 * HC * 2 * (window * LAT * 256 + 2 * tok * window * (NOPE + ROPE + VDIM))
    attend = pl.pallas_call(
        attend_kernel,
        grid=(HC // 2,),
        out_shape=[shape((tok, HC * VDIM))] * QUAD,
        in_specs=[
            smem,
            pl.BlockSpec((6 * tok, EXT), lambda i: (0, 0)),
            pl.BlockSpec((6 * tok, EXT), lambda i: (0, 0)),
            pl.BlockSpec((LAT, 512), lambda i: (0, i)),
        ]
        + [pl.BlockSpec((tok, 256), lambda i: (0, i))] * QUAD
        + [pl.BlockSpec((tok, 128), lambda i: (0, HC + i))] * QUAD,
        out_specs=[pl.BlockSpec((tok, 256), lambda i: (0, i))] * QUAD,
        scratch_shapes=[
            VMEM((2, window, LAT), jnp.bfloat16),
            VMEM((2, window, 128), jnp.bfloat16),
            VMEM((2, window, 128), jnp.bfloat16),
            VMEM((2, 2 * tok, window), jnp.float32),
        ],
        compiler_params=params,
        cost_estimate=pl.CostEstimate(
            flops=flops, bytes_accessed=8 << 20, transcendentals=HC * 4 * tok * window
        ),
        name="attend",
    )
    results = [
        attend(mine_info, own_rows, other_rows, weights[j], *moved[j], *moved[j])
        for j in range(CHUNKS)
    ]
    pieces = [
        results[j][r] if r == 0 else quad_swap(results[j][r], r)
        for r in range(QUAD)
        for j in range(CHUNKS)
    ]
    anywhere = pl.BlockSpec(memory_space=pl.ANY)
    attn_out = pl.pallas_call(
        gather_kernel,
        out_shape=shape((tok, H * VDIM)),
        in_specs=[smem] + [anywhere] * len(pieces),
        out_specs=anywhere,
        scratch_shapes=[pltpu.SemaphoreType.DMA((len(pieces),))],
        compiler_params=params,
        name="place",
    )(quarter_info, *pieces)
    return (attn_out, decode_cache)


def solution(mesh):
    return jax.shard_map(
        body,
        mesh=mesh,
        in_specs=(
            P(("groups", "ctx"), None),
            P(("groups", "ctx"), None),
            P(),
            P("ctx", None),
            P(("groups", "ctx"), None),
            P("groups"),
        ),
        out_specs=(P(("groups", "ctx"), None), P(("groups", "ctx"), None)),
        check_vma=False,
    )
```

```python
import functools
import math

import jax
import jax.numpy as jnp
import numpy as np
from jax import lax
from jax.experimental import pallas as pl
from jax.experimental.pallas import tpu as pltpu
from jax.sharding import PartitionSpec as P

H = 64
NOPE = 128
ROPE = 64
VDIM = 128
LAT = 512
REACH = 3
QUAD = 4
HQ = H // QUAD
CHUNK_HEADS = (8, 4, 4)
CHUNKS = len(CHUNK_HEADS)
FIRST_HEAD = tuple(sum(CHUNK_HEADS[:j]) for j in range(CHUNKS))
ROW = LAT + ROPE
EXT = 640
VMEM_LIMIT = 48 * 1024 * 1024
SMEM = pltpu.SMEM
VMEM = pltpu.VMEM


def rows_kernel(slot_count, info, kv, gain, ranks, freq, rows_out, cos_out, sin_out, outgoing_out):
    tok = kv.shape[0]
    base = info[0] * tok
    spots = base + lax.broadcasted_iota(jnp.int32, (tok, 128), 0)
    lane = lax.broadcasted_iota(jnp.int32, (tok, 128), 1)
    begin = jnp.int32(0)
    own_start = jnp.zeros((tok, 128), jnp.int32)
    for r in range(info.shape[0] - 1):
        own_start = jnp.where(spots >= begin, begin, own_start)
        begin = begin + info[1 + r]
    offset = spots - own_start
    angles = offset.astype(jnp.float32) * freq[...]
    cosine = jnp.cos(angles)
    sine = jnp.where((lane & 32) == 0, -jnp.sin(angles), jnp.sin(angles))
    cos_out[...] = cosine
    sin_out[...] = sine
    raw = kv[...].astype(jnp.float32)
    latent = raw[:, :LAT]
    mean = jnp.sum(latent * latent, axis=1, keepdims=True) * (1.0 / LAT)
    latent = latent * lax.rsqrt(mean + 1e-06) * gain[...]
    key = raw[:, LAT:]
    swapped = jnp.concatenate([key[:, ROPE // 2 :], key[:, : ROPE // 2]], axis=1)
    turned = key * cosine[:, :ROPE] + swapped * sine[:, :ROPE]
    high = (offset >> 8).astype(jnp.float32)
    low = (offset & 255).astype(jnp.float32)
    meta = jnp.where(lane == 0, high, jnp.where(lane == 1, low, 0.0))
    tail = jnp.concatenate([turned, meta[:, :ROPE]], axis=1)
    rows_out[:, :LAT] = latent.astype(jnp.bfloat16)
    rows_out[:, LAT:] = tail.astype(jnp.bfloat16)

    rank_col = jnp.broadcast_to(ranks[...], (tok, tok)).astype(jnp.float32)
    rank_row = rank_col.T
    earlier = lax.broadcasted_iota(jnp.int32, (tok, tok), 0) < lax.broadcasted_iota(
        jnp.int32, (tok, tok), 1
    )
    same = jnp.where((rank_col == rank_row) & earlier, 1.0, 0.0)
    slot = jnp.sum(same, axis=0, keepdims=True)
    target = (rank_row[:1] * slot_count + slot).astype(jnp.int32)
    spots_out = lax.broadcasted_iota(jnp.int32, (outgoing_out.shape[0], tok), 0)
    selector = jnp.where(spots_out == target, 1.0, 0.0).astype(jnp.bfloat16)
    picked = jnp.dot(selector, rows_out[:, :ROW], preferred_element_type=jnp.float32)
    outgoing_out[...] = picked.astype(jnp.bfloat16)


def query_kernel(info, query, cosine, sine, *outs):
    tok = query.shape[0]
    lane = lax.broadcasted_iota(jnp.int32, (tok, 128), 1)
    low_half = lane < 64
    first_quarter = (lane & 32) == 0
    cos_table = cosine[...]
    sin_table = sine[...]
    for r in range(QUAD):
        first = (info[0] ^ r) * (HQ * (NOPE + ROPE))
        for pair in range(HQ // 2):
            j = max(j for j in range(CHUNKS) if FIRST_HEAD[j] <= 2 * pair)
            out = outs[r * CHUNKS + j]
            at = pair - FIRST_HEAD[j] // 2
            rope_at = CHUNK_HEADS[j] * NOPE + at * 128
            begin = pl.multiple_of(first + pair * 2 * (NOPE + ROPE), 128)
            both = query[:, pl.ds(begin, 2 * (NOPE + ROPE))]
            mid = both[:, 128:256].astype(jnp.float32)
            end = both[:, 256:384].astype(jnp.float32)
            turned = jnp.where(low_half, mid, end)
            odd_nope = pltpu.roll(jnp.where(low_half, end, mid), 64, 1)
            swapped = jnp.where(
                first_quarter, pltpu.roll(turned, 96, 1), pltpu.roll(turned, 32, 1)
            )
            turned = turned * cos_table + swapped * sin_table
            out[:, at * 256 : at * 256 + 128] = both[:, :128]
            out[:, at * 256 + 128 : at * 256 + 256] = odd_nope.astype(jnp.bfloat16)
            out[:, rope_at : rope_at + 128] = turned.astype(jnp.bfloat16)


def pair_kernel(info, w_up, got, *refs):
    outs, sems = refs[:-1], refs[-1]
    rows = got.shape[0]
    copies = []
    for j, out in enumerate(outs):
        width = out.shape[1]
        first = FIRST_HEAD[j] * (NOPE + VDIM)
        begin = pl.multiple_of(info[0] * (HQ * (NOPE + VDIM)) + first, 128)
        copies.append(
            pltpu.make_async_copy(
                w_up.at[:, pl.ds(begin, width)], out.at[pl.ds(0, rows)], sems.at[2 * j]
            )
        )
        copies.append(
            pltpu.make_async_copy(
                got.at[:, pl.ds(first, width)], out.at[pl.ds(rows, rows)], sems.at[2 * j + 1]
            )
        )
    for copy in copies:
        copy.start()
    for copy in copies:
        copy.wait()


def attend_kernel(outer, info, own, other, *refs):
    pieces_count = 2 * outer if outer else 1
    pieces_of_weight, refs = refs[:pieces_count], refs[pieces_count:]
    nope = refs[0:QUAD]
    rope = refs[QUAD : 2 * QUAD]
    outs = refs[2 * QUAD : 3 * QUAD]
    latent, rope_even, rope_odd, bias, held = refs[3 * QUAD :]
    tok = nope[0].shape[0]
    blocks = REACH + 2
    mine = info[0]
    partner = mine ^ 1
    scale = (NOPE + ROPE) ** (-0.5) * math.log2(math.e)

    @pl.when(pl.program_id(0) == 0)
    def _():
        has_last = (mine & 1) == 1
        starts = [mine, partner, mine - 2, partner - 2, (mine >> 1) * 2 - 3]
        blank = jnp.zeros((tok, ROPE), jnp.bfloat16)
        lane = lax.broadcasted_iota(jnp.int32, (tok, tok), 1)
        row = lax.broadcasted_iota(jnp.int32, (tok, tok), 0)
        for g in range(2):
            pieces = [
                own[g * tok : (g + 1) * tok],
                other[g * tok : (g + 1) * tok],
                own[(2 + g) * tok : (3 + g) * tok],
                other[(2 + g) * tok : (3 + g) * tok],
                jnp.where(
                    has_last,
                    own[(4 + g) * tok : (5 + g) * tok],
                    other[(4 + g) * tok : (5 + g) * tok],
                ),
            ]
            for b, piece in enumerate(pieces):
                here = slice(b * tok, (b + 1) * tok)
                latent[g, here] = piece[:, :LAT]
                turned = piece[:, LAT : LAT + ROPE]
                rope_even[g, here] = jnp.concatenate([turned, blank], axis=1)
                rope_odd[g, here] = jnp.concatenate([blank, turned], axis=1)
            for half in range(2):
                meta = pieces[half][:, LAT:].astype(jnp.float32)
                offset = (meta[:, ROPE : ROPE + 1] * 256.0 + meta[:, ROPE + 1 : ROPE + 2]).astype(
                    jnp.int32
                )
                spots = starts[half] * tok + row
                lowest = jnp.maximum(spots - offset, (starts[half] - REACH) * tok)
                for b in range(blocks):
                    keys = starts[b] * tok + lane
                    allowed = (keys >= lowest) & (keys <= spots)
                    bias[g, half * tok : (half + 1) * tok, b * tok : (b + 1) * tok] = jnp.where(
                        allowed, 0.0, -1e30
                    )

    if outer:
        weight = held
        for i, piece in enumerate(pieces_of_weight):
            side, behind = i // outer, i % outer
            chip = ((mine >> 2) + outer - behind) % outer * 2 + (((mine >> 1) & 1) ^ side)
            rows = piece.shape[0] // 2
            for core in range(2):
                begin = pl.multiple_of(chip * 2 * rows + ((mine & 1) ^ core) * rows, rows)
                held[pl.ds(begin, rows)] = piece[core * rows : (core + 1) * rows]
    else:
        weight = pieces_of_weight[0]

    for g in range(2):
        expanded = jnp.dot(latent[g], weight[...], preferred_element_type=jnp.float32).astype(
            jnp.bfloat16
        )
        query_rope = jnp.concatenate([rope[2 * g][...], rope[2 * g + 1][...]], axis=0)
        for b in range(2):
            at = slice(b * 128, (b + 1) * 128)
            key_rope = (rope_even, rope_odd)[b][g]
            key = jnp.concatenate([expanded[:, b * 256 : b * 256 + 128], key_rope], axis=1)
            value = expanded[:, b * 256 + 128 : b * 256 + 256]
            query = jnp.concatenate([nope[2 * g][:, at], nope[2 * g + 1][:, at]], axis=0)
            query = jnp.concatenate([query, query_rope], axis=1)
            scores = lax.dot_general(
                query, key, (((1,), (1,)), ((), ())), preferred_element_type=jnp.float32
            )
            scores = scores * scale + bias[g]
            largest = jnp.max(scores, axis=1, keepdims=True)
            expo = jnp.exp2(scores - largest)
            total = jnp.sum(expo, axis=1, keepdims=True)
            mixed = jnp.dot(expo.astype(jnp.bfloat16), value, preferred_element_type=jnp.float32)
            mixed = (mixed / total).astype(jnp.bfloat16)
            outs[2 * g][:, at] = mixed[:tok]
            outs[2 * g + 1][:, at] = mixed[tok:]


def gather_kernel(info, *refs):
    pieces, out, sems = refs[:-2], refs[-2], refs[-1]
    copies = []
    for i, piece in enumerate(pieces):
        r, j = i // CHUNKS, i % CHUNKS
        begin = (info[0] ^ r) * (HQ * VDIM) + FIRST_HEAD[j] * VDIM
        begin = pl.multiple_of(begin, 128)
        copies.append(
            pltpu.make_async_copy(piece, out.at[:, pl.ds(begin, piece.shape[1])], sems.at[i])
        )
    for copy in copies:
        copy.start()
    for copy in copies:
        copy.wait()


class Stream:
    def __init__(self, window):
        self.window = window
        self.arrived = []

    def after(self, array):
        if len(self.arrived) < self.window:
            return array
        return lax.optimization_barrier((array, self.arrived[-self.window]))[0]

    def send(self, permute, array, *args):
        self.arrived.append(permute(self.after(array), *args))
        return self.arrived[-1]


def shape(dims, kind=jnp.bfloat16):
    return jax.ShapeDtypeStruct(dims, kind)


def body(q_heads, kv_latent, latent_gain, w_up, page_ranks, lengths):
    tok = q_heads.shape[0]
    size = lax.axis_size("ctx")
    groups = lax.axis_size("groups")
    mine = lax.axis_index("ctx")
    quarter = lax.axis_index("groups") * 2 + mine % 2
    slot_count = max(2, 2 * tok // size)
    smem = pl.BlockSpec(memory_space=SMEM)
    whole = pl.BlockSpec(memory_space=VMEM)
    params = pltpu.CompilerParams(vmem_limit_bytes=VMEM_LIMIT)

    def quad_swap(array, r):
        dx, dc = r // 2, r % 2
        pairs = [
            (g * size + i, (g ^ dx) * size + (i ^ dc)) for g in range(groups) for i in range(size)
        ]
        return lax.ppermute(array, ("groups", "ctx"), pairs)

    def send_in_quad(array, r):
        return quad_swap(array, r) if r == 1 else group_stream.send(quad_swap, array, r)

    def around(array, by):
        return lax.ppermute(array, "ctx", [(i, (i + by) % size) for i in range(size)])

    def inner_swap(array):
        return lax.ppermute(array, "ctx", [(i, i ^ 2) for i in range(size)])

    def from_behind(array, by, odd_only):
        first = 1 if odd_only else 0
        step = 2 if odd_only else 1
        pairs = [(i, i + by) for i in range(first, size - by, step)]
        return lax.ppermute(array, "ctx", pairs)

    outer_stream, inner_stream, group_stream = Stream(3), Stream(2), Stream(2)

    width = HQ * (NOPE + VDIM)
    quarter_info = quarter[None].astype(jnp.int32)
    anywhere = pl.BlockSpec(memory_space=pl.ANY)
    give = lax.dynamic_slice_in_dim(w_up, (quarter ^ 1) * width, width, 1)
    got = quad_swap(give, 1)
    widths = [heads * (NOPE + VDIM) for heads in CHUNK_HEADS]
    outer = size // 4 if size % 4 == 0 and size // 4 <= 4 else 0
    if outer:
        pairs_of_rows = pl.pallas_call(
            pair_kernel,
            out_shape=[shape((2 * w_up.shape[0], w)) for w in widths],
            in_specs=[smem, anywhere, anywhere],
            out_specs=[anywhere] * CHUNKS,
            scratch_shapes=[pltpu.SemaphoreType.DMA((2 * CHUNKS,))],
            compiler_params=params,
            name="pair",
        )(quarter_info, w_up, got)
        weights = []
        for piece in pairs_of_rows:
            line = [piece] + [outer_stream.send(around, piece, 4 * k) for k in range(1, outer)]
            weights.append(line + [inner_stream.send(inner_swap, one) for one in line])
    else:
        keep = lax.dynamic_slice_in_dim(w_up, quarter * width, width, 1)
        even = mine % 2 == 0
        both = jnp.concatenate(
            [jnp.where(even, keep, got), jnp.where(even, got, keep)], axis=0
        )
        same_core = [list(range(c, size, 2)) for c in range(2)]
        weights = [
            [
                lax.all_gather(
                    both[:, FIRST_HEAD[j] * 256 : FIRST_HEAD[j] * 256 + widths[j]],
                    "ctx",
                    axis=0,
                    tiled=True,
                    axis_index_groups=same_core,
                )
            ]
            for j in range(CHUNKS)
        ]

    frequency = np.exp(-np.arange(ROPE // 2) * (2.0 * math.log(10000.0) / ROPE))
    frequency = jnp.asarray(np.tile(frequency, 4)[None, :], jnp.float32)
    info = jnp.concatenate([mine[None].astype(jnp.int32), lengths.astype(jnp.int32)])
    rows, cosine, sine, outgoing = pl.pallas_call(
        functools.partial(rows_kernel, slot_count),
        out_shape=(
            shape((tok, EXT)),
            shape((tok, 128), jnp.float32),
            shape((tok, 128), jnp.float32),
            shape((size * slot_count, ROW)),
        ),
        in_specs=[smem] + [whole] * 4,
        out_specs=[whole] * 4,
        compiler_params=params,
        name="rows",
    )(info, kv_latent, latent_gain[None, :], page_ranks, frequency)

    queries = pl.pallas_call(
        query_kernel,
        out_shape=[shape((tok, h * (NOPE + ROPE))) for h in CHUNK_HEADS] * QUAD,
        in_specs=[smem] + [whole] * 3,
        out_specs=[whole] * (QUAD * CHUNKS),
        compiler_params=params,
        name="queries",
    )(quarter_info, q_heads, cosine, sine)

    both_groups = jnp.concatenate([rows, group_stream.send(quad_swap, rows, 2)], axis=0)
    behind = from_behind(both_groups, 2, False)
    far_behind = from_behind(both_groups, 4, True)
    own_rows = jnp.concatenate([both_groups, behind, far_behind], axis=0)
    other_rows = quad_swap(own_rows, 1)

    moved = [
        [
            queries[r * CHUNKS + j] if r == 0 else send_in_quad(queries[r * CHUNKS + j], r)
            for r in range(QUAD)
        ]
        for j in range(CHUNKS)
    ]

    outgoing = lax.optimization_barrier((outgoing, moved[0][2]))[0]
    arrived = lax.all_to_all(
        outgoing.reshape(size, slot_count, ROW), "ctx", split_axis=0, concat_axis=0, tiled=True
    )
    decode_cache = arrived.reshape(size * slot_count, ROW)

    mine_info = mine[None].astype(jnp.int32)
    mine_info, decode_cache = lax.optimization_barrier((mine_info, decode_cache))
    window = (REACH + 2) * tok

    def attend(j):
        heads = CHUNK_HEADS[j]
        steps = heads // 2
        flops = 2 * heads * 2 * (window * LAT * 256 + 2 * tok * window * (NOPE + ROPE + VDIM))
        return pl.pallas_call(
            functools.partial(attend_kernel, outer),
            grid=(steps,),
            out_shape=[shape((tok, heads * VDIM))] * QUAD,
            in_specs=[
                smem,
                pl.BlockSpec((6 * tok, EXT), lambda i: (0, 0)),
                pl.BlockSpec((6 * tok, EXT), lambda i: (0, 0)),
            ]
            + [pl.BlockSpec((piece.shape[0], 512), lambda i: (0, i)) for piece in weights[j]]
            + [pl.BlockSpec((tok, 256), lambda i: (0, i))] * QUAD
            + [pl.BlockSpec((tok, 128), lambda i: (0, heads + i))] * QUAD,
            out_specs=[pl.BlockSpec((tok, 256), lambda i: (0, i))] * QUAD,
            scratch_shapes=[
                VMEM((2, window, LAT), jnp.bfloat16),
                VMEM((2, window, 128), jnp.bfloat16),
                VMEM((2, window, 128), jnp.bfloat16),
                VMEM((2, 2 * tok, window), jnp.float32),
                VMEM((LAT, 512), jnp.bfloat16),
            ],
            compiler_params=params,
            cost_estimate=pl.CostEstimate(
                flops=flops,
                bytes_accessed=heads << 20,
                transcendentals=heads * 4 * tok * window,
            ),
            name="attend",
        )(mine_info, own_rows, other_rows, *weights[j], *moved[j], *moved[j])

    results = []
    for j in range(CHUNKS):
        parts = attend(j)
        results.append([parts[0]] + [send_in_quad(parts[r], r) for r in range(1, QUAD)])
    pieces = [results[j][r] for r in range(QUAD) for j in range(CHUNKS)]
    attn_out = pl.pallas_call(
        gather_kernel,
        out_shape=shape((tok, H * VDIM)),
        in_specs=[smem] + [anywhere] * len(pieces),
        out_specs=anywhere,
        scratch_shapes=[pltpu.SemaphoreType.DMA((len(pieces),))],
        compiler_params=params,
        name="place",
    )(quarter_info, *pieces)
    return (attn_out, decode_cache)


def solution(mesh):
    return jax.shard_map(
        body,
        mesh=mesh,
        in_specs=(
            P(("groups", "ctx"), None),
            P(("groups", "ctx"), None),
            P(),
            P("ctx", None),
            P(("groups", "ctx"), None),
            P("groups"),
        ),
        out_specs=(P(("groups", "ctx"), None), P(("groups", "ctx"), None)),
        check_vma=False,
    )
```

```python
import functools
import math

import jax
import jax.numpy as jnp
import numpy as np
from jax import lax
from jax.experimental import pallas as pl
from jax.experimental.pallas import tpu as pltpu
from jax.sharding import PartitionSpec as P

H = 64
NOPE = 128
ROPE = 64
VDIM = 128
LAT = 512
REACH = 3
QUAD = 4
HQ = H // QUAD
CHUNK_HEADS = (4, 4, 4, 4)
CHUNKS = len(CHUNK_HEADS)
FIRST_HEAD = tuple(sum(CHUNK_HEADS[:j]) for j in range(CHUNKS))
ROW = LAT + ROPE
EXT = 640
VMEM_LIMIT = 48 * 1024 * 1024
SMEM = pltpu.SMEM
VMEM = pltpu.VMEM


def rows_kernel(slot_count, info, kv, gain, ranks, freq, rows_out, cos_out, sin_out, outgoing_out):
    tok = kv.shape[0]
    base = info[0] * tok
    spots = base + lax.broadcasted_iota(jnp.int32, (tok, 128), 0)
    lane = lax.broadcasted_iota(jnp.int32, (tok, 128), 1)
    begin = jnp.int32(0)
    own_start = jnp.zeros((tok, 128), jnp.int32)
    for r in range(info.shape[0] - 1):
        own_start = jnp.where(spots >= begin, begin, own_start)
        begin = begin + info[1 + r]
    offset = spots - own_start
    angles = offset.astype(jnp.float32) * freq[...]
    cosine = jnp.cos(angles)
    sine = jnp.where((lane & 32) == 0, -jnp.sin(angles), jnp.sin(angles))
    cos_out[...] = cosine
    sin_out[...] = sine
    raw = kv[...].astype(jnp.float32)
    latent = raw[:, :LAT]
    mean = jnp.sum(latent * latent, axis=1, keepdims=True) * (1.0 / LAT)
    latent = latent * lax.rsqrt(mean + 1e-06) * gain[...]
    key = raw[:, LAT:]
    swapped = jnp.concatenate([key[:, ROPE // 2 :], key[:, : ROPE // 2]], axis=1)
    turned = key * cosine[:, :ROPE] + swapped * sine[:, :ROPE]
    high = (offset >> 8).astype(jnp.float32)
    low = (offset & 255).astype(jnp.float32)
    meta = jnp.where(lane == 0, high, jnp.where(lane == 1, low, 0.0))
    tail = jnp.concatenate([turned, meta[:, :ROPE]], axis=1)
    rows_out[:, :LAT] = latent.astype(jnp.bfloat16)
    rows_out[:, LAT:] = tail.astype(jnp.bfloat16)

    rank_col = jnp.broadcast_to(ranks[...], (tok, tok)).astype(jnp.float32)
    rank_row = rank_col.T
    earlier = lax.broadcasted_iota(jnp.int32, (tok, tok), 0) < lax.broadcasted_iota(
        jnp.int32, (tok, tok), 1
    )
    same = jnp.where((rank_col == rank_row) & earlier, 1.0, 0.0)
    slot = jnp.sum(same, axis=0, keepdims=True)
    target = (rank_row[:1] * slot_count + slot).astype(jnp.int32)
    spots_out = lax.broadcasted_iota(jnp.int32, (outgoing_out.shape[0], tok), 0)
    selector = jnp.where(spots_out == target, 1.0, 0.0).astype(jnp.bfloat16)
    picked = jnp.dot(selector, rows_out[:, :ROW], preferred_element_type=jnp.float32)
    outgoing_out[...] = picked.astype(jnp.bfloat16)


def query_kernel(query, cosine, sine, *outs):
    tok = query.shape[0]
    lane = lax.broadcasted_iota(jnp.int32, (tok, 128), 1)
    low_half = lane < 64
    first_quarter = (lane & 32) == 0
    cos_table = cosine[...]
    sin_table = sine[...]
    for member in range(QUAD):
        for pair in range(HQ // 2):
            j = max(j for j in range(CHUNKS) if FIRST_HEAD[j] <= 2 * pair)
            out = outs[j]
            at = pair - FIRST_HEAD[j] // 2
            rope_at = CHUNK_HEADS[j] * NOPE + at * 128
            begin = (member * HQ + pair * 2) * (NOPE + ROPE)
            both = query[:, begin : begin + 2 * (NOPE + ROPE)]
            mid = both[:, 128:256].astype(jnp.float32)
            end = both[:, 256:384].astype(jnp.float32)
            turned = jnp.where(low_half, mid, end)
            odd_nope = pltpu.roll(jnp.where(low_half, end, mid), 64, 1)
            swapped = jnp.where(
                first_quarter, pltpu.roll(turned, 96, 1), pltpu.roll(turned, 32, 1)
            )
            turned = turned * cos_table + swapped * sin_table
            out[member, :, at * 256 : at * 256 + 128] = both[:, :128]
            out[member, :, at * 256 + 128 : at * 256 + 256] = odd_nope.astype(jnp.bfloat16)
            out[member, :, rope_at : rope_at + 128] = turned.astype(jnp.bfloat16)


def spread_kernel(outer, info, w_up, *refs):
    outs, sem = refs[:-1], refs[-1]
    rows = w_up.shape[0]
    copies = []
    for j, out in enumerate(outs):
        width = out.shape[1]
        for core in range(2):
            begin = (info[1] * 2 + core) * (HQ * (NOPE + VDIM)) + FIRST_HEAD[j] * (NOPE + VDIM)
            begin = pl.multiple_of(begin, 128)
            for place in range(outer):
                copies.append(
                    pltpu.make_async_copy(
                        w_up.at[:, pl.ds(begin, width)],
                        out.at[pl.ds((place * 2 + core) * rows, rows)],
                        sem.at[len(copies)],
                    )
                )
    for copy in copies:
        copy.start()
    for copy in copies:
        copy.wait()


def attend_kernel(outer, info, own, other, *refs):
    count = 2 if outer else 1
    pieces_of_weight, refs = refs[:count], refs[count:]
    nope, rope, out, latent, rope_even, rope_odd, bias, held = refs
    tok = nope.shape[1]
    blocks = REACH + 2
    mine = info[0]
    group = info[1]
    partner = mine ^ 1
    scale = (NOPE + ROPE) ** (-0.5) * math.log2(math.e)

    @pl.when(pl.program_id(0) == 0)
    def _():
        has_last = (mine & 1) == 1
        starts = [mine, partner, mine - 2, partner - 2, (mine >> 1) * 2 - 3]
        blank = jnp.zeros((tok, ROPE), jnp.bfloat16)
        lane = lax.broadcasted_iota(jnp.int32, (tok, tok), 1)
        row = lax.broadcasted_iota(jnp.int32, (tok, tok), 0)
        for g in range(2):
            pieces = [
                own[g * tok : (g + 1) * tok],
                other[g * tok : (g + 1) * tok],
                own[(2 + g) * tok : (3 + g) * tok],
                other[(2 + g) * tok : (3 + g) * tok],
                jnp.where(
                    has_last,
                    own[(4 + g) * tok : (5 + g) * tok],
                    other[(4 + g) * tok : (5 + g) * tok],
                ),
            ]
            for b, piece in enumerate(pieces):
                here = slice(b * tok, (b + 1) * tok)
                latent[g, here] = piece[:, :LAT]
                turned = piece[:, LAT : LAT + ROPE]
                rope_even[g, here] = jnp.concatenate([turned, blank], axis=1)
                rope_odd[g, here] = jnp.concatenate([blank, turned], axis=1)
            for half in range(2):
                meta = jnp.where((mine & 1) == half, pieces[0][:, LAT:], pieces[1][:, LAT:])
                meta = meta.astype(jnp.float32)
                block = (mine >> 1) * 2 + half
                offset = (meta[:, ROPE : ROPE + 1] * 256.0 + meta[:, ROPE + 1 : ROPE + 2]).astype(
                    jnp.int32
                )
                spots = block * tok + row
                lowest = jnp.maximum(spots - offset, (block - REACH) * tok)
                for b in range(blocks):
                    keys = starts[b] * tok + lane
                    allowed = (keys >= lowest) & (keys <= spots)
                    bias[g, half * tok : (half + 1) * tok, b * tok : (b + 1) * tok] = jnp.where(
                        allowed, 0.0, -1e30
                    )

    if outer:
        weight = held
        for side, piece in enumerate(pieces_of_weight):
            rows = piece.shape[0] // outer
            for place in range(outer):
                chip = place * 2 + (((mine >> 1) & 1) ^ side)
                begin = pl.multiple_of(chip * rows, rows)
                held[pl.ds(begin, rows)] = piece[place * rows : (place + 1) * rows]
    else:
        weight = pieces_of_weight[0]

    for g in range(2):
        expanded = jnp.dot(latent[g], weight[...], preferred_element_type=jnp.float32).astype(
            jnp.bfloat16
        )
        first = (group ^ g) * 2
        query_rope = jnp.concatenate([rope[first], rope[first + 1]], axis=0)
        for b in range(2):
            at = slice(b * 128, (b + 1) * 128)
            key_rope = (rope_even, rope_odd)[b][g]
            key = jnp.concatenate([expanded[:, b * 256 : b * 256 + 128], key_rope], axis=1)
            value = expanded[:, b * 256 + 128 : b * 256 + 256]
            query = jnp.concatenate([nope[first, :, at], nope[first + 1, :, at]], axis=0)
            query = jnp.concatenate([query, query_rope], axis=1)
            scores = lax.dot_general(
                query, key, (((1,), (1,)), ((), ())), preferred_element_type=jnp.float32
            )
            scores = scores * scale + bias[g]
            largest = jnp.max(scores, axis=1, keepdims=True)
            expo = jnp.exp2(scores - largest)
            total = jnp.sum(expo, axis=1, keepdims=True)
            mixed = jnp.dot(expo.astype(jnp.bfloat16), value, preferred_element_type=jnp.float32)
            mixed = (mixed / total).astype(jnp.bfloat16)
            out[first, :, at] = mixed[:tok]
            out[first + 1, :, at] = mixed[tok:]


def place_kernel(*refs):
    pieces, out, sem = refs[:-2], refs[-2], refs[-1]
    copies = []
    for j, piece in enumerate(pieces):
        for member in range(QUAD):
            begin = (member * HQ + FIRST_HEAD[j]) * VDIM
            copies.append(
                pltpu.make_async_copy(
                    piece.at[member],
                    out.at[:, pl.ds(begin, piece.shape[2])],
                    sem.at[len(copies)],
                )
            )
    for copy in copies:
        copy.start()
    for copy in copies:
        copy.wait()


class Stream:
    def __init__(self, window):
        self.window = window
        self.arrived = []

    def after(self, array):
        if len(self.arrived) < self.window:
            return array
        return lax.optimization_barrier((array, self.arrived[-self.window]))[0]

    def send(self, permute, array, *args):
        self.arrived.append(permute(self.after(array), *args))
        return self.arrived[-1]


def shape(dims, kind=jnp.bfloat16):
    return jax.ShapeDtypeStruct(dims, kind)


def body(q_heads, kv_latent, latent_gain, w_up, page_ranks, lengths):
    tok = q_heads.shape[0]
    size = lax.axis_size("ctx")
    groups = lax.axis_size("groups")
    mine = lax.axis_index("ctx")
    group = lax.axis_index("groups")
    slot_count = max(2, 2 * tok // size)
    smem = pl.BlockSpec(memory_space=SMEM)
    whole = pl.BlockSpec(memory_space=VMEM)
    params = pltpu.CompilerParams(vmem_limit_bytes=VMEM_LIMIT)

    def quad_swap(array, r):
        dx, dc = r // 2, r % 2
        pairs = [
            (g * size + i, (g ^ dx) * size + (i ^ dc)) for g in range(groups) for i in range(size)
        ]
        return lax.ppermute(array, ("groups", "ctx"), pairs)

    quads = [
        [g * size + chip * 2 + c for g in range(groups) for c in range(2)]
        for chip in range(size // 2)
    ]

    def deal(array):
        return lax.all_to_all(
            array, ("groups", "ctx"), 0, 0, axis_index_groups=quads, tiled=True
        )

    def inner_swap(array):
        return lax.ppermute(array, "ctx", [(i, i ^ 2) for i in range(size)])

    def from_behind(array, by, odd_only):
        first = 1 if odd_only else 0
        step = 2 if odd_only else 1
        pairs = [(i, i + by) for i in range(first, size - by, step)]
        return lax.ppermute(array, "ctx", pairs)

    outer_stream, inner_stream, group_stream = Stream(2), Stream(2), Stream(2)
    anywhere = pl.BlockSpec(memory_space=pl.ANY)
    place_info = jnp.stack([mine, group]).astype(jnp.int32)

    width = HQ * (NOPE + VDIM)
    widths = [heads * (NOPE + VDIM) for heads in CHUNK_HEADS]
    outer = size // 4 if size % 4 == 0 and size // 4 <= 4 else 0
    weights = []
    if outer:
        lines = [
            [(z * 2 + y) * 2 + c for z in range(outer) for c in range(2)] for y in range(2)
        ]

        def along(array):
            return lax.all_to_all(array, "ctx", 0, 0, axis_index_groups=lines, tiled=True)

        spread = pl.pallas_call(
            functools.partial(spread_kernel, outer),
            out_shape=[shape((2 * outer * w_up.shape[0], w)) for w in widths],
            in_specs=[smem, anywhere],
            out_specs=[anywhere] * CHUNKS,
            scratch_shapes=[pltpu.SemaphoreType.DMA((2 * outer * CHUNKS,))],
            compiler_params=params,
            name="spread",
        )(place_info, w_up)
        for part in spread:
            line = outer_stream.send(along, part)
            weights.append([line, inner_stream.send(inner_swap, line)])
    else:
        quarter = group * 2 + mine % 2
        keep = lax.dynamic_slice_in_dim(w_up, quarter * width, width, 1)
        got = quad_swap(lax.dynamic_slice_in_dim(w_up, (quarter ^ 1) * width, width, 1), 1)
        even = mine % 2 == 0
        both = jnp.concatenate(
            [jnp.where(even, keep, got), jnp.where(even, got, keep)], axis=0
        )
        same_core = [list(range(c, size, 2)) for c in range(2)]
        for j in range(CHUNKS):
            part = both[:, FIRST_HEAD[j] * 256 : FIRST_HEAD[j] * 256 + widths[j]]
            weights.append(
                [lax.all_gather(part, "ctx", axis=0, tiled=True, axis_index_groups=same_core)]
            )

    frequency = np.exp(-np.arange(ROPE // 2) * (2.0 * math.log(10000.0) / ROPE))
    frequency = jnp.asarray(np.tile(frequency, 4)[None, :], jnp.float32)
    info = jnp.concatenate([mine[None].astype(jnp.int32), lengths.astype(jnp.int32)])
    rows, cosine, sine, outgoing = pl.pallas_call(
        functools.partial(rows_kernel, slot_count),
        out_shape=(
            shape((tok, EXT)),
            shape((tok, 128), jnp.float32),
            shape((tok, 128), jnp.float32),
            shape((size * slot_count, ROW)),
        ),
        in_specs=[smem] + [whole] * 4,
        out_specs=[whole] * 4,
        compiler_params=params,
        name="rows",
    )(info, kv_latent, latent_gain[None, :], page_ranks, frequency)

    queries = pl.pallas_call(
        query_kernel,
        out_shape=[shape((QUAD, tok, h * (NOPE + ROPE))) for h in CHUNK_HEADS],
        in_specs=[whole] * 3,
        out_specs=[whole] * CHUNKS,
        compiler_params=params,
        name="queries",
    )(q_heads, cosine, sine)

    both_groups = jnp.concatenate([rows, quad_swap(rows, 2)], axis=0)
    behind = from_behind(both_groups, 2, False)
    far_behind = from_behind(both_groups, 4, True)
    own_rows = jnp.concatenate([both_groups, behind, far_behind], axis=0)
    other_rows = quad_swap(own_rows, 1)

    moved = [group_stream.send(deal, one) for one in queries]

    outgoing = lax.optimization_barrier((outgoing, moved[0]))[0]
    arrived = lax.all_to_all(
        outgoing.reshape(size, slot_count, ROW), "ctx", split_axis=0, concat_axis=0, tiled=True
    )
    decode_cache = arrived.reshape(size * slot_count, ROW)

    place_info, decode_cache = lax.optimization_barrier((place_info, decode_cache))
    window = (REACH + 2) * tok

    def attend(j):
        heads = CHUNK_HEADS[j]
        steps = heads // 2
        flops = 2 * heads * 2 * (window * LAT * 256 + 2 * tok * window * (NOPE + ROPE + VDIM))
        return pl.pallas_call(
            functools.partial(attend_kernel, outer),
            grid=(steps,),
            out_shape=shape((QUAD, tok, heads * VDIM)),
            in_specs=[
                smem,
                pl.BlockSpec((6 * tok, EXT), lambda i: (0, 0)),
                pl.BlockSpec((6 * tok, EXT), lambda i: (0, 0)),
            ]
            + [pl.BlockSpec((piece.shape[0], 512), lambda i: (0, i)) for piece in weights[j]]
            + [
                pl.BlockSpec((QUAD, tok, 256), lambda i: (0, 0, i)),
                pl.BlockSpec((QUAD, tok, 128), lambda i: (0, 0, heads + i)),
            ],
            out_specs=pl.BlockSpec((QUAD, tok, 256), lambda i: (0, 0, i)),
            scratch_shapes=[
                VMEM((2, window, LAT), jnp.bfloat16),
                VMEM((2, window, 128), jnp.bfloat16),
                VMEM((2, window, 128), jnp.bfloat16),
                VMEM((2, 2 * tok, window), jnp.float32),
                VMEM((LAT, 512), jnp.bfloat16),
            ],
            compiler_params=params,
            cost_estimate=pl.CostEstimate(
                flops=flops,
                bytes_accessed=heads << 20,
                transcendentals=heads * 4 * tok * window,
            ),
            name="attend",
        )(place_info, own_rows, other_rows, *weights[j], moved[j], moved[j])

    pieces = [group_stream.send(deal, attend(j)) for j in range(CHUNKS)]
    attn_out = pl.pallas_call(
        place_kernel,
        out_shape=shape((tok, H * VDIM)),
        in_specs=[anywhere] * CHUNKS,
        out_specs=anywhere,
        scratch_shapes=[pltpu.SemaphoreType.DMA((QUAD * CHUNKS,))],
        compiler_params=params,
        name="place",
    )(*pieces)
    return (attn_out, decode_cache)


def solution(mesh):
    return jax.shard_map(
        body,
        mesh=mesh,
        in_specs=(
            P(("groups", "ctx"), None),
            P(("groups", "ctx"), None),
            P(),
            P("ctx", None),
            P(("groups", "ctx"), None),
            P("groups"),
        ),
        out_specs=(P(("groups", "ctx"), None), P(("groups", "ctx"), None)),
        check_vma=False,
    )
```

```python
import functools
import math

import jax
import jax.numpy as jnp
import numpy as np
from jax import lax
from jax.experimental import pallas as pl
from jax.experimental.pallas import tpu as pltpu
from jax.sharding import PartitionSpec as P

H = 64
NOPE = 128
ROPE = 64
VDIM = 128
LAT = 512
REACH = 3
QUAD = 4
HQ = H // QUAD
CHUNK_HEADS = (8, 8)
CHUNKS = len(CHUNK_HEADS)
FIRST_HEAD = tuple(sum(CHUNK_HEADS[:j]) for j in range(CHUNKS))
ROW = LAT + ROPE
EXT = 640
VMEM_LIMIT = 20 * 1024 * 1024
CALLS = ((0, 0, 2), (0, 2, 2), (1, 0, 2), (1, 2, 2))
SMEM = pltpu.SMEM
VMEM = pltpu.VMEM


def rows_kernel(
    slot_count, info, lengths, kv, gain, ranks, freq, rows_out, cos_out, sin_out, outgoing_out
):
    tok = kv.shape[1]
    base = info[0] * tok
    spots = base + lax.broadcasted_iota(jnp.int32, (tok, 128), 0)
    lane = lax.broadcasted_iota(jnp.int32, (tok, 128), 1)
    begin = jnp.int32(0)
    own_start = jnp.zeros((tok, 128), jnp.int32)
    for r in range(lengths.shape[0]):
        own_start = jnp.where(spots >= begin, begin, own_start)
        begin = begin + lengths[r]
    offset = spots - own_start
    angles = offset.astype(jnp.float32) * freq[...]
    cosine = jnp.cos(angles)
    sine = jnp.where((lane & 32) == 0, -jnp.sin(angles), jnp.sin(angles))
    cos_out[...] = cosine
    sin_out[...] = sine
    raw = kv[...].astype(jnp.float32).T
    latent = raw[:, :LAT]
    mean = jnp.sum(latent * latent, axis=1, keepdims=True) * (1.0 / LAT)
    latent = latent * lax.rsqrt(mean + 1e-06) * gain[...]
    key = raw[:, LAT:]
    swapped = jnp.concatenate([key[:, ROPE // 2 :], key[:, : ROPE // 2]], axis=1)
    turned = key * cosine[:, :ROPE] + swapped * sine[:, :ROPE]
    high = (offset >> 8).astype(jnp.float32)
    low = (offset & 255).astype(jnp.float32)
    meta = jnp.where(lane == 0, high, jnp.where(lane == 1, low, 0.0))
    tail = jnp.concatenate([turned, meta[:, :ROPE]], axis=1)
    rows_out[:, :LAT] = latent.astype(jnp.bfloat16)
    rows_out[:, LAT:] = tail.astype(jnp.bfloat16)

    rank_row = jnp.broadcast_to(ranks[...], (tok, tok)).astype(jnp.float32)
    rank_col = rank_row.T
    earlier = lax.broadcasted_iota(jnp.int32, (tok, tok), 0) < lax.broadcasted_iota(
        jnp.int32, (tok, tok), 1
    )
    same = jnp.where((rank_col == rank_row) & earlier, 1.0, 0.0)
    slot = jnp.sum(same, axis=0, keepdims=True)
    target = (rank_row[:1] * slot_count + slot).astype(jnp.int32)
    spots_out = lax.broadcasted_iota(jnp.int32, (outgoing_out.shape[0], tok), 0)
    selector = jnp.where(spots_out == target, 1.0, 0.0).astype(jnp.bfloat16)
    picked = jnp.dot(selector, rows_out[:, :ROW], preferred_element_type=jnp.float32)
    outgoing_out[...] = picked.astype(jnp.bfloat16)


def query_kernel(info, query, cosine, sine, *outs):
    tok = query.shape[0]
    lane = lax.broadcasted_iota(jnp.int32, (tok, 128), 1)
    low_half = lane < 64
    first_quarter = (lane & 32) == 0
    cos_table = cosine[...]
    sin_table = sine[...]
    for r in range(QUAD):
        first = (info[0] ^ r) * (HQ * (NOPE + ROPE))
        for pair in range(HQ // 2):
            j = max(j for j in range(CHUNKS) if FIRST_HEAD[j] <= 2 * pair)
            out = outs[r * CHUNKS + j]
            at = pair - FIRST_HEAD[j] // 2
            rope_at = CHUNK_HEADS[j] * NOPE + at * 128
            begin = pl.multiple_of(first + pair * 2 * (NOPE + ROPE), 128)
            both = query[:, pl.ds(begin, 2 * (NOPE + ROPE))]
            mid = both[:, 128:256].astype(jnp.float32)
            end = both[:, 256:384].astype(jnp.float32)
            turned = jnp.where(low_half, mid, end)
            odd_nope = pltpu.roll(jnp.where(low_half, end, mid), 64, 1)
            swapped = jnp.where(
                first_quarter, pltpu.roll(turned, 96, 1), pltpu.roll(turned, 32, 1)
            )
            turned = turned * cos_table + swapped * sin_table
            out[:, at * 256 : at * 256 + 128] = both[:, :128]
            out[:, at * 256 + 128 : at * 256 + 256] = odd_nope.astype(jnp.bfloat16)
            out[:, rope_at : rope_at + 128] = turned.astype(jnp.bfloat16)


def pair_kernel(info, w_up, got, *refs):
    outs, sems = refs[:-1], refs[-1]
    rows = got.shape[0]
    copies = []
    for j, out in enumerate(outs):
        width = out.shape[1]
        first = FIRST_HEAD[j] * (NOPE + VDIM)
        begin = pl.multiple_of(info[0] * (HQ * (NOPE + VDIM)) + first, 128)
        copies.append(
            pltpu.make_async_copy(
                w_up.at[:, pl.ds(begin, width)], out.at[pl.ds(0, rows)], sems.at[2 * j]
            )
        )
        copies.append(
            pltpu.make_async_copy(
                got.at[:, pl.ds(first, width)], out.at[pl.ds(rows, rows)], sems.at[2 * j + 1]
            )
        )
    for copy in copies:
        copy.start()
    for copy in copies:
        copy.wait()


def attend_kernel(outer, info, own, other, *refs):
    pieces_count = 2 * outer if outer else 1
    pieces_of_weight, refs = refs[:pieces_count], refs[pieces_count:]
    nope = refs[0:QUAD]
    rope = refs[QUAD : 2 * QUAD]
    outs = refs[2 * QUAD : 3 * QUAD]
    latent, rope_even, rope_odd, bias, held = refs[3 * QUAD :]
    tok = nope[0].shape[0]
    blocks = REACH + 2
    mine = info[0]
    partner = mine ^ 1
    scale = (NOPE + ROPE) ** (-0.5) * math.log2(math.e)

    @pl.when(pl.program_id(0) == 0)
    def _():
        has_last = (mine & 1) == 1
        starts = [mine, partner, mine - 2, partner - 2, (mine >> 1) * 2 - 3]
        blank = jnp.zeros((tok, ROPE), jnp.bfloat16)
        lane = lax.broadcasted_iota(jnp.int32, (tok, tok), 1)
        row = lax.broadcasted_iota(jnp.int32, (tok, tok), 0)
        for g in range(2):
            pieces = [
                own[g * tok : (g + 1) * tok],
                other[g * tok : (g + 1) * tok],
                own[(2 + g) * tok : (3 + g) * tok],
                other[(2 + g) * tok : (3 + g) * tok],
                jnp.where(
                    has_last,
                    own[(4 + g) * tok : (5 + g) * tok],
                    other[(4 + g) * tok : (5 + g) * tok],
                ),
            ]
            for b, piece in enumerate(pieces):
                here = slice(b * tok, (b + 1) * tok)
                latent[g, here] = piece[:, :LAT]
                turned = piece[:, LAT : LAT + ROPE]
                rope_even[g, here] = jnp.concatenate([turned, blank], axis=1)
                rope_odd[g, here] = jnp.concatenate([blank, turned], axis=1)
            for half in range(2):
                meta = pieces[half][:, LAT:].astype(jnp.float32)
                offset = (meta[:, ROPE : ROPE + 1] * 256.0 + meta[:, ROPE + 1 : ROPE + 2]).astype(
                    jnp.int32
                )
                spots = starts[half] * tok + row
                lowest = jnp.maximum(spots - offset, (starts[half] - REACH) * tok)
                for b in range(blocks):
                    keys = starts[b] * tok + lane
                    allowed = (keys >= lowest) & (keys <= spots)
                    bias[g, half * tok : (half + 1) * tok, b * tok : (b + 1) * tok] = jnp.where(
                        allowed, 0.0, -1e30
                    )

    if outer:
        weight = held
        for i, piece in enumerate(pieces_of_weight):
            side, behind = i // outer, i % outer
            chip = ((mine >> 2) + outer - behind) % outer * 2 + (((mine >> 1) & 1) ^ side)
            rows = piece.shape[0] // 2
            for core in range(2):
                begin = pl.multiple_of(chip * 2 * rows + ((mine & 1) ^ core) * rows, rows)
                held[pl.ds(begin, rows)] = piece[core * rows : (core + 1) * rows]
    else:
        weight = pieces_of_weight[0]

    for g in range(2):
        expanded = jnp.dot(latent[g], weight[...], preferred_element_type=jnp.float32).astype(
            jnp.bfloat16
        )
        query_rope = jnp.concatenate([rope[2 * g][...], rope[2 * g + 1][...]], axis=0)
        for b in range(2):
            at = slice(b * 128, (b + 1) * 128)
            key_rope = (rope_even, rope_odd)[b][g]
            key = jnp.concatenate([expanded[:, b * 256 : b * 256 + 128], key_rope], axis=1)
            value = expanded[:, b * 256 + 128 : b * 256 + 256]
            query = jnp.concatenate([nope[2 * g][:, at], nope[2 * g + 1][:, at]], axis=0)
            query = jnp.concatenate([query, query_rope], axis=1)
            scores = lax.dot_general(
                query, key, (((1,), (1,)), ((), ())), preferred_element_type=jnp.float32
            )
            scores = scores * scale + bias[g]
            largest = jnp.max(scores, axis=1, keepdims=True)
            expo = jnp.exp2(scores - largest)
            total = jnp.sum(expo, axis=1, keepdims=True)
            mixed = jnp.dot(expo.astype(jnp.bfloat16), value, preferred_element_type=jnp.float32)
            mixed = (mixed / total).astype(jnp.bfloat16)
            outs[2 * g][:, at] = mixed[:tok]
            outs[2 * g + 1][:, at] = mixed[tok:]


def gather_kernel(info, *refs):
    pieces, out, sems = refs[:-2], refs[-2], refs[-1]
    copies = []
    for i, piece in enumerate(pieces):
        r, (j, first, steps) = i // len(CALLS), CALLS[i % len(CALLS)]
        begin = ((info[0] ^ r) * HQ + FIRST_HEAD[j] + 2 * first) * VDIM
        begin = pl.multiple_of(begin, 128)
        copies.append(
            pltpu.make_async_copy(piece, out.at[:, pl.ds(begin, piece.shape[1])], sems.at[i])
        )
    for copy in copies:
        copy.start()
    for copy in copies:
        copy.wait()


def tie(array, *others):
    return lax.optimization_barrier((array,) + others)[0]


class Stream:
    def __init__(self, window):
        self.window = window
        self.arrived = []

    def after(self, array):
        if len(self.arrived) < self.window:
            return array
        return tie(array, self.arrived[-self.window])

    def send(self, permute, array, *args):
        self.arrived.append(permute(self.after(array), *args))
        return self.arrived[-1]


def shape(dims, kind=jnp.bfloat16):
    return jax.ShapeDtypeStruct(dims, kind)


def body(q_heads, kv_latent, latent_gain, w_up, page_ranks, lengths):
    tok = q_heads.shape[0]
    size = lax.axis_size("ctx")
    groups = lax.axis_size("groups")
    mine = lax.axis_index("ctx")
    quarter = lax.axis_index("groups") * 2 + mine % 2
    slot_count = max(2, 2 * tok // size)
    smem = pl.BlockSpec(memory_space=SMEM)
    params = pltpu.CompilerParams(vmem_limit_bytes=VMEM_LIMIT)
    alone = pltpu.CompilerParams(vmem_limit_bytes=3 * VMEM_LIMIT)

    def quad_swap(array, r):
        dx, dc = r // 2, r % 2
        pairs = [
            (g * size + i, (g ^ dx) * size + (i ^ dc)) for g in range(groups) for i in range(size)
        ]
        return lax.ppermute(array, ("groups", "ctx"), pairs)

    def send_in_quad(array, r):
        if r == 1 and len(group_stream.arrived) < 4:
            array = tie(array, weights[0][outer if outer else 0])
        return quad_swap(array, r) if r == 1 else group_stream.send(quad_swap, array, r)

    def around(array, by):
        return lax.ppermute(array, "ctx", [(i, (i + by) % size) for i in range(size)])

    def inner_swap(array):
        return lax.ppermute(array, "ctx", [(i, i ^ 2) for i in range(size)])

    def along_and_across(pieces):
        count = len(pieces)
        turns = [(k - j, j) for k in range(outer + count) for j in range(count)]
        lines = [[piece] for piece in pieces]
        sides = [[] for piece in pieces]
        outer_done, inner_done = [], []
        for k, j in turns:
            if not 0 <= k < outer:
                continue
            if k:
                at = len(outer_done)
                before = outer_done[-2:-1] + ([inner_done[max(0, at - 2)]] if at else [])
                outer_done.append(around(tie(lines[j][-1], *before), 4))
                lines[j].append(outer_done[-1])
            sides[j].append(inner_swap(tie(lines[j][k], *inner_done[-2:-1])))
            inner_done.append(sides[j][-1])
        return [line + side for line, side in zip(lines, sides)]

    def from_behind(array, by, odd_only):
        first = 1 if odd_only else 0
        step = 2 if odd_only else 1
        pairs = [(i, i + by) for i in range(first, size - by, step)]
        return lax.ppermute(array, "ctx", pairs)

    group_stream = Stream(2)

    width = HQ * (NOPE + VDIM)
    quarter_info = quarter[None].astype(jnp.int32)
    anywhere = pl.BlockSpec(memory_space=pl.ANY)
    give = lax.dynamic_slice_in_dim(w_up, (quarter ^ 1) * width, width, 1)
    give, lengths = lax.optimization_barrier((give, lengths))
    got = quad_swap(give, 1)
    widths = [heads * (NOPE + VDIM) for heads in CHUNK_HEADS]
    outer = size // 4 if size % 4 == 0 and size // 4 <= 4 else 0
    if outer:
        pairs_of_rows = pl.pallas_call(
            pair_kernel,
            out_shape=[shape((2 * w_up.shape[0], w)) for w in widths],
            in_specs=[smem, pl.BlockSpec(memory_space=pltpu.HBM), anywhere],
            out_specs=[anywhere] * CHUNKS,
            scratch_shapes=[pltpu.SemaphoreType.DMA((2 * CHUNKS,))],
            compiler_params=params,
            name="pair",
        )(quarter_info, w_up, got)
        weights = along_and_across(pairs_of_rows)
    else:
        keep = lax.dynamic_slice_in_dim(w_up, quarter * width, width, 1)
        even = mine % 2 == 0
        both = jnp.concatenate(
            [jnp.where(even, keep, got), jnp.where(even, got, keep)], axis=0
        )
        same_core = [list(range(c, size, 2)) for c in range(2)]
        weights = [
            [
                lax.all_gather(
                    both[:, FIRST_HEAD[j] * 256 : FIRST_HEAD[j] * 256 + widths[j]],
                    "ctx",
                    axis=0,
                    tiled=True,
                    axis_index_groups=same_core,
                )
            ]
            for j in range(CHUNKS)
        ]

    frequency = np.exp(-np.arange(ROPE // 2) * (2.0 * math.log(10000.0) / ROPE))
    frequency = jnp.asarray(np.tile(frequency, 4)[None, :], jnp.float32)
    mine_info = mine[None].astype(jnp.int32)

    def block(*dims):
        return pl.BlockSpec(dims, lambda i: (0,) * len(dims))

    rows, cosine, sine, outgoing = pl.pallas_call(
        functools.partial(rows_kernel, slot_count),
        grid=(1,),
        out_shape=(
            shape((tok, EXT)),
            shape((tok, 128), jnp.float32),
            shape((tok, 128), jnp.float32),
            shape((size * slot_count, ROW)),
        ),
        in_specs=[smem, smem, block(ROW, tok), block(1, LAT), block(1, tok), block(1, 128)],
        out_specs=[
            block(tok, EXT),
            block(tok, 128),
            block(tok, 128),
            block(size * slot_count, ROW),
        ],
        compiler_params=alone,
        name="rows",
    )(mine_info, lengths, kv_latent.T, latent_gain[None, :], page_ranks.T, frequency)

    queries = pl.pallas_call(
        query_kernel,
        out_shape=[shape((tok, h * (NOPE + ROPE))) for h in CHUNK_HEADS] * QUAD,
        grid=(1,),
        in_specs=[smem, block(*q_heads.shape), block(tok, 128), block(tok, 128)],
        out_specs=[block(tok, h * (NOPE + ROPE)) for h in CHUNK_HEADS] * QUAD,
        compiler_params=params,
        name="queries",
    )(quarter_info, q_heads, cosine, sine)

    both_groups = jnp.concatenate([rows, group_stream.send(quad_swap, rows, 2)], axis=0)
    behind = from_behind(both_groups, 2, False)
    far_behind = from_behind(both_groups, 4, True)
    own_rows = jnp.concatenate([both_groups, behind, far_behind], axis=0)
    other_rows = quad_swap(own_rows, 1)

    moved = [
        [
            queries[r * CHUNKS + j] if r == 0 else send_in_quad(queries[r * CHUNKS + j], r)
            for r in range(QUAD)
        ]
        for j in range(CHUNKS)
    ]

    outgoing = tie(outgoing, moved[0][2])
    arrived = lax.all_to_all(
        outgoing.reshape(size, slot_count, ROW), "ctx", split_axis=0, concat_axis=0, tiled=True
    )
    decode_cache = arrived.reshape(size * slot_count, ROW)

    mine_info, decode_cache = lax.optimization_barrier((mine_info, decode_cache))
    window = (REACH + 2) * tok

    def attend(j, first, steps):
        heads = 2 * steps
        flops = 2 * heads * 2 * (window * LAT * 256 + 2 * tok * window * (NOPE + ROPE + VDIM))
        return pl.pallas_call(
            functools.partial(attend_kernel, outer),
            grid=(steps,),
            out_shape=[shape((tok, heads * VDIM))] * QUAD,
            in_specs=[smem, block(6 * tok, EXT), block(6 * tok, EXT)]
            + [
                pl.BlockSpec((piece.shape[0], 512), lambda i: (0, first + i))
                for piece in weights[j]
            ]
            + [pl.BlockSpec((tok, 256), lambda i: (0, first + i))] * QUAD
            + [pl.BlockSpec((tok, 128), lambda i: (0, CHUNK_HEADS[j] + first + i))] * QUAD,
            out_specs=[pl.BlockSpec((tok, 256), lambda i: (0, i))] * QUAD,
            scratch_shapes=[
                VMEM((2, window, LAT), jnp.bfloat16),
                VMEM((2, window, 128), jnp.bfloat16),
                VMEM((2, window, 128), jnp.bfloat16),
                VMEM((2, 2 * tok, window), jnp.float32),
                VMEM((LAT, 512), jnp.bfloat16),
            ],
            compiler_params=params,
            cost_estimate=pl.CostEstimate(
                flops=flops,
                bytes_accessed=heads << 20,
                transcendentals=heads * 4 * tok * window,
            ),
            name="attend",
        )(mine_info, own_rows, other_rows, *weights[j], *moved[j], *moved[j])

    results = []
    for call in CALLS:
        parts = attend(*call)
        results.append([parts[0]] + [send_in_quad(parts[r], r) for r in range(1, QUAD)])
    pieces = [one[r] for r in range(QUAD) for one in results]
    attn_out = pl.pallas_call(
        gather_kernel,
        out_shape=shape((tok, H * VDIM)),
        in_specs=[smem] + [anywhere] * len(pieces),
        out_specs=anywhere,
        scratch_shapes=[pltpu.SemaphoreType.DMA((len(pieces),))],
        compiler_params=params,
        name="place",
    )(quarter_info, *pieces)
    return (attn_out, decode_cache)


def solution(mesh):
    return jax.shard_map(
        body,
        mesh=mesh,
        in_specs=(
            P(("groups", "ctx"), None),
            P(("groups", "ctx"), None),
            P(),
            P("ctx", None),
            P(("groups", "ctx"), None),
            P("groups"),
        ),
        out_specs=(P(("groups", "ctx"), None), P(("groups", "ctx"), None)),
        check_vma=False,
    )
```

```python
import functools
import math

import jax
import jax.numpy as jnp
import numpy as np
from jax import lax
from jax.experimental import pallas as pl
from jax.experimental.pallas import tpu as pltpu
from jax.sharding import PartitionSpec as P

H = 64
NOPE = 128
ROPE = 64
VDIM = 128
LAT = 512
REACH = 3
QUAD = 4
HQ = H // QUAD
CHUNK_HEADS = (8, 8)
CHUNKS = len(CHUNK_HEADS)
FIRST_HEAD = tuple(sum(CHUNK_HEADS[:j]) for j in range(CHUNKS))
ROW = LAT + ROPE
EXT = 640
VMEM_LIMIT = 20 * 1024 * 1024
CALLS = ((0, 0, 4), (1, 0, 2), (1, 2, 2))
SMEM = pltpu.SMEM
VMEM = pltpu.VMEM


def rows_kernel(
    slot_count, info, lengths, kv, gain, ranks, freq, rows_out, cos_out, sin_out, outgoing_out
):
    tok = kv.shape[1]
    base = info[0] * tok
    spots = base + lax.broadcasted_iota(jnp.int32, (tok, 128), 0)
    lane = lax.broadcasted_iota(jnp.int32, (tok, 128), 1)
    begin = jnp.int32(0)
    own_start = jnp.zeros((tok, 128), jnp.int32)
    for r in range(lengths.shape[0]):
        own_start = jnp.where(spots >= begin, begin, own_start)
        begin = begin + lengths[r]
    offset = spots - own_start
    angles = offset.astype(jnp.float32) * freq[...]
    cosine = jnp.cos(angles)
    sine = jnp.where((lane & 32) == 0, -jnp.sin(angles), jnp.sin(angles))
    cos_out[...] = cosine
    sin_out[...] = sine
    raw = kv[...].astype(jnp.float32).T
    latent = raw[:, :LAT]
    mean = jnp.sum(latent * latent, axis=1, keepdims=True) * (1.0 / LAT)
    latent = latent * lax.rsqrt(mean + 1e-06) * gain[...]
    key = raw[:, LAT:]
    swapped = jnp.concatenate([key[:, ROPE // 2 :], key[:, : ROPE // 2]], axis=1)
    turned = key * cosine[:, :ROPE] + swapped * sine[:, :ROPE]
    high = (offset >> 8).astype(jnp.float32)
    low = (offset & 255).astype(jnp.float32)
    meta = jnp.where(lane == 0, high, jnp.where(lane == 1, low, 0.0))
    tail = jnp.concatenate([turned, meta[:, :ROPE]], axis=1)
    rows_out[:, :LAT] = latent.astype(jnp.bfloat16)
    rows_out[:, LAT:] = tail.astype(jnp.bfloat16)

    rank_row = jnp.broadcast_to(ranks[...], (tok, tok)).astype(jnp.float32)
    rank_col = rank_row.T
    earlier = lax.broadcasted_iota(jnp.int32, (tok, tok), 0) < lax.broadcasted_iota(
        jnp.int32, (tok, tok), 1
    )
    same = jnp.where((rank_col == rank_row) & earlier, 1.0, 0.0)
    slot = jnp.sum(same, axis=0, keepdims=True)
    target = (rank_row[:1] * slot_count + slot).astype(jnp.int32)
    spots_out = lax.broadcasted_iota(jnp.int32, (outgoing_out.shape[0], tok), 0)
    selector = jnp.where(spots_out == target, 1.0, 0.0).astype(jnp.bfloat16)
    picked = jnp.dot(selector, rows_out[:, :ROW], preferred_element_type=jnp.float32)
    outgoing_out[...] = picked.astype(jnp.bfloat16)


def query_kernel(info, query, cosine, sine, *outs):
    tok = query.shape[0]
    lane = lax.broadcasted_iota(jnp.int32, (tok, 128), 1)
    low_half = lane < 64
    first_quarter = (lane & 32) == 0
    cos_table = cosine[...]
    sin_table = sine[...]
    for r in range(QUAD):
        first = (info[0] ^ r) * (HQ * (NOPE + ROPE))
        for pair in range(HQ // 2):
            j = max(j for j in range(CHUNKS) if FIRST_HEAD[j] <= 2 * pair)
            out = outs[r * CHUNKS + j]
            at = pair - FIRST_HEAD[j] // 2
            rope_at = CHUNK_HEADS[j] * NOPE + at * 128
            begin = pl.multiple_of(first + pair * 2 * (NOPE + ROPE), 128)
            both = query[:, pl.ds(begin, 2 * (NOPE + ROPE))]
            mid = both[:, 128:256].astype(jnp.float32)
            end = both[:, 256:384].astype(jnp.float32)
            turned = jnp.where(low_half, mid, end)
            odd_nope = pltpu.roll(jnp.where(low_half, end, mid), 64, 1)
            swapped = jnp.where(
                first_quarter, pltpu.roll(turned, 96, 1), pltpu.roll(turned, 32, 1)
            )
            turned = turned * cos_table + swapped * sin_table
            out[:, at * 256 : at * 256 + 128] = both[:, :128]
            out[:, at * 256 + 128 : at * 256 + 256] = odd_nope.astype(jnp.bfloat16)
            out[:, rope_at : rope_at + 128] = turned.astype(jnp.bfloat16)


def pair_kernel(info, w_up, got, *refs):
    outs, sems = refs[:-1], refs[-1]
    rows = got.shape[0]
    copies = []
    for j, out in enumerate(outs):
        width = out.shape[1]
        first = FIRST_HEAD[j] * (NOPE + VDIM)
        begin = pl.multiple_of(info[0] * (HQ * (NOPE + VDIM)) + first, 128)
        copies.append(
            pltpu.make_async_copy(
                w_up.at[:, pl.ds(begin, width)], out.at[pl.ds(0, rows)], sems.at[2 * j]
            )
        )
        copies.append(
            pltpu.make_async_copy(
                got.at[:, pl.ds(first, width)], out.at[pl.ds(rows, rows)], sems.at[2 * j + 1]
            )
        )
    for copy in copies:
        copy.start()
    for copy in copies:
        copy.wait()


def attend_kernel(outer, info, own, other, *refs):
    pieces_count = 2 * outer if outer else 1
    pieces_of_weight, refs = refs[:pieces_count], refs[pieces_count:]
    nope = refs[0:QUAD]
    rope = refs[QUAD : 2 * QUAD]
    outs = refs[2 * QUAD : 3 * QUAD]
    latent, rope_even, rope_odd, bias, held = refs[3 * QUAD :]
    tok = nope[0].shape[0]
    blocks = REACH + 2
    mine = info[0]
    partner = mine ^ 1
    scale = (NOPE + ROPE) ** (-0.5) * math.log2(math.e)

    @pl.when(pl.program_id(0) == 0)
    def _():
        has_last = (mine & 1) == 1
        starts = [mine, partner, mine - 2, partner - 2, (mine >> 1) * 2 - 3]
        blank = jnp.zeros((tok, ROPE), jnp.bfloat16)
        lane = lax.broadcasted_iota(jnp.int32, (tok, tok), 1)
        row = lax.broadcasted_iota(jnp.int32, (tok, tok), 0)
        for g in range(2):
            pieces = [
                own[g * tok : (g + 1) * tok],
                other[g * tok : (g + 1) * tok],
                own[(2 + g) * tok : (3 + g) * tok],
                other[(2 + g) * tok : (3 + g) * tok],
                jnp.where(
                    has_last,
                    own[(4 + g) * tok : (5 + g) * tok],
                    other[(4 + g) * tok : (5 + g) * tok],
                ),
            ]
            for b, piece in enumerate(pieces):
                here = slice(b * tok, (b + 1) * tok)
                latent[g, here] = piece[:, :LAT]
                turned = piece[:, LAT : LAT + ROPE]
                rope_even[g, here] = jnp.concatenate([turned, blank], axis=1)
                rope_odd[g, here] = jnp.concatenate([blank, turned], axis=1)
            for half in range(2):
                meta = pieces[half][:, LAT:].astype(jnp.float32)
                offset = (meta[:, ROPE : ROPE + 1] * 256.0 + meta[:, ROPE + 1 : ROPE + 2]).astype(
                    jnp.int32
                )
                spots = starts[half] * tok + row
                lowest = jnp.maximum(spots - offset, (starts[half] - REACH) * tok)
                for b in range(blocks):
                    keys = starts[b] * tok + lane
                    allowed = (keys >= lowest) & (keys <= spots)
                    bias[g, half * tok : (half + 1) * tok, b * tok : (b + 1) * tok] = jnp.where(
                        allowed, 0.0, -1e30
                    )

    if outer:
        weight = held
        for i, piece in enumerate(pieces_of_weight):
            side, behind = i // outer, i % outer
            chip = ((mine >> 2) + outer - behind) % outer * 2 + (((mine >> 1) & 1) ^ side)
            rows = piece.shape[0] // 2
            for core in range(2):
                begin = pl.multiple_of(chip * 2 * rows + ((mine & 1) ^ core) * rows, rows)
                held[pl.ds(begin, rows)] = piece[core * rows : (core + 1) * rows]
    else:
        weight = pieces_of_weight[0]

    for g in range(2):
        expanded = jnp.dot(latent[g], weight[...], preferred_element_type=jnp.float32).astype(
            jnp.bfloat16
        )
        query_rope = jnp.concatenate([rope[2 * g][...], rope[2 * g + 1][...]], axis=0)
        for b in range(2):
            at = slice(b * 128, (b + 1) * 128)
            key_rope = (rope_even, rope_odd)[b][g]
            key = jnp.concatenate([expanded[:, b * 256 : b * 256 + 128], key_rope], axis=1)
            value = expanded[:, b * 256 + 128 : b * 256 + 256]
            query = jnp.concatenate([nope[2 * g][:, at], nope[2 * g + 1][:, at]], axis=0)
            query = jnp.concatenate([query, query_rope], axis=1)
            scores = lax.dot_general(
                query, key, (((1,), (1,)), ((), ())), preferred_element_type=jnp.float32
            )
            scores = scores * scale + bias[g]
            largest = jnp.max(scores, axis=1, keepdims=True)
            expo = jnp.exp2(scores - largest)
            total = jnp.sum(expo, axis=1, keepdims=True)
            mixed = jnp.dot(expo.astype(jnp.bfloat16), value, preferred_element_type=jnp.float32)
            mixed = (mixed / total).astype(jnp.bfloat16)
            outs[2 * g][:, at] = mixed[:tok]
            outs[2 * g + 1][:, at] = mixed[tok:]


def gather_kernel(info, *refs):
    pieces, out, sems = refs[:-2], refs[-2], refs[-1]
    copies = []
    for i, piece in enumerate(pieces):
        r, (j, first, steps) = i // len(CALLS), CALLS[i % len(CALLS)]
        begin = ((info[0] ^ r) * HQ + FIRST_HEAD[j] + 2 * first) * VDIM
        begin = pl.multiple_of(begin, 128)
        copies.append(
            pltpu.make_async_copy(piece, out.at[:, pl.ds(begin, piece.shape[1])], sems.at[i])
        )
    for copy in copies:
        copy.start()
    for copy in copies:
        copy.wait()


def tie(array, *others):
    return lax.optimization_barrier((array,) + others)[0]


class Stream:
    def __init__(self, window):
        self.window = window
        self.arrived = []

    def after(self, array):
        if len(self.arrived) < self.window:
            return array
        return tie(array, self.arrived[-self.window])

    def send(self, permute, array, *args):
        self.arrived.append(permute(self.after(array), *args))
        return self.arrived[-1]


def shape(dims, kind=jnp.bfloat16):
    return jax.ShapeDtypeStruct(dims, kind)


def in_hbm(*arrays):
    return [pltpu.with_memory_space_constraint(array, pltpu.HBM) for array in arrays]


def body(q_heads, kv_latent, latent_gain, w_up, page_ranks, lengths):
    tok = q_heads.shape[0]
    size = lax.axis_size("ctx")
    groups = lax.axis_size("groups")
    mine = lax.axis_index("ctx")
    quarter = lax.axis_index("groups") * 2 + mine % 2
    slot_count = max(2, 2 * tok // size)
    smem = pl.BlockSpec(memory_space=SMEM)
    params = pltpu.CompilerParams(vmem_limit_bytes=VMEM_LIMIT)
    alone = pltpu.CompilerParams(vmem_limit_bytes=3 * VMEM_LIMIT)

    def quad_swap(array, r):
        dx, dc = r // 2, r % 2
        pairs = [
            (g * size + i, (g ^ dx) * size + (i ^ dc)) for g in range(groups) for i in range(size)
        ]
        return lax.ppermute(array, ("groups", "ctx"), pairs)

    def send_in_quad(array, r):
        return quad_swap(array, r) if r == 1 else group_stream.send(quad_swap, array, r)

    def around(array, by):
        return lax.ppermute(array, "ctx", [(i, (i + by) % size) for i in range(size)])

    def inner_swap(array):
        return lax.ppermute(array, "ctx", [(i, i ^ 2) for i in range(size)])

    def along_and_across(pieces, share_rows, gates):
        count = len(pieces)
        turns = [(k - j, j) for k in range(outer + count) for j in range(count)]
        lines = [[piece] for piece in pieces]
        sides = [[] for piece in pieces]
        outer_done, inner_done = [], []
        for k, j in turns:
            if not 0 <= k < outer:
                continue
            if k:
                at = len(outer_done)
                before = outer_done[-2:-1] + ([inner_done[max(0, at - 2)]] if at else [])
                before += gates.get(at, [])
                outer_done.append(around(tie(lines[j][-1], *before), 4))
                lines[j].append(outer_done[-1])
                if not at:
                    share_rows(inner_done[0], outer_done[0])
            sides[j].append(inner_swap(tie(lines[j][k], *inner_done[-2:-1])))
            inner_done.append(sides[j][-1])
        return [line + side for line, side in zip(lines, sides)]

    def from_behind(array, by, odd_only):
        first = 1 if odd_only else 0
        step = 2 if odd_only else 1
        pairs = [(i, i + by) for i in range(first, size - by, step)]
        return lax.ppermute(array, "ctx", pairs)

    group_stream = Stream(2)

    width = HQ * (NOPE + VDIM)
    quarter_info = quarter[None].astype(jnp.int32)
    anywhere = pl.BlockSpec(memory_space=pl.ANY)
    give = lax.dynamic_slice_in_dim(w_up, (quarter ^ 1) * width, width, 1)
    give, lengths = lax.optimization_barrier((give, lengths))
    got = quad_swap(give, 1)
    widths = [heads * (NOPE + VDIM) for heads in CHUNK_HEADS]
    outer = size // 4 if size % 4 == 0 and size // 4 <= 4 else 0
    if outer:
        pairs_of_rows = pl.pallas_call(
            pair_kernel,
            out_shape=[shape((2 * w_up.shape[0], w)) for w in widths],
            in_specs=[smem, pl.BlockSpec(memory_space=pltpu.HBM), anywhere],
            out_specs=[anywhere] * CHUNKS,
            scratch_shapes=[pltpu.SemaphoreType.DMA((2 * CHUNKS,))],
            compiler_params=params,
            name="pair",
        )(quarter_info, *in_hbm(w_up), got)
    else:
        keep = lax.dynamic_slice_in_dim(w_up, quarter * width, width, 1)
        even = mine % 2 == 0
        both = jnp.concatenate(
            [jnp.where(even, keep, got), jnp.where(even, got, keep)], axis=0
        )
        same_core = [list(range(c, size, 2)) for c in range(2)]
        weights = [
            [
                lax.all_gather(
                    both[:, FIRST_HEAD[j] * 256 : FIRST_HEAD[j] * 256 + widths[j]],
                    "ctx",
                    axis=0,
                    tiled=True,
                    axis_index_groups=same_core,
                )
            ]
            for j in range(CHUNKS)
        ]

    frequency = np.exp(-np.arange(ROPE // 2) * (2.0 * math.log(10000.0) / ROPE))
    frequency = jnp.asarray(np.tile(frequency, 4)[None, :], jnp.float32)
    mine_info = mine[None].astype(jnp.int32)

    def block(*dims):
        return pl.BlockSpec(dims, lambda i: (0,) * len(dims))

    rows, cosine, sine, outgoing = pl.pallas_call(
        functools.partial(rows_kernel, slot_count),
        grid=(1,),
        out_shape=(
            shape((tok, EXT)),
            shape((tok, 128), jnp.float32),
            shape((tok, 128), jnp.float32),
            shape((size * slot_count, ROW)),
        ),
        in_specs=[smem, smem, block(ROW, tok), block(1, LAT), block(1, tok), block(1, 128)],
        out_specs=[
            block(tok, EXT),
            block(tok, 128),
            block(tok, 128),
            block(size * slot_count, ROW),
        ],
        compiler_params=alone,
        name="rows",
    )(
        mine_info,
        lengths,
        *in_hbm(kv_latent.T, latent_gain[None, :], page_ranks.T, frequency),
    )

    queries = pl.pallas_call(
        query_kernel,
        out_shape=[shape((tok, h * (NOPE + ROPE))) for h in CHUNK_HEADS] * QUAD,
        grid=(1,),
        in_specs=[smem, block(*q_heads.shape), block(tok, 128), block(tok, 128)],
        out_specs=[block(tok, h * (NOPE + ROPE)) for h in CHUNK_HEADS] * QUAD,
        compiler_params=params,
        cost_estimate=pl.CostEstimate(
            flops=0, bytes_accessed=4 * q_heads.size, transcendentals=0
        ),
        name="queries",
    )(quarter_info, *in_hbm(q_heads), tie(cosine, pairs_of_rows[0] if outer else got), sine)

    shared = []

    def share_rows(*others):
        swapped = quad_swap(tie(rows, queries[0], *others), 2)
        both_groups = jnp.concatenate([rows, swapped], axis=0)
        behind = from_behind(both_groups, 2, False)
        far_behind = from_behind(both_groups, 4, True)
        own_rows = jnp.concatenate([both_groups, behind, far_behind], axis=0)
        shared.extend([own_rows, quad_swap(own_rows, 1)])

    across = [
        [group_stream.send(quad_swap, queries[r * CHUNKS + j], r) for r in (2, 3)]
        for j in range(CHUNKS)
    ]
    if outer:
        gates = {3: [across[0][0]], 4: [across[0][1]], 5: [across[1][0]]}
        weights = along_and_across(pairs_of_rows, share_rows, gates)
    else:
        share_rows()
    own_rows, other_rows = shared
    moved = [
        [queries[j], quad_swap(tie(queries[CHUNKS + j], across[j][0]), 1)] + across[j]
        for j in range(CHUNKS)
    ]

    window = (REACH + 2) * tok

    def attend(j, first, steps):
        heads = 2 * steps
        flops = 2 * heads * 2 * (window * LAT * 256 + 2 * tok * window * (NOPE + ROPE + VDIM))
        return pl.pallas_call(
            functools.partial(attend_kernel, outer),
            grid=(steps,),
            out_shape=[shape((tok, heads * VDIM))] * QUAD,
            in_specs=[smem, block(6 * tok, EXT), block(6 * tok, EXT)]
            + [
                pl.BlockSpec((piece.shape[0], 512), lambda i: (0, first + i))
                for piece in weights[j]
            ]
            + [pl.BlockSpec((tok, 256), lambda i: (0, first + i))] * QUAD
            + [pl.BlockSpec((tok, 128), lambda i: (0, CHUNK_HEADS[j] + first + i))] * QUAD,
            out_specs=[pl.BlockSpec((tok, 256), lambda i: (0, i))] * QUAD,
            scratch_shapes=[
                VMEM((2, window, LAT), jnp.bfloat16),
                VMEM((2, window, 128), jnp.bfloat16),
                VMEM((2, window, 128), jnp.bfloat16),
                VMEM((2, 2 * tok, window), jnp.float32),
                VMEM((LAT, 512), jnp.bfloat16),
            ],
            compiler_params=params,
            cost_estimate=pl.CostEstimate(
                flops=flops,
                bytes_accessed=heads << 20,
                transcendentals=heads * 4 * tok * window,
            ),
            name="attend",
        )(mine_info, own_rows, other_rows, *weights[j], *moved[j], *moved[j])

    results = []
    for call in CALLS:
        parts = attend(*call)
        results.append([parts[0]] + [send_in_quad(parts[r], r) for r in range(1, QUAD)])
    pieces = [one[r] for r in range(QUAD) for one in results]
    arrived = lax.all_to_all(
        tie(outgoing, pieces[len(CALLS) - 1]).reshape(size, slot_count, ROW),
        "ctx",
        split_axis=0,
        concat_axis=0,
        tiled=True,
    )
    decode_cache = arrived.reshape(size * slot_count, ROW)
    attn_out = pl.pallas_call(
        gather_kernel,
        out_shape=shape((tok, H * VDIM)),
        in_specs=[smem] + [anywhere] * len(pieces),
        out_specs=anywhere,
        scratch_shapes=[pltpu.SemaphoreType.DMA((len(pieces),))],
        compiler_params=params,
        name="place",
    )(quarter_info, *pieces)
    return (attn_out, decode_cache)


def solution(mesh):
    return jax.shard_map(
        body,
        mesh=mesh,
        in_specs=(
            P(("groups", "ctx"), None),
            P(("groups", "ctx"), None),
            P(),
            P("ctx", None),
            P(("groups", "ctx"), None),
            P("groups"),
        ),
        out_specs=(P(("groups", "ctx"), None), P(("groups", "ctx"), None)),
        check_vma=False,
    )
```

```python
import functools
import math

import jax
import jax.numpy as jnp
import numpy as np
from jax import lax
from jax.experimental import pallas as pl
from jax.experimental.pallas import tpu as pltpu
from jax.sharding import PartitionSpec as P

H = 64
NOPE = 128
ROPE = 64
VDIM = 128
LAT = 512
REACH = 3
QUAD = 4
HQ = H // QUAD
CHUNK_HEADS = (8, 8)
PHASES = "z y0 b~ f~ q02 | z y1 k q01 | z y2 p q03 q12~ | y3 q13~ q11"
CHUNKS = len(CHUNK_HEADS)
FIRST_HEAD = tuple(sum(CHUNK_HEADS[:j]) for j in range(CHUNKS))
ROW = LAT + ROPE
EXT = 640
VMEM_LIMIT = 20 * 1024 * 1024
CALLS = ((0, 0, 4), (1, 0, 2), (1, 2, 2))
SMEM = pltpu.SMEM
VMEM = pltpu.VMEM


def rows_kernel(
    slot_count, info, lengths, kv, gain, ranks, freq, rows_out, cos_out, sin_out, outgoing_out
):
    tok = kv.shape[1]
    base = info[0] * tok
    spots = base + lax.broadcasted_iota(jnp.int32, (tok, 128), 0)
    lane = lax.broadcasted_iota(jnp.int32, (tok, 128), 1)
    begin = jnp.int32(0)
    own_start = jnp.zeros((tok, 128), jnp.int32)
    for r in range(lengths.shape[0]):
        own_start = jnp.where(spots >= begin, begin, own_start)
        begin = begin + lengths[r]
    offset = spots - own_start
    angles = offset.astype(jnp.float32) * freq[...]
    cosine = jnp.cos(angles)
    sine = jnp.where((lane & 32) == 0, -jnp.sin(angles), jnp.sin(angles))
    cos_out[...] = cosine
    sin_out[...] = sine
    raw = kv[...].astype(jnp.float32).T
    latent = raw[:, :LAT]
    mean = jnp.sum(latent * latent, axis=1, keepdims=True) * (1.0 / LAT)
    latent = latent * lax.rsqrt(mean + 1e-06) * gain[...]
    key = raw[:, LAT:]
    swapped = jnp.concatenate([key[:, ROPE // 2 :], key[:, : ROPE // 2]], axis=1)
    turned = key * cosine[:, :ROPE] + swapped * sine[:, :ROPE]
    high = (offset >> 8).astype(jnp.float32)
    low = (offset & 255).astype(jnp.float32)
    meta = jnp.where(lane == 0, high, jnp.where(lane == 1, low, 0.0))
    tail = jnp.concatenate([turned, meta[:, :ROPE]], axis=1)
    rows_out[:, :LAT] = latent.astype(jnp.bfloat16)
    rows_out[:, LAT:] = tail.astype(jnp.bfloat16)

    rank_row = jnp.broadcast_to(ranks[...], (tok, tok)).astype(jnp.float32)
    rank_col = rank_row.T
    earlier = lax.broadcasted_iota(jnp.int32, (tok, tok), 0) < lax.broadcasted_iota(
        jnp.int32, (tok, tok), 1
    )
    same = jnp.where((rank_col == rank_row) & earlier, 1.0, 0.0)
    slot = jnp.sum(same, axis=0, keepdims=True)
    target = (rank_row[:1] * slot_count + slot).astype(jnp.int32)
    spots_out = lax.broadcasted_iota(jnp.int32, (outgoing_out.shape[0], tok), 0)
    selector = jnp.where(spots_out == target, 1.0, 0.0).astype(jnp.bfloat16)
    picked = jnp.dot(selector, rows_out[:, :ROW], preferred_element_type=jnp.float32)
    outgoing_out[...] = picked.astype(jnp.bfloat16)


def query_kernel(info, query, cosine, sine, *outs):
    tok = query.shape[0]
    lane = lax.broadcasted_iota(jnp.int32, (tok, 128), 1)
    low_half = lane < 64
    first_quarter = (lane & 32) == 0
    cos_table = cosine[...]
    sin_table = sine[...]
    for r in range(QUAD):
        first = (info[0] ^ r) * (HQ * (NOPE + ROPE))
        for pair in range(HQ // 2):
            j = max(j for j in range(CHUNKS) if FIRST_HEAD[j] <= 2 * pair)
            out = outs[r * CHUNKS + j]
            at = pair - FIRST_HEAD[j] // 2
            rope_at = CHUNK_HEADS[j] * NOPE + at * 128
            begin = pl.multiple_of(first + pair * 2 * (NOPE + ROPE), 128)
            both = query[:, pl.ds(begin, 2 * (NOPE + ROPE))]
            mid = both[:, 128:256].astype(jnp.float32)
            end = both[:, 256:384].astype(jnp.float32)
            turned = jnp.where(low_half, mid, end)
            odd_nope = pltpu.roll(jnp.where(low_half, end, mid), 64, 1)
            swapped = jnp.where(
                first_quarter, pltpu.roll(turned, 96, 1), pltpu.roll(turned, 32, 1)
            )
            turned = turned * cos_table + swapped * sin_table
            out[:, at * 256 : at * 256 + 128] = both[:, :128]
            out[:, at * 256 + 128 : at * 256 + 256] = odd_nope.astype(jnp.bfloat16)
            out[:, rope_at : rope_at + 128] = turned.astype(jnp.bfloat16)


def pair_kernel(info, w_up, got, out, sem):
    rows, width = got.shape
    begin = pl.multiple_of(info[0] * width, 128)
    copies = [
        pltpu.make_async_copy(w_up.at[:, pl.ds(begin, width)], out.at[pl.ds(0, rows)], sem.at[0]),
        pltpu.make_async_copy(got, out.at[pl.ds(rows, rows)], sem.at[1]),
    ]
    for copy in copies:
        copy.start()
    for copy in copies:
        copy.wait()


def attend_kernel(outer, info, own, other, *refs):
    pieces_count = 2 * outer if outer else 1
    pieces_of_weight, refs = refs[:pieces_count], refs[pieces_count:]
    nope = refs[0:QUAD]
    rope = refs[QUAD : 2 * QUAD]
    outs = refs[2 * QUAD : 3 * QUAD]
    latent, rope_even, rope_odd, bias, held = refs[3 * QUAD :]
    tok = nope[0].shape[0]
    blocks = REACH + 2
    mine = info[0]
    partner = mine ^ 1
    scale = (NOPE + ROPE) ** (-0.5) * math.log2(math.e)

    @pl.when(pl.program_id(0) == 0)
    def _():
        has_last = (mine & 1) == 1
        starts = [mine, partner, mine - 2, partner - 2, (mine >> 1) * 2 - 3]
        blank = jnp.zeros((tok, ROPE), jnp.bfloat16)
        lane = lax.broadcasted_iota(jnp.int32, (tok, tok), 1)
        row = lax.broadcasted_iota(jnp.int32, (tok, tok), 0)
        for g in range(2):
            mine_of, other_of = [
                [ref[(3 * g + n) * tok : (3 * g + n + 1) * tok] for n in range(3)]
                for ref in (own, other)
            ]
            pieces = [
                mine_of[0],
                other_of[0],
                mine_of[1],
                other_of[1],
                jnp.where(has_last, mine_of[2], other_of[2]),
            ]
            for b, piece in enumerate(pieces):
                here = slice(b * tok, (b + 1) * tok)
                latent[g, here] = piece[:, :LAT]
                turned = piece[:, LAT : LAT + ROPE]
                rope_even[g, here] = jnp.concatenate([turned, blank], axis=1)
                rope_odd[g, here] = jnp.concatenate([blank, turned], axis=1)
            for half in range(2):
                meta = pieces[half][:, LAT:].astype(jnp.float32)
                offset = (meta[:, ROPE : ROPE + 1] * 256.0 + meta[:, ROPE + 1 : ROPE + 2]).astype(
                    jnp.int32
                )
                spots = starts[half] * tok + row
                lowest = jnp.maximum(spots - offset, (starts[half] - REACH) * tok)
                for b in range(blocks):
                    keys = starts[b] * tok + lane
                    allowed = (keys >= lowest) & (keys <= spots)
                    bias[g, half * tok : (half + 1) * tok, b * tok : (b + 1) * tok] = jnp.where(
                        allowed, 0.0, -1e30
                    )

    if outer:
        weight = held
        for i, piece in enumerate(pieces_of_weight):
            side, behind = i // outer, i % outer
            chip = ((mine >> 2) + outer - behind) % outer * 2 + (((mine >> 1) & 1) ^ side)
            rows = piece.shape[0] // 2
            for core in range(2):
                begin = pl.multiple_of(chip * 2 * rows + ((mine & 1) ^ core) * rows, rows)
                held[pl.ds(begin, rows)] = piece[core * rows : (core + 1) * rows]
    else:
        weight = pieces_of_weight[0]

    for g in range(2):
        expanded = jnp.dot(latent[g], weight[...], preferred_element_type=jnp.float32).astype(
            jnp.bfloat16
        )
        query_rope = jnp.concatenate([rope[2 * g][...], rope[2 * g + 1][...]], axis=0)
        for b in range(2):
            at = slice(b * 128, (b + 1) * 128)
            key_rope = (rope_even, rope_odd)[b][g]
            key = jnp.concatenate([expanded[:, b * 256 : b * 256 + 128], key_rope], axis=1)
            value = expanded[:, b * 256 + 128 : b * 256 + 256]
            query = jnp.concatenate([nope[2 * g][:, at], nope[2 * g + 1][:, at]], axis=0)
            query = jnp.concatenate([query, query_rope], axis=1)
            scores = lax.dot_general(
                query, key, (((1,), (1,)), ((), ())), preferred_element_type=jnp.float32
            )
            scores = scores * scale + bias[g]
            largest = jnp.max(scores, axis=1, keepdims=True)
            expo = jnp.exp2(scores - largest)
            total = jnp.sum(expo, axis=1, keepdims=True)
            mixed = jnp.dot(expo.astype(jnp.bfloat16), value, preferred_element_type=jnp.float32)
            mixed = (mixed / total).astype(jnp.bfloat16)
            outs[2 * g][:, at] = mixed[:tok]
            outs[2 * g + 1][:, at] = mixed[tok:]


def gather_kernel(info, *refs):
    pieces, out, sems = refs[:-2], refs[-2], refs[-1]
    copies = []
    for i, piece in enumerate(pieces):
        r, (j, first, steps) = i // len(CALLS), CALLS[i % len(CALLS)]
        begin = ((info[0] ^ r) * HQ + FIRST_HEAD[j] + 2 * first) * VDIM
        begin = pl.multiple_of(begin, 128)
        copies.append(
            pltpu.make_async_copy(piece, out.at[:, pl.ds(begin, piece.shape[1])], sems.at[i])
        )
    for copy in copies:
        copy.start()
    for copy in copies:
        copy.wait()


def tie(array, *others):
    return lax.optimization_barrier((array,) + others)[0]


class Phases:
    def __init__(self):
        self.before, self.before_late, self.now, self.late = [], [], [], []

    def turn(self):
        self.before = self.now + self.before_late
        self.before_late, self.now, self.late = self.late, [], []

    def send(self, late, permute, array, *args):
        arrived = permute(tie(array, *self.before) if self.before else array, *args)
        (self.late if late else self.now).append(arrived)
        return arrived


def shape(dims, kind=jnp.bfloat16):
    return jax.ShapeDtypeStruct(dims, kind)


def in_hbm(*arrays):
    return [pltpu.with_memory_space_constraint(array, pltpu.HBM) for array in arrays]


def body(q_heads, kv_latent, latent_gain, w_up, page_ranks, lengths):
    tok = q_heads.shape[0]
    size = lax.axis_size("ctx")
    groups = lax.axis_size("groups")
    mine = lax.axis_index("ctx")
    quarter = lax.axis_index("groups") * 2 + mine % 2
    slot_count = max(2, 2 * tok // size)
    smem = pl.BlockSpec(memory_space=SMEM)
    params = pltpu.CompilerParams(vmem_limit_bytes=VMEM_LIMIT)
    alone = pltpu.CompilerParams(vmem_limit_bytes=3 * VMEM_LIMIT)

    def quad_swap(array, r):
        dx, dc = r // 2, r % 2
        pairs = [
            (g * size + i, (g ^ dx) * size + (i ^ dc)) for g in range(groups) for i in range(size)
        ]
        return lax.ppermute(array, ("groups", "ctx"), pairs)

    def around(array, by):
        return lax.ppermute(array, "ctx", [(i, (i + by) % size) for i in range(size)])

    def inner_swap(array):
        return lax.ppermute(array, "ctx", [(i, i ^ 2) for i in range(size)])

    def from_behind(array, by, odd_only):
        first = 1 if odd_only else 0
        step = 2 if odd_only else 1
        pairs = [(i, i + by) for i in range(first, size - by, step)]
        return lax.ppermute(array, "ctx", pairs)

    width = HQ * (NOPE + VDIM)
    quarter_info = quarter[None].astype(jnp.int32)
    anywhere = pl.BlockSpec(memory_space=pl.ANY)
    give = lax.dynamic_slice_in_dim(w_up, (quarter ^ 1) * width, width, 1)
    give, lengths = lax.optimization_barrier((give, lengths))
    got = quad_swap(give, 1)
    outer = size // 4 if size % 4 == 0 and size // 4 <= 4 else 0
    if outer:
        pair_rows = pl.pallas_call(
            pair_kernel,
            out_shape=shape((2 * w_up.shape[0], width)),
            in_specs=[smem, pl.BlockSpec(memory_space=pltpu.HBM), anywhere],
            out_specs=anywhere,
            scratch_shapes=[pltpu.SemaphoreType.DMA((2,))],
            compiler_params=params,
            name="pair",
        )(quarter_info, *in_hbm(w_up), got)
    else:
        keep = lax.dynamic_slice_in_dim(w_up, quarter * width, width, 1)
        even = mine % 2 == 0
        both = jnp.concatenate(
            [jnp.where(even, keep, got), jnp.where(even, got, keep)], axis=0
        )
        same_core = [list(range(c, size, 2)) for c in range(2)]
        gathered = lax.all_gather(both, "ctx", axis=0, tiled=True, axis_index_groups=same_core)

    frequency = np.exp(-np.arange(ROPE // 2) * (2.0 * math.log(10000.0) / ROPE))
    frequency = jnp.asarray(np.tile(frequency, 4)[None, :], jnp.float32)
    mine_info = mine[None].astype(jnp.int32)

    def block(*dims):
        return pl.BlockSpec(dims, lambda i: (0,) * len(dims))

    rows, cosine, sine, outgoing = pl.pallas_call(
        functools.partial(rows_kernel, slot_count),
        grid=(1,),
        out_shape=(
            shape((tok, EXT)),
            shape((tok, 128), jnp.float32),
            shape((tok, 128), jnp.float32),
            shape((size * slot_count, ROW)),
        ),
        in_specs=[smem, smem, block(ROW, tok), block(1, LAT), block(1, tok), block(1, 128)],
        out_specs=[
            block(tok, EXT),
            block(tok, 128),
            block(tok, 128),
            block(size * slot_count, ROW),
        ],
        compiler_params=alone,
        name="rows",
    )(
        mine_info,
        lengths,
        *in_hbm(kv_latent.T, latent_gain[None, :], page_ranks.T, frequency),
    )

    queries = pl.pallas_call(
        query_kernel,
        out_shape=[shape((tok, h * (NOPE + ROPE))) for h in CHUNK_HEADS] * QUAD,
        grid=(1,),
        in_specs=[smem, block(*q_heads.shape), block(tok, 128), block(tok, 128)],
        out_specs=[block(tok, h * (NOPE + ROPE)) for h in CHUNK_HEADS] * QUAD,
        compiler_params=params,
        cost_estimate=pl.CostEstimate(
            flops=0, bytes_accessed=4 * q_heads.size, transcendentals=0
        ),
        name="queries",
    )(quarter_info, *in_hbm(q_heads, tie(cosine, pair_rows if outer else got), sine))

    phases = Phases()
    line = [pair_rows] if outer else []
    side = []
    halves = []
    moved = [[queries[j]] + [None] * (QUAD - 1) for j in range(CHUNKS)]
    parts = {"r": tie(rows, pair_rows if outer else got)}
    for name in PHASES.split():
        kind, late = name[0], name[-1] == "~"
        if kind == "|":
            phases.turn()
        elif kind == "z" and outer:
            line.append(phases.send(late, around, line[-1], 4))
        elif kind == "y" and outer:
            step = int(name[1])
            if step < outer - 1:
                side.append(phases.send(late, inner_swap, line[step]))
            else:
                half = line[step].shape[1] // CHUNKS
                halves = [
                    phases.send(late, inner_swap, line[step][:, j * half : (j + 1) * half])
                    for j in range(CHUNKS)
                ]
        elif kind == "b":
            parts["b"] = phases.send(late, from_behind, parts["r"], 2, False)
        elif kind == "f":
            parts["f"] = phases.send(late, from_behind, parts["r"], 4, True)
        elif kind == "k":
            have = jnp.concatenate([parts["r"], parts["b"], parts["f"]], axis=0)
            swapped = phases.send(late, quad_swap, have, 2)
        elif kind == "p":
            own_rows = jnp.concatenate([have, swapped], axis=0)
            other_rows = phases.send(late, quad_swap, own_rows, 1)
        elif kind == "q":
            j, r = int(name[1]), int(name[2])
            moved[j][r] = phases.send(late, quad_swap, queries[r * CHUNKS + j], r)

    def weights_for(j):
        if not outer:
            return [(gathered, FIRST_HEAD[j] // 2)]
        return [(piece, FIRST_HEAD[j] // 2) for piece in line + side] + [(halves[j], 0)]

    window = (REACH + 2) * tok

    def attend(j, first, steps):
        heads = 2 * steps
        pieces_of_weight = [piece for piece, begin in weights_for(j)]
        flops = 2 * heads * 2 * (window * LAT * 256 + 2 * tok * window * (NOPE + ROPE + VDIM))
        return pl.pallas_call(
            functools.partial(attend_kernel, outer),
            grid=(steps,),
            out_shape=[shape((tok, heads * VDIM))] * QUAD,
            in_specs=[smem, block(6 * tok, EXT), block(6 * tok, EXT)]
            + [
                pl.BlockSpec((piece.shape[0], 512), lambda i, begin=begin: (0, begin + first + i))
                for piece, begin in weights_for(j)
            ]
            + [pl.BlockSpec((tok, 256), lambda i: (0, first + i))] * QUAD
            + [pl.BlockSpec((tok, 128), lambda i: (0, CHUNK_HEADS[j] + first + i))] * QUAD,
            out_specs=[pl.BlockSpec((tok, 256), lambda i: (0, i))] * QUAD,
            scratch_shapes=[
                VMEM((2, window, LAT), jnp.bfloat16),
                VMEM((2, window, 128), jnp.bfloat16),
                VMEM((2, window, 128), jnp.bfloat16),
                VMEM((2, 2 * tok, window), jnp.float32),
                VMEM((LAT, 512), jnp.bfloat16),
            ],
            compiler_params=params,
            cost_estimate=pl.CostEstimate(
                flops=flops,
                bytes_accessed=heads << 20,
                transcendentals=heads * 4 * tok * window,
            ),
            name="attend",
        )(mine_info, own_rows, other_rows, *pieces_of_weight, *moved[j], *moved[j])

    results = []
    for call in CALLS:
        if len(results) > 1:
            mine_info = tie(mine_info, results[-2][2])
        pieces = attend(*call)
        mine_info = tie(mine_info, pieces[0])
        results.append([pieces[0]] + [quad_swap(pieces[r], r) for r in range(1, QUAD)])
    pieces = [one[r] for r in range(QUAD) for one in results]
    arrived = lax.all_to_all(
        tie(outgoing, results[-1][0]).reshape(size, slot_count, ROW),
        "ctx",
        split_axis=0,
        concat_axis=0,
        tiled=True,
    )
    decode_cache = arrived.reshape(size * slot_count, ROW)
    attn_out = pl.pallas_call(
        gather_kernel,
        out_shape=shape((tok, H * VDIM)),
        in_specs=[smem] + [anywhere] * len(pieces),
        out_specs=anywhere,
        scratch_shapes=[pltpu.SemaphoreType.DMA((len(pieces),))],
        compiler_params=params,
        name="place",
    )(quarter_info, *pieces)
    return (attn_out, decode_cache)


def solution(mesh):
    return jax.shard_map(
        body,
        mesh=mesh,
        in_specs=(
            P(("groups", "ctx"), None),
            P(("groups", "ctx"), None),
            P(),
            P("ctx", None),
            P(("groups", "ctx"), None),
            P("groups"),
        ),
        out_specs=(P(("groups", "ctx"), None), P(("groups", "ctx"), None)),
        check_vma=False,
    )
```

```python
import functools
import math

import jax
import jax.numpy as jnp
import numpy as np
from jax import lax
from jax.experimental import pallas as pl
from jax.experimental.pallas import tpu as pltpu
from jax.sharding import PartitionSpec as P

H = 64
NOPE = 128
ROPE = 64
VDIM = 128
LAT = 512
REACH = 3
QUAD = 4
HQ = H // QUAD
CHUNK_HEADS = (8, 8)
PHASES = (
    ("z", "y0", "b~", "f~", "q02"),
    ("z", "y1", "k", "q01"),
    ("z", "y2", "p", "q03", "q12~"),
    ("y3", "q13~", "q11"),
)
CHUNKS = len(CHUNK_HEADS)
FIRST_HEAD = tuple(sum(CHUNK_HEADS[:j]) for j in range(CHUNKS))
ROW = LAT + ROPE
EXT = 640
VMEM_LIMIT = 20 * 1024 * 1024
CALLS = ((0, 0, 4), (1, 0, 2), (1, 2, 2))
SMEM = pltpu.SMEM
VMEM = pltpu.VMEM


def rows_kernel(
    slot_count, info, lengths, kv, gain, ranks, freq, rows_out, cos_out, sin_out, outgoing_out
):
    tok = kv.shape[1]
    base = info[0] * tok
    spots = base + lax.broadcasted_iota(jnp.int32, (tok, 128), 0)
    lane = lax.broadcasted_iota(jnp.int32, (tok, 128), 1)
    begin = jnp.int32(0)
    own_start = jnp.zeros((tok, 128), jnp.int32)
    for r in range(lengths.shape[0]):
        own_start = jnp.where(spots >= begin, begin, own_start)
        begin = begin + lengths[r]
    offset = spots - own_start
    angles = offset.astype(jnp.float32) * freq[...]
    cosine = jnp.cos(angles)
    sine = jnp.where((lane & 32) == 0, -jnp.sin(angles), jnp.sin(angles))
    cos_out[...] = cosine
    sin_out[...] = sine
    raw = kv[...].astype(jnp.float32).T
    latent = raw[:, :LAT]
    mean = jnp.sum(latent * latent, axis=1, keepdims=True) * (1.0 / LAT)
    latent = latent * lax.rsqrt(mean + 1e-06) * gain[...]
    key = raw[:, LAT:]
    swapped = jnp.concatenate([key[:, ROPE // 2 :], key[:, : ROPE // 2]], axis=1)
    turned = key * cosine[:, :ROPE] + swapped * sine[:, :ROPE]
    high = (offset >> 8).astype(jnp.float32)
    low = (offset & 255).astype(jnp.float32)
    meta = jnp.where(lane == 0, high, jnp.where(lane == 1, low, 0.0))
    tail = jnp.concatenate([turned, meta[:, :ROPE]], axis=1)
    rows_out[:, :LAT] = latent.astype(jnp.bfloat16)
    rows_out[:, LAT:] = tail.astype(jnp.bfloat16)

    rank_row = jnp.broadcast_to(ranks[...], (tok, tok)).astype(jnp.float32)
    rank_col = rank_row.T
    earlier = lax.broadcasted_iota(jnp.int32, (tok, tok), 0) < lax.broadcasted_iota(
        jnp.int32, (tok, tok), 1
    )
    same = jnp.where((rank_col == rank_row) & earlier, 1.0, 0.0)
    slot = jnp.sum(same, axis=0, keepdims=True)
    target = (rank_row[:1] * slot_count + slot).astype(jnp.int32)
    spots_out = lax.broadcasted_iota(jnp.int32, (outgoing_out.shape[0], tok), 0)
    selector = jnp.where(spots_out == target, 1.0, 0.0).astype(jnp.bfloat16)
    picked = jnp.dot(selector, rows_out[:, :ROW], preferred_element_type=jnp.float32)
    outgoing_out[...] = picked.astype(jnp.bfloat16)


def query_kernel(info, query, cosine, sine, *outs):
    tok = query.shape[0]
    lane = lax.broadcasted_iota(jnp.int32, (tok, 128), 1)
    low_half = lane < 64
    first_quarter = (lane & 32) == 0
    cos_table = cosine[...]
    sin_table = sine[...]
    for r in range(QUAD):
        first = (info[0] ^ r) * (HQ * (NOPE + ROPE))
        for pair in range(HQ // 2):
            j = max(j for j in range(CHUNKS) if FIRST_HEAD[j] <= 2 * pair)
            out = outs[r * CHUNKS + j]
            at = pair - FIRST_HEAD[j] // 2
            rope_at = CHUNK_HEADS[j] * NOPE + at * 128
            begin = pl.multiple_of(first + pair * 2 * (NOPE + ROPE), 128)
            both = query[:, pl.ds(begin, 2 * (NOPE + ROPE))]
            mid = both[:, 128:256].astype(jnp.float32)
            end = both[:, 256:384].astype(jnp.float32)
            turned = jnp.where(low_half, mid, end)
            odd_nope = pltpu.roll(jnp.where(low_half, end, mid), 64, 1)
            swapped = jnp.where(
                first_quarter, pltpu.roll(turned, 96, 1), pltpu.roll(turned, 32, 1)
            )
            turned = turned * cos_table + swapped * sin_table
            out[:, at * 256 : at * 256 + 128] = both[:, :128]
            out[:, at * 256 + 128 : at * 256 + 256] = odd_nope.astype(jnp.bfloat16)
            out[:, rope_at : rope_at + 128] = turned.astype(jnp.bfloat16)


def pair_kernel(info, w_up, got, out, sem):
    rows, width = got.shape
    begin = pl.multiple_of(info[0] * width, 128)
    copies = [
        pltpu.make_async_copy(w_up.at[:, pl.ds(begin, width)], out.at[pl.ds(0, rows)], sem.at[0]),
        pltpu.make_async_copy(got, out.at[pl.ds(rows, rows)], sem.at[1]),
    ]
    for copy in copies:
        copy.start()
    for copy in copies:
        copy.wait()


def attend_kernel(outer, info, own, other, *refs):
    pieces_count = 2 * outer if outer else 1
    pieces_of_weight, refs = refs[:pieces_count], refs[pieces_count:]
    nope = refs[0:QUAD]
    rope = refs[QUAD : 2 * QUAD]
    outs = refs[2 * QUAD : 3 * QUAD]
    latent, rope_even, rope_odd, bias, held = refs[3 * QUAD :]
    tok = nope[0].shape[0]
    blocks = REACH + 2
    mine = info[0]
    partner = mine ^ 1
    scale = (NOPE + ROPE) ** (-0.5) * math.log2(math.e)

    @pl.when(pl.program_id(0) == 0)
    def _():
        has_last = (mine & 1) == 1
        starts = [mine, partner, mine - 2, partner - 2, (mine >> 1) * 2 - 3]
        blank = jnp.zeros((tok, ROPE), jnp.bfloat16)
        lane = lax.broadcasted_iota(jnp.int32, (tok, tok), 1)
        row = lax.broadcasted_iota(jnp.int32, (tok, tok), 0)
        for g in range(2):
            mine_of, other_of = [
                [ref[(3 * g + n) * tok : (3 * g + n + 1) * tok] for n in range(3)]
                for ref in (own, other)
            ]
            pieces = [
                mine_of[0],
                other_of[0],
                mine_of[1],
                other_of[1],
                jnp.where(has_last, mine_of[2], other_of[2]),
            ]
            for b, piece in enumerate(pieces):
                here = slice(b * tok, (b + 1) * tok)
                latent[g, here] = piece[:, :LAT]
                turned = piece[:, LAT : LAT + ROPE]
                rope_even[g, here] = jnp.concatenate([turned, blank], axis=1)
                rope_odd[g, here] = jnp.concatenate([blank, turned], axis=1)
            for half in range(2):
                meta = pieces[half][:, LAT:].astype(jnp.float32)
                offset = (meta[:, ROPE : ROPE + 1] * 256.0 + meta[:, ROPE + 1 : ROPE + 2]).astype(
                    jnp.int32
                )
                spots = starts[half] * tok + row
                lowest = jnp.maximum(spots - offset, (starts[half] - REACH) * tok)
                for b in range(blocks):
                    keys = starts[b] * tok + lane
                    allowed = (keys >= lowest) & (keys <= spots)
                    bias[g, half * tok : (half + 1) * tok, b * tok : (b + 1) * tok] = jnp.where(
                        allowed, 0.0, -1e30
                    )

    if outer:
        weight = held
        for i, piece in enumerate(pieces_of_weight):
            side, behind = i // outer, i % outer
            chip = ((mine >> 2) + outer - behind) % outer * 2 + (((mine >> 1) & 1) ^ side)
            rows = piece.shape[0] // 2
            for core in range(2):
                begin = pl.multiple_of(chip * 2 * rows + ((mine & 1) ^ core) * rows, rows)
                held[pl.ds(begin, rows)] = piece[core * rows : (core + 1) * rows]
    else:
        weight = pieces_of_weight[0]

    for g in range(2):
        expanded = jnp.dot(latent[g], weight[...], preferred_element_type=jnp.float32).astype(
            jnp.bfloat16
        )
        query_rope = jnp.concatenate([rope[2 * g][...], rope[2 * g + 1][...]], axis=0)
        for b in range(2):
            at = slice(b * 128, (b + 1) * 128)
            key_rope = (rope_even, rope_odd)[b][g]
            key = jnp.concatenate([expanded[:, b * 256 : b * 256 + 128], key_rope], axis=1)
            value = expanded[:, b * 256 + 128 : b * 256 + 256]
            query = jnp.concatenate([nope[2 * g][:, at], nope[2 * g + 1][:, at]], axis=0)
            query = jnp.concatenate([query, query_rope], axis=1)
            scores = lax.dot_general(
                query, key, (((1,), (1,)), ((), ())), preferred_element_type=jnp.float32
            )
            scores = scores * scale + bias[g]
            largest = jnp.max(scores, axis=1, keepdims=True)
            expo = jnp.exp2(scores - largest)
            total = jnp.sum(expo, axis=1, keepdims=True)
            mixed = jnp.dot(expo.astype(jnp.bfloat16), value, preferred_element_type=jnp.float32)
            mixed = (mixed / total).astype(jnp.bfloat16)
            outs[2 * g][:, at] = mixed[:tok]
            outs[2 * g + 1][:, at] = mixed[tok:]


def gather_kernel(info, *refs):
    pieces, out, sems = refs[:-2], refs[-2], refs[-1]
    copies = []
    for i, piece in enumerate(pieces):
        r, (j, first, steps) = i // len(CALLS), CALLS[i % len(CALLS)]
        begin = ((info[0] ^ r) * HQ + FIRST_HEAD[j] + 2 * first) * VDIM
        begin = pl.multiple_of(begin, 128)
        copies.append(
            pltpu.make_async_copy(piece, out.at[:, pl.ds(begin, piece.shape[1])], sems.at[i])
        )
    for copy in copies:
        copy.start()
    for copy in copies:
        copy.wait()


def tie(array, *others):
    return lax.optimization_barrier((array,) + others)[0]


class Phases:
    def __init__(self):
        self.before, self.before_late, self.now, self.late = [], [], [], []

    def turn(self):
        self.before = self.now + self.before_late
        self.before_late, self.now, self.late = self.late, [], []

    def send(self, late, permute, array, *args):
        arrived = permute(tie(array, *self.before) if self.before else array, *args)
        (self.late if late else self.now).append(arrived)
        return arrived


def shape(dims, kind=jnp.bfloat16):
    return jax.ShapeDtypeStruct(dims, kind)


def in_hbm(*arrays):
    return [pltpu.with_memory_space_constraint(array, pltpu.HBM) for array in arrays]


def body(q_heads, kv_latent, latent_gain, w_up, page_ranks, lengths):
    tok = q_heads.shape[0]
    size = lax.axis_size("ctx")
    groups = lax.axis_size("groups")
    mine = lax.axis_index("ctx")
    quarter = lax.axis_index("groups") * 2 + mine % 2
    slot_count = max(2, 2 * tok // size)
    smem = pl.BlockSpec(memory_space=SMEM)
    params = pltpu.CompilerParams(vmem_limit_bytes=VMEM_LIMIT)
    alone = pltpu.CompilerParams(vmem_limit_bytes=3 * VMEM_LIMIT)

    def quad_swap(array, r):
        dx, dc = r // 2, r % 2
        pairs = [
            (g * size + i, (g ^ dx) * size + (i ^ dc)) for g in range(groups) for i in range(size)
        ]
        return lax.ppermute(array, ("groups", "ctx"), pairs)

    def around(array, by):
        return lax.ppermute(array, "ctx", [(i, (i + by) % size) for i in range(size)])

    def inner_swap(array):
        return lax.ppermute(array, "ctx", [(i, i ^ 2) for i in range(size)])

    def from_behind(array, by, odd_only):
        first = 1 if odd_only else 0
        step = 2 if odd_only else 1
        pairs = [(i, i + by) for i in range(first, size - by, step)]
        return lax.ppermute(array, "ctx", pairs)

    width = HQ * (NOPE + VDIM)
    quarter_info = quarter[None].astype(jnp.int32)
    anywhere = pl.BlockSpec(memory_space=pl.ANY)
    give = lax.dynamic_slice_in_dim(w_up, (quarter ^ 1) * width, width, 1)
    give, lengths = lax.optimization_barrier((give, lengths))
    got = quad_swap(give, 1)
    outer = 4 if size == 16 else 0
    if outer:
        pair_rows = pl.pallas_call(
            pair_kernel,
            out_shape=shape((2 * w_up.shape[0], width)),
            in_specs=[smem, pl.BlockSpec(memory_space=pltpu.HBM), anywhere],
            out_specs=anywhere,
            scratch_shapes=[pltpu.SemaphoreType.DMA((2,))],
            compiler_params=params,
            name="pair",
        )(quarter_info, *in_hbm(w_up), got)
    else:
        keep = lax.dynamic_slice_in_dim(w_up, quarter * width, width, 1)
        even = mine % 2 == 0
        both = jnp.concatenate(
            [jnp.where(even, keep, got), jnp.where(even, got, keep)], axis=0
        )
        same_core = [list(range(c, size, 2)) for c in range(2)]
        gathered = lax.all_gather(both, "ctx", axis=0, tiled=True, axis_index_groups=same_core)

    frequency = np.exp(-np.arange(ROPE // 2) * (2.0 * math.log(10000.0) / ROPE))
    frequency = jnp.asarray(np.tile(frequency, 4)[None, :], jnp.float32)
    mine_info = mine[None].astype(jnp.int32)

    def block(*dims):
        return pl.BlockSpec(dims, lambda i: (0,) * len(dims))

    rows, cosine, sine, outgoing = pl.pallas_call(
        functools.partial(rows_kernel, slot_count),
        grid=(1,),
        out_shape=(
            shape((tok, EXT)),
            shape((tok, 128), jnp.float32),
            shape((tok, 128), jnp.float32),
            shape((size * slot_count, ROW)),
        ),
        in_specs=[smem, smem, block(ROW, tok), block(1, LAT), block(1, tok), block(1, 128)],
        out_specs=[
            block(tok, EXT),
            block(tok, 128),
            block(tok, 128),
            block(size * slot_count, ROW),
        ],
        compiler_params=alone,
        name="rows",
    )(
        mine_info,
        lengths,
        *in_hbm(kv_latent.T, latent_gain[None, :], page_ranks.T, frequency),
    )

    queries = pl.pallas_call(
        query_kernel,
        out_shape=[shape((tok, h * (NOPE + ROPE))) for h in CHUNK_HEADS] * QUAD,
        grid=(1,),
        in_specs=[smem, block(*q_heads.shape), block(tok, 128), block(tok, 128)],
        out_specs=[block(tok, h * (NOPE + ROPE)) for h in CHUNK_HEADS] * QUAD,
        compiler_params=params,
        cost_estimate=pl.CostEstimate(
            flops=0, bytes_accessed=4 * q_heads.size, transcendentals=0
        ),
        name="queries",
    )(quarter_info, *in_hbm(q_heads, tie(cosine, pair_rows if outer else got), sine))

    phases = Phases()
    line = [pair_rows] if outer else []
    side = []
    halves = []
    moved = [[queries[j]] + [None] * (QUAD - 1) for j in range(CHUNKS)]
    parts = {"r": tie(rows, pair_rows if outer else got)}
    for name in [name for phase in PHASES for name in phase + ("|",)]:
        kind, late = name[0], name[-1] == "~"
        if kind == "|":
            phases.now.append(queries[0])
            phases.turn()
        elif kind == "z" and outer:
            line.append(phases.send(late, around, line[-1], 4))
        elif kind == "y" and outer:
            step = int(name[1])
            if step < outer - 1:
                side.append(phases.send(late, inner_swap, line[step]))
            else:
                half = line[step].shape[1] // CHUNKS
                halves = [
                    phases.send(late, inner_swap, line[step][:, j * half : (j + 1) * half])
                    for j in range(CHUNKS)
                ]
        elif kind == "b":
            parts["b"] = phases.send(late, from_behind, parts["r"], 2, False)
        elif kind == "f":
            parts["f"] = phases.send(late, from_behind, parts["r"], 4, True)
        elif kind == "k":
            have = jnp.concatenate([parts["r"], parts["b"], parts["f"]], axis=0)
            swapped = phases.send(late, quad_swap, have, 2)
        elif kind == "p":
            own_rows = jnp.concatenate([have, swapped], axis=0)
            other_rows = phases.send(late, quad_swap, own_rows, 1)
        elif kind == "q":
            j, r = int(name[1]), int(name[2])
            moved[j][r] = phases.send(late, quad_swap, queries[r * CHUNKS + j], r)

    def weights_for(j):
        if not outer:
            return [(gathered, FIRST_HEAD[j] // 2)]
        return [(piece, FIRST_HEAD[j] // 2) for piece in line + side] + [(halves[j], 0)]

    window = (REACH + 2) * tok

    def attend(j, first, steps):
        heads = 2 * steps
        pieces_of_weight = [piece for piece, begin in weights_for(j)]
        flops = 2 * heads * 2 * (window * LAT * 256 + 2 * tok * window * (NOPE + ROPE + VDIM))
        return pl.pallas_call(
            functools.partial(attend_kernel, outer),
            grid=(steps,),
            out_shape=[shape((tok, heads * VDIM))] * QUAD,
            in_specs=[smem, block(6 * tok, EXT), block(6 * tok, EXT)]
            + [
                pl.BlockSpec((piece.shape[0], 512), lambda i, begin=begin: (0, begin + first + i))
                for piece, begin in weights_for(j)
            ]
            + [pl.BlockSpec((tok, 256), lambda i: (0, first + i))] * QUAD
            + [pl.BlockSpec((tok, 128), lambda i: (0, CHUNK_HEADS[j] + first + i))] * QUAD,
            out_specs=[pl.BlockSpec((tok, 256), lambda i: (0, i))] * QUAD,
            scratch_shapes=[
                VMEM((2, window, LAT), jnp.bfloat16),
                VMEM((2, window, 128), jnp.bfloat16),
                VMEM((2, window, 128), jnp.bfloat16),
                VMEM((2, 2 * tok, window), jnp.float32),
                VMEM((LAT, 512), jnp.bfloat16),
            ],
            compiler_params=params,
            cost_estimate=pl.CostEstimate(
                flops=flops,
                bytes_accessed=heads << 20,
                transcendentals=heads * 4 * tok * window,
            ),
            name="attend",
        )(mine_info, own_rows, other_rows, *pieces_of_weight, *moved[j], *moved[j])

    results = []
    for call in CALLS:
        if len(results) > 1:
            mine_info = tie(mine_info, *results[-2][1:3])
        pieces = attend(*call)
        mine_info = tie(mine_info, pieces[0])
        results.append(
            [pieces[0]] + [quad_swap(pieces[r], r) for r in range(1, QUAD)]
        )
    pieces = [one[r] for r in range(QUAD) for one in results]
    arrived = lax.all_to_all(
        tie(outgoing, results[-1][2]).reshape(size, slot_count, ROW),
        "ctx",
        split_axis=0,
        concat_axis=0,
        tiled=True,
    )
    decode_cache = arrived.reshape(size * slot_count, ROW)
    attn_out = pl.pallas_call(
        gather_kernel,
        out_shape=shape((tok, H * VDIM)),
        in_specs=[smem] + [anywhere] * len(pieces),
        out_specs=anywhere,
        scratch_shapes=[pltpu.SemaphoreType.DMA((len(pieces),))],
        compiler_params=params,
        name="place",
    )(quarter_info, *pieces)
    return (attn_out, decode_cache)


def solution(mesh):
    return jax.shard_map(
        body,
        mesh=mesh,
        in_specs=(
            P(("groups", "ctx"), None),
            P(("groups", "ctx"), None),
            P(),
            P("ctx", None),
            P(("groups", "ctx"), None),
            P("groups"),
        ),
        out_specs=(P(("groups", "ctx"), None), P(("groups", "ctx"), None)),
        check_vma=False,
    )
```

```python
import functools
import math

import jax
import jax.numpy as jnp
import numpy as np
from jax import lax
from jax.experimental import pallas as pl
from jax.experimental.pallas import tpu as pltpu
from jax.sharding import PartitionSpec as P

H = 64
NOPE = 128
ROPE = 64
VDIM = 128
LAT = 512
REACH = 3
QUAD = 4
HQ = H // QUAD
CHUNK_HEADS = (8, 8)
PHASES = (
    ("z", "y0", "b~", "f~", "q02"),
    ("z", "y1", "k", "q01"),
    ("z", "y2", "p", "q03", "q12~"),
    ("y3", "w", "q13~", "q11"),
)
CHUNKS = len(CHUNK_HEADS)
FIRST_HEAD = tuple(sum(CHUNK_HEADS[:j]) for j in range(CHUNKS))
ROW = LAT + ROPE
EXT = 640
VMEM_LIMIT = 20 * 1024 * 1024
CALLS = ((0, 0, 4), (1, 0, 2), (1, 2, 2))
SMEM = pltpu.SMEM
VMEM = pltpu.VMEM


def rows_kernel(
    slot_count, info, lengths, kv, gain, ranks, freq, rows_out, cos_out, sin_out, outgoing_out
):
    tok = kv.shape[1]
    base = info[0] * tok
    spots = base + lax.broadcasted_iota(jnp.int32, (tok, 128), 0)
    lane = lax.broadcasted_iota(jnp.int32, (tok, 128), 1)
    begin = jnp.int32(0)
    own_start = jnp.zeros((tok, 128), jnp.int32)
    for r in range(lengths.shape[0]):
        own_start = jnp.where(spots >= begin, begin, own_start)
        begin = begin + lengths[r]
    offset = spots - own_start
    angles = offset.astype(jnp.float32) * freq[...]
    cosine = jnp.cos(angles)
    sine = jnp.where((lane & 32) == 0, -jnp.sin(angles), jnp.sin(angles))
    cos_out[...] = cosine
    sin_out[...] = sine
    raw = kv[...].astype(jnp.float32).T
    latent = raw[:, :LAT]
    mean = jnp.sum(latent * latent, axis=1, keepdims=True) * (1.0 / LAT)
    latent = latent * lax.rsqrt(mean + 1e-06) * gain[...]
    key = raw[:, LAT:]
    swapped = jnp.concatenate([key[:, ROPE // 2 :], key[:, : ROPE // 2]], axis=1)
    turned = key * cosine[:, :ROPE] + swapped * sine[:, :ROPE]
    high = (offset >> 8).astype(jnp.float32)
    low = (offset & 255).astype(jnp.float32)
    meta = jnp.where(lane == 0, high, jnp.where(lane == 1, low, 0.0))
    tail = jnp.concatenate([turned, meta[:, :ROPE]], axis=1)
    rows_out[:, :LAT] = latent.astype(jnp.bfloat16)
    rows_out[:, LAT:] = tail.astype(jnp.bfloat16)

    rank_row = jnp.broadcast_to(ranks[...], (tok, tok)).astype(jnp.float32)
    rank_col = rank_row.T
    earlier = lax.broadcasted_iota(jnp.int32, (tok, tok), 0) < lax.broadcasted_iota(
        jnp.int32, (tok, tok), 1
    )
    same = jnp.where((rank_col == rank_row) & earlier, 1.0, 0.0)
    slot = jnp.sum(same, axis=0, keepdims=True)
    target = (rank_row[:1] * slot_count + slot).astype(jnp.int32)
    spots_out = lax.broadcasted_iota(jnp.int32, (outgoing_out.shape[0], tok), 0)
    selector = jnp.where(spots_out == target, 1.0, 0.0).astype(jnp.bfloat16)
    picked = jnp.dot(selector, rows_out[:, :ROW], preferred_element_type=jnp.float32)
    outgoing_out[...] = picked.astype(jnp.bfloat16)


def query_kernel(info, query, cosine, sine, *outs):
    tok = query.shape[0]
    lane = lax.broadcasted_iota(jnp.int32, (tok, 128), 1)
    low_half = lane < 64
    first_quarter = (lane & 32) == 0
    cos_table = cosine[...]
    sin_table = sine[...]
    for r in range(QUAD):
        first = (info[0] ^ r) * (HQ * (NOPE + ROPE))
        for pair in range(HQ // 2):
            j = max(j for j in range(CHUNKS) if FIRST_HEAD[j] <= 2 * pair)
            out = outs[r * CHUNKS + j]
            at = pair - FIRST_HEAD[j] // 2
            rope_at = CHUNK_HEADS[j] * NOPE + at * 128
            begin = pl.multiple_of(first + pair * 2 * (NOPE + ROPE), 128)
            both = query[:, pl.ds(begin, 2 * (NOPE + ROPE))]
            mid = both[:, 128:256].astype(jnp.float32)
            end = both[:, 256:384].astype(jnp.float32)
            turned = jnp.where(low_half, mid, end)
            odd_nope = pltpu.roll(jnp.where(low_half, end, mid), 64, 1)
            swapped = jnp.where(
                first_quarter, pltpu.roll(turned, 96, 1), pltpu.roll(turned, 32, 1)
            )
            turned = turned * cos_table + swapped * sin_table
            out[:, at * 256 : at * 256 + 128] = both[:, :128]
            out[:, at * 256 + 128 : at * 256 + 256] = odd_nope.astype(jnp.bfloat16)
            out[:, rope_at : rope_at + 128] = turned.astype(jnp.bfloat16)


def pair_kernel(info, w_up, got, out, sem):
    rows, width = got.shape
    begin = pl.multiple_of(info[0] * width, 128)
    copies = [
        pltpu.make_async_copy(w_up.at[:, pl.ds(begin, width)], out.at[pl.ds(0, rows)], sem.at[0]),
        pltpu.make_async_copy(got, out.at[pl.ds(rows, rows)], sem.at[1]),
    ]
    for copy in copies:
        copy.start()
    for copy in copies:
        copy.wait()


def keys_kernel(info, own, other, latent, rope_even, rope_odd, bias):
    tok = own.shape[0] // 6
    mine = info[0]
    partner = mine ^ 1
    has_last = (mine & 1) == 1
    starts = [mine, partner, mine - 2, partner - 2, (mine >> 1) * 2 - 3]
    blank = jnp.zeros((tok, ROPE), jnp.bfloat16)
    lane = lax.broadcasted_iota(jnp.int32, (tok, tok), 1)
    row = lax.broadcasted_iota(jnp.int32, (tok, tok), 0)
    for g in range(2):
        mine_of, other_of = [
            [ref[(3 * g + n) * tok : (3 * g + n + 1) * tok] for n in range(3)]
            for ref in (own, other)
        ]
        pieces = [
            mine_of[0],
            other_of[0],
            mine_of[1],
            other_of[1],
            jnp.where(has_last, mine_of[2], other_of[2]),
        ]
        for b, piece in enumerate(pieces):
            here = slice(b * tok, (b + 1) * tok)
            latent[g, here] = piece[:, :LAT]
            turned = piece[:, LAT : LAT + ROPE]
            rope_even[g, here] = jnp.concatenate([turned, blank], axis=1)
            rope_odd[g, here] = jnp.concatenate([blank, turned], axis=1)
        for half in range(2):
            meta = pieces[half][:, LAT:].astype(jnp.float32)
            offset = (meta[:, ROPE : ROPE + 1] * 256.0 + meta[:, ROPE + 1 : ROPE + 2]).astype(
                jnp.int32
            )
            spots = starts[half] * tok + row
            lowest = jnp.maximum(spots - offset, (starts[half] - REACH) * tok)
            for b in range(REACH + 2):
                keys = starts[b] * tok + lane
                allowed = (keys >= lowest) & (keys <= spots)
                bias[g, half * tok : (half + 1) * tok, b * tok : (b + 1) * tok] = jnp.where(
                    allowed, 0.0, -1e30
                )


def attend_kernel(outer, info, latent, rope_even, rope_odd, bias, *refs):
    pieces_count = 2 * outer if outer else 1
    pieces_of_weight, refs = refs[:pieces_count], refs[pieces_count:]
    nope = refs[0:QUAD]
    rope = refs[QUAD : 2 * QUAD]
    outs = refs[2 * QUAD : 3 * QUAD]
    held = refs[3 * QUAD]
    tok = nope[0].shape[0]
    mine = info[0]
    scale = (NOPE + ROPE) ** (-0.5) * math.log2(math.e)

    if outer:
        weight = held
        for i, piece in enumerate(pieces_of_weight):
            side, behind = i // outer, i % outer
            chip = ((mine >> 2) + outer - behind) % outer * 2 + (((mine >> 1) & 1) ^ side)
            rows = piece.shape[0] // 2
            for core in range(2):
                begin = pl.multiple_of(chip * 2 * rows + ((mine & 1) ^ core) * rows, rows)
                held[pl.ds(begin, rows)] = piece[core * rows : (core + 1) * rows]
    else:
        weight = pieces_of_weight[0]

    def expand(g):
        wide = jnp.dot(latent[g], weight[...], preferred_element_type=jnp.float32)
        return wide.astype(jnp.bfloat16)

    def score(g, b, expanded):
        at = slice(b * 128, (b + 1) * 128)
        key_rope = (rope_even, rope_odd)[b][g]
        key = jnp.concatenate([expanded[:, b * 256 : b * 256 + 128], key_rope], axis=1)
        query = jnp.concatenate(
            [
                jnp.concatenate([nope[2 * g][:, at], rope[2 * g][...]], axis=1),
                jnp.concatenate([nope[2 * g + 1][:, at], rope[2 * g + 1][...]], axis=1),
            ],
            axis=0,
        )
        return lax.dot_general(
            query, key, (((1,), (1,)), ((), ())), preferred_element_type=jnp.float32
        )

    def weigh(g, scores):
        scores = scores * scale + bias[g]
        largest = jnp.max(scores, axis=1, keepdims=True)
        expo = jnp.exp2(scores - largest)
        return expo.astype(jnp.bfloat16), jnp.sum(expo, axis=1, keepdims=True)

    def mix(g, b, expanded, weights, total):
        at = slice(b * 128, (b + 1) * 128)
        value = expanded[:, b * 256 + 128 : b * 256 + 256]
        mixed = jnp.dot(weights, value, preferred_element_type=jnp.float32)
        mixed = (mixed / total).astype(jnp.bfloat16)
        outs[2 * g][:, at] = mixed[:tok]
        outs[2 * g + 1][:, at] = mixed[tok:]

    first = expand(0)
    scores = score(0, 0, first)
    second = expand(1)
    weighed = weigh(0, scores)
    scores = score(0, 1, first)
    mix(0, 0, first, *weighed)
    weighed = weigh(0, scores)
    scores = score(1, 0, second)
    mix(0, 1, first, *weighed)
    weighed = weigh(1, scores)
    scores = score(1, 1, second)
    mix(1, 0, second, *weighed)
    weighed = weigh(1, scores)
    mix(1, 1, second, *weighed)


def gather_kernel(info, *refs):
    pieces, out, sems = refs[:-2], refs[-2], refs[-1]
    copies = []
    for i, piece in enumerate(pieces):
        r, (j, first, steps) = i // len(CALLS), CALLS[i % len(CALLS)]
        begin = ((info[0] ^ r) * HQ + FIRST_HEAD[j] + 2 * first) * VDIM
        begin = pl.multiple_of(begin, 128)
        copies.append(
            pltpu.make_async_copy(piece, out.at[:, pl.ds(begin, piece.shape[1])], sems.at[i])
        )
    for copy in copies:
        copy.start()
    for copy in copies:
        copy.wait()


def tie(array, *others):
    return lax.optimization_barrier((array,) + others)[0]


class Phases:
    def __init__(self):
        self.before, self.before_late, self.now, self.late = [], [], [], []

    def turn(self):
        self.before = self.now + self.before_late
        self.before_late, self.now, self.late = self.late, [], []

    def send(self, late, permute, array, *args):
        arrived = permute(tie(array, *self.before) if self.before else array, *args)
        (self.late if late else self.now).append(arrived)
        return arrived


def shape(dims, kind=jnp.bfloat16):
    return jax.ShapeDtypeStruct(dims, kind)


def in_hbm(*arrays):
    return [pltpu.with_memory_space_constraint(array, pltpu.HBM) for array in arrays]


def body(q_heads, kv_latent, latent_gain, w_up, page_ranks, lengths):
    tok = q_heads.shape[0]
    size = lax.axis_size("ctx")
    groups = lax.axis_size("groups")
    mine = lax.axis_index("ctx")
    quarter = lax.axis_index("groups") * 2 + mine % 2
    slot_count = max(2, 2 * tok // size)
    smem = pl.BlockSpec(memory_space=SMEM)
    params = pltpu.CompilerParams(vmem_limit_bytes=VMEM_LIMIT)
    alone = pltpu.CompilerParams(vmem_limit_bytes=3 * VMEM_LIMIT)

    def quad_swap(array, r):
        dx, dc = r // 2, r % 2
        pairs = [
            (g * size + i, (g ^ dx) * size + (i ^ dc)) for g in range(groups) for i in range(size)
        ]
        return lax.ppermute(array, ("groups", "ctx"), pairs)

    def around(array, by):
        return lax.ppermute(array, "ctx", [(i, (i + by) % size) for i in range(size)])

    def inner_swap(array):
        return lax.ppermute(array, "ctx", [(i, i ^ 2) for i in range(size)])

    def from_behind(array, by, odd_only):
        first = 1 if odd_only else 0
        step = 2 if odd_only else 1
        pairs = [(i, i + by) for i in range(first, size - by, step)]
        return lax.ppermute(array, "ctx", pairs)

    width = HQ * (NOPE + VDIM)
    quarter_info = quarter[None].astype(jnp.int32)
    anywhere = pl.BlockSpec(memory_space=pl.ANY)
    give = lax.dynamic_slice_in_dim(w_up, (quarter ^ 1) * width, width, 1)
    give, lengths = lax.optimization_barrier((give, lengths))
    got = quad_swap(give, 1)
    outer = 4 if size == 16 else 0
    if outer:
        pair_rows = pl.pallas_call(
            pair_kernel,
            out_shape=shape((2 * w_up.shape[0], width)),
            in_specs=[smem, pl.BlockSpec(memory_space=pltpu.HBM), anywhere],
            out_specs=anywhere,
            scratch_shapes=[pltpu.SemaphoreType.DMA((2,))],
            compiler_params=params,
            name="pair",
        )(quarter_info, *in_hbm(w_up), got)
    else:
        keep = lax.dynamic_slice_in_dim(w_up, quarter * width, width, 1)
        even = mine % 2 == 0
        both = jnp.concatenate(
            [jnp.where(even, keep, got), jnp.where(even, got, keep)], axis=0
        )
        same_core = [list(range(c, size, 2)) for c in range(2)]
        gathered = lax.all_gather(both, "ctx", axis=0, tiled=True, axis_index_groups=same_core)

    frequency = np.exp(-np.arange(ROPE // 2) * (2.0 * math.log(10000.0) / ROPE))
    frequency = jnp.asarray(np.tile(frequency, 4)[None, :], jnp.float32)
    mine_info = mine[None].astype(jnp.int32)

    def block(*dims):
        return pl.BlockSpec(dims, lambda i: (0,) * len(dims))

    rows, cosine, sine, outgoing = pl.pallas_call(
        functools.partial(rows_kernel, slot_count),
        grid=(1,),
        out_shape=(
            shape((tok, EXT)),
            shape((tok, 128), jnp.float32),
            shape((tok, 128), jnp.float32),
            shape((size * slot_count, ROW)),
        ),
        in_specs=[smem, smem, block(ROW, tok), block(1, LAT), block(1, tok), block(1, 128)],
        out_specs=[
            block(tok, EXT),
            block(tok, 128),
            block(tok, 128),
            block(size * slot_count, ROW),
        ],
        compiler_params=alone,
        name="rows",
    )(
        mine_info,
        lengths,
        *in_hbm(kv_latent.T, latent_gain[None, :], page_ranks.T, frequency),
    )

    queries = pl.pallas_call(
        query_kernel,
        out_shape=[shape((tok, h * (NOPE + ROPE))) for h in CHUNK_HEADS] * QUAD,
        grid=(1,),
        in_specs=[smem, block(*q_heads.shape), block(tok, 128), block(tok, 128)],
        out_specs=[block(tok, h * (NOPE + ROPE)) for h in CHUNK_HEADS] * QUAD,
        compiler_params=params,
        cost_estimate=pl.CostEstimate(
            flops=0, bytes_accessed=4 * q_heads.size, transcendentals=0
        ),
        name="queries",
    )(quarter_info, *in_hbm(q_heads, tie(cosine, pair_rows if outer else got), sine))

    phases = Phases()
    line = [pair_rows] if outer else []
    side = []
    half = width // CHUNKS
    halves = []
    moved = [[queries[j]] + [None] * (QUAD - 1) for j in range(CHUNKS)]
    parts = {"r": tie(rows, pair_rows if outer else got)}
    for name in [name for phase in PHASES for name in phase + ("|",)]:
        kind, late = name[0], name[-1] == "~"
        if kind == "|":
            phases.now.append(queries[0])
            phases.turn()
        elif kind == "z" and outer:
            line.append(phases.send(late, around, line[-1], 4))
        elif kind == "y" and outer:
            step = int(name[1])
            if step < outer - 1:
                side.append(phases.send(late, inner_swap, line[step]))
            else:
                halves.append(phases.send(late, inner_swap, line[step][:, :half]))
        elif kind == "w" and outer:
            halves.append(phases.send(late, around, side[-1][:, half:], 4))
        elif kind == "b":
            parts["b"] = phases.send(late, from_behind, parts["r"], 2, False)
        elif kind == "f":
            parts["f"] = phases.send(late, from_behind, parts["r"], 4, True)
        elif kind == "k":
            have = jnp.concatenate([parts["r"], parts["b"], parts["f"]], axis=0)
            swapped = phases.send(late, quad_swap, have, 2)
        elif kind == "p":
            own_rows = jnp.concatenate([have, swapped], axis=0)
            other_rows = phases.send(late, quad_swap, own_rows, 1)
        elif kind == "q":
            j, r = int(name[1]), int(name[2])
            moved[j][r] = phases.send(late, quad_swap, queries[r * CHUNKS + j], r)

    def weights_for(j):
        if not outer:
            return [(gathered, FIRST_HEAD[j] // 2)]
        return [(piece, FIRST_HEAD[j] // 2) for piece in line + side] + [(halves[j], 0)]

    window = (REACH + 2) * tok
    resident = pl.BlockSpec(memory_space=VMEM)
    keys = pl.pallas_call(
        keys_kernel,
        out_shape=(
            shape((2, window, LAT)),
            shape((2, window, 128)),
            shape((2, window, 128)),
            shape((2, 2 * tok, window), jnp.float32),
        ),
        in_specs=[smem, resident, resident],
        out_specs=[resident] * 4,
        compiler_params=params,
        cost_estimate=pl.CostEstimate(flops=0, bytes_accessed=8 << 20, transcendentals=0),
        name="keys",
    )(mine_info, own_rows, other_rows)

    def attend(j, first, steps):
        heads = 2 * steps
        pieces_of_weight = [piece for piece, begin in weights_for(j)]
        flops = 2 * heads * 2 * (window * LAT * 256 + 2 * tok * window * (NOPE + ROPE + VDIM))
        return pl.pallas_call(
            functools.partial(attend_kernel, outer),
            grid=(steps,),
            out_shape=[shape((tok, heads * VDIM))] * QUAD,
            in_specs=[smem] + [resident] * 4
            + [
                pl.BlockSpec((piece.shape[0], 512), lambda i, begin=begin: (0, begin + first + i))
                for piece, begin in weights_for(j)
            ]
            + [pl.BlockSpec((tok, 256), lambda i: (0, first + i))] * QUAD
            + [pl.BlockSpec((tok, 128), lambda i: (0, CHUNK_HEADS[j] + first + i))] * QUAD,
            out_specs=[pl.BlockSpec((tok, 256), lambda i: (0, i))] * QUAD,
            scratch_shapes=[VMEM((LAT, 512), jnp.bfloat16)],
            compiler_params=params,
            cost_estimate=pl.CostEstimate(
                flops=flops,
                bytes_accessed=heads << 20,
                transcendentals=heads * 4 * tok * window,
            ),
            name="attend",
        )(mine_info, *keys, *pieces_of_weight, *moved[j], *moved[j])

    results = []
    for call in CALLS:
        sent = [piece for one in results for piece in one[1:]]
        last = len(results) + 1 == len(CALLS)
        mine_info = tie(mine_info, *(results[0][2:3] if last else []))
        pieces = attend(*call)
        mine_info = tie(mine_info, pieces[0])
        before = sent[:-1] if last else []
        results.append(
            [pieces[0]] + [quad_swap(tie(pieces[r], *before), r) for r in range(1, QUAD)]
        )
    pieces = [one[r] for r in range(QUAD) for one in results]
    sent = [piece for one in results for piece in one[1:]]
    arrived = lax.all_to_all(
        tie(outgoing, *sent).reshape(size, slot_count, ROW),
        "ctx",
        split_axis=0,
        concat_axis=0,
        tiled=True,
    )
    decode_cache = arrived.reshape(size * slot_count, ROW)
    attn_out = pl.pallas_call(
        gather_kernel,
        out_shape=shape((tok, H * VDIM)),
        in_specs=[smem] + [anywhere] * len(pieces),
        out_specs=anywhere,
        scratch_shapes=[pltpu.SemaphoreType.DMA((len(pieces),))],
        compiler_params=params,
        name="place",
    )(quarter_info, *pieces)
    return (attn_out, decode_cache)


def solution(mesh):
    return jax.shard_map(
        body,
        mesh=mesh,
        in_specs=(
            P(("groups", "ctx"), None),
            P(("groups", "ctx"), None),
            P(),
            P("ctx", None),
            P(("groups", "ctx"), None),
            P("groups"),
        ),
        out_specs=(P(("groups", "ctx"), None), P(("groups", "ctx"), None)),
        check_vma=False,
    )
```

```python
import functools
import math

import jax
import jax.numpy as jnp
import numpy as np
from jax import lax
from jax.experimental import pallas as pl
from jax.experimental.pallas import tpu as pltpu
from jax.sharding import PartitionSpec as P

H = 64
NOPE = 128
ROPE = 64
VDIM = 128
LAT = 512
REACH = 3
QUAD = 4
HQ = H // QUAD
CHUNK_HEADS = (8, 8)
PHASES = (
    ("z", "y0", "b~", "f~", "q02", "d~"),
    ("z", "y1", "k", "q01"),
    ("z", "y2", "p", "q03"),
    ("y3", "w", "q12~", "q13~", "q11"),
)
CHUNKS = len(CHUNK_HEADS)
FIRST_HEAD = tuple(sum(CHUNK_HEADS[:j]) for j in range(CHUNKS))
ROW = LAT + ROPE
EXT = 640
VMEM_LIMIT = 20 * 1024 * 1024
CALLS = ((0, 0, 2), (0, 2, 2), (1, 0, 2), (1, 2, 2))
SMEM = pltpu.SMEM
VMEM = pltpu.VMEM


def rows_kernel(
    slot_count, info, lengths, kv, gain, ranks, freq, rows_out, cos_out, sin_out, outgoing_out
):
    tok = kv.shape[1]
    base = info[0] * tok
    spots = base + lax.broadcasted_iota(jnp.int32, (tok, 128), 0)
    lane = lax.broadcasted_iota(jnp.int32, (tok, 128), 1)
    begin = jnp.int32(0)
    own_start = jnp.zeros((tok, 128), jnp.int32)
    for r in range(lengths.shape[0]):
        own_start = jnp.where(spots >= begin, begin, own_start)
        begin = begin + lengths[r]
    offset = spots - own_start
    angles = offset.astype(jnp.float32) * freq[...]
    cosine = jnp.cos(angles)
    sine = jnp.where((lane & 32) == 0, -jnp.sin(angles), jnp.sin(angles))
    cos_out[...] = cosine
    sin_out[...] = sine
    raw = kv[...].astype(jnp.float32).T
    latent = raw[:, :LAT]
    mean = jnp.sum(latent * latent, axis=1, keepdims=True) * (1.0 / LAT)
    latent = latent * lax.rsqrt(mean + 1e-06) * gain[...]
    key = raw[:, LAT:]
    swapped = jnp.concatenate([key[:, ROPE // 2 :], key[:, : ROPE // 2]], axis=1)
    turned = key * cosine[:, :ROPE] + swapped * sine[:, :ROPE]
    high = (offset >> 8).astype(jnp.float32)
    low = (offset & 255).astype(jnp.float32)
    meta = jnp.where(lane == 0, high, jnp.where(lane == 1, low, 0.0))
    tail = jnp.concatenate([turned, meta[:, :ROPE]], axis=1)
    rows_out[:, :LAT] = latent.astype(jnp.bfloat16)
    rows_out[:, LAT:] = tail.astype(jnp.bfloat16)

    rank_row = jnp.broadcast_to(ranks[...], (tok, tok)).astype(jnp.float32)
    rank_col = rank_row.T
    earlier = lax.broadcasted_iota(jnp.int32, (tok, tok), 0) < lax.broadcasted_iota(
        jnp.int32, (tok, tok), 1
    )
    same = jnp.where((rank_col == rank_row) & earlier, 1.0, 0.0)
    slot = jnp.sum(same, axis=0, keepdims=True)
    target = (rank_row[:1] * slot_count + slot).astype(jnp.int32)
    spots_out = lax.broadcasted_iota(jnp.int32, (outgoing_out.shape[0], tok), 0)
    selector = jnp.where(spots_out == target, 1.0, 0.0).astype(jnp.bfloat16)
    picked = jnp.dot(selector, rows_out[:, :ROW], preferred_element_type=jnp.float32)
    outgoing_out[...] = picked.astype(jnp.bfloat16)


def query_kernel(info, query, cosine, sine, *outs):
    tok = query.shape[0]
    lane = lax.broadcasted_iota(jnp.int32, (tok, 128), 1)
    low_half = lane < 64
    first_quarter = (lane & 32) == 0
    cos_table = cosine[...]
    sin_table = sine[...]
    for r in range(QUAD):
        first = (info[0] ^ r) * (HQ * (NOPE + ROPE))
        for pair in range(HQ // 2):
            j = max(j for j in range(CHUNKS) if FIRST_HEAD[j] <= 2 * pair)
            out = outs[r * CHUNKS + j]
            at = pair - FIRST_HEAD[j] // 2
            rope_at = CHUNK_HEADS[j] * NOPE + at * 128
            begin = pl.multiple_of(first + pair * 2 * (NOPE + ROPE), 128)
            both = query[:, pl.ds(begin, 2 * (NOPE + ROPE))]
            mid = both[:, 128:256].astype(jnp.float32)
            end = both[:, 256:384].astype(jnp.float32)
            turned = jnp.where(low_half, mid, end)
            odd_nope = pltpu.roll(jnp.where(low_half, end, mid), 64, 1)
            swapped = jnp.where(
                first_quarter, pltpu.roll(turned, 96, 1), pltpu.roll(turned, 32, 1)
            )
            turned = turned * cos_table + swapped * sin_table
            out[:, at * 256 : at * 256 + 128] = both[:, :128]
            out[:, at * 256 + 128 : at * 256 + 256] = odd_nope.astype(jnp.bfloat16)
            out[:, rope_at : rope_at + 128] = turned.astype(jnp.bfloat16)


def pair_kernel(info, w_up, got, out, sem):
    rows, width = got.shape
    begin = pl.multiple_of(info[0] * width, 128)
    copies = [
        pltpu.make_async_copy(w_up.at[:, pl.ds(begin, width)], out.at[pl.ds(0, rows)], sem.at[0]),
        pltpu.make_async_copy(got, out.at[pl.ds(rows, rows)], sem.at[1]),
    ]
    for copy in copies:
        copy.start()
    for copy in copies:
        copy.wait()


def keys_kernel(info, own, other, latent, rope_even, rope_odd, bias):
    tok = own.shape[0] // 6
    mine = info[0]
    partner = mine ^ 1
    has_last = (mine & 1) == 1
    starts = [mine, partner, mine - 2, partner - 2, (mine >> 1) * 2 - 3]
    blank = jnp.zeros((tok, ROPE), jnp.bfloat16)
    lane = lax.broadcasted_iota(jnp.int32, (tok, tok), 1)
    row = lax.broadcasted_iota(jnp.int32, (tok, tok), 0)
    for g in range(2):
        mine_of, other_of = [
            [ref[(3 * g + n) * tok : (3 * g + n + 1) * tok] for n in range(3)]
            for ref in (own, other)
        ]
        pieces = [
            mine_of[0],
            other_of[0],
            mine_of[1],
            other_of[1],
            jnp.where(has_last, mine_of[2], other_of[2]),
        ]
        for b, piece in enumerate(pieces):
            here = slice(b * tok, (b + 1) * tok)
            latent[g, here] = piece[:, :LAT]
            turned = piece[:, LAT : LAT + ROPE]
            rope_even[g, here] = jnp.concatenate([turned, blank], axis=1)
            rope_odd[g, here] = jnp.concatenate([blank, turned], axis=1)
        for half in range(2):
            meta = pieces[half][:, LAT:].astype(jnp.float32)
            offset = (meta[:, ROPE : ROPE + 1] * 256.0 + meta[:, ROPE + 1 : ROPE + 2]).astype(
                jnp.int32
            )
            spots = starts[half] * tok + row
            lowest = jnp.maximum(spots - offset, (starts[half] - REACH) * tok)
            for b in range(REACH + 2):
                keys = starts[b] * tok + lane
                allowed = (keys >= lowest) & (keys <= spots)
                bias[g, half * tok : (half + 1) * tok, b * tok : (b + 1) * tok] = jnp.where(
                    allowed, 0.0, -1e30
                )


def attend_kernel(outer, info, latent, rope_even, rope_odd, bias, *refs):
    pieces_count = 2 * outer if outer else 1
    pieces_of_weight, refs = refs[:pieces_count], refs[pieces_count:]
    nope = refs[0:QUAD]
    rope = refs[QUAD : 2 * QUAD]
    outs = refs[2 * QUAD : 3 * QUAD]
    held = refs[3 * QUAD]
    tok = nope[0].shape[0]
    mine = info[0]
    scale = (NOPE + ROPE) ** (-0.5) * math.log2(math.e)

    if outer:
        weight = held
        for i, piece in enumerate(pieces_of_weight):
            side, behind = i // outer, i % outer
            chip = ((mine >> 2) + outer - behind) % outer * 2 + (((mine >> 1) & 1) ^ side)
            rows = piece.shape[0] // 2
            for core in range(2):
                begin = pl.multiple_of(chip * 2 * rows + ((mine & 1) ^ core) * rows, rows)
                held[pl.ds(begin, rows)] = piece[core * rows : (core + 1) * rows]
    else:
        weight = pieces_of_weight[0]

    def expand(g):
        wide = jnp.dot(latent[g], weight[...], preferred_element_type=jnp.float32)
        return wide.astype(jnp.bfloat16)

    def score(g, b, expanded):
        at = slice(b * 128, (b + 1) * 128)
        key_rope = (rope_even, rope_odd)[b][g]
        key = jnp.concatenate([expanded[:, b * 256 : b * 256 + 128], key_rope], axis=1)
        query = jnp.concatenate(
            [
                jnp.concatenate([nope[2 * g][:, at], rope[2 * g][...]], axis=1),
                jnp.concatenate([nope[2 * g + 1][:, at], rope[2 * g + 1][...]], axis=1),
            ],
            axis=0,
        )
        return lax.dot_general(
            query, key, (((1,), (1,)), ((), ())), preferred_element_type=jnp.float32
        )

    def weigh(g, scores):
        scores = scores * scale + bias[g]
        largest = jnp.max(scores, axis=1, keepdims=True)
        expo = jnp.exp2(scores - largest)
        return expo.astype(jnp.bfloat16), jnp.sum(expo, axis=1, keepdims=True)

    def mix(g, b, expanded, weights, total):
        at = slice(b * 128, (b + 1) * 128)
        value = expanded[:, b * 256 + 128 : b * 256 + 256]
        mixed = jnp.dot(weights, value, preferred_element_type=jnp.float32)
        mixed = (mixed / total).astype(jnp.bfloat16)
        outs[2 * g][:, at] = mixed[:tok]
        outs[2 * g + 1][:, at] = mixed[tok:]

    first = expand(0)
    scores = score(0, 0, first)
    second = expand(1)
    weighed = weigh(0, scores)
    scores = score(0, 1, first)
    mix(0, 0, first, *weighed)
    weighed = weigh(0, scores)
    scores = score(1, 0, second)
    mix(0, 1, first, *weighed)
    weighed = weigh(1, scores)
    scores = score(1, 1, second)
    mix(1, 0, second, *weighed)
    weighed = weigh(1, scores)
    mix(1, 1, second, *weighed)


def gather_kernel(info, *refs):
    pieces, out, sems = refs[:-2], refs[-2], refs[-1]
    copies = []
    for i, piece in enumerate(pieces):
        r, (j, first, steps) = i // len(CALLS), CALLS[i % len(CALLS)]
        begin = ((info[0] ^ r) * HQ + FIRST_HEAD[j] + 2 * first) * VDIM
        begin = pl.multiple_of(begin, 128)
        copies.append(
            pltpu.make_async_copy(piece, out.at[:, pl.ds(begin, piece.shape[1])], sems.at[i])
        )
    for copy in copies:
        copy.start()
    for copy in copies:
        copy.wait()


def tie(array, *others):
    return lax.optimization_barrier((array,) + others)[0]


class Phases:
    def __init__(self):
        self.before, self.before_late, self.now, self.late = [], [], [], []

    def turn(self):
        self.before = self.now + self.before_late
        self.before_late, self.now, self.late = self.late, [], []

    def send(self, late, permute, array, *args):
        arrived = permute(tie(array, *self.before) if self.before else array, *args)
        (self.late if late else self.now).append(arrived)
        return arrived


def shape(dims, kind=jnp.bfloat16):
    return jax.ShapeDtypeStruct(dims, kind)


def in_hbm(*arrays):
    return [pltpu.with_memory_space_constraint(array, pltpu.HBM) for array in arrays]


def body(q_heads, kv_latent, latent_gain, w_up, page_ranks, lengths):
    tok = q_heads.shape[0]
    size = lax.axis_size("ctx")
    groups = lax.axis_size("groups")
    mine = lax.axis_index("ctx")
    quarter = lax.axis_index("groups") * 2 + mine % 2
    slot_count = max(2, 2 * tok // size)
    smem = pl.BlockSpec(memory_space=SMEM)
    params = pltpu.CompilerParams(vmem_limit_bytes=VMEM_LIMIT)
    alone = pltpu.CompilerParams(vmem_limit_bytes=3 * VMEM_LIMIT)

    def quad_swap(array, r):
        dx, dc = r // 2, r % 2
        pairs = [
            (g * size + i, (g ^ dx) * size + (i ^ dc)) for g in range(groups) for i in range(size)
        ]
        return lax.ppermute(array, ("groups", "ctx"), pairs)

    def around(array, by):
        return lax.ppermute(array, "ctx", [(i, (i + by) % size) for i in range(size)])

    def inner_swap(array):
        return lax.ppermute(array, "ctx", [(i, i ^ 2) for i in range(size)])

    def from_behind(array, by, odd_only):
        first = 1 if odd_only else 0
        step = 2 if odd_only else 1
        pairs = [(i, i + by) for i in range(first, size - by, step)]
        return lax.ppermute(array, "ctx", pairs)

    width = HQ * (NOPE + VDIM)
    quarter_info = quarter[None].astype(jnp.int32)
    anywhere = pl.BlockSpec(memory_space=pl.ANY)
    give = lax.dynamic_slice_in_dim(w_up, (quarter ^ 1) * width, width, 1)
    give, lengths = lax.optimization_barrier((give, lengths))
    got = quad_swap(give, 1)
    outer = 4 if size == 16 else 0
    if outer:
        pair_rows = pl.pallas_call(
            pair_kernel,
            out_shape=shape((2 * w_up.shape[0], width)),
            in_specs=[smem, pl.BlockSpec(memory_space=pltpu.HBM), anywhere],
            out_specs=anywhere,
            scratch_shapes=[pltpu.SemaphoreType.DMA((2,))],
            compiler_params=params,
            name="pair",
        )(quarter_info, *in_hbm(w_up), got)
    else:
        keep = lax.dynamic_slice_in_dim(w_up, quarter * width, width, 1)
        even = mine % 2 == 0
        both = jnp.concatenate(
            [jnp.where(even, keep, got), jnp.where(even, got, keep)], axis=0
        )
        same_core = [list(range(c, size, 2)) for c in range(2)]
        gathered = lax.all_gather(both, "ctx", axis=0, tiled=True, axis_index_groups=same_core)

    frequency = np.exp(-np.arange(ROPE // 2) * (2.0 * math.log(10000.0) / ROPE))
    frequency = jnp.asarray(np.tile(frequency, 4)[None, :], jnp.float32)
    mine_info = mine[None].astype(jnp.int32)

    def block(*dims):
        return pl.BlockSpec(dims, lambda i: (0,) * len(dims))

    rows, cosine, sine, outgoing = pl.pallas_call(
        functools.partial(rows_kernel, slot_count),
        grid=(1,),
        out_shape=(
            shape((tok, EXT)),
            shape((tok, 128), jnp.float32),
            shape((tok, 128), jnp.float32),
            shape((size * slot_count, ROW)),
        ),
        in_specs=[smem, smem, block(ROW, tok), block(1, LAT), block(1, tok), block(1, 128)],
        out_specs=[
            block(tok, EXT),
            block(tok, 128),
            block(tok, 128),
            block(size * slot_count, ROW),
        ],
        compiler_params=alone,
        name="rows",
    )(
        mine_info,
        lengths,
        *in_hbm(kv_latent.T, latent_gain[None, :], page_ranks.T, frequency),
    )

    queries = pl.pallas_call(
        query_kernel,
        out_shape=[shape((tok, h * (NOPE + ROPE))) for h in CHUNK_HEADS] * QUAD,
        grid=(1,),
        in_specs=[smem, block(*q_heads.shape), block(tok, 128), block(tok, 128)],
        out_specs=[block(tok, h * (NOPE + ROPE)) for h in CHUNK_HEADS] * QUAD,
        compiler_params=params,
        cost_estimate=pl.CostEstimate(
            flops=0, bytes_accessed=4 * q_heads.size, transcendentals=0
        ),
        name="queries",
    )(quarter_info, *in_hbm(q_heads, tie(cosine, pair_rows if outer else got), sine))

    def to_decode(array):
        array = array.reshape(size, slot_count, ROW)
        return lax.all_to_all(array, "ctx", split_axis=0, concat_axis=0, tiled=True)

    phases = Phases()
    line = [pair_rows] if outer else []
    side = []
    half = width // CHUNKS
    halves = []
    moved = [[queries[j]] + [None] * (QUAD - 1) for j in range(CHUNKS)]
    parts = {"r": tie(rows, pair_rows if outer else got)}
    for name in [name for phase in PHASES for name in phase + ("|",)]:
        kind, late = name[0], name[-1] == "~"
        if kind == "|":
            phases.now.append(queries[0])
            phases.turn()
        elif kind == "z" and outer:
            line.append(phases.send(late, around, line[-1], 4))
        elif kind == "y" and outer:
            step = int(name[1])
            if step < outer - 1:
                side.append(phases.send(late, inner_swap, line[step]))
            else:
                halves.append(phases.send(late, inner_swap, line[step][:, :half]))
        elif kind == "w" and outer:
            halves.append(phases.send(late, around, side[-1][:, half:], 4))
        elif kind == "d":
            decode_cache = phases.send(late, to_decode, tie(outgoing, queries[0]))
        elif kind == "b":
            parts["b"] = phases.send(late, from_behind, parts["r"], 2, False)
        elif kind == "f":
            parts["f"] = phases.send(late, from_behind, parts["r"], 4, True)
        elif kind == "k":
            have = jnp.concatenate([parts["r"], parts["b"], parts["f"]], axis=0)
            swapped = phases.send(late, quad_swap, have, 2)
        elif kind == "p":
            own_rows = jnp.concatenate([have, swapped], axis=0)
            other_rows = phases.send(late, quad_swap, own_rows, 1)
        elif kind == "q":
            j, r = int(name[1]), int(name[2])
            moved[j][r] = phases.send(late, quad_swap, queries[r * CHUNKS + j], r)

    def weights_for(j):
        if not outer:
            return [(gathered, FIRST_HEAD[j] // 2)]
        return [(piece, FIRST_HEAD[j] // 2) for piece in line + side] + [(halves[j], 0)]

    window = (REACH + 2) * tok
    resident = pl.BlockSpec(memory_space=VMEM)
    keys = pl.pallas_call(
        keys_kernel,
        out_shape=(
            shape((2, window, LAT)),
            shape((2, window, 128)),
            shape((2, window, 128)),
            shape((2, 2 * tok, window), jnp.float32),
        ),
        in_specs=[smem, resident, resident],
        out_specs=[resident] * 4,
        compiler_params=params,
        cost_estimate=pl.CostEstimate(flops=0, bytes_accessed=8 << 20, transcendentals=0),
        name="keys",
    )(mine_info, own_rows, other_rows)

    def attend(j, first, steps):
        heads = 2 * steps
        pieces_of_weight = [piece for piece, begin in weights_for(j)]
        flops = 2 * heads * 2 * (window * LAT * 256 + 2 * tok * window * (NOPE + ROPE + VDIM))
        return pl.pallas_call(
            functools.partial(attend_kernel, outer),
            grid=(steps,),
            out_shape=[shape((tok, heads * VDIM))] * QUAD,
            in_specs=[smem] + [resident] * 4
            + [
                pl.BlockSpec((piece.shape[0], 512), lambda i, begin=begin: (0, begin + first + i))
                for piece, begin in weights_for(j)
            ]
            + [pl.BlockSpec((tok, 256), lambda i: (0, first + i))] * QUAD
            + [pl.BlockSpec((tok, 128), lambda i: (0, CHUNK_HEADS[j] + first + i))] * QUAD,
            out_specs=[pl.BlockSpec((tok, 256), lambda i: (0, i))] * QUAD,
            scratch_shapes=[VMEM((LAT, 512), jnp.bfloat16)],
            compiler_params=params,
            cost_estimate=pl.CostEstimate(
                flops=flops,
                bytes_accessed=heads << 20,
                transcendentals=heads * 4 * tok * window,
            ),
            name="attend",
        )(mine_info, *keys, *pieces_of_weight, *moved[j], *moved[j])

    results = []
    for call in CALLS:
        mine_info = tie(mine_info, *[piece for one in results[-2:-1] for piece in one[2:]])
        pieces = attend(*call)
        mine_info = tie(mine_info, pieces[0])
        before = results[-1][2:3] if len(results) + 1 == len(CALLS) else []
        results.append(
            [pieces[0]] + [quad_swap(tie(pieces[r], *before), r) for r in range(1, QUAD)]
        )
    pieces = [one[r] for r in range(QUAD) for one in results]
    attn_out = pl.pallas_call(
        gather_kernel,
        out_shape=shape((tok, H * VDIM)),
        in_specs=[smem] + [anywhere] * len(pieces),
        out_specs=anywhere,
        scratch_shapes=[pltpu.SemaphoreType.DMA((len(pieces),))],
        compiler_params=params,
        name="place",
    )(quarter_info, *pieces)
    return (attn_out, decode_cache.reshape(size * slot_count, ROW))


def solution(mesh):
    return jax.shard_map(
        body,
        mesh=mesh,
        in_specs=(
            P(("groups", "ctx"), None),
            P(("groups", "ctx"), None),
            P(),
            P("ctx", None),
            P(("groups", "ctx"), None),
            P("groups"),
        ),
        out_specs=(P(("groups", "ctx"), None), P(("groups", "ctx"), None)),
        check_vma=False,
    )
```

```python
import functools
import math

import jax
import jax.numpy as jnp
import numpy as np
from jax import lax
from jax.experimental import pallas as pl
from jax.experimental.pallas import tpu as pltpu
from jax.sharding import PartitionSpec as P

H = 64
NOPE = 128
ROPE = 64
VDIM = 128
LAT = 512
REACH = 3
QUAD = 4
HQ = H // QUAD
CHUNK_HEADS = (8, 8)
PHASES = (
    ("z", "y0", "b~", "f~", "q02"),
    ("z", "y1", "k", "q01"),
    ("z", "y2", "p", "q03"),
    ("y3", "w", "q12~", "q13~", "q11"),
)
CHUNKS = len(CHUNK_HEADS)
FIRST_HEAD = tuple(sum(CHUNK_HEADS[:j]) for j in range(CHUNKS))
ROW = LAT + ROPE
EXT = 640
VMEM_LIMIT = 20 * 1024 * 1024
CALLS = ((0, 0, 4), (1, 0, 2), (1, 2, 2))
SMEM = pltpu.SMEM
VMEM = pltpu.VMEM


def rows_kernel(
    slot_count, info, lengths, kv, gain, ranks, freq, rows_out, cos_out, sin_out, outgoing_out
):
    tok = kv.shape[1]
    base = info[0] * tok
    spots = base + lax.broadcasted_iota(jnp.int32, (tok, 128), 0)
    lane = lax.broadcasted_iota(jnp.int32, (tok, 128), 1)
    begin = jnp.int32(0)
    own_start = jnp.zeros((tok, 128), jnp.int32)
    for r in range(lengths.shape[0]):
        own_start = jnp.where(spots >= begin, begin, own_start)
        begin = begin + lengths[r]
    offset = spots - own_start
    angles = offset.astype(jnp.float32) * freq[...]
    cosine = jnp.cos(angles)
    sine = jnp.where((lane & 32) == 0, -jnp.sin(angles), jnp.sin(angles))
    cos_out[...] = cosine
    sin_out[...] = sine
    raw = kv[...].astype(jnp.float32).T
    latent = raw[:, :LAT]
    mean = jnp.sum(latent * latent, axis=1, keepdims=True) * (1.0 / LAT)
    latent = latent * lax.rsqrt(mean + 1e-06) * gain[...]
    key = raw[:, LAT:]
    swapped = jnp.concatenate([key[:, ROPE // 2 :], key[:, : ROPE // 2]], axis=1)
    turned = key * cosine[:, :ROPE] + swapped * sine[:, :ROPE]
    high = (offset >> 8).astype(jnp.float32)
    low = (offset & 255).astype(jnp.float32)
    meta = jnp.where(lane == 0, high, jnp.where(lane == 1, low, 0.0))
    tail = jnp.concatenate([turned, meta[:, :ROPE]], axis=1)
    rows_out[:, :LAT] = latent.astype(jnp.bfloat16)
    rows_out[:, LAT:] = tail.astype(jnp.bfloat16)

    rank_row = jnp.broadcast_to(ranks[...], (tok, tok)).astype(jnp.float32)
    rank_col = rank_row.T
    earlier = lax.broadcasted_iota(jnp.int32, (tok, tok), 0) < lax.broadcasted_iota(
        jnp.int32, (tok, tok), 1
    )
    same = jnp.where((rank_col == rank_row) & earlier, 1.0, 0.0)
    slot = jnp.sum(same, axis=0, keepdims=True)
    target = (rank_row[:1] * slot_count + slot).astype(jnp.int32)
    spots_out = lax.broadcasted_iota(jnp.int32, (outgoing_out.shape[0], tok), 0)
    selector = jnp.where(spots_out == target, 1.0, 0.0).astype(jnp.bfloat16)
    picked = jnp.dot(selector, rows_out[:, :ROW], preferred_element_type=jnp.float32)
    outgoing_out[...] = picked.astype(jnp.bfloat16)


def query_kernel(info, query, cosine, sine, *outs):
    tok = query.shape[0]
    lane = lax.broadcasted_iota(jnp.int32, (tok, 128), 1)
    low_half = lane < 64
    first_quarter = (lane & 32) == 0
    cos_table = cosine[...]
    sin_table = sine[...]
    for r in range(QUAD):
        first = (info[0] ^ r) * (HQ * (NOPE + ROPE))
        for pair in range(HQ // 2):
            j = max(j for j in range(CHUNKS) if FIRST_HEAD[j] <= 2 * pair)
            out = outs[r * CHUNKS + j]
            at = pair - FIRST_HEAD[j] // 2
            rope_at = CHUNK_HEADS[j] * NOPE + at * 128
            begin = pl.multiple_of(first + pair * 2 * (NOPE + ROPE), 128)
            both = query[:, pl.ds(begin, 2 * (NOPE + ROPE))]
            mid = both[:, 128:256].astype(jnp.float32)
            end = both[:, 256:384].astype(jnp.float32)
            turned = jnp.where(low_half, mid, end)
            odd_nope = pltpu.roll(jnp.where(low_half, end, mid), 64, 1)
            swapped = jnp.where(
                first_quarter, pltpu.roll(turned, 96, 1), pltpu.roll(turned, 32, 1)
            )
            turned = turned * cos_table + swapped * sin_table
            out[:, at * 256 : at * 256 + 128] = both[:, :128]
            out[:, at * 256 + 128 : at * 256 + 256] = odd_nope.astype(jnp.bfloat16)
            out[:, rope_at : rope_at + 128] = turned.astype(jnp.bfloat16)


def pair_kernel(info, w_up, got, out, sem):
    rows, width = got.shape
    begin = pl.multiple_of(info[0] * width, 128)
    copies = [
        pltpu.make_async_copy(w_up.at[:, pl.ds(begin, width)], out.at[pl.ds(0, rows)], sem.at[0]),
        pltpu.make_async_copy(got, out.at[pl.ds(rows, rows)], sem.at[1]),
    ]
    for copy in copies:
        copy.start()
    for copy in copies:
        copy.wait()


def keys_kernel(info, own, other, latent, rope_even, rope_odd, bias):
    tok = own.shape[0] // 6
    mine = info[0]
    partner = mine ^ 1
    has_last = (mine & 1) == 1
    starts = [mine, partner, mine - 2, partner - 2, (mine >> 1) * 2 - 3]
    blank = jnp.zeros((tok, ROPE), jnp.bfloat16)
    lane = lax.broadcasted_iota(jnp.int32, (tok, tok), 1)
    row = lax.broadcasted_iota(jnp.int32, (tok, tok), 0)
    for g in range(2):
        mine_of, other_of = [
            [ref[(3 * g + n) * tok : (3 * g + n + 1) * tok] for n in range(3)]
            for ref in (own, other)
        ]
        pieces = [
            mine_of[0],
            other_of[0],
            mine_of[1],
            other_of[1],
            jnp.where(has_last, mine_of[2], other_of[2]),
        ]
        for b, piece in enumerate(pieces):
            here = slice(b * tok, (b + 1) * tok)
            latent[g, here] = piece[:, :LAT]
            turned = piece[:, LAT : LAT + ROPE]
            rope_even[g, here] = jnp.concatenate([turned, blank], axis=1)
            rope_odd[g, here] = jnp.concatenate([blank, turned], axis=1)
        for half in range(2):
            meta = pieces[half][:, LAT:].astype(jnp.float32)
            offset = (meta[:, ROPE : ROPE + 1] * 256.0 + meta[:, ROPE + 1 : ROPE + 2]).astype(
                jnp.int32
            )
            spots = starts[half] * tok + row
            lowest = jnp.maximum(spots - offset, (starts[half] - REACH) * tok)
            for b in range(REACH + 2):
                keys = starts[b] * tok + lane
                allowed = (keys >= lowest) & (keys <= spots)
                bias[g, half * tok : (half + 1) * tok, b * tok : (b + 1) * tok] = jnp.where(
                    allowed, 0.0, -1e30
                )


def attend_kernel(outer, info, latent, rope_even, rope_odd, bias, *refs):
    pieces_count = 2 * outer if outer else 1
    pieces_of_weight, refs = refs[:pieces_count], refs[pieces_count:]
    nope = refs[0:QUAD]
    rope = refs[QUAD : 2 * QUAD]
    outs = refs[2 * QUAD : 3 * QUAD]
    held = refs[3 * QUAD]
    tok = nope[0].shape[0]
    mine = info[0]
    scale = (NOPE + ROPE) ** (-0.5) * math.log2(math.e)

    if outer:
        weight = held
        for i, piece in enumerate(pieces_of_weight):
            side, behind = i // outer, i % outer
            chip = ((mine >> 2) + outer - behind) % outer * 2 + (((mine >> 1) & 1) ^ side)
            rows = piece.shape[0] // 2
            for core in range(2):
                begin = pl.multiple_of(chip * 2 * rows + ((mine & 1) ^ core) * rows, rows)
                held[pl.ds(begin, rows)] = piece[core * rows : (core + 1) * rows]
    else:
        weight = pieces_of_weight[0]

    def expand(g):
        wide = jnp.dot(latent[g], weight[...], preferred_element_type=jnp.float32)
        return wide.astype(jnp.bfloat16)

    def score(g, b, expanded):
        at = slice(b * 128, (b + 1) * 128)
        key_rope = (rope_even, rope_odd)[b][g]
        key = jnp.concatenate([expanded[:, b * 256 : b * 256 + 128], key_rope], axis=1)
        query = jnp.concatenate(
            [
                jnp.concatenate([nope[2 * g][:, at], rope[2 * g][...]], axis=1),
                jnp.concatenate([nope[2 * g + 1][:, at], rope[2 * g + 1][...]], axis=1),
            ],
            axis=0,
        )
        return lax.dot_general(
            query, key, (((1,), (1,)), ((), ())), preferred_element_type=jnp.float32
        )

    def weigh(g, scores):
        scores = scores * scale + bias[g]
        largest = jnp.max(scores, axis=1, keepdims=True)
        expo = jnp.exp2(scores - largest)
        return expo.astype(jnp.bfloat16), jnp.sum(expo, axis=1, keepdims=True)

    def mix(g, b, expanded, weights, total):
        at = slice(b * 128, (b + 1) * 128)
        value = expanded[:, b * 256 + 128 : b * 256 + 256]
        mixed = jnp.dot(weights, value, preferred_element_type=jnp.float32)
        mixed = (mixed / total).astype(jnp.bfloat16)
        outs[2 * g][:, at] = mixed[:tok]
        outs[2 * g + 1][:, at] = mixed[tok:]

    first = expand(0)
    scores = score(0, 0, first)
    second = expand(1)
    weighed = weigh(0, scores)
    scores = score(0, 1, first)
    mix(0, 0, first, *weighed)
    weighed = weigh(0, scores)
    scores = score(1, 0, second)
    mix(0, 1, first, *weighed)
    weighed = weigh(1, scores)
    scores = score(1, 1, second)
    mix(1, 0, second, *weighed)
    weighed = weigh(1, scores)
    mix(1, 1, second, *weighed)


def gather_kernel(info, *refs):
    pieces, out, sems = refs[:-2], refs[-2], refs[-1]
    copies = []
    for i, piece in enumerate(pieces):
        r, (j, first, steps) = i // len(CALLS), CALLS[i % len(CALLS)]
        begin = ((info[0] ^ r) * HQ + FIRST_HEAD[j] + 2 * first) * VDIM
        begin = pl.multiple_of(begin, 128)
        copies.append(
            pltpu.make_async_copy(piece, out.at[:, pl.ds(begin, piece.shape[1])], sems.at[i])
        )
    for copy in copies:
        copy.start()
    for copy in copies:
        copy.wait()


def tie(array, *others):
    return lax.optimization_barrier((array,) + others)[0]


class Phases:
    def __init__(self):
        self.before, self.before_late, self.now, self.late = [], [], [], []

    def turn(self):
        self.before = self.now + self.before_late
        self.before_late, self.now, self.late = self.late, [], []

    def send(self, late, permute, array, *args):
        arrived = permute(tie(array, *self.before) if self.before else array, *args)
        (self.late if late else self.now).append(arrived)
        return arrived


def shape(dims, kind=jnp.bfloat16):
    return jax.ShapeDtypeStruct(dims, kind)


def in_hbm(*arrays):
    return [pltpu.with_memory_space_constraint(array, pltpu.HBM) for array in arrays]


def body(q_heads, kv_latent, latent_gain, w_up, page_ranks, lengths):
    tok = q_heads.shape[0]
    size = lax.axis_size("ctx")
    groups = lax.axis_size("groups")
    mine = lax.axis_index("ctx")
    quarter = lax.axis_index("groups") * 2 + mine % 2
    slot_count = max(2, 2 * tok // size)
    smem = pl.BlockSpec(memory_space=SMEM)
    params = pltpu.CompilerParams(vmem_limit_bytes=VMEM_LIMIT)
    alone = pltpu.CompilerParams(vmem_limit_bytes=3 * VMEM_LIMIT)

    def quad_swap(array, r):
        dx, dc = r // 2, r % 2
        pairs = [
            (g * size + i, (g ^ dx) * size + (i ^ dc)) for g in range(groups) for i in range(size)
        ]
        return lax.ppermute(array, ("groups", "ctx"), pairs)

    def around(array, by):
        return lax.ppermute(array, "ctx", [(i, (i + by) % size) for i in range(size)])

    def inner_swap(array):
        return lax.ppermute(array, "ctx", [(i, i ^ 2) for i in range(size)])

    def from_behind(array, by, odd_only):
        first = 1 if odd_only else 0
        step = 2 if odd_only else 1
        pairs = [(i, i + by) for i in range(first, size - by, step)]
        return lax.ppermute(array, "ctx", pairs)

    width = HQ * (NOPE + VDIM)
    quarter_info = quarter[None].astype(jnp.int32)
    anywhere = pl.BlockSpec(memory_space=pl.ANY)
    give = lax.dynamic_slice_in_dim(w_up, (quarter ^ 1) * width, width, 1)
    give, lengths = lax.optimization_barrier((give, lengths))
    got = quad_swap(give, 1)
    outer = 4 if size == 16 else 0
    if outer:
        pair_rows = pl.pallas_call(
            pair_kernel,
            out_shape=shape((2 * w_up.shape[0], width)),
            in_specs=[smem, pl.BlockSpec(memory_space=pltpu.HBM), anywhere],
            out_specs=anywhere,
            scratch_shapes=[pltpu.SemaphoreType.DMA((2,))],
            compiler_params=params,
            name="pair",
        )(quarter_info, *in_hbm(w_up), got)
    else:
        keep = lax.dynamic_slice_in_dim(w_up, quarter * width, width, 1)
        even = mine % 2 == 0
        both = jnp.concatenate(
            [jnp.where(even, keep, got), jnp.where(even, got, keep)], axis=0
        )
        same_core = [list(range(c, size, 2)) for c in range(2)]
        gathered = lax.all_gather(both, "ctx", axis=0, tiled=True, axis_index_groups=same_core)

    frequency = np.exp(-np.arange(ROPE // 2) * (2.0 * math.log(10000.0) / ROPE))
    frequency = jnp.asarray(np.tile(frequency, 4)[None, :], jnp.float32)
    mine_info = mine[None].astype(jnp.int32)

    def block(*dims):
        return pl.BlockSpec(dims, lambda i: (0,) * len(dims))

    rows, cosine, sine, outgoing = pl.pallas_call(
        functools.partial(rows_kernel, slot_count),
        grid=(1,),
        out_shape=(
            shape((tok, EXT)),
            shape((tok, 128), jnp.float32),
            shape((tok, 128), jnp.float32),
            shape((size * slot_count, ROW)),
        ),
        in_specs=[smem, smem, block(ROW, tok), block(1, LAT), block(1, tok), block(1, 128)],
        out_specs=[
            block(tok, EXT),
            block(tok, 128),
            block(tok, 128),
            block(size * slot_count, ROW),
        ],
        compiler_params=alone,
        name="rows",
    )(
        mine_info,
        lengths,
        *in_hbm(kv_latent.T, latent_gain[None, :], page_ranks.T, frequency),
    )

    queries = pl.pallas_call(
        query_kernel,
        out_shape=[shape((tok, h * (NOPE + ROPE))) for h in CHUNK_HEADS] * QUAD,
        grid=(1,),
        in_specs=[smem, block(*q_heads.shape), block(tok, 128), block(tok, 128)],
        out_specs=[block(tok, h * (NOPE + ROPE)) for h in CHUNK_HEADS] * QUAD,
        compiler_params=params,
        cost_estimate=pl.CostEstimate(
            flops=0, bytes_accessed=4 * q_heads.size, transcendentals=0
        ),
        name="queries",
    )(quarter_info, *in_hbm(q_heads, tie(cosine, pair_rows if outer else got), sine))

    phases = Phases()
    line = [pair_rows] if outer else []
    side = []
    half = width // CHUNKS
    halves = []
    moved = [[queries[j]] + [None] * (QUAD - 1) for j in range(CHUNKS)]
    parts = {"r": tie(rows, pair_rows if outer else got)}
    for name in [name for phase in PHASES for name in phase + ("|",)]:
        kind, late = name[0], name[-1] == "~"
        if kind == "|":
            phases.now.append(queries[0])
            phases.turn()
        elif kind == "z" and outer:
            line.append(phases.send(late, around, line[-1], 4))
        elif kind == "y" and outer:
            step = int(name[1])
            if step < outer - 1:
                side.append(phases.send(late, inner_swap, line[step]))
            else:
                halves.append(phases.send(late, inner_swap, line[step][:, :half]))
        elif kind == "w" and outer:
            halves.append(phases.send(late, around, side[-1][:, half:], 4))
        elif kind == "b":
            parts["b"] = phases.send(late, from_behind, parts["r"], 2, False)
        elif kind == "f":
            parts["f"] = phases.send(late, from_behind, parts["r"], 4, True)
        elif kind == "k":
            have = jnp.concatenate([parts["r"], parts["b"], parts["f"]], axis=0)
            swapped = phases.send(late, quad_swap, have, 2)
        elif kind == "p":
            own_rows = jnp.concatenate([have, swapped], axis=0)
            other_rows = phases.send(late, quad_swap, own_rows, 1)
        elif kind == "q":
            j, r = int(name[1]), int(name[2])
            moved[j][r] = phases.send(late, quad_swap, queries[r * CHUNKS + j], r)

    def weights_for(j):
        if not outer:
            return [(gathered, FIRST_HEAD[j] // 2)]
        return [(piece, FIRST_HEAD[j] // 2) for piece in line + side] + [(halves[j], 0)]

    window = (REACH + 2) * tok
    resident = pl.BlockSpec(memory_space=VMEM)
    keys = pl.pallas_call(
        keys_kernel,
        out_shape=(
            shape((2, window, LAT)),
            shape((2, window, 128)),
            shape((2, window, 128)),
            shape((2, 2 * tok, window), jnp.float32),
        ),
        in_specs=[smem, resident, resident],
        out_specs=[resident] * 4,
        compiler_params=params,
        cost_estimate=pl.CostEstimate(flops=0, bytes_accessed=8 << 20, transcendentals=0),
        name="keys",
    )(mine_info, own_rows, other_rows)

    def attend(j, first, steps):
        heads = 2 * steps
        pieces_of_weight = [piece for piece, begin in weights_for(j)]
        flops = 2 * heads * 2 * (window * LAT * 256 + 2 * tok * window * (NOPE + ROPE + VDIM))
        return pl.pallas_call(
            functools.partial(attend_kernel, outer),
            grid=(steps,),
            out_shape=[shape((tok, heads * VDIM))] * QUAD,
            in_specs=[smem] + [resident] * 4
            + [
                pl.BlockSpec((piece.shape[0], 512), lambda i, begin=begin: (0, begin + first + i))
                for piece, begin in weights_for(j)
            ]
            + [pl.BlockSpec((tok, 256), lambda i: (0, first + i))] * QUAD
            + [pl.BlockSpec((tok, 128), lambda i: (0, CHUNK_HEADS[j] + first + i))] * QUAD,
            out_specs=[pl.BlockSpec((tok, 256), lambda i: (0, i))] * QUAD,
            scratch_shapes=[VMEM((LAT, 512), jnp.bfloat16)],
            compiler_params=params,
            cost_estimate=pl.CostEstimate(
                flops=flops,
                bytes_accessed=heads << 20,
                transcendentals=heads * 4 * tok * window,
            ),
            name="attend",
        )(mine_info, *keys, *pieces_of_weight, *moved[j], *moved[j])

    results = []
    for call in CALLS:
        last = len(results) + 1 == len(CALLS)
        mine_info = tie(mine_info, *(results[0][2:3] if last else []))
        pieces = attend(*call)
        mine_info = tie(mine_info, pieces[0])
        before = [piece for one in results for piece in one[1:]] if last else []
        results.append(
            [pieces[0]] + [quad_swap(tie(pieces[r], *before), r) for r in range(1, QUAD)]
        )
    pieces = [one[r] for r in range(QUAD) for one in results]
    arrived = lax.all_to_all(
        tie(outgoing, results[-1][0], *before).reshape(size, slot_count, ROW),
        "ctx",
        split_axis=0,
        concat_axis=0,
        tiled=True,
    )
    decode_cache = arrived.reshape(size * slot_count, ROW)
    attn_out = pl.pallas_call(
        gather_kernel,
        out_shape=shape((tok, H * VDIM)),
        in_specs=[smem] + [anywhere] * len(pieces),
        out_specs=anywhere,
        scratch_shapes=[pltpu.SemaphoreType.DMA((len(pieces),))],
        compiler_params=params,
        name="place",
    )(quarter_info, *pieces)
    return (attn_out, decode_cache)


def solution(mesh):
    return jax.shard_map(
        body,
        mesh=mesh,
        in_specs=(
            P(("groups", "ctx"), None),
            P(("groups", "ctx"), None),
            P(),
            P("ctx", None),
            P(("groups", "ctx"), None),
            P("groups"),
        ),
        out_specs=(P(("groups", "ctx"), None), P(("groups", "ctx"), None)),
        check_vma=False,
    )
```

```python
import functools
import math

import jax
import jax.numpy as jnp
import numpy as np
from jax import lax
from jax.experimental import pallas as pl
from jax.experimental.pallas import tpu as pltpu
from jax.sharding import PartitionSpec as P

H = 64
NOPE = 128
ROPE = 64
VDIM = 128
LAT = 512
REACH = 3
QUAD = 4
HQ = H // QUAD
CHUNK_HEADS = (8, 8)
PHASES = (
    ("z", "y0", "k", "q02", "b~", "f~"),
    ("z", "y1", "q03", "q01"),
    ("z", "y2", "p", "q12"),
    ("y3", "w", "q13~", "q11"),
)
CHUNKS = len(CHUNK_HEADS)
FIRST_HEAD = tuple(sum(CHUNK_HEADS[:j]) for j in range(CHUNKS))
ROW = LAT + ROPE
EXT = 640
VMEM_LIMIT = 20 * 1024 * 1024
CALLS = ((0, 0, 4), (1, 0, 2), (1, 2, 2))
SMEM = pltpu.SMEM
VMEM = pltpu.VMEM


def rows_kernel(
    slot_count, info, lengths, kv, gain, ranks, freq, rows_out, cos_out, sin_out, outgoing_out
):
    tok = kv.shape[1]
    base = info[0] * tok
    spots = base + lax.broadcasted_iota(jnp.int32, (tok, 128), 0)
    lane = lax.broadcasted_iota(jnp.int32, (tok, 128), 1)
    begin = jnp.int32(0)
    own_start = jnp.zeros((tok, 128), jnp.int32)
    for r in range(lengths.shape[0]):
        own_start = jnp.where(spots >= begin, begin, own_start)
        begin = begin + lengths[r]
    offset = spots - own_start
    angles = offset.astype(jnp.float32) * freq[...]
    cosine = jnp.cos(angles)
    sine = jnp.where((lane & 32) == 0, -jnp.sin(angles), jnp.sin(angles))
    cos_out[...] = cosine
    sin_out[...] = sine
    raw = kv[...].astype(jnp.float32).T
    latent = raw[:, :LAT]
    mean = jnp.sum(latent * latent, axis=1, keepdims=True) * (1.0 / LAT)
    latent = latent * lax.rsqrt(mean + 1e-06) * gain[...]
    key = raw[:, LAT:]
    swapped = jnp.concatenate([key[:, ROPE // 2 :], key[:, : ROPE // 2]], axis=1)
    turned = key * cosine[:, :ROPE] + swapped * sine[:, :ROPE]
    high = (offset >> 8).astype(jnp.float32)
    low = (offset & 255).astype(jnp.float32)
    meta = jnp.where(lane == 0, high, jnp.where(lane == 1, low, 0.0))
    tail = jnp.concatenate([turned, meta[:, :ROPE]], axis=1)
    rows_out[:, :LAT] = latent.astype(jnp.bfloat16)
    rows_out[:, LAT:] = tail.astype(jnp.bfloat16)

    rank_row = jnp.broadcast_to(ranks[...], (tok, tok)).astype(jnp.float32)
    rank_col = rank_row.T
    earlier = lax.broadcasted_iota(jnp.int32, (tok, tok), 0) < lax.broadcasted_iota(
        jnp.int32, (tok, tok), 1
    )
    same = jnp.where((rank_col == rank_row) & earlier, 1.0, 0.0)
    slot = jnp.sum(same, axis=0, keepdims=True)
    target = (rank_row[:1] * slot_count + slot).astype(jnp.int32)
    spots_out = lax.broadcasted_iota(jnp.int32, (outgoing_out.shape[0], tok), 0)
    selector = jnp.where(spots_out == target, 1.0, 0.0).astype(jnp.bfloat16)
    picked = jnp.dot(selector, rows_out[:, :ROW], preferred_element_type=jnp.float32)
    outgoing_out[...] = picked.astype(jnp.bfloat16)


def query_kernel(info, query, cosine, sine, *outs):
    tok = query.shape[0]
    lane = lax.broadcasted_iota(jnp.int32, (tok, 128), 1)
    low_half = lane < 64
    first_quarter = (lane & 32) == 0
    cos_table = cosine[...]
    sin_table = sine[...]
    for r in range(QUAD):
        first = (info[0] ^ r) * (HQ * (NOPE + ROPE))
        for pair in range(HQ // 2):
            j = max(j for j in range(CHUNKS) if FIRST_HEAD[j] <= 2 * pair)
            out = outs[r * CHUNKS + j]
            at = pair - FIRST_HEAD[j] // 2
            rope_at = CHUNK_HEADS[j] * NOPE + at * 128
            begin = pl.multiple_of(first + pair * 2 * (NOPE + ROPE), 128)
            both = query[:, pl.ds(begin, 2 * (NOPE + ROPE))]
            mid = both[:, 128:256].astype(jnp.float32)
            end = both[:, 256:384].astype(jnp.float32)
            turned = jnp.where(low_half, mid, end)
            odd_nope = pltpu.roll(jnp.where(low_half, end, mid), 64, 1)
            swapped = jnp.where(
                first_quarter, pltpu.roll(turned, 96, 1), pltpu.roll(turned, 32, 1)
            )
            turned = turned * cos_table + swapped * sin_table
            out[:, at * 256 : at * 256 + 128] = both[:, :128]
            out[:, at * 256 + 128 : at * 256 + 256] = odd_nope.astype(jnp.bfloat16)
            out[:, rope_at : rope_at + 128] = turned.astype(jnp.bfloat16)


def pair_kernel(info, w_up, got, out, sem):
    rows, width = got.shape
    begin = pl.multiple_of(info[0] * width, 128)
    copies = [
        pltpu.make_async_copy(w_up.at[:, pl.ds(begin, width)], out.at[pl.ds(0, rows)], sem.at[0]),
        pltpu.make_async_copy(got, out.at[pl.ds(rows, rows)], sem.at[1]),
    ]
    for copy in copies:
        copy.start()
    for copy in copies:
        copy.wait()


def keys_kernel(info, own, other, latent, rope_even, rope_odd, bias):
    tok = own.shape[0] // 6
    mine = info[0]
    partner = mine ^ 1
    has_last = (mine & 1) == 1
    starts = [mine, partner, mine - 2, partner - 2, (mine >> 1) * 2 - 3]
    blank = jnp.zeros((tok, ROPE), jnp.bfloat16)
    lane = lax.broadcasted_iota(jnp.int32, (tok, tok), 1)
    row = lax.broadcasted_iota(jnp.int32, (tok, tok), 0)
    for g in range(2):
        mine_of, other_of = [
            [ref[(2 * n + g) * tok : (2 * n + g + 1) * tok] for n in range(3)]
            for ref in (own, other)
        ]
        pieces = [
            mine_of[0],
            other_of[0],
            mine_of[1],
            other_of[1],
            jnp.where(has_last, mine_of[2], other_of[2]),
        ]
        for b, piece in enumerate(pieces):
            here = slice(b * tok, (b + 1) * tok)
            latent[g, here] = piece[:, :LAT]
            turned = piece[:, LAT : LAT + ROPE]
            rope_even[g, here] = jnp.concatenate([turned, blank], axis=1)
            rope_odd[g, here] = jnp.concatenate([blank, turned], axis=1)
        for half in range(2):
            meta = pieces[half][:, LAT:].astype(jnp.float32)
            offset = (meta[:, ROPE : ROPE + 1] * 256.0 + meta[:, ROPE + 1 : ROPE + 2]).astype(
                jnp.int32
            )
            spots = starts[half] * tok + row
            lowest = jnp.maximum(spots - offset, (starts[half] - REACH) * tok)
            for b in range(REACH + 2):
                keys = starts[b] * tok + lane
                allowed = (keys >= lowest) & (keys <= spots)
                bias[g, half * tok : (half + 1) * tok, b * tok : (b + 1) * tok] = jnp.where(
                    allowed, 0.0, -1e30
                )


def attend_kernel(outer, info, latent, rope_even, rope_odd, bias, *refs):
    pieces_count = 2 * outer if outer else 1
    pieces_of_weight, refs = refs[:pieces_count], refs[pieces_count:]
    nope = refs[0:QUAD]
    rope = refs[QUAD : 2 * QUAD]
    outs = refs[2 * QUAD : 3 * QUAD]
    held = refs[3 * QUAD]
    tok = nope[0].shape[0]
    mine = info[0]
    scale = (NOPE + ROPE) ** (-0.5) * math.log2(math.e)

    if outer:
        weight = held
        for i, piece in enumerate(pieces_of_weight):
            side, behind = i // outer, i % outer
            chip = ((mine >> 2) + outer - behind) % outer * 2 + (((mine >> 1) & 1) ^ side)
            rows = piece.shape[0] // 2
            for core in range(2):
                begin = pl.multiple_of(chip * 2 * rows + ((mine & 1) ^ core) * rows, rows)
                held[pl.ds(begin, rows)] = piece[core * rows : (core + 1) * rows]
    else:
        weight = pieces_of_weight[0]

    def expand(g):
        wide = jnp.dot(latent[g], weight[...], preferred_element_type=jnp.float32)
        return wide.astype(jnp.bfloat16)

    def score(g, b, expanded):
        at = slice(b * 128, (b + 1) * 128)
        key_rope = (rope_even, rope_odd)[b][g]
        key = jnp.concatenate([expanded[:, b * 256 : b * 256 + 128], key_rope], axis=1)
        query = jnp.concatenate(
            [
                jnp.concatenate([nope[2 * g][:, at], rope[2 * g][...]], axis=1),
                jnp.concatenate([nope[2 * g + 1][:, at], rope[2 * g + 1][...]], axis=1),
            ],
            axis=0,
        )
        return lax.dot_general(
            query, key, (((1,), (1,)), ((), ())), preferred_element_type=jnp.float32
        )

    def weigh(g, scores):
        scores = scores * scale + bias[g]
        largest = jnp.max(scores, axis=1, keepdims=True)
        expo = jnp.exp2(scores - largest)
        return expo.astype(jnp.bfloat16), jnp.sum(expo, axis=1, keepdims=True)

    def mix(g, b, expanded, weights, total):
        at = slice(b * 128, (b + 1) * 128)
        value = expanded[:, b * 256 + 128 : b * 256 + 256]
        mixed = jnp.dot(weights, value, preferred_element_type=jnp.float32)
        mixed = (mixed / total).astype(jnp.bfloat16)
        outs[2 * g][:, at] = mixed[:tok]
        outs[2 * g + 1][:, at] = mixed[tok:]

    first = expand(0)
    scores = score(0, 0, first)
    second = expand(1)
    weighed = weigh(0, scores)
    scores = score(0, 1, first)
    mix(0, 0, first, *weighed)
    weighed = weigh(0, scores)
    scores = score(1, 0, second)
    mix(0, 1, first, *weighed)
    weighed = weigh(1, scores)
    scores = score(1, 1, second)
    mix(1, 0, second, *weighed)
    weighed = weigh(1, scores)
    mix(1, 1, second, *weighed)


def gather_kernel(info, *refs):
    pieces, out, sems = refs[:-2], refs[-2], refs[-1]
    copies = []
    for i, piece in enumerate(pieces):
        r, (j, first, steps) = i // len(CALLS), CALLS[i % len(CALLS)]
        begin = ((info[0] ^ r) * HQ + FIRST_HEAD[j] + 2 * first) * VDIM
        begin = pl.multiple_of(begin, 128)
        copies.append(
            pltpu.make_async_copy(piece, out.at[:, pl.ds(begin, piece.shape[1])], sems.at[i])
        )
    for copy in copies:
        copy.start()
    for copy in copies:
        copy.wait()


def tie(array, *others):
    return lax.optimization_barrier((array,) + others)[0]


class Phases:
    def __init__(self):
        self.before, self.before_late, self.now, self.late = [], [], [], []

    def turn(self):
        self.before = self.now + self.before_late
        self.before_late, self.now, self.late = self.late, [], []

    def send(self, late, permute, array, *args):
        arrived = permute(tie(array, *self.before) if self.before else array, *args)
        if late != "-":
            (self.late if late == "~" else self.now).append(arrived)
        return arrived


def shape(dims, kind=jnp.bfloat16):
    return jax.ShapeDtypeStruct(dims, kind)


def in_hbm(*arrays):
    return [pltpu.with_memory_space_constraint(array, pltpu.HBM) for array in arrays]


def body(q_heads, kv_latent, latent_gain, w_up, page_ranks, lengths):
    tok = q_heads.shape[0]
    size = lax.axis_size("ctx")
    groups = lax.axis_size("groups")
    mine = lax.axis_index("ctx")
    quarter = lax.axis_index("groups") * 2 + mine % 2
    slot_count = max(2, 2 * tok // size)
    smem = pl.BlockSpec(memory_space=SMEM)
    params = pltpu.CompilerParams(vmem_limit_bytes=VMEM_LIMIT)
    alone = pltpu.CompilerParams(vmem_limit_bytes=3 * VMEM_LIMIT)

    def quad_swap(array, r):
        dx, dc = r // 2, r % 2
        pairs = [
            (g * size + i, (g ^ dx) * size + (i ^ dc)) for g in range(groups) for i in range(size)
        ]
        return lax.ppermute(array, ("groups", "ctx"), pairs)

    def around(array, by):
        return lax.ppermute(array, "ctx", [(i, (i + by) % size) for i in range(size)])

    def inner_swap(array):
        return lax.ppermute(array, "ctx", [(i, i ^ 2) for i in range(size)])

    def from_behind(array, by, odd_only):
        first = 1 if odd_only else 0
        step = 2 if odd_only else 1
        pairs = [(i, i + by) for i in range(first, size - by, step)]
        return lax.ppermute(array, "ctx", pairs)

    width = HQ * (NOPE + VDIM)
    quarter_info = quarter[None].astype(jnp.int32)
    anywhere = pl.BlockSpec(memory_space=pl.ANY)
    give = lax.dynamic_slice_in_dim(w_up, (quarter ^ 1) * width, width, 1)
    give, lengths = lax.optimization_barrier((give, lengths))
    got = quad_swap(give, 1)
    outer = 4 if size == 16 else 0
    if outer:
        pair_rows = pl.pallas_call(
            pair_kernel,
            out_shape=shape((2 * w_up.shape[0], width)),
            in_specs=[smem, pl.BlockSpec(memory_space=pltpu.HBM), anywhere],
            out_specs=anywhere,
            scratch_shapes=[pltpu.SemaphoreType.DMA((2,))],
            compiler_params=params,
            name="pair",
        )(quarter_info, *in_hbm(w_up), got)
    else:
        keep = lax.dynamic_slice_in_dim(w_up, quarter * width, width, 1)
        even = mine % 2 == 0
        both = jnp.concatenate(
            [jnp.where(even, keep, got), jnp.where(even, got, keep)], axis=0
        )
        same_core = [list(range(c, size, 2)) for c in range(2)]
        gathered = lax.all_gather(both, "ctx", axis=0, tiled=True, axis_index_groups=same_core)

    frequency = np.exp(-np.arange(ROPE // 2) * (2.0 * math.log(10000.0) / ROPE))
    frequency = jnp.asarray(np.tile(frequency, 4)[None, :], jnp.float32)
    mine_info = mine[None].astype(jnp.int32)

    def block(*dims):
        return pl.BlockSpec(dims, lambda i: (0,) * len(dims))

    rows, cosine, sine, outgoing = pl.pallas_call(
        functools.partial(rows_kernel, slot_count),
        grid=(1,),
        out_shape=(
            shape((tok, EXT)),
            shape((tok, 128), jnp.float32),
            shape((tok, 128), jnp.float32),
            shape((size * slot_count, ROW)),
        ),
        in_specs=[smem, smem, block(ROW, tok), block(1, LAT), block(1, tok), block(1, 128)],
        out_specs=[
            block(tok, EXT),
            block(tok, 128),
            block(tok, 128),
            block(size * slot_count, ROW),
        ],
        compiler_params=alone,
        name="rows",
    )(
        mine_info,
        lengths,
        *in_hbm(kv_latent.T, latent_gain[None, :], page_ranks.T, frequency),
    )

    queries = pl.pallas_call(
        query_kernel,
        out_shape=[shape((tok, h * (NOPE + ROPE))) for h in CHUNK_HEADS] * QUAD,
        grid=(1,),
        in_specs=[smem, block(*q_heads.shape), block(tok, 128), block(tok, 128)],
        out_specs=[block(tok, h * (NOPE + ROPE)) for h in CHUNK_HEADS] * QUAD,
        compiler_params=params,
        cost_estimate=pl.CostEstimate(
            flops=0, bytes_accessed=4 * q_heads.size, transcendentals=0
        ),
        name="queries",
    )(quarter_info, *in_hbm(q_heads, tie(cosine, pair_rows if outer else got), sine))

    phases = Phases()
    line = [pair_rows] if outer else []
    side = []
    half = width // CHUNKS
    halves = []
    moved = [[queries[j]] + [None] * (QUAD - 1) for j in range(CHUNKS)]
    parts = {"r": tie(rows, pair_rows if outer else got)}
    for name in [name for phase in PHASES for name in phase + ("|",)]:
        kind, late = name[0], name[-1]
        if kind == "|":
            phases.now.append(queries[0])
            phases.turn()
        elif kind == "z" and outer:
            line.append(phases.send(late, around, line[-1], 4))
        elif kind == "y" and outer:
            step = int(name[1])
            if step < outer - 1:
                side.append(phases.send(late, inner_swap, line[step]))
            else:
                halves.append(phases.send(late, inner_swap, line[step][:, :half]))
        elif kind == "w" and outer:
            halves.append(phases.send(late, around, side[-1][:, half:], 4))
        elif kind == "k":
            swapped = phases.send(late, quad_swap, parts["r"], 2)
            both_groups = jnp.concatenate([parts["r"], swapped], axis=0)
        elif kind == "b":
            behind = phases.send(late, from_behind, both_groups, 2, False)
        elif kind == "f":
            far_behind = phases.send(late, from_behind, both_groups, 4, True)
        elif kind == "p":
            own_rows = jnp.concatenate([both_groups, behind, far_behind], axis=0)
            other_rows = phases.send(late, quad_swap, own_rows, 1)
        elif kind == "q":
            j, r = int(name[1]), int(name[2])
            moved[j][r] = phases.send(late, quad_swap, queries[r * CHUNKS + j], r)

    def weights_for(j):
        if not outer:
            return [(gathered, FIRST_HEAD[j] // 2)]
        return [(piece, FIRST_HEAD[j] // 2) for piece in line + side] + [(halves[j], 0)]

    window = (REACH + 2) * tok
    resident = pl.BlockSpec(memory_space=VMEM)
    keys = pl.pallas_call(
        keys_kernel,
        out_shape=(
            shape((2, window, LAT)),
            shape((2, window, 128)),
            shape((2, window, 128)),
            shape((2, 2 * tok, window), jnp.float32),
        ),
        in_specs=[smem, resident, resident],
        out_specs=[resident] * 4,
        compiler_params=params,
        cost_estimate=pl.CostEstimate(flops=0, bytes_accessed=8 << 20, transcendentals=0),
        name="keys",
    )(mine_info, own_rows, other_rows)

    def attend(j, first, steps):
        heads = 2 * steps
        pieces_of_weight = [piece for piece, begin in weights_for(j)]
        flops = 2 * heads * 2 * (window * LAT * 256 + 2 * tok * window * (NOPE + ROPE + VDIM))
        return pl.pallas_call(
            functools.partial(attend_kernel, outer),
            grid=(steps,),
            out_shape=[shape((tok, heads * VDIM))] * QUAD,
            in_specs=[smem] + [resident] * 4
            + [
                pl.BlockSpec((piece.shape[0], 512), lambda i, begin=begin: (0, begin + first + i))
                for piece, begin in weights_for(j)
            ]
            + [pl.BlockSpec((tok, 256), lambda i: (0, first + i))] * QUAD
            + [pl.BlockSpec((tok, 128), lambda i: (0, CHUNK_HEADS[j] + first + i))] * QUAD,
            out_specs=[pl.BlockSpec((tok, 256), lambda i: (0, i))] * QUAD,
            scratch_shapes=[VMEM((LAT, 512), jnp.bfloat16)],
            compiler_params=params,
            cost_estimate=pl.CostEstimate(
                flops=flops,
                bytes_accessed=heads << 20,
                transcendentals=heads * 4 * tok * window,
            ),
            name="attend",
        )(mine_info, *keys, *pieces_of_weight, *moved[j], *moved[j])

    results = []
    for call in CALLS:
        last = len(results) + 1 == len(CALLS)
        mine_info = tie(mine_info, *(results[0][2:3] if last else []))
        pieces = attend(*call)
        mine_info = tie(mine_info, pieces[0])
        before = [piece for one in results for piece in one[1:]]
        results.append([pieces[0]] + [quad_swap(pieces[r], r) for r in range(1, QUAD)])
    pieces = [one[r] for r in range(QUAD) for one in results]
    arrived = lax.all_to_all(
        tie(outgoing, results[-1][0], *before).reshape(size, slot_count, ROW),
        "ctx",
        split_axis=0,
        concat_axis=0,
        tiled=True,
    )
    decode_cache = arrived.reshape(size * slot_count, ROW)
    attn_out = pl.pallas_call(
        gather_kernel,
        out_shape=shape((tok, H * VDIM)),
        in_specs=[smem] + [anywhere] * len(pieces),
        out_specs=anywhere,
        scratch_shapes=[pltpu.SemaphoreType.DMA((len(pieces),))],
        compiler_params=params,
        name="place",
    )(quarter_info, *pieces)
    return (attn_out, decode_cache)


def solution(mesh):
    return jax.shard_map(
        body,
        mesh=mesh,
        in_specs=(
            P(("groups", "ctx"), None),
            P(("groups", "ctx"), None),
            P(),
            P("ctx", None),
            P(("groups", "ctx"), None),
            P("groups"),
        ),
        out_specs=(P(("groups", "ctx"), None), P(("groups", "ctx"), None)),
        check_vma=False,
    )
```

```python
import functools
import math

import jax
import jax.numpy as jnp
import numpy as np
from jax import lax
from jax.experimental import pallas as pl
from jax.experimental.pallas import tpu as pltpu
from jax.sharding import PartitionSpec as P

H = 64
NOPE = 128
ROPE = 64
VDIM = 128
LAT = 512
REACH = 3
QUAD = 4
HQ = H // QUAD
CHUNK_HEADS = (8, 8)
PHASES = (
    ("z", "y0", "k", "b~", "f~"),
    ("z", "y1", "q02", "q01"),
    ("z", "y2", "p", "q03"),
    ("y3", "w", "q12~", "q13~", "q11"),
)
CHUNKS = len(CHUNK_HEADS)
FIRST_HEAD = tuple(sum(CHUNK_HEADS[:j]) for j in range(CHUNKS))
ROW = LAT + ROPE
EXT = 640
VMEM_LIMIT = 20 * 1024 * 1024
CALLS = ((0, 0, 4), (1, 0, 2), (1, 2, 2))
SMEM = pltpu.SMEM
VMEM = pltpu.VMEM


def rows_kernel(
    slot_count, info, lengths, kv, gain, ranks, freq, rows_out, cos_out, sin_out, outgoing_out
):
    tok = kv.shape[1]
    base = info[0] * tok
    spots = base + lax.broadcasted_iota(jnp.int32, (tok, 128), 0)
    lane = lax.broadcasted_iota(jnp.int32, (tok, 128), 1)
    begin = jnp.int32(0)
    own_start = jnp.zeros((tok, 128), jnp.int32)
    for r in range(lengths.shape[0]):
        own_start = jnp.where(spots >= begin, begin, own_start)
        begin = begin + lengths[r]
    offset = spots - own_start
    angles = offset.astype(jnp.float32) * freq[...]
    cosine = jnp.cos(angles)
    sine = jnp.where((lane & 32) == 0, -jnp.sin(angles), jnp.sin(angles))
    cos_out[...] = cosine
    sin_out[...] = sine
    raw = kv[...].astype(jnp.float32).T
    latent = raw[:, :LAT]
    mean = jnp.sum(latent * latent, axis=1, keepdims=True) * (1.0 / LAT)
    latent = latent * lax.rsqrt(mean + 1e-06) * gain[...]
    key = raw[:, LAT:]
    swapped = jnp.concatenate([key[:, ROPE // 2 :], key[:, : ROPE // 2]], axis=1)
    turned = key * cosine[:, :ROPE] + swapped * sine[:, :ROPE]
    high = (offset >> 8).astype(jnp.float32)
    low = (offset & 255).astype(jnp.float32)
    meta = jnp.where(lane == 0, high, jnp.where(lane == 1, low, 0.0))
    tail = jnp.concatenate([turned, meta[:, :ROPE]], axis=1)
    rows_out[:, :LAT] = latent.astype(jnp.bfloat16)
    rows_out[:, LAT:] = tail.astype(jnp.bfloat16)

    rank_row = jnp.broadcast_to(ranks[...], (tok, tok)).astype(jnp.float32)
    rank_col = rank_row.T
    earlier = lax.broadcasted_iota(jnp.int32, (tok, tok), 0) < lax.broadcasted_iota(
        jnp.int32, (tok, tok), 1
    )
    same = jnp.where((rank_col == rank_row) & earlier, 1.0, 0.0)
    slot = jnp.sum(same, axis=0, keepdims=True)
    target = (rank_row[:1] * slot_count + slot).astype(jnp.int32)
    spots_out = lax.broadcasted_iota(jnp.int32, (outgoing_out.shape[0], tok), 0)
    selector = jnp.where(spots_out == target, 1.0, 0.0).astype(jnp.bfloat16)
    picked = jnp.dot(selector, rows_out[:, :ROW], preferred_element_type=jnp.float32)
    outgoing_out[...] = picked.astype(jnp.bfloat16)


def query_kernel(info, query, cosine, sine, *outs):
    tok = query.shape[0]
    lane = lax.broadcasted_iota(jnp.int32, (tok, 128), 1)
    low_half = lane < 64
    first_quarter = (lane & 32) == 0
    cos_table = cosine[...]
    sin_table = sine[...]
    for r in range(QUAD):
        first = (info[0] ^ r) * (HQ * (NOPE + ROPE))
        for pair in range(HQ // 2):
            j = max(j for j in range(CHUNKS) if FIRST_HEAD[j] <= 2 * pair)
            out = outs[r * CHUNKS + j]
            at = pair - FIRST_HEAD[j] // 2
            rope_at = CHUNK_HEADS[j] * NOPE + at * 128
            begin = pl.multiple_of(first + pair * 2 * (NOPE + ROPE), 128)
            both = query[:, pl.ds(begin, 2 * (NOPE + ROPE))]
            mid = both[:, 128:256].astype(jnp.float32)
            end = both[:, 256:384].astype(jnp.float32)
            turned = jnp.where(low_half, mid, end)
            odd_nope = pltpu.roll(jnp.where(low_half, end, mid), 64, 1)
            swapped = jnp.where(
                first_quarter, pltpu.roll(turned, 96, 1), pltpu.roll(turned, 32, 1)
            )
            turned = turned * cos_table + swapped * sin_table
            out[:, at * 256 : at * 256 + 128] = both[:, :128]
            out[:, at * 256 + 128 : at * 256 + 256] = odd_nope.astype(jnp.bfloat16)
            out[:, rope_at : rope_at + 128] = turned.astype(jnp.bfloat16)


def pair_kernel(info, w_up, got, out, sem):
    rows, width = got.shape
    begin = pl.multiple_of(info[0] * width, 128)
    copies = [
        pltpu.make_async_copy(w_up.at[:, pl.ds(begin, width)], out.at[pl.ds(0, rows)], sem.at[0]),
        pltpu.make_async_copy(got, out.at[pl.ds(rows, rows)], sem.at[1]),
    ]
    for copy in copies:
        copy.start()
    for copy in copies:
        copy.wait()


def keys_kernel(info, own, other, latent, rope_even, rope_odd, bias):
    tok = own.shape[0] // 6
    mine = info[0]
    partner = mine ^ 1
    has_last = (mine & 1) == 1
    starts = [mine, partner, mine - 2, partner - 2, (mine >> 1) * 2 - 3]
    blank = jnp.zeros((tok, ROPE), jnp.bfloat16)
    lane = lax.broadcasted_iota(jnp.int32, (tok, tok), 1)
    row = lax.broadcasted_iota(jnp.int32, (tok, tok), 0)
    for g in range(2):
        mine_of, other_of = [
            [ref[(2 * n + g) * tok : (2 * n + g + 1) * tok] for n in range(3)]
            for ref in (own, other)
        ]
        pieces = [
            mine_of[0],
            other_of[0],
            mine_of[1],
            other_of[1],
            jnp.where(has_last, mine_of[2], other_of[2]),
        ]
        for b, piece in enumerate(pieces):
            here = slice(b * tok, (b + 1) * tok)
            latent[g, here] = piece[:, :LAT]
            turned = piece[:, LAT : LAT + ROPE]
            rope_even[g, here] = jnp.concatenate([turned, blank], axis=1)
            rope_odd[g, here] = jnp.concatenate([blank, turned], axis=1)
        for half in range(2):
            meta = pieces[half][:, LAT:].astype(jnp.float32)
            offset = (meta[:, ROPE : ROPE + 1] * 256.0 + meta[:, ROPE + 1 : ROPE + 2]).astype(
                jnp.int32
            )
            spots = starts[half] * tok + row
            lowest = jnp.maximum(spots - offset, (starts[half] - REACH) * tok)
            for b in range(REACH + 2):
                keys = starts[b] * tok + lane
                allowed = (keys >= lowest) & (keys <= spots)
                bias[g, half * tok : (half + 1) * tok, b * tok : (b + 1) * tok] = jnp.where(
                    allowed, 0.0, -1e30
                )


def attend_kernel(outer, info, latent, rope_even, rope_odd, bias, *refs):
    pieces_count = 2 * outer if outer else 1
    pieces_of_weight, refs = refs[:pieces_count], refs[pieces_count:]
    nope = refs[0:QUAD]
    rope = refs[QUAD : 2 * QUAD]
    outs = refs[2 * QUAD : 3 * QUAD]
    held = refs[3 * QUAD]
    tok = nope[0].shape[0]
    mine = info[0]
    scale = (NOPE + ROPE) ** (-0.5) * math.log2(math.e)

    if outer:
        weight = held
        for i, piece in enumerate(pieces_of_weight):
            side, behind = i // outer, i % outer
            chip = ((mine >> 2) + outer - behind) % outer * 2 + (((mine >> 1) & 1) ^ side)
            rows = piece.shape[0] // 2
            for core in range(2):
                begin = pl.multiple_of(chip * 2 * rows + ((mine & 1) ^ core) * rows, rows)
                held[pl.ds(begin, rows)] = piece[core * rows : (core + 1) * rows]
    else:
        weight = pieces_of_weight[0]

    def expand(g):
        wide = jnp.dot(latent[g], weight[...], preferred_element_type=jnp.float32)
        return wide.astype(jnp.bfloat16)

    def score(g, b, expanded):
        at = slice(b * 128, (b + 1) * 128)
        key_rope = (rope_even, rope_odd)[b][g]
        key = jnp.concatenate([expanded[:, b * 256 : b * 256 + 128], key_rope], axis=1)
        query = jnp.concatenate(
            [
                jnp.concatenate([nope[2 * g][:, at], rope[2 * g][...]], axis=1),
                jnp.concatenate([nope[2 * g + 1][:, at], rope[2 * g + 1][...]], axis=1),
            ],
            axis=0,
        )
        return lax.dot_general(
            query, key, (((1,), (1,)), ((), ())), preferred_element_type=jnp.float32
        )

    def weigh(g, scores):
        scores = scores * scale + bias[g]
        largest = jnp.max(scores, axis=1, keepdims=True)
        expo = jnp.exp2(scores - largest)
        return expo.astype(jnp.bfloat16), jnp.sum(expo, axis=1, keepdims=True)

    def mix(g, b, expanded, weights, total):
        at = slice(b * 128, (b + 1) * 128)
        value = expanded[:, b * 256 + 128 : b * 256 + 256]
        mixed = jnp.dot(weights, value, preferred_element_type=jnp.float32)
        mixed = (mixed / total).astype(jnp.bfloat16)
        outs[2 * g][:, at] = mixed[:tok]
        outs[2 * g + 1][:, at] = mixed[tok:]

    first = expand(0)
    scores = score(0, 0, first)
    second = expand(1)
    weighed = weigh(0, scores)
    scores = score(0, 1, first)
    mix(0, 0, first, *weighed)
    weighed = weigh(0, scores)
    scores = score(1, 0, second)
    mix(0, 1, first, *weighed)
    weighed = weigh(1, scores)
    scores = score(1, 1, second)
    mix(1, 0, second, *weighed)
    weighed = weigh(1, scores)
    mix(1, 1, second, *weighed)


def gather_kernel(info, *refs):
    pieces, out, sems = refs[:-2], refs[-2], refs[-1]
    copies = []
    for i, piece in enumerate(pieces):
        r, (j, first, steps) = i // len(CALLS), CALLS[i % len(CALLS)]
        begin = ((info[0] ^ r) * HQ + FIRST_HEAD[j] + 2 * first) * VDIM
        begin = pl.multiple_of(begin, 128)
        copies.append(
            pltpu.make_async_copy(piece, out.at[:, pl.ds(begin, piece.shape[1])], sems.at[i])
        )
    for copy in copies:
        copy.start()
    for copy in copies:
        copy.wait()


def tie(array, *others):
    return lax.optimization_barrier((array,) + others)[0]


class Phases:
    def __init__(self):
        self.before, self.before_late, self.now, self.late = [], [], [], []

    def turn(self):
        self.before = self.now + self.before_late
        self.before_late, self.now, self.late = self.late, [], []

    def send(self, late, permute, array, *args):
        arrived = permute(tie(array, *self.before) if self.before else array, *args)
        if late != "-":
            (self.late if late == "~" else self.now).append(arrived)
        return arrived


def shape(dims, kind=jnp.bfloat16):
    return jax.ShapeDtypeStruct(dims, kind)


def in_hbm(*arrays):
    return [pltpu.with_memory_space_constraint(array, pltpu.HBM) for array in arrays]


def body(q_heads, kv_latent, latent_gain, w_up, page_ranks, lengths):
    tok = q_heads.shape[0]
    size = lax.axis_size("ctx")
    groups = lax.axis_size("groups")
    mine = lax.axis_index("ctx")
    quarter = lax.axis_index("groups") * 2 + mine % 2
    slot_count = max(2, 2 * tok // size)
    smem = pl.BlockSpec(memory_space=SMEM)
    params = pltpu.CompilerParams(vmem_limit_bytes=VMEM_LIMIT)
    alone = pltpu.CompilerParams(vmem_limit_bytes=3 * VMEM_LIMIT)

    def quad_swap(array, r):
        dx, dc = r // 2, r % 2
        pairs = [
            (g * size + i, (g ^ dx) * size + (i ^ dc)) for g in range(groups) for i in range(size)
        ]
        return lax.ppermute(array, ("groups", "ctx"), pairs)

    def around(array, by):
        return lax.ppermute(array, "ctx", [(i, (i + by) % size) for i in range(size)])

    def inner_swap(array):
        return lax.ppermute(array, "ctx", [(i, i ^ 2) for i in range(size)])

    def from_behind(array, by, odd_only):
        first = 1 if odd_only else 0
        step = 2 if odd_only else 1
        pairs = [(i, i + by) for i in range(first, size - by, step)]
        return lax.ppermute(array, "ctx", pairs)

    width = HQ * (NOPE + VDIM)
    quarter_info = quarter[None].astype(jnp.int32)
    anywhere = pl.BlockSpec(memory_space=pl.ANY)
    give = lax.dynamic_slice_in_dim(w_up, (quarter ^ 1) * width, width, 1)
    give, lengths = lax.optimization_barrier((give, lengths))
    got = quad_swap(give, 1)
    outer = 4 if size == 16 else 0
    if outer:
        pair_rows = pl.pallas_call(
            pair_kernel,
            out_shape=shape((2 * w_up.shape[0], width)),
            in_specs=[smem, pl.BlockSpec(memory_space=pltpu.HBM), anywhere],
            out_specs=anywhere,
            scratch_shapes=[pltpu.SemaphoreType.DMA((2,))],
            compiler_params=params,
            name="pair",
        )(quarter_info, *in_hbm(w_up), got)
    else:
        keep = lax.dynamic_slice_in_dim(w_up, quarter * width, width, 1)
        even = mine % 2 == 0
        both = jnp.concatenate(
            [jnp.where(even, keep, got), jnp.where(even, got, keep)], axis=0
        )
        same_core = [list(range(c, size, 2)) for c in range(2)]
        gathered = lax.all_gather(both, "ctx", axis=0, tiled=True, axis_index_groups=same_core)

    frequency = np.exp(-np.arange(ROPE // 2) * (2.0 * math.log(10000.0) / ROPE))
    frequency = jnp.asarray(np.tile(frequency, 4)[None, :], jnp.float32)
    mine_info = mine[None].astype(jnp.int32)

    def block(*dims):
        return pl.BlockSpec(dims, lambda i: (0,) * len(dims))

    rows, cosine, sine, outgoing = pl.pallas_call(
        functools.partial(rows_kernel, slot_count),
        grid=(1,),
        out_shape=(
            shape((tok, EXT)),
            shape((tok, 128), jnp.float32),
            shape((tok, 128), jnp.float32),
            shape((size * slot_count, ROW)),
        ),
        in_specs=[smem, smem, block(ROW, tok), block(1, LAT), block(1, tok), block(1, 128)],
        out_specs=[
            block(tok, EXT),
            block(tok, 128),
            block(tok, 128),
            block(size * slot_count, ROW),
        ],
        compiler_params=alone,
        name="rows",
    )(
        mine_info,
        lengths,
        *in_hbm(kv_latent.T, latent_gain[None, :], page_ranks.T, frequency),
    )

    queries = pl.pallas_call(
        query_kernel,
        out_shape=[shape((tok, h * (NOPE + ROPE))) for h in CHUNK_HEADS] * QUAD,
        grid=(1,),
        in_specs=[smem, block(*q_heads.shape), block(tok, 128), block(tok, 128)],
        out_specs=[block(tok, h * (NOPE + ROPE)) for h in CHUNK_HEADS] * QUAD,
        compiler_params=params,
        cost_estimate=pl.CostEstimate(
            flops=0, bytes_accessed=4 * q_heads.size, transcendentals=0
        ),
        name="queries",
    )(quarter_info, *in_hbm(q_heads, tie(cosine, pair_rows if outer else got), sine))

    phases = Phases()
    line = [pair_rows] if outer else []
    side = []
    half = width // CHUNKS
    halves = []
    moved = [[queries[j]] + [None] * (QUAD - 1) for j in range(CHUNKS)]
    parts = {"r": tie(rows, pair_rows if outer else got)}
    for name in [name for phase in PHASES for name in phase + ("|",)]:
        kind, late = name[0], name[-1]
        if kind == "|":
            phases.now.append(queries[0])
            phases.turn()
        elif kind == "z" and outer:
            line.append(phases.send(late, around, line[-1], 4))
        elif kind == "y" and outer:
            step = int(name[1])
            if step < outer - 1:
                side.append(phases.send(late, inner_swap, line[step]))
            else:
                halves.append(phases.send(late, inner_swap, line[step][:, :half]))
        elif kind == "w" and outer:
            halves.append(phases.send(late, around, side[-1][:, half:], 4))
        elif kind == "k":
            swapped = phases.send(late, quad_swap, parts["r"], 2)
            both_groups = jnp.concatenate([parts["r"], swapped], axis=0)
        elif kind == "b":
            behind = phases.send(late, from_behind, both_groups, 2, False)
        elif kind == "f":
            far_behind = phases.send(late, from_behind, both_groups, 4, True)
        elif kind == "p":
            own_rows = jnp.concatenate([both_groups, behind, far_behind], axis=0)
            other_rows = phases.send(late, quad_swap, own_rows, 1)
        elif kind == "q":
            j, r = int(name[1]), int(name[2])
            moved[j][r] = phases.send(late, quad_swap, queries[r * CHUNKS + j], r)

    def weights_for(j):
        if not outer:
            return [(gathered, FIRST_HEAD[j] // 2)]
        return [(piece, FIRST_HEAD[j] // 2) for piece in line + side] + [(halves[j], 0)]

    window = (REACH + 2) * tok
    resident = pl.BlockSpec(memory_space=VMEM)
    keys = pl.pallas_call(
        keys_kernel,
        out_shape=(
            shape((2, window, LAT)),
            shape((2, window, 128)),
            shape((2, window, 128)),
            shape((2, 2 * tok, window), jnp.float32),
        ),
        in_specs=[smem, resident, resident],
        out_specs=[resident] * 4,
        compiler_params=params,
        cost_estimate=pl.CostEstimate(flops=0, bytes_accessed=8 << 20, transcendentals=0),
        name="keys",
    )(mine_info, own_rows, other_rows)

    def attend(j, first, steps):
        heads = 2 * steps
        pieces_of_weight = [piece for piece, begin in weights_for(j)]
        flops = 2 * heads * 2 * (window * LAT * 256 + 2 * tok * window * (NOPE + ROPE + VDIM))
        return pl.pallas_call(
            functools.partial(attend_kernel, outer),
            grid=(steps,),
            out_shape=[shape((tok, heads * VDIM))] * QUAD,
            in_specs=[smem] + [resident] * 4
            + [
                pl.BlockSpec((piece.shape[0], 512), lambda i, begin=begin: (0, begin + first + i))
                for piece, begin in weights_for(j)
            ]
            + [pl.BlockSpec((tok, 256), lambda i: (0, first + i))] * QUAD
            + [pl.BlockSpec((tok, 128), lambda i: (0, CHUNK_HEADS[j] + first + i))] * QUAD,
            out_specs=[pl.BlockSpec((tok, 256), lambda i: (0, i))] * QUAD,
            scratch_shapes=[VMEM((LAT, 512), jnp.bfloat16)],
            compiler_params=params,
            cost_estimate=pl.CostEstimate(
                flops=flops,
                bytes_accessed=heads << 20,
                transcendentals=heads * 4 * tok * window,
            ),
            name="attend",
        )(mine_info, *keys, *pieces_of_weight, *moved[j], *moved[j])

    results = []
    for call in CALLS:
        last = len(results) + 1 == len(CALLS)
        mine_info = tie(mine_info, *(results[0][2:3] if last else []))
        pieces = attend(*call)
        mine_info = tie(mine_info, pieces[0])
        before = [piece for one in results for piece in one[1:]]
        results.append([pieces[0]] + [quad_swap(pieces[r], r) for r in range(1, QUAD)])
    pieces = [one[r] for r in range(QUAD) for one in results]
    arrived = lax.all_to_all(
        tie(outgoing, results[-1][0], *before).reshape(size, slot_count, ROW),
        "ctx",
        split_axis=0,
        concat_axis=0,
        tiled=True,
    )
    decode_cache = arrived.reshape(size * slot_count, ROW)
    attn_out = pl.pallas_call(
        gather_kernel,
        out_shape=shape((tok, H * VDIM)),
        in_specs=[smem] + [anywhere] * len(pieces),
        out_specs=anywhere,
        scratch_shapes=[pltpu.SemaphoreType.DMA((len(pieces),))],
        compiler_params=params,
        name="place",
    )(quarter_info, *pieces)
    return (attn_out, decode_cache)


def solution(mesh):
    return jax.shard_map(
        body,
        mesh=mesh,
        in_specs=(
            P(("groups", "ctx"), None),
            P(("groups", "ctx"), None),
            P(),
            P("ctx", None),
            P(("groups", "ctx"), None),
            P("groups"),
        ),
        out_specs=(P(("groups", "ctx"), None), P(("groups", "ctx"), None)),
        check_vma=False,
    )
```

```python
import functools
import math

import jax
import jax.numpy as jnp
import numpy as np
from jax import lax
from jax.experimental import pallas as pl
from jax.experimental.pallas import tpu as pltpu
from jax.sharding import PartitionSpec as P

H = 64
NOPE = 128
ROPE = 64
VDIM = 128
LAT = 512
REACH = 3
QUAD = 4
HQ = H // QUAD
CHUNK_HEADS = (8, 8)
PHASES = (
    ("z", "y0", "k", "q02", "b~", "f~"),
    ("z", "y1", "q03", "q01", "e"),
    ("z", "y2", "p", "q12", "e"),
    ("y3", "w", "q13~", "q11", "e-", "e-"),
)
CHUNKS = len(CHUNK_HEADS)
FIRST_HEAD = tuple(sum(CHUNK_HEADS[:j]) for j in range(CHUNKS))
ROW = LAT + ROPE
EXT = 640
VMEM_LIMIT = 20 * 1024 * 1024
CALLS = ((0, 0, 4), (1, 0, 2), (1, 2, 2))
SMEM = pltpu.SMEM
VMEM = pltpu.VMEM


def rows_kernel(
    slot_count,
    relative,
    info,
    lengths,
    kv,
    gain,
    ranks,
    freq,
    rows_out,
    cos_out,
    sin_out,
    outgoing_out,
):
    tok = kv.shape[1]
    base = info[0] * tok
    spots = base + lax.broadcasted_iota(jnp.int32, (tok, 128), 0)
    lane = lax.broadcasted_iota(jnp.int32, (tok, 128), 1)
    begin = jnp.int32(0)
    own_start = jnp.zeros((tok, 128), jnp.int32)
    for r in range(lengths.shape[0]):
        own_start = jnp.where(spots >= begin, begin, own_start)
        begin = begin + lengths[r]
    offset = spots - own_start
    angles = offset.astype(jnp.float32) * freq[...]
    cosine = jnp.cos(angles)
    sine = jnp.where((lane & 32) == 0, -jnp.sin(angles), jnp.sin(angles))
    cos_out[...] = cosine
    sin_out[...] = sine
    raw = kv[...].astype(jnp.float32).T
    latent = raw[:, :LAT]
    mean = jnp.sum(latent * latent, axis=1, keepdims=True) * (1.0 / LAT)
    latent = latent * lax.rsqrt(mean + 1e-06) * gain[...]
    key = raw[:, LAT:]
    swapped = jnp.concatenate([key[:, ROPE // 2 :], key[:, : ROPE // 2]], axis=1)
    turned = key * cosine[:, :ROPE] + swapped * sine[:, :ROPE]
    high = (offset >> 8).astype(jnp.float32)
    low = (offset & 255).astype(jnp.float32)
    meta = jnp.where(lane == 0, high, jnp.where(lane == 1, low, 0.0))
    tail = jnp.concatenate([turned, meta[:, :ROPE]], axis=1)
    rows_out[:, :LAT] = latent.astype(jnp.bfloat16)
    rows_out[:, LAT:] = tail.astype(jnp.bfloat16)

    block = ranks[...]
    if relative:
        away = block ^ info[0]
        block = ((away & 1) << 3) | ((away & 2) << 1) | ((away & 4) >> 1) | (away >> 3)
    rank_row = jnp.broadcast_to(block, (tok, tok)).astype(jnp.float32)
    rank_col = rank_row.T
    earlier = lax.broadcasted_iota(jnp.int32, (tok, tok), 0) < lax.broadcasted_iota(
        jnp.int32, (tok, tok), 1
    )
    same = jnp.where((rank_col == rank_row) & earlier, 1.0, 0.0)
    slot = jnp.sum(same, axis=0, keepdims=True)
    target = (rank_row[:1] * slot_count + slot).astype(jnp.int32)
    spots_out = lax.broadcasted_iota(jnp.int32, (outgoing_out.shape[0], tok), 0)
    selector = jnp.where(spots_out == target, 1.0, 0.0).astype(jnp.bfloat16)
    picked = jnp.dot(selector, rows_out[:, :ROW], preferred_element_type=jnp.float32)
    outgoing_out[...] = picked.astype(jnp.bfloat16)


def query_kernel(info, query, cosine, sine, *outs):
    tok = query.shape[0]
    lane = lax.broadcasted_iota(jnp.int32, (tok, 128), 1)
    low_half = lane < 64
    first_quarter = (lane & 32) == 0
    cos_table = cosine[...]
    sin_table = sine[...]
    for r in range(QUAD):
        first = (info[0] ^ r) * (HQ * (NOPE + ROPE))
        for pair in range(HQ // 2):
            j = max(j for j in range(CHUNKS) if FIRST_HEAD[j] <= 2 * pair)
            out = outs[r * CHUNKS + j]
            at = pair - FIRST_HEAD[j] // 2
            rope_at = CHUNK_HEADS[j] * NOPE + at * 128
            begin = pl.multiple_of(first + pair * 2 * (NOPE + ROPE), 128)
            both = query[:, pl.ds(begin, 2 * (NOPE + ROPE))]
            mid = both[:, 128:256].astype(jnp.float32)
            end = both[:, 256:384].astype(jnp.float32)
            turned = jnp.where(low_half, mid, end)
            odd_nope = pltpu.roll(jnp.where(low_half, end, mid), 64, 1)
            swapped = jnp.where(
                first_quarter, pltpu.roll(turned, 96, 1), pltpu.roll(turned, 32, 1)
            )
            turned = turned * cos_table + swapped * sin_table
            out[:, at * 256 : at * 256 + 128] = both[:, :128]
            out[:, at * 256 + 128 : at * 256 + 256] = odd_nope.astype(jnp.bfloat16)
            out[:, rope_at : rope_at + 128] = turned.astype(jnp.bfloat16)


def pair_kernel(info, w_up, got, out, sem):
    rows, width = got.shape
    begin = pl.multiple_of(info[0] * width, 128)
    copies = [
        pltpu.make_async_copy(w_up.at[:, pl.ds(begin, width)], out.at[pl.ds(0, rows)], sem.at[0]),
        pltpu.make_async_copy(got, out.at[pl.ds(rows, rows)], sem.at[1]),
    ]
    for copy in copies:
        copy.start()
    for copy in copies:
        copy.wait()


def keys_kernel(info, own, other, latent, rope_even, rope_odd, bias):
    tok = own.shape[0] // 6
    mine = info[0]
    partner = mine ^ 1
    has_last = (mine & 1) == 1
    starts = [mine, partner, mine - 2, partner - 2, (mine >> 1) * 2 - 3]
    blank = jnp.zeros((tok, ROPE), jnp.bfloat16)
    lane = lax.broadcasted_iota(jnp.int32, (tok, tok), 1)
    row = lax.broadcasted_iota(jnp.int32, (tok, tok), 0)
    for g in range(2):
        mine_of, other_of = [
            [ref[(2 * n + g) * tok : (2 * n + g + 1) * tok] for n in range(3)]
            for ref in (own, other)
        ]
        pieces = [
            mine_of[0],
            other_of[0],
            mine_of[1],
            other_of[1],
            jnp.where(has_last, mine_of[2], other_of[2]),
        ]
        for b, piece in enumerate(pieces):
            here = slice(b * tok, (b + 1) * tok)
            latent[g, here] = piece[:, :LAT]
            turned = piece[:, LAT : LAT + ROPE]
            rope_even[g, here] = jnp.concatenate([turned, blank], axis=1)
            rope_odd[g, here] = jnp.concatenate([blank, turned], axis=1)
        for half in range(2):
            meta = pieces[half][:, LAT:].astype(jnp.float32)
            offset = (meta[:, ROPE : ROPE + 1] * 256.0 + meta[:, ROPE + 1 : ROPE + 2]).astype(
                jnp.int32
            )
            spots = starts[half] * tok + row
            lowest = jnp.maximum(spots - offset, (starts[half] - REACH) * tok)
            for b in range(REACH + 2):
                keys = starts[b] * tok + lane
                allowed = (keys >= lowest) & (keys <= spots)
                bias[g, half * tok : (half + 1) * tok, b * tok : (b + 1) * tok] = jnp.where(
                    allowed, 0.0, -1e30
                )


def attend_kernel(outer, info, latent, rope_even, rope_odd, bias, *refs):
    pieces_count = 2 * outer if outer else 1
    pieces_of_weight, refs = refs[:pieces_count], refs[pieces_count:]
    nope = refs[0:QUAD]
    rope = refs[QUAD : 2 * QUAD]
    outs = refs[2 * QUAD : 3 * QUAD]
    held = refs[3 * QUAD]
    tok = nope[0].shape[0]
    mine = info[0]
    scale = (NOPE + ROPE) ** (-0.5) * math.log2(math.e)

    if outer:
        weight = held
        for i, piece in enumerate(pieces_of_weight):
            side, behind = i // outer, i % outer
            chip = ((mine >> 2) + outer - behind) % outer * 2 + (((mine >> 1) & 1) ^ side)
            rows = piece.shape[0] // 2
            for core in range(2):
                begin = pl.multiple_of(chip * 2 * rows + ((mine & 1) ^ core) * rows, rows)
                held[pl.ds(begin, rows)] = piece[core * rows : (core + 1) * rows]
    else:
        weight = pieces_of_weight[0]

    def expand(g):
        wide = jnp.dot(latent[g], weight[...], preferred_element_type=jnp.float32)
        return wide.astype(jnp.bfloat16)

    def score(g, b, expanded):
        at = slice(b * 128, (b + 1) * 128)
        key_rope = (rope_even, rope_odd)[b][g]
        key = jnp.concatenate([expanded[:, b * 256 : b * 256 + 128], key_rope], axis=1)
        query = jnp.concatenate(
            [
                jnp.concatenate([nope[2 * g][:, at], rope[2 * g][...]], axis=1),
                jnp.concatenate([nope[2 * g + 1][:, at], rope[2 * g + 1][...]], axis=1),
            ],
            axis=0,
        )
        return lax.dot_general(
            query, key, (((1,), (1,)), ((), ())), preferred_element_type=jnp.float32
        )

    def weigh(g, scores):
        scores = scores * scale + bias[g]
        largest = jnp.max(scores, axis=1, keepdims=True)
        expo = jnp.exp2(scores - largest)
        return expo.astype(jnp.bfloat16), jnp.sum(expo, axis=1, keepdims=True)

    def mix(g, b, expanded, weights, total):
        at = slice(b * 128, (b + 1) * 128)
        value = expanded[:, b * 256 + 128 : b * 256 + 256]
        mixed = jnp.dot(weights, value, preferred_element_type=jnp.float32)
        mixed = (mixed / total).astype(jnp.bfloat16)
        outs[2 * g][:, at] = mixed[:tok]
        outs[2 * g + 1][:, at] = mixed[tok:]

    first = expand(0)
    scores = score(0, 0, first)
    second = expand(1)
    weighed = weigh(0, scores)
    scores = score(0, 1, first)
    mix(0, 0, first, *weighed)
    weighed = weigh(0, scores)
    scores = score(1, 0, second)
    mix(0, 1, first, *weighed)
    weighed = weigh(1, scores)
    scores = score(1, 1, second)
    mix(1, 0, second, *weighed)
    weighed = weigh(1, scores)
    mix(1, 1, second, *weighed)


def sort_kernel(info, relative, out, sem):
    rows = relative.shape[1]
    copies = []
    for d in range(relative.shape[0]):
        begin = pl.multiple_of((info[0] ^ d) * rows, rows)
        copies.append(
            pltpu.make_async_copy(relative.at[d], out.at[pl.ds(begin, rows)], sem.at[d])
        )
    for copy in copies:
        copy.start()
    for copy in copies:
        copy.wait()


def gather_kernel(info, *refs):
    pieces, out, sems = refs[:-2], refs[-2], refs[-1]
    copies = []
    for i, piece in enumerate(pieces):
        r, (j, first, steps) = i // len(CALLS), CALLS[i % len(CALLS)]
        begin = ((info[0] ^ r) * HQ + FIRST_HEAD[j] + 2 * first) * VDIM
        begin = pl.multiple_of(begin, 128)
        copies.append(
            pltpu.make_async_copy(piece, out.at[:, pl.ds(begin, piece.shape[1])], sems.at[i])
        )
    for copy in copies:
        copy.start()
    for copy in copies:
        copy.wait()


def tie(array, *others):
    return lax.optimization_barrier((array,) + others)[0]


class Phases:
    def __init__(self):
        self.before, self.before_late, self.now, self.late = [], [], [], []

    def turn(self):
        self.before = self.now + self.before_late
        self.before_late, self.now, self.late = self.late, [], []

    def send(self, late, permute, array, *args):
        arrived = permute(tie(array, *self.before) if self.before else array, *args)
        if late != "-":
            (self.late if late == "~" else self.now).append(arrived)
        return arrived


def shape(dims, kind=jnp.bfloat16):
    return jax.ShapeDtypeStruct(dims, kind)


def in_hbm(*arrays):
    return [pltpu.with_memory_space_constraint(array, pltpu.HBM) for array in arrays]


def body(q_heads, kv_latent, latent_gain, w_up, page_ranks, lengths):
    tok = q_heads.shape[0]
    size = lax.axis_size("ctx")
    groups = lax.axis_size("groups")
    mine = lax.axis_index("ctx")
    quarter = lax.axis_index("groups") * 2 + mine % 2
    slot_count = max(2, 2 * tok // size)
    smem = pl.BlockSpec(memory_space=SMEM)
    params = pltpu.CompilerParams(vmem_limit_bytes=VMEM_LIMIT)
    alone = pltpu.CompilerParams(vmem_limit_bytes=3 * VMEM_LIMIT)

    def quad_swap(array, r):
        dx, dc = r // 2, r % 2
        pairs = [
            (g * size + i, (g ^ dx) * size + (i ^ dc)) for g in range(groups) for i in range(size)
        ]
        return lax.ppermute(array, ("groups", "ctx"), pairs)

    def around(array, by):
        return lax.ppermute(array, "ctx", [(i, (i + by) % size) for i in range(size)])

    def inner_swap(array):
        return lax.ppermute(array, "ctx", [(i, i ^ 2) for i in range(size)])

    def pair_swap(array, distance):
        return lax.ppermute(array, "ctx", [(i, i ^ distance) for i in range(size)])

    def from_behind(array, by, odd_only):
        first = 1 if odd_only else 0
        step = 2 if odd_only else 1
        pairs = [(i, i + by) for i in range(first, size - by, step)]
        return lax.ppermute(array, "ctx", pairs)

    width = HQ * (NOPE + VDIM)
    quarter_info = quarter[None].astype(jnp.int32)
    anywhere = pl.BlockSpec(memory_space=pl.ANY)
    give = lax.dynamic_slice_in_dim(w_up, (quarter ^ 1) * width, width, 1)
    give, lengths = lax.optimization_barrier((give, lengths))
    got = quad_swap(give, 1)
    outer = 4 if size == 16 else 0
    if outer:
        pair_rows = pl.pallas_call(
            pair_kernel,
            out_shape=shape((2 * w_up.shape[0], width)),
            in_specs=[smem, pl.BlockSpec(memory_space=pltpu.HBM), anywhere],
            out_specs=anywhere,
            scratch_shapes=[pltpu.SemaphoreType.DMA((2,))],
            compiler_params=params,
            name="pair",
        )(quarter_info, *in_hbm(w_up), got)
    else:
        keep = lax.dynamic_slice_in_dim(w_up, quarter * width, width, 1)
        even = mine % 2 == 0
        both = jnp.concatenate(
            [jnp.where(even, keep, got), jnp.where(even, got, keep)], axis=0
        )
        same_core = [list(range(c, size, 2)) for c in range(2)]
        gathered = lax.all_gather(both, "ctx", axis=0, tiled=True, axis_index_groups=same_core)

    frequency = np.exp(-np.arange(ROPE // 2) * (2.0 * math.log(10000.0) / ROPE))
    frequency = jnp.asarray(np.tile(frequency, 4)[None, :], jnp.float32)
    mine_info = mine[None].astype(jnp.int32)

    def block(*dims):
        return pl.BlockSpec(dims, lambda i: (0,) * len(dims))

    rows, cosine, sine, outgoing = pl.pallas_call(
        functools.partial(rows_kernel, slot_count, outer > 0),
        grid=(1,),
        out_shape=(
            shape((tok, EXT)),
            shape((tok, 128), jnp.float32),
            shape((tok, 128), jnp.float32),
            shape((size * slot_count, ROW)),
        ),
        in_specs=[smem, smem, block(ROW, tok), block(1, LAT), block(1, tok), block(1, 128)],
        out_specs=[
            block(tok, EXT),
            block(tok, 128),
            block(tok, 128),
            block(size * slot_count, ROW),
        ],
        compiler_params=alone,
        name="rows",
    )(
        mine_info,
        lengths,
        *in_hbm(kv_latent.T, latent_gain[None, :], page_ranks.T, frequency),
    )

    queries = pl.pallas_call(
        query_kernel,
        out_shape=[shape((tok, h * (NOPE + ROPE))) for h in CHUNK_HEADS] * QUAD,
        grid=(1,),
        in_specs=[smem, block(*q_heads.shape), block(tok, 128), block(tok, 128)],
        out_specs=[block(tok, h * (NOPE + ROPE)) for h in CHUNK_HEADS] * QUAD,
        compiler_params=params,
        cost_estimate=pl.CostEstimate(
            flops=0, bytes_accessed=4 * q_heads.size, transcendentals=0
        ),
        name="queries",
    )(quarter_info, *in_hbm(q_heads, tie(cosine, pair_rows if outer else got), sine))

    phases = Phases()
    line = [pair_rows] if outer else []
    side = []
    half = width // CHUNKS
    halves = []
    moved = [[queries[j]] + [None] * (QUAD - 1) for j in range(CHUNKS)]
    held = outgoing.reshape(1, size, slot_count, ROW)
    exchanged = []
    parts = {"r": tie(rows, pair_rows if outer else got)}
    for name in [name for phase in PHASES for name in phase + ("|",)]:
        kind, late = name[0], name[-1]
        if kind == "|":
            phases.now.append(queries[0])
            phases.turn()
        elif kind == "z" and outer:
            line.append(phases.send(late, around, line[-1], 4))
        elif kind == "y" and outer:
            step = int(name[1])
            if step < outer - 1:
                side.append(phases.send(late, inner_swap, line[step]))
            else:
                halves.append(phases.send(late, inner_swap, line[step][:, :half]))
        elif kind == "w" and outer:
            halves.append(phases.send(late, around, side[-1][:, half:], 4))
        elif kind == "k":
            swapped = phases.send(late, quad_swap, parts["r"], 2)
            both_groups = jnp.concatenate([parts["r"], swapped], axis=0)
        elif kind == "b":
            behind = phases.send(late, from_behind, both_groups, 2, False)
        elif kind == "f":
            far_behind = phases.send(late, from_behind, both_groups, 4, True)
        elif kind == "p":
            own_rows = jnp.concatenate([both_groups, behind, far_behind], axis=0)
            other_rows = phases.send(late, quad_swap, own_rows, 1)
        elif kind == "e" and outer:
            half_of = held.shape[1] // 2
            distance = 1 << len(exchanged)
            exchanged.append(phases.send(late, pair_swap, held[:, half_of:], distance))
            held = jnp.concatenate([held[:, :half_of], exchanged[-1]], axis=0)
        elif kind == "q":
            j, r = int(name[1]), int(name[2])
            moved[j][r] = phases.send(late, quad_swap, queries[r * CHUNKS + j], r)

    def weights_for(j):
        if not outer:
            return [(gathered, FIRST_HEAD[j] // 2)]
        return [(piece, FIRST_HEAD[j] // 2) for piece in line + side] + [(halves[j], 0)]

    window = (REACH + 2) * tok
    resident = pl.BlockSpec(memory_space=VMEM)
    keys = pl.pallas_call(
        keys_kernel,
        out_shape=(
            shape((2, window, LAT)),
            shape((2, window, 128)),
            shape((2, window, 128)),
            shape((2, 2 * tok, window), jnp.float32),
        ),
        in_specs=[smem, resident, resident],
        out_specs=[resident] * 4,
        compiler_params=params,
        cost_estimate=pl.CostEstimate(flops=0, bytes_accessed=8 << 20, transcendentals=0),
        name="keys",
    )(mine_info, own_rows, other_rows)

    def attend(j, first, steps):
        heads = 2 * steps
        pieces_of_weight = [piece for piece, begin in weights_for(j)]
        flops = 2 * heads * 2 * (window * LAT * 256 + 2 * tok * window * (NOPE + ROPE + VDIM))
        return pl.pallas_call(
            functools.partial(attend_kernel, outer),
            grid=(steps,),
            out_shape=[shape((tok, heads * VDIM))] * QUAD,
            in_specs=[smem] + [resident] * 4
            + [
                pl.BlockSpec((piece.shape[0], 512), lambda i, begin=begin: (0, begin + first + i))
                for piece, begin in weights_for(j)
            ]
            + [pl.BlockSpec((tok, 256), lambda i: (0, first + i))] * QUAD
            + [pl.BlockSpec((tok, 128), lambda i: (0, CHUNK_HEADS[j] + first + i))] * QUAD,
            out_specs=[pl.BlockSpec((tok, 256), lambda i: (0, i))] * QUAD,
            scratch_shapes=[VMEM((LAT, 512), jnp.bfloat16)],
            compiler_params=params,
            cost_estimate=pl.CostEstimate(
                flops=flops,
                bytes_accessed=heads << 20,
                transcendentals=heads * 4 * tok * window,
            ),
            name="attend",
        )(mine_info, *keys, *pieces_of_weight, *moved[j], *moved[j])

    results = []
    for call in CALLS:
        last = len(results) + 1 == len(CALLS)
        mine_info = tie(mine_info, *(results[0][2:3] + exchanged[3:] if last else exchanged[2:3]))
        pieces = attend(*call)
        mine_info = tie(mine_info, pieces[0])
        before = results[-1][2:] if last else []
        results.append(
            [pieces[0], quad_swap(tie(pieces[1], *before), 1)]
            + [quad_swap(pieces[r], r) for r in (2, 3)]
        )
    pieces = [one[r] for r in range(QUAD) for one in results]
    if outer:
        decode_cache = pl.pallas_call(
            sort_kernel,
            out_shape=shape((size * slot_count, ROW)),
            in_specs=[smem, anywhere],
            out_specs=anywhere,
            scratch_shapes=[pltpu.SemaphoreType.DMA((size,))],
            compiler_params=params,
            name="sort",
        )(mine_info, held.reshape(size, slot_count, ROW))
    else:
        outgoing = tie(outgoing, results[-1][0]).reshape(size, slot_count, ROW)
        arrived = lax.all_to_all(outgoing, "ctx", split_axis=0, concat_axis=0, tiled=True)
        decode_cache = arrived.reshape(size * slot_count, ROW)
    attn_out = pl.pallas_call(
        gather_kernel,
        out_shape=shape((tok, H * VDIM)),
        in_specs=[smem] + [anywhere] * len(pieces),
        out_specs=anywhere,
        scratch_shapes=[pltpu.SemaphoreType.DMA((len(pieces),))],
        compiler_params=params,
        name="place",
    )(quarter_info, *pieces)
    return (attn_out, decode_cache)


def solution(mesh):
    return jax.shard_map(
        body,
        mesh=mesh,
        in_specs=(
            P(("groups", "ctx"), None),
            P(("groups", "ctx"), None),
            P(),
            P("ctx", None),
            P(("groups", "ctx"), None),
            P("groups"),
        ),
        out_specs=(P(("groups", "ctx"), None), P(("groups", "ctx"), None)),
        check_vma=False,
    )
```

```python
import functools
import math

import jax
import jax.numpy as jnp
import numpy as np
from jax import lax
from jax.experimental import pallas as pl
from jax.experimental.pallas import tpu as pltpu
from jax.sharding import PartitionSpec as P

H = 64
NOPE = 128
ROPE = 64
VDIM = 128
LAT = 512
REACH = 3
QUAD = 4
HQ = H // QUAD
CHUNK_HEADS = (8, 8)
PHASES = (
    ("z", "y0", "k", "q02", "b~", "f~"),
    ("z", "y1", "q03", "q01", "e-"),
    ("z", "y2", "p", "q12"),
    ("y3", "w", "q13~", "q11", "e-", "e-", "e-"),
)
CHUNKS = len(CHUNK_HEADS)
FIRST_HEAD = tuple(sum(CHUNK_HEADS[:j]) for j in range(CHUNKS))
ROW = LAT + ROPE
EXT = 640
VMEM_LIMIT = 20 * 1024 * 1024
CALLS = ((0, 0, 4), (1, 0, 2), (1, 2, 2))
SMEM = pltpu.SMEM
VMEM = pltpu.VMEM


def rows_kernel(
    slot_count,
    relative,
    info,
    lengths,
    kv,
    gain,
    ranks,
    freq,
    rows_out,
    cos_out,
    sin_out,
    outgoing_out,
):
    tok = kv.shape[1]
    base = info[0] * tok
    spots = base + lax.broadcasted_iota(jnp.int32, (tok, 128), 0)
    lane = lax.broadcasted_iota(jnp.int32, (tok, 128), 1)
    begin = jnp.int32(0)
    own_start = jnp.zeros((tok, 128), jnp.int32)
    for r in range(lengths.shape[0]):
        own_start = jnp.where(spots >= begin, begin, own_start)
        begin = begin + lengths[r]
    offset = spots - own_start
    angles = offset.astype(jnp.float32) * freq[...]
    cosine = jnp.cos(angles)
    sine = jnp.where((lane & 32) == 0, -jnp.sin(angles), jnp.sin(angles))
    cos_out[...] = cosine
    sin_out[...] = sine
    raw = kv[...].astype(jnp.float32).T
    latent = raw[:, :LAT]
    mean = jnp.sum(latent * latent, axis=1, keepdims=True) * (1.0 / LAT)
    latent = latent * lax.rsqrt(mean + 1e-06) * gain[...]
    key = raw[:, LAT:]
    swapped = jnp.concatenate([key[:, ROPE // 2 :], key[:, : ROPE // 2]], axis=1)
    turned = key * cosine[:, :ROPE] + swapped * sine[:, :ROPE]
    high = (offset >> 8).astype(jnp.float32)
    low = (offset & 255).astype(jnp.float32)
    meta = jnp.where(lane == 0, high, jnp.where(lane == 1, low, 0.0))
    tail = jnp.concatenate([turned, meta[:, :ROPE]], axis=1)
    rows_out[:, :LAT] = latent.astype(jnp.bfloat16)
    rows_out[:, LAT:] = tail.astype(jnp.bfloat16)

    block = ranks[...]
    if relative:
        away = block ^ info[0]
        block = ((away & 1) << 3) | ((away & 2) << 1) | ((away & 4) >> 1) | (away >> 3)
    rank_row = jnp.broadcast_to(block, (tok, tok)).astype(jnp.float32)
    rank_col = rank_row.T
    earlier = lax.broadcasted_iota(jnp.int32, (tok, tok), 0) < lax.broadcasted_iota(
        jnp.int32, (tok, tok), 1
    )
    same = jnp.where((rank_col == rank_row) & earlier, 1.0, 0.0)
    slot = jnp.sum(same, axis=0, keepdims=True)
    target = (rank_row[:1] * slot_count + slot).astype(jnp.int32)
    spots_out = lax.broadcasted_iota(jnp.int32, (outgoing_out.shape[0], tok), 0)
    selector = jnp.where(spots_out == target, 1.0, 0.0).astype(jnp.bfloat16)
    picked = jnp.dot(selector, rows_out[:, :ROW], preferred_element_type=jnp.float32)
    outgoing_out[...] = picked.astype(jnp.bfloat16)


def query_kernel(info, query, cosine, sine, *outs):
    tok = query.shape[0]
    lane = lax.broadcasted_iota(jnp.int32, (tok, 128), 1)
    low_half = lane < 64
    first_quarter = (lane & 32) == 0
    cos_table = cosine[...]
    sin_table = sine[...]
    for r in range(QUAD):
        first = (info[0] ^ r) * (HQ * (NOPE + ROPE))
        for pair in range(HQ // 2):
            j = max(j for j in range(CHUNKS) if FIRST_HEAD[j] <= 2 * pair)
            out = outs[r * CHUNKS + j]
            at = pair - FIRST_HEAD[j] // 2
            rope_at = CHUNK_HEADS[j] * NOPE + at * 128
            begin = pl.multiple_of(first + pair * 2 * (NOPE + ROPE), 128)
            both = query[:, pl.ds(begin, 2 * (NOPE + ROPE))]
            mid = both[:, 128:256].astype(jnp.float32)
            end = both[:, 256:384].astype(jnp.float32)
            turned = jnp.where(low_half, mid, end)
            odd_nope = pltpu.roll(jnp.where(low_half, end, mid), 64, 1)
            swapped = jnp.where(
                first_quarter, pltpu.roll(turned, 96, 1), pltpu.roll(turned, 32, 1)
            )
            turned = turned * cos_table + swapped * sin_table
            out[:, at * 256 : at * 256 + 128] = both[:, :128]
            out[:, at * 256 + 128 : at * 256 + 256] = odd_nope.astype(jnp.bfloat16)
            out[:, rope_at : rope_at + 128] = turned.astype(jnp.bfloat16)


def pair_kernel(info, w_up, got, out, sem):
    rows, width = got.shape
    begin = pl.multiple_of(info[0] * width, 128)
    copies = [
        pltpu.make_async_copy(w_up.at[:, pl.ds(begin, width)], out.at[pl.ds(0, rows)], sem.at[0]),
        pltpu.make_async_copy(got, out.at[pl.ds(rows, rows)], sem.at[1]),
    ]
    for copy in copies:
        copy.start()
    for copy in copies:
        copy.wait()


def keys_kernel(info, own, other, latent, rope_even, rope_odd, bias):
    tok = own.shape[0] // 6
    mine = info[0]
    partner = mine ^ 1
    has_last = (mine & 1) == 1
    starts = [mine, partner, mine - 2, partner - 2, (mine >> 1) * 2 - 3]
    blank = jnp.zeros((tok, ROPE), jnp.bfloat16)
    lane = lax.broadcasted_iota(jnp.int32, (tok, tok), 1)
    row = lax.broadcasted_iota(jnp.int32, (tok, tok), 0)
    for g in range(2):
        mine_of, other_of = [
            [ref[(2 * n + g) * tok : (2 * n + g + 1) * tok] for n in range(3)]
            for ref in (own, other)
        ]
        pieces = [
            mine_of[0],
            other_of[0],
            mine_of[1],
            other_of[1],
            jnp.where(has_last, mine_of[2], other_of[2]),
        ]
        for b, piece in enumerate(pieces):
            here = slice(b * tok, (b + 1) * tok)
            latent[g, here] = piece[:, :LAT]
            turned = piece[:, LAT : LAT + ROPE]
            rope_even[g, here] = jnp.concatenate([turned, blank], axis=1)
            rope_odd[g, here] = jnp.concatenate([blank, turned], axis=1)
        for half in range(2):
            meta = pieces[half][:, LAT:].astype(jnp.float32)
            offset = (meta[:, ROPE : ROPE + 1] * 256.0 + meta[:, ROPE + 1 : ROPE + 2]).astype(
                jnp.int32
            )
            spots = starts[half] * tok + row
            lowest = jnp.maximum(spots - offset, (starts[half] - REACH) * tok)
            for b in range(REACH + 2):
                keys = starts[b] * tok + lane
                allowed = (keys >= lowest) & (keys <= spots)
                bias[g, half * tok : (half + 1) * tok, b * tok : (b + 1) * tok] = jnp.where(
                    allowed, 0.0, -1e30
                )


def attend_kernel(outer, info, latent, rope_even, rope_odd, bias, *refs):
    pieces_count = 2 * outer if outer else 1
    pieces_of_weight, refs = refs[:pieces_count], refs[pieces_count:]
    nope = refs[0:QUAD]
    rope = refs[QUAD : 2 * QUAD]
    outs = refs[2 * QUAD : 3 * QUAD]
    held = refs[3 * QUAD]
    tok = nope[0].shape[0]
    mine = info[0]
    scale = (NOPE + ROPE) ** (-0.5) * math.log2(math.e)

    if outer:
        weight = held
        for i, piece in enumerate(pieces_of_weight):
            side, behind = i // outer, i % outer
            chip = ((mine >> 2) + outer - behind) % outer * 2 + (((mine >> 1) & 1) ^ side)
            rows = piece.shape[0] // 2
            for core in range(2):
                begin = pl.multiple_of(chip * 2 * rows + ((mine & 1) ^ core) * rows, rows)
                held[pl.ds(begin, rows)] = piece[core * rows : (core + 1) * rows]
    else:
        weight = pieces_of_weight[0]

    def expand(g):
        wide = jnp.dot(latent[g], weight[...], preferred_element_type=jnp.float32)
        return wide.astype(jnp.bfloat16)

    def score(g, b, expanded):
        at = slice(b * 128, (b + 1) * 128)
        key_rope = (rope_even, rope_odd)[b][g]
        key = jnp.concatenate([expanded[:, b * 256 : b * 256 + 128], key_rope], axis=1)
        query = jnp.concatenate(
            [
                jnp.concatenate([nope[2 * g][:, at], rope[2 * g][...]], axis=1),
                jnp.concatenate([nope[2 * g + 1][:, at], rope[2 * g + 1][...]], axis=1),
            ],
            axis=0,
        )
        return lax.dot_general(
            query, key, (((1,), (1,)), ((), ())), preferred_element_type=jnp.float32
        )

    def weigh(g, scores):
        scores = scores * scale + bias[g]
        largest = jnp.max(scores, axis=1, keepdims=True)
        expo = jnp.exp2(scores - largest)
        return expo.astype(jnp.bfloat16), jnp.sum(expo, axis=1, keepdims=True)

    def mix(g, b, expanded, weights, total):
        at = slice(b * 128, (b + 1) * 128)
        value = expanded[:, b * 256 + 128 : b * 256 + 256]
        mixed = jnp.dot(weights, value, preferred_element_type=jnp.float32)
        mixed = (mixed / total).astype(jnp.bfloat16)
        outs[2 * g][:, at] = mixed[:tok]
        outs[2 * g + 1][:, at] = mixed[tok:]

    first = expand(0)
    scores = score(0, 0, first)
    second = expand(1)
    weighed = weigh(0, scores)
    scores = score(0, 1, first)
    mix(0, 0, first, *weighed)
    weighed = weigh(0, scores)
    scores = score(1, 0, second)
    mix(0, 1, first, *weighed)
    weighed = weigh(1, scores)
    scores = score(1, 1, second)
    mix(1, 0, second, *weighed)
    weighed = weigh(1, scores)
    mix(1, 1, second, *weighed)


def sort_kernel(info, relative, out, sem):
    rows = relative.shape[1]
    copies = []
    for d in range(relative.shape[0]):
        begin = pl.multiple_of((info[0] ^ d) * rows, rows)
        copies.append(
            pltpu.make_async_copy(relative.at[d], out.at[pl.ds(begin, rows)], sem.at[d])
        )
    for copy in copies:
        copy.start()
    for copy in copies:
        copy.wait()


def gather_kernel(info, *refs):
    pieces, out, sems = refs[:-2], refs[-2], refs[-1]
    copies = []
    for i, piece in enumerate(pieces):
        r, (j, first, steps) = i // len(CALLS), CALLS[i % len(CALLS)]
        begin = ((info[0] ^ r) * HQ + FIRST_HEAD[j] + 2 * first) * VDIM
        begin = pl.multiple_of(begin, 128)
        copies.append(
            pltpu.make_async_copy(piece, out.at[:, pl.ds(begin, piece.shape[1])], sems.at[i])
        )
    for copy in copies:
        copy.start()
    for copy in copies:
        copy.wait()


def tie(array, *others):
    return lax.optimization_barrier((array,) + others)[0]


class Phases:
    def __init__(self):
        self.before, self.before_late, self.now, self.late = [], [], [], []

    def turn(self):
        self.before = self.now + self.before_late
        self.before_late, self.now, self.late = self.late, [], []

    def send(self, late, permute, array, *args):
        arrived = permute(tie(array, *self.before) if self.before else array, *args)
        if late != "-":
            (self.late if late == "~" else self.now).append(arrived)
        return arrived


def shape(dims, kind=jnp.bfloat16):
    return jax.ShapeDtypeStruct(dims, kind)


def in_hbm(*arrays):
    return [pltpu.with_memory_space_constraint(array, pltpu.HBM) for array in arrays]


def body(q_heads, kv_latent, latent_gain, w_up, page_ranks, lengths):
    tok = q_heads.shape[0]
    size = lax.axis_size("ctx")
    groups = lax.axis_size("groups")
    mine = lax.axis_index("ctx")
    quarter = lax.axis_index("groups") * 2 + mine % 2
    slot_count = max(2, 2 * tok // size)
    smem = pl.BlockSpec(memory_space=SMEM)
    params = pltpu.CompilerParams(vmem_limit_bytes=VMEM_LIMIT)
    alone = pltpu.CompilerParams(vmem_limit_bytes=3 * VMEM_LIMIT)

    def quad_swap(array, r):
        dx, dc = r // 2, r % 2
        pairs = [
            (g * size + i, (g ^ dx) * size + (i ^ dc)) for g in range(groups) for i in range(size)
        ]
        return lax.ppermute(array, ("groups", "ctx"), pairs)

    def around(array, by):
        return lax.ppermute(array, "ctx", [(i, (i + by) % size) for i in range(size)])

    def inner_swap(array):
        return lax.ppermute(array, "ctx", [(i, i ^ 2) for i in range(size)])

    def pair_swap(array, distance):
        return lax.ppermute(array, "ctx", [(i, i ^ distance) for i in range(size)])

    def from_behind(array, by, odd_only):
        first = 1 if odd_only else 0
        step = 2 if odd_only else 1
        pairs = [(i, i + by) for i in range(first, size - by, step)]
        return lax.ppermute(array, "ctx", pairs)

    width = HQ * (NOPE + VDIM)
    quarter_info = quarter[None].astype(jnp.int32)
    anywhere = pl.BlockSpec(memory_space=pl.ANY)
    give = lax.dynamic_slice_in_dim(w_up, (quarter ^ 1) * width, width, 1)
    give, lengths = lax.optimization_barrier((give, lengths))
    got = quad_swap(give, 1)
    outer = 4 if size == 16 else 0
    if outer:
        pair_rows = pl.pallas_call(
            pair_kernel,
            out_shape=shape((2 * w_up.shape[0], width)),
            in_specs=[smem, pl.BlockSpec(memory_space=pltpu.HBM), anywhere],
            out_specs=anywhere,
            scratch_shapes=[pltpu.SemaphoreType.DMA((2,))],
            compiler_params=params,
            name="pair",
        )(quarter_info, *in_hbm(w_up), got)
    else:
        keep = lax.dynamic_slice_in_dim(w_up, quarter * width, width, 1)
        even = mine % 2 == 0
        both = jnp.concatenate(
            [jnp.where(even, keep, got), jnp.where(even, got, keep)], axis=0
        )
        same_core = [list(range(c, size, 2)) for c in range(2)]
        gathered = lax.all_gather(both, "ctx", axis=0, tiled=True, axis_index_groups=same_core)

    frequency = np.exp(-np.arange(ROPE // 2) * (2.0 * math.log(10000.0) / ROPE))
    frequency = jnp.asarray(np.tile(frequency, 4)[None, :], jnp.float32)
    mine_info = mine[None].astype(jnp.int32)

    def block(*dims):
        return pl.BlockSpec(dims, lambda i: (0,) * len(dims))

    rows, cosine, sine, outgoing = pl.pallas_call(
        functools.partial(rows_kernel, slot_count, outer > 0),
        grid=(1,),
        out_shape=(
            shape((tok, EXT)),
            shape((tok, 128), jnp.float32),
            shape((tok, 128), jnp.float32),
            shape((size * slot_count, ROW)),
        ),
        in_specs=[smem, smem, block(ROW, tok), block(1, LAT), block(1, tok), block(1, 128)],
        out_specs=[
            block(tok, EXT),
            block(tok, 128),
            block(tok, 128),
            block(size * slot_count, ROW),
        ],
        compiler_params=alone,
        name="rows",
    )(
        mine_info,
        lengths,
        *in_hbm(kv_latent.T, latent_gain[None, :], page_ranks.T, frequency),
    )

    queries = pl.pallas_call(
        query_kernel,
        out_shape=[shape((tok, h * (NOPE + ROPE))) for h in CHUNK_HEADS] * QUAD,
        grid=(1,),
        in_specs=[smem, block(*q_heads.shape), block(tok, 128), block(tok, 128)],
        out_specs=[block(tok, h * (NOPE + ROPE)) for h in CHUNK_HEADS] * QUAD,
        compiler_params=params,
        cost_estimate=pl.CostEstimate(
            flops=0, bytes_accessed=4 * q_heads.size, transcendentals=0
        ),
        name="queries",
    )(quarter_info, *in_hbm(q_heads, tie(cosine, pair_rows if outer else got), sine))

    phases = Phases()
    line = [pair_rows] if outer else []
    side = []
    half = width // CHUNKS
    halves = []
    moved = [[queries[j]] + [None] * (QUAD - 1) for j in range(CHUNKS)]
    held = outgoing.reshape(1, size, slot_count, ROW)
    exchanged = []
    parts = {"r": tie(rows, pair_rows if outer else got)}
    for name in [name for phase in PHASES for name in phase + ("|",)]:
        kind, late = name[0], name[-1]
        if kind == "|":
            phases.now.append(queries[0])
            phases.turn()
        elif kind == "z" and outer:
            line.append(phases.send(late, around, line[-1], 4))
        elif kind == "y" and outer:
            step = int(name[1])
            if step < outer - 1:
                side.append(phases.send(late, inner_swap, line[step]))
            else:
                halves.append(phases.send(late, inner_swap, line[step][:, :half]))
        elif kind == "w" and outer:
            halves.append(phases.send(late, around, side[-1][:, half:], 4))
        elif kind == "k":
            swapped = phases.send(late, quad_swap, parts["r"], 2)
            both_groups = jnp.concatenate([parts["r"], swapped], axis=0)
        elif kind == "b":
            behind = phases.send(late, from_behind, both_groups, 2, False)
        elif kind == "f":
            far_behind = phases.send(late, from_behind, both_groups, 4, True)
        elif kind == "p":
            own_rows = jnp.concatenate([both_groups, behind, far_behind], axis=0)
            other_rows = phases.send(late, quad_swap, own_rows, 1)
        elif kind == "e" and outer:
            half_of = held.shape[1] // 2
            distance = 1 << len(exchanged)
            exchanged.append(phases.send(late, pair_swap, held[:, half_of:], distance))
            held = jnp.concatenate([held[:, :half_of], exchanged[-1]], axis=0)
        elif kind == "q":
            j, r = int(name[1]), int(name[2])
            moved[j][r] = phases.send(late, quad_swap, queries[r * CHUNKS + j], r)

    def weights_for(j):
        if not outer:
            return [(gathered, FIRST_HEAD[j] // 2)]
        return [(piece, FIRST_HEAD[j] // 2) for piece in line + side] + [(halves[j], 0)]

    window = (REACH + 2) * tok
    resident = pl.BlockSpec(memory_space=VMEM)
    keys = pl.pallas_call(
        keys_kernel,
        out_shape=(
            shape((2, window, LAT)),
            shape((2, window, 128)),
            shape((2, window, 128)),
            shape((2, 2 * tok, window), jnp.float32),
        ),
        in_specs=[smem, resident, resident],
        out_specs=[resident] * 4,
        compiler_params=params,
        cost_estimate=pl.CostEstimate(flops=0, bytes_accessed=8 << 20, transcendentals=0),
        name="keys",
    )(mine_info, own_rows, other_rows)

    def attend(j, first, steps):
        heads = 2 * steps
        pieces_of_weight = [piece for piece, begin in weights_for(j)]
        flops = 2 * heads * 2 * (window * LAT * 256 + 2 * tok * window * (NOPE + ROPE + VDIM))
        return pl.pallas_call(
            functools.partial(attend_kernel, outer),
            grid=(steps,),
            out_shape=[shape((tok, heads * VDIM))] * QUAD,
            in_specs=[smem] + [resident] * 4
            + [
                pl.BlockSpec((piece.shape[0], 512), lambda i, begin=begin: (0, begin + first + i))
                for piece, begin in weights_for(j)
            ]
            + [pl.BlockSpec((tok, 256), lambda i: (0, first + i))] * QUAD
            + [pl.BlockSpec((tok, 128), lambda i: (0, CHUNK_HEADS[j] + first + i))] * QUAD,
            out_specs=[pl.BlockSpec((tok, 256), lambda i: (0, i))] * QUAD,
            scratch_shapes=[VMEM((LAT, 512), jnp.bfloat16)],
            compiler_params=params,
            cost_estimate=pl.CostEstimate(
                flops=flops,
                bytes_accessed=heads << 20,
                transcendentals=heads * 4 * tok * window,
            ),
            name="attend",
        )(mine_info, *keys, *pieces_of_weight, *moved[j], *moved[j])

    results = []
    for call in CALLS:
        last = len(results) + 1 == len(CALLS)
        mine_info = tie(mine_info, *exchanged[len(results) : len(results) + 1])
        mine_info = tie(mine_info, *(results[0][2:3] if last else []))
        pieces = attend(*call)
        mine_info = tie(mine_info, pieces[0])
        before = results[-1][2:] if last else []
        results.append(
            [pieces[0], quad_swap(tie(pieces[1], *before), 1)]
            + [quad_swap(pieces[r], r) for r in (2, 3)]
        )
    pieces = [one[r] for r in range(QUAD) for one in results]
    if outer:
        decode_cache = pl.pallas_call(
            sort_kernel,
            out_shape=shape((size * slot_count, ROW)),
            in_specs=[smem, anywhere],
            out_specs=anywhere,
            scratch_shapes=[pltpu.SemaphoreType.DMA((size,))],
            compiler_params=params,
            name="sort",
        )(mine_info, held.reshape(size, slot_count, ROW))
    else:
        outgoing = tie(outgoing, results[-1][0]).reshape(size, slot_count, ROW)
        arrived = lax.all_to_all(outgoing, "ctx", split_axis=0, concat_axis=0, tiled=True)
        decode_cache = arrived.reshape(size * slot_count, ROW)
    attn_out = pl.pallas_call(
        gather_kernel,
        out_shape=shape((tok, H * VDIM)),
        in_specs=[smem] + [anywhere] * len(pieces),
        out_specs=anywhere,
        scratch_shapes=[pltpu.SemaphoreType.DMA((len(pieces),))],
        compiler_params=params,
        name="place",
    )(quarter_info, *pieces)
    return (attn_out, decode_cache)


def solution(mesh):
    return jax.shard_map(
        body,
        mesh=mesh,
        in_specs=(
            P(("groups", "ctx"), None),
            P(("groups", "ctx"), None),
            P(),
            P("ctx", None),
            P(("groups", "ctx"), None),
            P("groups"),
        ),
        out_specs=(P(("groups", "ctx"), None), P(("groups", "ctx"), None)),
        check_vma=False,
    )
```

```python
import functools
import math

import jax
import jax.numpy as jnp
import numpy as np
from jax import lax
from jax.experimental import pallas as pl
from jax.experimental.pallas import tpu as pltpu
from jax.sharding import PartitionSpec as P

H = 64
NOPE = 128
ROPE = 64
VDIM = 128
LAT = 512
REACH = 3
QUAD = 4
HQ = H // QUAD
CHUNK_HEADS = (8, 8)
PHASES = (
    ("z", "y0", "k", "q02", "b~", "f~"),
    ("z", "y1", "q03", "q01"),
    ("z", "y2", "p", "q12"),
    ("y3", "w", "q13~", "q11"),
)
CHUNKS = len(CHUNK_HEADS)
FIRST_HEAD = tuple(sum(CHUNK_HEADS[:j]) for j in range(CHUNKS))
ROW = LAT + ROPE
EXT = 640
VMEM_LIMIT = 20 * 1024 * 1024
CALLS = ((0, 0, 2), (0, 2, 2), (1, 0, 2), (1, 2, 2))
SMEM = pltpu.SMEM
VMEM = pltpu.VMEM


def rows_kernel(
    slot_count,
    relative,
    info,
    lengths,
    kv,
    gain,
    ranks,
    freq,
    rows_out,
    cos_out,
    sin_out,
    outgoing_out,
):
    tok = kv.shape[1]
    base = info[0] * tok
    spots = base + lax.broadcasted_iota(jnp.int32, (tok, 128), 0)
    lane = lax.broadcasted_iota(jnp.int32, (tok, 128), 1)
    begin = jnp.int32(0)
    own_start = jnp.zeros((tok, 128), jnp.int32)
    for r in range(lengths.shape[0]):
        own_start = jnp.where(spots >= begin, begin, own_start)
        begin = begin + lengths[r]
    offset = spots - own_start
    angles = offset.astype(jnp.float32) * freq[...]
    cosine = jnp.cos(angles)
    sine = jnp.where((lane & 32) == 0, -jnp.sin(angles), jnp.sin(angles))
    cos_out[...] = cosine
    sin_out[...] = sine
    raw = kv[...].astype(jnp.float32).T
    latent = raw[:, :LAT]
    mean = jnp.sum(latent * latent, axis=1, keepdims=True) * (1.0 / LAT)
    latent = latent * lax.rsqrt(mean + 1e-06) * gain[...]
    key = raw[:, LAT:]
    swapped = jnp.concatenate([key[:, ROPE // 2 :], key[:, : ROPE // 2]], axis=1)
    turned = key * cosine[:, :ROPE] + swapped * sine[:, :ROPE]
    high = (offset >> 8).astype(jnp.float32)
    low = (offset & 255).astype(jnp.float32)
    meta = jnp.where(lane == 0, high, jnp.where(lane == 1, low, 0.0))
    tail = jnp.concatenate([turned, meta[:, :ROPE]], axis=1)
    rows_out[:, :LAT] = latent.astype(jnp.bfloat16)
    rows_out[:, LAT:] = tail.astype(jnp.bfloat16)

    block = ranks[...]
    if relative:
        away = block ^ info[0]
        block = ((away & 1) << 3) | ((away & 2) << 1) | ((away & 4) >> 1) | (away >> 3)
    rank_row = jnp.broadcast_to(block, (tok, tok)).astype(jnp.float32)
    rank_col = rank_row.T
    earlier = lax.broadcasted_iota(jnp.int32, (tok, tok), 0) < lax.broadcasted_iota(
        jnp.int32, (tok, tok), 1
    )
    same = jnp.where((rank_col == rank_row) & earlier, 1.0, 0.0)
    slot = jnp.sum(same, axis=0, keepdims=True)
    target = (rank_row[:1] * slot_count + slot).astype(jnp.int32)
    spots_out = lax.broadcasted_iota(jnp.int32, (outgoing_out.shape[0], tok), 0)
    selector = jnp.where(spots_out == target, 1.0, 0.0).astype(jnp.bfloat16)
    picked = jnp.dot(selector, rows_out[:, :ROW], preferred_element_type=jnp.float32)
    outgoing_out[...] = picked.astype(jnp.bfloat16)


def query_kernel(info, query, cosine, sine, *outs):
    tok = query.shape[0]
    lane = lax.broadcasted_iota(jnp.int32, (tok, 128), 1)
    low_half = lane < 64
    first_quarter = (lane & 32) == 0
    cos_table = cosine[...]
    sin_table = sine[...]
    for r in range(QUAD):
        first = (info[0] ^ r) * (HQ * (NOPE + ROPE))
        for pair in range(HQ // 2):
            j = max(j for j in range(CHUNKS) if FIRST_HEAD[j] <= 2 * pair)
            out = outs[r * CHUNKS + j]
            at = pair - FIRST_HEAD[j] // 2
            rope_at = CHUNK_HEADS[j] * NOPE + at * 128
            begin = pl.multiple_of(first + pair * 2 * (NOPE + ROPE), 128)
            both = query[:, pl.ds(begin, 2 * (NOPE + ROPE))]
            mid = both[:, 128:256].astype(jnp.float32)
            end = both[:, 256:384].astype(jnp.float32)
            turned = jnp.where(low_half, mid, end)
            odd_nope = pltpu.roll(jnp.where(low_half, end, mid), 64, 1)
            swapped = jnp.where(
                first_quarter, pltpu.roll(turned, 96, 1), pltpu.roll(turned, 32, 1)
            )
            turned = turned * cos_table + swapped * sin_table
            out[:, at * 256 : at * 256 + 128] = both[:, :128]
            out[:, at * 256 + 128 : at * 256 + 256] = odd_nope.astype(jnp.bfloat16)
            out[:, rope_at : rope_at + 128] = turned.astype(jnp.bfloat16)


def pair_kernel(info, w_up, got, out, sem):
    rows, width = got.shape
    begin = pl.multiple_of(info[0] * width, 128)
    copies = [
        pltpu.make_async_copy(w_up.at[:, pl.ds(begin, width)], out.at[pl.ds(0, rows)], sem.at[0]),
        pltpu.make_async_copy(got, out.at[pl.ds(rows, rows)], sem.at[1]),
    ]
    for copy in copies:
        copy.start()
    for copy in copies:
        copy.wait()


def keys_kernel(info, own, other, latent, rope_even, rope_odd, bias):
    tok = own.shape[0] // 6
    mine = info[0]
    partner = mine ^ 1
    has_last = (mine & 1) == 1
    starts = [mine, partner, mine - 2, partner - 2, (mine >> 1) * 2 - 3]
    blank = jnp.zeros((tok, ROPE), jnp.bfloat16)
    lane = lax.broadcasted_iota(jnp.int32, (tok, tok), 1)
    row = lax.broadcasted_iota(jnp.int32, (tok, tok), 0)
    for g in range(2):
        mine_of, other_of = [
            [ref[(2 * n + g) * tok : (2 * n + g + 1) * tok] for n in range(3)]
            for ref in (own, other)
        ]
        pieces = [
            mine_of[0],
            other_of[0],
            mine_of[1],
            other_of[1],
            jnp.where(has_last, mine_of[2], other_of[2]),
        ]
        for b, piece in enumerate(pieces):
            here = slice(b * tok, (b + 1) * tok)
            latent[g, here] = piece[:, :LAT]
            turned = piece[:, LAT : LAT + ROPE]
            rope_even[g, here] = jnp.concatenate([turned, blank], axis=1)
            rope_odd[g, here] = jnp.concatenate([blank, turned], axis=1)
        for half in range(2):
            meta = pieces[half][:, LAT:].astype(jnp.float32)
            offset = (meta[:, ROPE : ROPE + 1] * 256.0 + meta[:, ROPE + 1 : ROPE + 2]).astype(
                jnp.int32
            )
            spots = starts[half] * tok + row
            lowest = jnp.maximum(spots - offset, (starts[half] - REACH) * tok)
            for b in range(REACH + 2):
                keys = starts[b] * tok + lane
                allowed = (keys >= lowest) & (keys <= spots)
                bias[g, half * tok : (half + 1) * tok, b * tok : (b + 1) * tok] = jnp.where(
                    allowed, 0.0, -1e30
                )


def attend_kernel(outer, info, latent, rope_even, rope_odd, bias, *refs):
    pieces_count = 2 * outer if outer else 1
    pieces_of_weight, refs = refs[:pieces_count], refs[pieces_count:]
    nope = refs[0:QUAD]
    rope = refs[QUAD : 2 * QUAD]
    outs = refs[2 * QUAD : 3 * QUAD]
    held = refs[3 * QUAD]
    tok = nope[0].shape[0]
    mine = info[0]
    scale = (NOPE + ROPE) ** (-0.5) * math.log2(math.e)

    if outer:
        weight = held
        for i, piece in enumerate(pieces_of_weight):
            side, behind = i // outer, i % outer
            chip = ((mine >> 2) + outer - behind) % outer * 2 + (((mine >> 1) & 1) ^ side)
            rows = piece.shape[0] // 2
            for core in range(2):
                begin = pl.multiple_of(chip * 2 * rows + ((mine & 1) ^ core) * rows, rows)
                held[pl.ds(begin, rows)] = piece[core * rows : (core + 1) * rows]
    else:
        weight = pieces_of_weight[0]

    def expand(g):
        wide = jnp.dot(latent[g], weight[...], preferred_element_type=jnp.float32)
        return wide.astype(jnp.bfloat16)

    def score(g, b, expanded):
        at = slice(b * 128, (b + 1) * 128)
        key_rope = (rope_even, rope_odd)[b][g]
        key = jnp.concatenate([expanded[:, b * 256 : b * 256 + 128], key_rope], axis=1)
        query = jnp.concatenate(
            [
                jnp.concatenate([nope[2 * g][:, at], rope[2 * g][...]], axis=1),
                jnp.concatenate([nope[2 * g + 1][:, at], rope[2 * g + 1][...]], axis=1),
            ],
            axis=0,
        )
        return lax.dot_general(
            query, key, (((1,), (1,)), ((), ())), preferred_element_type=jnp.float32
        )

    def weigh(g, scores):
        scores = scores * scale + bias[g]
        largest = jnp.max(scores, axis=1, keepdims=True)
        expo = jnp.exp2(scores - largest)
        return expo.astype(jnp.bfloat16), jnp.sum(expo, axis=1, keepdims=True)

    def mix(g, b, expanded, weights, total):
        at = slice(b * 128, (b + 1) * 128)
        value = expanded[:, b * 256 + 128 : b * 256 + 256]
        mixed = jnp.dot(weights, value, preferred_element_type=jnp.float32)
        mixed = (mixed / total).astype(jnp.bfloat16)
        outs[2 * g][:, at] = mixed[:tok]
        outs[2 * g + 1][:, at] = mixed[tok:]

    first = expand(0)
    scores = score(0, 0, first)
    second = expand(1)
    weighed = weigh(0, scores)
    scores = score(0, 1, first)
    mix(0, 0, first, *weighed)
    weighed = weigh(0, scores)
    scores = score(1, 0, second)
    mix(0, 1, first, *weighed)
    weighed = weigh(1, scores)
    scores = score(1, 1, second)
    mix(1, 0, second, *weighed)
    weighed = weigh(1, scores)
    mix(1, 1, second, *weighed)


def sort_kernel(info, relative, out, sem):
    rows = relative.shape[1]
    copies = []
    for d in range(relative.shape[0]):
        begin = pl.multiple_of((info[0] ^ d) * rows, rows)
        copies.append(
            pltpu.make_async_copy(relative.at[d], out.at[pl.ds(begin, rows)], sem.at[d])
        )
    for copy in copies:
        copy.start()
    for copy in copies:
        copy.wait()


def gather_kernel(info, *refs):
    pieces, out, sems = refs[:-2], refs[-2], refs[-1]
    copies = []
    for i, piece in enumerate(pieces):
        r, (j, first, steps) = i // len(CALLS), CALLS[i % len(CALLS)]
        begin = ((info[0] ^ r) * HQ + FIRST_HEAD[j] + 2 * first) * VDIM
        begin = pl.multiple_of(begin, 128)
        copies.append(
            pltpu.make_async_copy(piece, out.at[:, pl.ds(begin, piece.shape[1])], sems.at[i])
        )
    for copy in copies:
        copy.start()
    for copy in copies:
        copy.wait()


def tie(array, *others):
    return lax.optimization_barrier((array,) + others)[0]


class Phases:
    def __init__(self):
        self.before, self.before_late, self.now, self.late = [], [], [], []

    def turn(self):
        self.before = self.now + self.before_late
        self.before_late, self.now, self.late = self.late, [], []

    def send(self, late, permute, array, *args):
        arrived = permute(tie(array, *self.before) if self.before else array, *args)
        if late != "-":
            (self.late if late == "~" else self.now).append(arrived)
        return arrived


def shape(dims, kind=jnp.bfloat16):
    return jax.ShapeDtypeStruct(dims, kind)


def in_hbm(*arrays):
    return [pltpu.with_memory_space_constraint(array, pltpu.HBM) for array in arrays]


def body(q_heads, kv_latent, latent_gain, w_up, page_ranks, lengths):
    tok = q_heads.shape[0]
    size = lax.axis_size("ctx")
    groups = lax.axis_size("groups")
    mine = lax.axis_index("ctx")
    quarter = lax.axis_index("groups") * 2 + mine % 2
    slot_count = max(2, 2 * tok // size)
    smem = pl.BlockSpec(memory_space=SMEM)
    params = pltpu.CompilerParams(vmem_limit_bytes=VMEM_LIMIT)
    alone = pltpu.CompilerParams(vmem_limit_bytes=3 * VMEM_LIMIT)

    def quad_swap(array, r):
        dx, dc = r // 2, r % 2
        pairs = [
            (g * size + i, (g ^ dx) * size + (i ^ dc)) for g in range(groups) for i in range(size)
        ]
        return lax.ppermute(array, ("groups", "ctx"), pairs)

    def around(array, by):
        return lax.ppermute(array, "ctx", [(i, (i + by) % size) for i in range(size)])

    def inner_swap(array):
        return lax.ppermute(array, "ctx", [(i, i ^ 2) for i in range(size)])

    def pair_swap(array, distance):
        return lax.ppermute(array, "ctx", [(i, i ^ distance) for i in range(size)])

    def from_behind(array, by, odd_only):
        first = 1 if odd_only else 0
        step = 2 if odd_only else 1
        pairs = [(i, i + by) for i in range(first, size - by, step)]
        return lax.ppermute(array, "ctx", pairs)

    width = HQ * (NOPE + VDIM)
    quarter_info = quarter[None].astype(jnp.int32)
    anywhere = pl.BlockSpec(memory_space=pl.ANY)
    give = lax.dynamic_slice_in_dim(w_up, (quarter ^ 1) * width, width, 1)
    give, lengths = lax.optimization_barrier((give, lengths))
    got = quad_swap(give, 1)
    outer = 4 if size == 16 else 0
    if outer:
        pair_rows = pl.pallas_call(
            pair_kernel,
            out_shape=shape((2 * w_up.shape[0], width)),
            in_specs=[smem, pl.BlockSpec(memory_space=pltpu.HBM), anywhere],
            out_specs=anywhere,
            scratch_shapes=[pltpu.SemaphoreType.DMA((2,))],
            compiler_params=params,
            name="pair",
        )(quarter_info, *in_hbm(w_up), got)
    else:
        keep = lax.dynamic_slice_in_dim(w_up, quarter * width, width, 1)
        even = mine % 2 == 0
        both = jnp.concatenate(
            [jnp.where(even, keep, got), jnp.where(even, got, keep)], axis=0
        )
        same_core = [list(range(c, size, 2)) for c in range(2)]
        gathered = lax.all_gather(both, "ctx", axis=0, tiled=True, axis_index_groups=same_core)

    frequency = np.exp(-np.arange(ROPE // 2) * (2.0 * math.log(10000.0) / ROPE))
    frequency = jnp.asarray(np.tile(frequency, 4)[None, :], jnp.float32)
    mine_info = mine[None].astype(jnp.int32)

    def block(*dims):
        return pl.BlockSpec(dims, lambda i: (0,) * len(dims))

    rows, cosine, sine, outgoing = pl.pallas_call(
        functools.partial(rows_kernel, slot_count, outer > 0),
        grid=(1,),
        out_shape=(
            shape((tok, EXT)),
            shape((tok, 128), jnp.float32),
            shape((tok, 128), jnp.float32),
            shape((size * slot_count, ROW)),
        ),
        in_specs=[smem, smem, block(ROW, tok), block(1, LAT), block(1, tok), block(1, 128)],
        out_specs=[
            block(tok, EXT),
            block(tok, 128),
            block(tok, 128),
            block(size * slot_count, ROW),
        ],
        compiler_params=alone,
        name="rows",
    )(
        mine_info,
        lengths,
        *in_hbm(kv_latent.T, latent_gain[None, :], page_ranks.T, frequency),
    )

    queries = pl.pallas_call(
        query_kernel,
        out_shape=[shape((tok, h * (NOPE + ROPE))) for h in CHUNK_HEADS] * QUAD,
        grid=(1,),
        in_specs=[smem, block(*q_heads.shape), block(tok, 128), block(tok, 128)],
        out_specs=[block(tok, h * (NOPE + ROPE)) for h in CHUNK_HEADS] * QUAD,
        compiler_params=params,
        cost_estimate=pl.CostEstimate(
            flops=0, bytes_accessed=4 * q_heads.size, transcendentals=0
        ),
        name="queries",
    )(quarter_info, *in_hbm(q_heads, tie(cosine, pair_rows if outer else got), sine))

    phases = Phases()
    line = [pair_rows] if outer else []
    side = []
    half = width // CHUNKS
    halves = []
    moved = [[queries[j]] + [None] * (QUAD - 1) for j in range(CHUNKS)]
    parts = {"r": tie(rows, pair_rows if outer else got)}
    for name in [name for phase in PHASES for name in phase + ("|",)]:
        kind, late = name[0], name[-1]
        if kind == "|":
            phases.now.append(queries[0])
            phases.turn()
        elif kind == "z" and outer:
            line.append(phases.send(late, around, line[-1], 4))
        elif kind == "y" and outer:
            step = int(name[1])
            if step < outer - 1:
                side.append(phases.send(late, inner_swap, line[step]))
            else:
                halves.append(phases.send(late, inner_swap, line[step][:, :half]))
        elif kind == "w" and outer:
            halves.append(phases.send(late, around, side[-1][:, half:], 4))
        elif kind == "k":
            swapped = phases.send(late, quad_swap, parts["r"], 2)
            both_groups = jnp.concatenate([parts["r"], swapped], axis=0)
        elif kind == "b":
            behind = phases.send(late, from_behind, both_groups, 2, False)
        elif kind == "f":
            far_behind = phases.send(late, from_behind, both_groups, 4, True)
        elif kind == "p":
            own_rows = jnp.concatenate([both_groups, behind, far_behind], axis=0)
            other_rows = phases.send(late, quad_swap, own_rows, 1)
        elif kind == "q":
            j, r = int(name[1]), int(name[2])
            moved[j][r] = phases.send(late, quad_swap, queries[r * CHUNKS + j], r)

    def weights_for(j):
        if not outer:
            return [(gathered, FIRST_HEAD[j] // 2)]
        return [(piece, FIRST_HEAD[j] // 2) for piece in line + side] + [(halves[j], 0)]

    window = (REACH + 2) * tok
    resident = pl.BlockSpec(memory_space=VMEM)
    keys = pl.pallas_call(
        keys_kernel,
        out_shape=(
            shape((2, window, LAT)),
            shape((2, window, 128)),
            shape((2, window, 128)),
            shape((2, 2 * tok, window), jnp.float32),
        ),
        in_specs=[smem, resident, resident],
        out_specs=[resident] * 4,
        compiler_params=params,
        cost_estimate=pl.CostEstimate(flops=0, bytes_accessed=8 << 20, transcendentals=0),
        name="keys",
    )(mine_info, own_rows, other_rows)

    def attend(j, first, steps):
        heads = 2 * steps
        pieces_of_weight = [piece for piece, begin in weights_for(j)]
        flops = 2 * heads * 2 * (window * LAT * 256 + 2 * tok * window * (NOPE + ROPE + VDIM))
        return pl.pallas_call(
            functools.partial(attend_kernel, outer),
            grid=(steps,),
            out_shape=[shape((tok, heads * VDIM))] * QUAD,
            in_specs=[smem] + [resident] * 4
            + [
                pl.BlockSpec((piece.shape[0], 512), lambda i, begin=begin: (0, begin + first + i))
                for piece, begin in weights_for(j)
            ]
            + [pl.BlockSpec((tok, 256), lambda i: (0, first + i))] * QUAD
            + [pl.BlockSpec((tok, 128), lambda i: (0, CHUNK_HEADS[j] + first + i))] * QUAD,
            out_specs=[pl.BlockSpec((tok, 256), lambda i: (0, i))] * QUAD,
            scratch_shapes=[VMEM((LAT, 512), jnp.bfloat16)],
            compiler_params=params,
            cost_estimate=pl.CostEstimate(
                flops=flops,
                bytes_accessed=heads << 20,
                transcendentals=heads * 4 * tok * window,
            ),
            name="attend",
        )(mine_info, *keys, *pieces_of_weight, *moved[j], *moved[j])

    held = outgoing.reshape(1, size, slot_count, ROW)
    exchanged = []

    def exchange(*others):
        half_of = held.shape[1] // 2
        moving = tie(held[:, half_of:], *others)
        exchanged.append(pair_swap(moving, 1 << len(exchanged)))
        return jnp.concatenate([held[:, :half_of], exchanged[-1]], axis=0)

    if outer:
        held = exchange(*line[outer - 1 :])
    results = []
    for call in CALLS:
        last = len(results) + 1 == len(CALLS)
        if results:
            mine_info = tie(mine_info, *halves[1:], *exchanged[len(results) - 1 : len(results)])
        mine_info = tie(mine_info, *[piece for one in results[-2:-1] for piece in one[2:]])
        pieces = attend(*call)
        mine_info = tie(mine_info, pieces[0])
        before = results[-1][2:] if last else []
        if outer and not last:
            held = exchange(pieces[0])
        results.append(
            [pieces[0], quad_swap(tie(pieces[1], *before), 1)]
            + [quad_swap(pieces[r], r) for r in (2, 3)]
        )
    pieces = [one[r] for r in range(QUAD) for one in results]
    if outer:
        decode_cache = pl.pallas_call(
            sort_kernel,
            out_shape=shape((size * slot_count, ROW)),
            in_specs=[smem, anywhere],
            out_specs=anywhere,
            scratch_shapes=[pltpu.SemaphoreType.DMA((size,))],
            compiler_params=params,
            name="sort",
        )(mine_info, held.reshape(size, slot_count, ROW))
    else:
        outgoing = tie(outgoing, results[-1][0]).reshape(size, slot_count, ROW)
        arrived = lax.all_to_all(outgoing, "ctx", split_axis=0, concat_axis=0, tiled=True)
        decode_cache = arrived.reshape(size * slot_count, ROW)
    attn_out = pl.pallas_call(
        gather_kernel,
        out_shape=shape((tok, H * VDIM)),
        in_specs=[smem] + [anywhere] * len(pieces),
        out_specs=anywhere,
        scratch_shapes=[pltpu.SemaphoreType.DMA((len(pieces),))],
        compiler_params=params,
        name="place",
    )(quarter_info, *pieces)
    return (attn_out, decode_cache)


def solution(mesh):
    return jax.shard_map(
        body,
        mesh=mesh,
        in_specs=(
            P(("groups", "ctx"), None),
            P(("groups", "ctx"), None),
            P(),
            P("ctx", None),
            P(("groups", "ctx"), None),
            P("groups"),
        ),
        out_specs=(P(("groups", "ctx"), None), P(("groups", "ctx"), None)),
        check_vma=False,
    )
```

```python
import functools
import math

import jax
import jax.numpy as jnp
import numpy as np
from jax import lax
from jax.experimental import pallas as pl
from jax.experimental.pallas import tpu as pltpu
from jax.sharding import PartitionSpec as P

H = 64
NOPE = 128
ROPE = 64
VDIM = 128
LAT = 512
REACH = 3
QUAD = 4
HQ = H // QUAD
CHUNK_HEADS = (8, 8)
PHASES = (
    ("z", "y0", "k", "q02", "b~", "f~"),
    ("z", "y1", "q03", "q01"),
    ("z", "y2", "p", "q12"),
    ("y3", "w", "q13~", "q11"),
)
CHUNKS = len(CHUNK_HEADS)
FIRST_HEAD = tuple(sum(CHUNK_HEADS[:j]) for j in range(CHUNKS))
ROW = LAT + ROPE
EXT = 640
VMEM_LIMIT = 20 * 1024 * 1024
CALLS = ((0, 0, 4), (1, 0, 2), (1, 2, 2))
SMEM = pltpu.SMEM
VMEM = pltpu.VMEM


def rows_kernel(
    slot_count,
    relative,
    info,
    lengths,
    kv,
    gain,
    ranks,
    freq,
    rows_out,
    cos_out,
    sin_out,
    outgoing_out,
):
    tok = kv.shape[1]
    base = info[0] * tok
    spots = base + lax.broadcasted_iota(jnp.int32, (tok, 128), 0)
    lane = lax.broadcasted_iota(jnp.int32, (tok, 128), 1)
    begin = jnp.int32(0)
    own_start = jnp.zeros((tok, 128), jnp.int32)
    for r in range(lengths.shape[0]):
        own_start = jnp.where(spots >= begin, begin, own_start)
        begin = begin + lengths[r]
    offset = spots - own_start
    angles = offset.astype(jnp.float32) * freq[...]
    cosine = jnp.cos(angles)
    sine = jnp.where((lane & 32) == 0, -jnp.sin(angles), jnp.sin(angles))
    cos_out[...] = cosine
    sin_out[...] = sine
    raw = kv[...].astype(jnp.float32).T
    latent = raw[:, :LAT]
    mean = jnp.sum(latent * latent, axis=1, keepdims=True) * (1.0 / LAT)
    latent = latent * lax.rsqrt(mean + 1e-06) * gain[...]
    key = raw[:, LAT:]
    swapped = jnp.concatenate([key[:, ROPE // 2 :], key[:, : ROPE // 2]], axis=1)
    turned = key * cosine[:, :ROPE] + swapped * sine[:, :ROPE]
    high = (offset >> 8).astype(jnp.float32)
    low = (offset & 255).astype(jnp.float32)
    meta = jnp.where(lane == 0, high, jnp.where(lane == 1, low, 0.0))
    tail = jnp.concatenate([turned, meta[:, :ROPE]], axis=1)
    rows_out[:, :LAT] = latent.astype(jnp.bfloat16)
    rows_out[:, LAT:] = tail.astype(jnp.bfloat16)

    block = ranks[...]
    if relative:
        away = block ^ info[0]
        block = ((away & 1) << 3) | ((away & 2) << 1) | ((away & 4) >> 1) | (away >> 3)
    rank_row = jnp.broadcast_to(block, (tok, tok)).astype(jnp.float32)
    rank_col = rank_row.T
    earlier = lax.broadcasted_iota(jnp.int32, (tok, tok), 0) < lax.broadcasted_iota(
        jnp.int32, (tok, tok), 1
    )
    same = jnp.where((rank_col == rank_row) & earlier, 1.0, 0.0)
    slot = jnp.sum(same, axis=0, keepdims=True)
    target = (rank_row[:1] * slot_count + slot).astype(jnp.int32)
    spots_out = lax.broadcasted_iota(jnp.int32, (outgoing_out.shape[0], tok), 0)
    selector = jnp.where(spots_out == target, 1.0, 0.0).astype(jnp.bfloat16)
    picked = jnp.dot(selector, rows_out[:, :ROW], preferred_element_type=jnp.float32)
    outgoing_out[...] = picked.astype(jnp.bfloat16)


def query_kernel(info, query, cosine, sine, *outs):
    tok = query.shape[0]
    lane = lax.broadcasted_iota(jnp.int32, (tok, 128), 1)
    low_half = lane < 64
    first_quarter = (lane & 32) == 0
    cos_table = cosine[...]
    sin_table = sine[...]
    for r in range(QUAD):
        first = (info[0] ^ r) * (HQ * (NOPE + ROPE))
        for pair in range(HQ // 2):
            j = max(j for j in range(CHUNKS) if FIRST_HEAD[j] <= 2 * pair)
            out = outs[r * CHUNKS + j]
            at = pair - FIRST_HEAD[j] // 2
            rope_at = CHUNK_HEADS[j] * NOPE + at * 128
            begin = pl.multiple_of(first + pair * 2 * (NOPE + ROPE), 128)
            both = query[:, pl.ds(begin, 2 * (NOPE + ROPE))]
            mid = both[:, 128:256].astype(jnp.float32)
            end = both[:, 256:384].astype(jnp.float32)
            turned = jnp.where(low_half, mid, end)
            odd_nope = pltpu.roll(jnp.where(low_half, end, mid), 64, 1)
            swapped = jnp.where(
                first_quarter, pltpu.roll(turned, 96, 1), pltpu.roll(turned, 32, 1)
            )
            turned = turned * cos_table + swapped * sin_table
            out[:, at * 256 : at * 256 + 128] = both[:, :128]
            out[:, at * 256 + 128 : at * 256 + 256] = odd_nope.astype(jnp.bfloat16)
            out[:, rope_at : rope_at + 128] = turned.astype(jnp.bfloat16)


def pair_kernel(info, w_up, got, out, sem):
    rows, width = got.shape
    begin = pl.multiple_of(info[0] * width, 128)
    copies = [
        pltpu.make_async_copy(w_up.at[:, pl.ds(begin, width)], out.at[pl.ds(0, rows)], sem.at[0]),
        pltpu.make_async_copy(got, out.at[pl.ds(rows, rows)], sem.at[1]),
    ]
    for copy in copies:
        copy.start()
    for copy in copies:
        copy.wait()


def keys_kernel(info, own, other, latent, rope_even, rope_odd, bias):
    tok = own.shape[0] // 6
    mine = info[0]
    partner = mine ^ 1
    has_last = (mine & 1) == 1
    starts = [mine, partner, mine - 2, partner - 2, (mine >> 1) * 2 - 3]
    blank = jnp.zeros((tok, ROPE), jnp.bfloat16)
    lane = lax.broadcasted_iota(jnp.int32, (tok, tok), 1)
    row = lax.broadcasted_iota(jnp.int32, (tok, tok), 0)
    for g in range(2):
        mine_of, other_of = [
            [ref[(2 * n + g) * tok : (2 * n + g + 1) * tok] for n in range(3)]
            for ref in (own, other)
        ]
        pieces = [
            mine_of[0],
            other_of[0],
            mine_of[1],
            other_of[1],
            jnp.where(has_last, mine_of[2], other_of[2]),
        ]
        for b, piece in enumerate(pieces):
            here = slice(b * tok, (b + 1) * tok)
            latent[g, here] = piece[:, :LAT]
            turned = piece[:, LAT : LAT + ROPE]
            rope_even[g, here] = jnp.concatenate([turned, blank], axis=1)
            rope_odd[g, here] = jnp.concatenate([blank, turned], axis=1)
        for half in range(2):
            meta = pieces[half][:, LAT:].astype(jnp.float32)
            offset = (meta[:, ROPE : ROPE + 1] * 256.0 + meta[:, ROPE + 1 : ROPE + 2]).astype(
                jnp.int32
            )
            spots = starts[half] * tok + row
            lowest = jnp.maximum(spots - offset, (starts[half] - REACH) * tok)
            for b in range(REACH + 2):
                keys = starts[b] * tok + lane
                allowed = (keys >= lowest) & (keys <= spots)
                bias[g, half * tok : (half + 1) * tok, b * tok : (b + 1) * tok] = jnp.where(
                    allowed, 0.0, -1e30
                )


def attend_kernel(outer, info, latent, rope_even, rope_odd, bias, *refs):
    pieces_count = 2 * outer if outer else 1
    pieces_of_weight, refs = refs[:pieces_count], refs[pieces_count:]
    nope = refs[0:QUAD]
    rope = refs[QUAD : 2 * QUAD]
    outs = refs[2 * QUAD : 3 * QUAD]
    held = refs[3 * QUAD]
    tok = nope[0].shape[0]
    mine = info[0]
    scale = (NOPE + ROPE) ** (-0.5) * math.log2(math.e)

    if outer:
        weight = held
        for i, piece in enumerate(pieces_of_weight):
            side, behind = i // outer, i % outer
            chip = ((mine >> 2) + outer - behind) % outer * 2 + (((mine >> 1) & 1) ^ side)
            rows = piece.shape[0] // 2
            for core in range(2):
                begin = pl.multiple_of(chip * 2 * rows + ((mine & 1) ^ core) * rows, rows)
                held[pl.ds(begin, rows)] = piece[core * rows : (core + 1) * rows]
    else:
        weight = pieces_of_weight[0]

    def expand(g):
        wide = jnp.dot(latent[g], weight[...], preferred_element_type=jnp.float32)
        return wide.astype(jnp.bfloat16)

    def score(g, b, expanded):
        at = slice(b * 128, (b + 1) * 128)
        key_rope = (rope_even, rope_odd)[b][g]
        key = jnp.concatenate([expanded[:, b * 256 : b * 256 + 128], key_rope], axis=1)
        query = jnp.concatenate(
            [
                jnp.concatenate([nope[2 * g][:, at], rope[2 * g][...]], axis=1),
                jnp.concatenate([nope[2 * g + 1][:, at], rope[2 * g + 1][...]], axis=1),
            ],
            axis=0,
        )
        return lax.dot_general(
            query, key, (((1,), (1,)), ((), ())), preferred_element_type=jnp.float32
        )

    def weigh(g, scores):
        scores = scores * scale + bias[g]
        largest = jnp.max(scores, axis=1, keepdims=True)
        expo = jnp.exp2(scores - largest)
        return expo.astype(jnp.bfloat16), jnp.sum(expo, axis=1, keepdims=True)

    def mix(g, b, expanded, weights, total):
        at = slice(b * 128, (b + 1) * 128)
        value = expanded[:, b * 256 + 128 : b * 256 + 256]
        mixed = jnp.dot(weights, value, preferred_element_type=jnp.float32)
        mixed = (mixed / total).astype(jnp.bfloat16)
        outs[2 * g][:, at] = mixed[:tok]
        outs[2 * g + 1][:, at] = mixed[tok:]

    first = expand(0)
    scores = score(0, 0, first)
    second = expand(1)
    weighed = weigh(0, scores)
    scores = score(0, 1, first)
    mix(0, 0, first, *weighed)
    weighed = weigh(0, scores)
    scores = score(1, 0, second)
    mix(0, 1, first, *weighed)
    weighed = weigh(1, scores)
    scores = score(1, 1, second)
    mix(1, 0, second, *weighed)
    weighed = weigh(1, scores)
    mix(1, 1, second, *weighed)


def sort_kernel(info, relative, out, sem):
    rows = relative.shape[1]
    copies = []
    for d in range(relative.shape[0]):
        begin = pl.multiple_of((info[0] ^ d) * rows, rows)
        copies.append(
            pltpu.make_async_copy(relative.at[d], out.at[pl.ds(begin, rows)], sem.at[d])
        )
    for copy in copies:
        copy.start()
    for copy in copies:
        copy.wait()


def gather_kernel(info, *refs):
    pieces, out, sems = refs[:-2], refs[-2], refs[-1]
    copies = []
    for i, piece in enumerate(pieces):
        r, (j, first, steps) = i // len(CALLS), CALLS[i % len(CALLS)]
        begin = ((info[0] ^ r) * HQ + FIRST_HEAD[j] + 2 * first) * VDIM
        begin = pl.multiple_of(begin, 128)
        copies.append(
            pltpu.make_async_copy(piece, out.at[:, pl.ds(begin, piece.shape[1])], sems.at[i])
        )
    for copy in copies:
        copy.start()
    for copy in copies:
        copy.wait()


def tie(array, *others):
    return lax.optimization_barrier((array,) + others)[0]


class Phases:
    def __init__(self):
        self.before, self.before_late, self.now, self.late = [], [], [], []

    def turn(self):
        self.before = self.now + self.before_late
        self.before_late, self.now, self.late = self.late, [], []

    def send(self, late, permute, array, *args):
        arrived = permute(tie(array, *self.before) if self.before else array, *args)
        if late != "-":
            (self.late if late == "~" else self.now).append(arrived)
        return arrived


def shape(dims, kind=jnp.bfloat16):
    return jax.ShapeDtypeStruct(dims, kind)


def in_hbm(*arrays):
    return [pltpu.with_memory_space_constraint(array, pltpu.HBM) for array in arrays]


def body(q_heads, kv_latent, latent_gain, w_up, page_ranks, lengths):
    tok = q_heads.shape[0]
    size = lax.axis_size("ctx")
    groups = lax.axis_size("groups")
    mine = lax.axis_index("ctx")
    quarter = lax.axis_index("groups") * 2 + mine % 2
    slot_count = max(2, 2 * tok // size)
    smem = pl.BlockSpec(memory_space=SMEM)
    params = pltpu.CompilerParams(vmem_limit_bytes=VMEM_LIMIT)
    alone = pltpu.CompilerParams(vmem_limit_bytes=3 * VMEM_LIMIT)

    def quad_swap(array, r):
        dx, dc = r // 2, r % 2
        pairs = [
            (g * size + i, (g ^ dx) * size + (i ^ dc)) for g in range(groups) for i in range(size)
        ]
        return lax.ppermute(array, ("groups", "ctx"), pairs)

    def around(array, by):
        return lax.ppermute(array, "ctx", [(i, (i + by) % size) for i in range(size)])

    def inner_swap(array):
        return lax.ppermute(array, "ctx", [(i, i ^ 2) for i in range(size)])

    def pair_swap(array, distance):
        return lax.ppermute(array, "ctx", [(i, i ^ distance) for i in range(size)])

    def from_behind(array, by, odd_only):
        first = 1 if odd_only else 0
        step = 2 if odd_only else 1
        pairs = [(i, i + by) for i in range(first, size - by, step)]
        return lax.ppermute(array, "ctx", pairs)

    width = HQ * (NOPE + VDIM)
    quarter_info = quarter[None].astype(jnp.int32)
    anywhere = pl.BlockSpec(memory_space=pl.ANY)
    give = lax.dynamic_slice_in_dim(w_up, (quarter ^ 1) * width, width, 1)
    give, lengths = lax.optimization_barrier((give, lengths))
    got = quad_swap(give, 1)
    outer = 4 if size == 16 else 0
    if outer:
        pair_rows = pl.pallas_call(
            pair_kernel,
            out_shape=shape((2 * w_up.shape[0], width)),
            in_specs=[smem, pl.BlockSpec(memory_space=pltpu.HBM), anywhere],
            out_specs=anywhere,
            scratch_shapes=[pltpu.SemaphoreType.DMA((2,))],
            compiler_params=params,
            name="pair",
        )(quarter_info, *in_hbm(w_up), got)
    else:
        keep = lax.dynamic_slice_in_dim(w_up, quarter * width, width, 1)
        even = mine % 2 == 0
        both = jnp.concatenate(
            [jnp.where(even, keep, got), jnp.where(even, got, keep)], axis=0
        )
        same_core = [list(range(c, size, 2)) for c in range(2)]
        gathered = lax.all_gather(both, "ctx", axis=0, tiled=True, axis_index_groups=same_core)

    frequency = np.exp(-np.arange(ROPE // 2) * (2.0 * math.log(10000.0) / ROPE))
    frequency = jnp.asarray(np.tile(frequency, 4)[None, :], jnp.float32)
    mine_info = mine[None].astype(jnp.int32)

    def block(*dims):
        return pl.BlockSpec(dims, lambda i: (0,) * len(dims))

    rows, cosine, sine, outgoing = pl.pallas_call(
        functools.partial(rows_kernel, slot_count, outer > 0),
        grid=(1,),
        out_shape=(
            shape((tok, EXT)),
            shape((tok, 128), jnp.float32),
            shape((tok, 128), jnp.float32),
            shape((size * slot_count, ROW)),
        ),
        in_specs=[smem, smem, block(ROW, tok), block(1, LAT), block(1, tok), block(1, 128)],
        out_specs=[
            block(tok, EXT),
            block(tok, 128),
            block(tok, 128),
            block(size * slot_count, ROW),
        ],
        compiler_params=alone,
        name="rows",
    )(
        mine_info,
        lengths,
        *in_hbm(kv_latent.T, latent_gain[None, :], page_ranks.T, frequency),
    )

    queries = pl.pallas_call(
        query_kernel,
        out_shape=[shape((tok, h * (NOPE + ROPE))) for h in CHUNK_HEADS] * QUAD,
        grid=(1,),
        in_specs=[smem, block(*q_heads.shape), block(tok, 128), block(tok, 128)],
        out_specs=[block(tok, h * (NOPE + ROPE)) for h in CHUNK_HEADS] * QUAD,
        compiler_params=params,
        cost_estimate=pl.CostEstimate(
            flops=0, bytes_accessed=4 * q_heads.size, transcendentals=0
        ),
        name="queries",
    )(quarter_info, *in_hbm(q_heads, tie(cosine, pair_rows if outer else got), sine))

    phases = Phases()
    line = [pair_rows] if outer else []
    side = []
    half = width // CHUNKS
    halves = []
    moved = [[queries[j]] + [None] * (QUAD - 1) for j in range(CHUNKS)]
    parts = {"r": tie(rows, pair_rows if outer else got)}
    for name in [name for phase in PHASES for name in phase + ("|",)]:
        kind, late = name[0], name[-1]
        if kind == "|":
            phases.now.append(queries[0])
            phases.turn()
        elif kind == "z" and outer:
            line.append(phases.send(late, around, line[-1], 4))
        elif kind == "y" and outer:
            step = int(name[1])
            if step < outer - 1:
                side.append(phases.send(late, inner_swap, line[step]))
            else:
                halves.append(phases.send(late, inner_swap, line[step][:, :half]))
        elif kind == "w" and outer:
            halves.append(phases.send(late, around, side[-1][:, half:], 4))
        elif kind == "k":
            swapped = phases.send(late, quad_swap, parts["r"], 2)
            both_groups = jnp.concatenate([parts["r"], swapped], axis=0)
        elif kind == "b":
            behind = phases.send(late, from_behind, both_groups, 2, False)
        elif kind == "f":
            far_behind = phases.send(late, from_behind, both_groups, 4, True)
        elif kind == "p":
            own_rows = jnp.concatenate([both_groups, behind, far_behind], axis=0)
            other_rows = phases.send(late, quad_swap, own_rows, 1)
        elif kind == "q":
            j, r = int(name[1]), int(name[2])
            moved[j][r] = phases.send(late, quad_swap, queries[r * CHUNKS + j], r)

    def weights_for(j):
        if not outer:
            return [(gathered, FIRST_HEAD[j] // 2)]
        return [(piece, FIRST_HEAD[j] // 2) for piece in line + side] + [(halves[j], 0)]

    window = (REACH + 2) * tok
    resident = pl.BlockSpec(memory_space=VMEM)
    keys = pl.pallas_call(
        keys_kernel,
        out_shape=(
            shape((2, window, LAT)),
            shape((2, window, 128)),
            shape((2, window, 128)),
            shape((2, 2 * tok, window), jnp.float32),
        ),
        in_specs=[smem, resident, resident],
        out_specs=[resident] * 4,
        compiler_params=params,
        cost_estimate=pl.CostEstimate(flops=0, bytes_accessed=8 << 20, transcendentals=0),
        name="keys",
    )(mine_info, own_rows, other_rows)

    def attend(j, first, steps):
        heads = 2 * steps
        pieces_of_weight = [piece for piece, begin in weights_for(j)]
        flops = 2 * heads * 2 * (window * LAT * 256 + 2 * tok * window * (NOPE + ROPE + VDIM))
        return pl.pallas_call(
            functools.partial(attend_kernel, outer),
            grid=(steps,),
            out_shape=[shape((tok, heads * VDIM))] * QUAD,
            in_specs=[smem] + [resident] * 4
            + [
                pl.BlockSpec((piece.shape[0], 512), lambda i, begin=begin: (0, begin + first + i))
                for piece, begin in weights_for(j)
            ]
            + [pl.BlockSpec((tok, 256), lambda i: (0, first + i))] * QUAD
            + [pl.BlockSpec((tok, 128), lambda i: (0, CHUNK_HEADS[j] + first + i))] * QUAD,
            out_specs=[pl.BlockSpec((tok, 256), lambda i: (0, i))] * QUAD,
            scratch_shapes=[VMEM((LAT, 512), jnp.bfloat16)],
            compiler_params=params,
            cost_estimate=pl.CostEstimate(
                flops=flops,
                bytes_accessed=heads << 20,
                transcendentals=heads * 4 * tok * window,
            ),
            name="attend",
        )(mine_info, *keys, *pieces_of_weight, *moved[j], *moved[j])

    held = outgoing.reshape(1, size, slot_count, ROW)
    exchanged = []

    def exchange(*others):
        half_of = held.shape[1] // 2
        moving = tie(held[:, half_of:], *others)
        exchanged.append(pair_swap(moving, 1 << len(exchanged)))
        return jnp.concatenate([held[:, :half_of], exchanged[-1]], axis=0)

    if outer:
        held = exchange(*line[outer - 1 :])
        held = exchange(halves[0])
    results = []
    for call in CALLS:
        last = len(results) + 1 == len(CALLS)
        if results:
            mine_info = tie(mine_info, *halves[1:], *exchanged[len(results) : len(results) + 1])
        mine_info = tie(mine_info, *(results[0][2:3] if last else []))
        pieces = attend(*call)
        mine_info = tie(mine_info, pieces[0])
        before = results[-1][2:] if last else []
        if outer and not last:
            held = exchange(pieces[0])
        results.append(
            [pieces[0], quad_swap(tie(pieces[1], *before), 1)]
            + [quad_swap(pieces[r], r) for r in (2, 3)]
        )
    pieces = [one[r] for r in range(QUAD) for one in results]
    if outer:
        decode_cache = pl.pallas_call(
            sort_kernel,
            out_shape=shape((size * slot_count, ROW)),
            in_specs=[smem, anywhere],
            out_specs=anywhere,
            scratch_shapes=[pltpu.SemaphoreType.DMA((size,))],
            compiler_params=params,
            name="sort",
        )(mine_info, held.reshape(size, slot_count, ROW))
    else:
        outgoing = tie(outgoing, results[-1][0]).reshape(size, slot_count, ROW)
        arrived = lax.all_to_all(outgoing, "ctx", split_axis=0, concat_axis=0, tiled=True)
        decode_cache = arrived.reshape(size * slot_count, ROW)
    attn_out = pl.pallas_call(
        gather_kernel,
        out_shape=shape((tok, H * VDIM)),
        in_specs=[smem] + [anywhere] * len(pieces),
        out_specs=anywhere,
        scratch_shapes=[pltpu.SemaphoreType.DMA((len(pieces),))],
        compiler_params=params,
        name="place",
    )(tie(quarter_info, decode_cache), *pieces)
    return (attn_out, decode_cache)


def solution(mesh):
    return jax.shard_map(
        body,
        mesh=mesh,
        in_specs=(
            P(("groups", "ctx"), None),
            P(("groups", "ctx"), None),
            P(),
            P("ctx", None),
            P(("groups", "ctx"), None),
            P("groups"),
        ),
        out_specs=(P(("groups", "ctx"), None), P(("groups", "ctx"), None)),
        check_vma=False,
    )
```

```python
import functools
import math

import jax
import jax.numpy as jnp
import numpy as np
from jax import lax
from jax.experimental import pallas as pl
from jax.experimental.pallas import tpu as pltpu
from jax.sharding import PartitionSpec as P

H = 64
NOPE = 128
ROPE = 64
VDIM = 128
LAT = 512
REACH = 3
QUAD = 4
HQ = H // QUAD
CHUNK_HEADS = (8, 8)
PHASES = (
    ("z", "y0", "k", "q02", "b~", "f~"),
    ("z", "y1", "q03", "q01"),
    ("z", "y2", "p", "q12"),
    ("y3", "w", "q13~", "q11"),
)
CHUNKS = len(CHUNK_HEADS)
FIRST_HEAD = tuple(sum(CHUNK_HEADS[:j]) for j in range(CHUNKS))
ROW = LAT + ROPE
EXT = 640
VMEM_LIMIT = 20 * 1024 * 1024
CALLS = ((0, 0, 4), (1, 0, 2), (1, 2, 2))
SMEM = pltpu.SMEM
VMEM = pltpu.VMEM


def rows_kernel(
    slot_count,
    relative,
    info,
    lengths,
    kv,
    gain,
    ranks,
    freq,
    rows_out,
    cos_out,
    sin_out,
    outgoing_out,
):
    tok = kv.shape[1]
    base = info[0] * tok
    spots = base + lax.broadcasted_iota(jnp.int32, (tok, 128), 0)
    lane = lax.broadcasted_iota(jnp.int32, (tok, 128), 1)
    begin = jnp.int32(0)
    own_start = jnp.zeros((tok, 128), jnp.int32)
    for r in range(lengths.shape[0]):
        own_start = jnp.where(spots >= begin, begin, own_start)
        begin = begin + lengths[r]
    offset = spots - own_start
    angles = offset.astype(jnp.float32) * freq[...]
    cosine = jnp.cos(angles)
    sine = jnp.where((lane & 32) == 0, -jnp.sin(angles), jnp.sin(angles))
    cos_out[...] = cosine
    sin_out[...] = sine
    raw = kv[...].astype(jnp.float32).T
    latent = raw[:, :LAT]
    mean = jnp.sum(latent * latent, axis=1, keepdims=True) * (1.0 / LAT)
    latent = latent * lax.rsqrt(mean + 1e-06) * gain[...]
    key = raw[:, LAT:]
    swapped = jnp.concatenate([key[:, ROPE // 2 :], key[:, : ROPE // 2]], axis=1)
    turned = key * cosine[:, :ROPE] + swapped * sine[:, :ROPE]
    high = (offset >> 8).astype(jnp.float32)
    low = (offset & 255).astype(jnp.float32)
    meta = jnp.where(lane == 0, high, jnp.where(lane == 1, low, 0.0))
    tail = jnp.concatenate([turned, meta[:, :ROPE]], axis=1)
    rows_out[:, :LAT] = latent.astype(jnp.bfloat16)
    rows_out[:, LAT:] = tail.astype(jnp.bfloat16)

    block = ranks[...]
    if relative:
        away = block ^ info[0]
        block = ((away & 1) << 3) | ((away & 2) << 1) | ((away & 4) >> 1) | (away >> 3)
    rank_row = jnp.broadcast_to(block, (tok, tok)).astype(jnp.float32)
    rank_col = rank_row.T
    earlier = lax.broadcasted_iota(jnp.int32, (tok, tok), 0) < lax.broadcasted_iota(
        jnp.int32, (tok, tok), 1
    )
    same = jnp.where((rank_col == rank_row) & earlier, 1.0, 0.0)
    slot = jnp.sum(same, axis=0, keepdims=True)
    target = (rank_row[:1] * slot_count + slot).astype(jnp.int32)
    spots_out = lax.broadcasted_iota(jnp.int32, (outgoing_out.shape[0], tok), 0)
    selector = jnp.where(spots_out == target, 1.0, 0.0).astype(jnp.bfloat16)
    picked = jnp.dot(selector, rows_out[:, :ROW], preferred_element_type=jnp.float32)
    outgoing_out[...] = picked.astype(jnp.bfloat16)


def query_kernel(info, query, cosine, sine, *outs):
    tok = query.shape[0]
    lane = lax.broadcasted_iota(jnp.int32, (tok, 128), 1)
    low_half = lane < 64
    first_quarter = (lane & 32) == 0
    cos_table = cosine[...]
    sin_table = sine[...]
    for r in range(QUAD):
        first = (info[0] ^ r) * (HQ * (NOPE + ROPE))
        for pair in range(HQ // 2):
            j = max(j for j in range(CHUNKS) if FIRST_HEAD[j] <= 2 * pair)
            out = outs[r * CHUNKS + j]
            at = pair - FIRST_HEAD[j] // 2
            rope_at = CHUNK_HEADS[j] * NOPE + at * 128
            begin = pl.multiple_of(first + pair * 2 * (NOPE + ROPE), 128)
            both = query[:, pl.ds(begin, 2 * (NOPE + ROPE))]
            mid = both[:, 128:256].astype(jnp.float32)
            end = both[:, 256:384].astype(jnp.float32)
            turned = jnp.where(low_half, mid, end)
            odd_nope = pltpu.roll(jnp.where(low_half, end, mid), 64, 1)
            swapped = jnp.where(
                first_quarter, pltpu.roll(turned, 96, 1), pltpu.roll(turned, 32, 1)
            )
            turned = turned * cos_table + swapped * sin_table
            out[:, at * 256 : at * 256 + 128] = both[:, :128]
            out[:, at * 256 + 128 : at * 256 + 256] = odd_nope.astype(jnp.bfloat16)
            out[:, rope_at : rope_at + 128] = turned.astype(jnp.bfloat16)


def pair_kernel(info, w_up, got, out, sem):
    rows, width = got.shape
    begin = pl.multiple_of(info[0] * width, 128)
    copies = [
        pltpu.make_async_copy(w_up.at[:, pl.ds(begin, width)], out.at[pl.ds(0, rows)], sem.at[0]),
        pltpu.make_async_copy(got, out.at[pl.ds(rows, rows)], sem.at[1]),
    ]
    for copy in copies:
        copy.start()
    for copy in copies:
        copy.wait()


def keys_kernel(info, own, other, latent, rope_even, rope_odd, bias):
    tok = own.shape[0] // 6
    mine = info[0]
    partner = mine ^ 1
    has_last = (mine & 1) == 1
    starts = [mine, partner, mine - 2, partner - 2, (mine >> 1) * 2 - 3]
    blank = jnp.zeros((tok, ROPE), jnp.bfloat16)
    lane = lax.broadcasted_iota(jnp.int32, (tok, tok), 1)
    row = lax.broadcasted_iota(jnp.int32, (tok, tok), 0)
    for g in range(2):
        mine_of, other_of = [
            [ref[(2 * n + g) * tok : (2 * n + g + 1) * tok] for n in range(3)]
            for ref in (own, other)
        ]
        pieces = [
            mine_of[0],
            other_of[0],
            mine_of[1],
            other_of[1],
            jnp.where(has_last, mine_of[2], other_of[2]),
        ]
        for b, piece in enumerate(pieces):
            here = slice(b * tok, (b + 1) * tok)
            latent[g, here] = piece[:, :LAT]
            turned = piece[:, LAT : LAT + ROPE]
            rope_even[g, here] = jnp.concatenate([turned, blank], axis=1)
            rope_odd[g, here] = jnp.concatenate([blank, turned], axis=1)
        for half in range(2):
            meta = pieces[half][:, LAT:].astype(jnp.float32)
            offset = (meta[:, ROPE : ROPE + 1] * 256.0 + meta[:, ROPE + 1 : ROPE + 2]).astype(
                jnp.int32
            )
            spots = starts[half] * tok + row
            lowest = jnp.maximum(spots - offset, (starts[half] - REACH) * tok)
            for b in range(REACH + 2):
                keys = starts[b] * tok + lane
                allowed = (keys >= lowest) & (keys <= spots)
                bias[g, half * tok : (half + 1) * tok, b * tok : (b + 1) * tok] = jnp.where(
                    allowed, 0.0, -1e30
                )


def attend_kernel(outer, info, latent, rope_even, rope_odd, bias, *refs):
    pieces_count = 2 * outer if outer else 1
    pieces_of_weight, refs = refs[:pieces_count], refs[pieces_count:]
    nope = refs[0:QUAD]
    rope = refs[QUAD : 2 * QUAD]
    outs = refs[2 * QUAD : 3 * QUAD]
    held = refs[3 * QUAD]
    tok = nope[0].shape[0]
    mine = info[0]
    scale = (NOPE + ROPE) ** (-0.5) * math.log2(math.e)

    if outer:
        weight = held
        for i, piece in enumerate(pieces_of_weight):
            side, behind = i // outer, i % outer
            chip = ((mine >> 2) + outer - behind) % outer * 2 + (((mine >> 1) & 1) ^ side)
            rows = piece.shape[0] // 2
            for core in range(2):
                begin = pl.multiple_of(chip * 2 * rows + ((mine & 1) ^ core) * rows, rows)
                held[pl.ds(begin, rows)] = piece[core * rows : (core + 1) * rows]
    else:
        weight = pieces_of_weight[0]

    def expand(g):
        wide = jnp.dot(latent[g], weight[...], preferred_element_type=jnp.float32)
        return wide.astype(jnp.bfloat16)

    def score(g, b, expanded):
        at = slice(b * 128, (b + 1) * 128)
        key_rope = (rope_even, rope_odd)[b][g]
        key = jnp.concatenate([expanded[:, b * 256 : b * 256 + 128], key_rope], axis=1)
        query = jnp.concatenate(
            [
                jnp.concatenate([nope[2 * g][:, at], rope[2 * g][...]], axis=1),
                jnp.concatenate([nope[2 * g + 1][:, at], rope[2 * g + 1][...]], axis=1),
            ],
            axis=0,
        )
        return lax.dot_general(
            query, key, (((1,), (1,)), ((), ())), preferred_element_type=jnp.float32
        )

    def weigh(g, scores):
        scores = scores * scale + bias[g]
        largest = jnp.max(scores, axis=1, keepdims=True)
        expo = jnp.exp2(scores - largest)
        return expo.astype(jnp.bfloat16), jnp.sum(expo, axis=1, keepdims=True)

    def mix(g, b, expanded, weights, total):
        at = slice(b * 128, (b + 1) * 128)
        value = expanded[:, b * 256 + 128 : b * 256 + 256]
        mixed = jnp.dot(weights, value, preferred_element_type=jnp.float32)
        mixed = (mixed / total).astype(jnp.bfloat16)
        outs[2 * g][:, at] = mixed[:tok]
        outs[2 * g + 1][:, at] = mixed[tok:]

    first = expand(0)
    scores = score(0, 0, first)
    second = expand(1)
    weighed = weigh(0, scores)
    scores = score(0, 1, first)
    mix(0, 0, first, *weighed)
    weighed = weigh(0, scores)
    scores = score(1, 0, second)
    mix(0, 1, first, *weighed)
    weighed = weigh(1, scores)
    scores = score(1, 1, second)
    mix(1, 0, second, *weighed)
    weighed = weigh(1, scores)
    mix(1, 1, second, *weighed)


def sort_kernel(info, relative, out, sem):
    rows = relative.shape[1]
    copies = []
    for d in range(relative.shape[0]):
        begin = pl.multiple_of((info[0] ^ d) * rows, rows)
        copies.append(
            pltpu.make_async_copy(relative.at[d], out.at[pl.ds(begin, rows)], sem.at[d])
        )
    for copy in copies:
        copy.start()
    for copy in copies:
        copy.wait()


def gather_kernel(info, *refs):
    pieces, out, sems = refs[:-2], refs[-2], refs[-1]
    copies = []
    for i, piece in enumerate(pieces):
        r, (j, first, steps) = i // len(CALLS), CALLS[i % len(CALLS)]
        begin = ((info[0] ^ r) * HQ + FIRST_HEAD[j] + 2 * first) * VDIM
        begin = pl.multiple_of(begin, 128)
        copies.append(
            pltpu.make_async_copy(piece, out.at[:, pl.ds(begin, piece.shape[1])], sems.at[i])
        )
    for copy in copies:
        copy.start()
    for copy in copies:
        copy.wait()


def tie(array, *others):
    return lax.optimization_barrier((array,) + others)[0]


class Phases:
    def __init__(self):
        self.before, self.before_late, self.now, self.late = [], [], [], []

    def turn(self):
        self.before = self.now + self.before_late
        self.before_late, self.now, self.late = self.late, [], []

    def send(self, late, permute, array, *args):
        arrived = permute(tie(array, *self.before) if self.before else array, *args)
        if late != "-":
            (self.late if late == "~" else self.now).append(arrived)
        return arrived


def shape(dims, kind=jnp.bfloat16):
    return jax.ShapeDtypeStruct(dims, kind)


def in_hbm(*arrays):
    return [pltpu.with_memory_space_constraint(array, pltpu.HBM) for array in arrays]


def body(q_heads, kv_latent, latent_gain, w_up, page_ranks, lengths):
    tok = q_heads.shape[0]
    size = lax.axis_size("ctx")
    groups = lax.axis_size("groups")
    mine = lax.axis_index("ctx")
    quarter = lax.axis_index("groups") * 2 + mine % 2
    slot_count = max(2, 2 * tok // size)
    smem = pl.BlockSpec(memory_space=SMEM)
    params = pltpu.CompilerParams(vmem_limit_bytes=VMEM_LIMIT)
    alone = pltpu.CompilerParams(vmem_limit_bytes=3 * VMEM_LIMIT)

    def quad_swap(array, r):
        dx, dc = r // 2, r % 2
        pairs = [
            (g * size + i, (g ^ dx) * size + (i ^ dc)) for g in range(groups) for i in range(size)
        ]
        return lax.ppermute(array, ("groups", "ctx"), pairs)

    def around(array, by):
        return lax.ppermute(array, "ctx", [(i, (i + by) % size) for i in range(size)])

    def inner_swap(array):
        return lax.ppermute(array, "ctx", [(i, i ^ 2) for i in range(size)])

    def pair_swap(array, distance):
        return lax.ppermute(array, "ctx", [(i, i ^ distance) for i in range(size)])

    def from_behind(array, by, odd_only):
        first = 1 if odd_only else 0
        step = 2 if odd_only else 1
        pairs = [(i, i + by) for i in range(first, size - by, step)]
        return lax.ppermute(array, "ctx", pairs)

    width = HQ * (NOPE + VDIM)
    quarter_info = quarter[None].astype(jnp.int32)
    anywhere = pl.BlockSpec(memory_space=pl.ANY)
    give = lax.dynamic_slice_in_dim(w_up, (quarter ^ 1) * width, width, 1)
    give, lengths = lax.optimization_barrier((give, lengths))
    got = quad_swap(give, 1)
    outer = 4 if size == 16 else 0
    if outer:
        pair_rows = pl.pallas_call(
            pair_kernel,
            out_shape=shape((2 * w_up.shape[0], width)),
            in_specs=[smem, pl.BlockSpec(memory_space=pltpu.HBM), anywhere],
            out_specs=anywhere,
            scratch_shapes=[pltpu.SemaphoreType.DMA((2,))],
            compiler_params=params,
            name="pair",
        )(quarter_info, *in_hbm(w_up), got)
    else:
        keep = lax.dynamic_slice_in_dim(w_up, quarter * width, width, 1)
        even = mine % 2 == 0
        both = jnp.concatenate(
            [jnp.where(even, keep, got), jnp.where(even, got, keep)], axis=0
        )
        same_core = [list(range(c, size, 2)) for c in range(2)]
        gathered = lax.all_gather(both, "ctx", axis=0, tiled=True, axis_index_groups=same_core)

    frequency = np.exp(-np.arange(ROPE // 2) * (2.0 * math.log(10000.0) / ROPE))
    frequency = jnp.asarray(np.tile(frequency, 4)[None, :], jnp.float32)
    mine_info = mine[None].astype(jnp.int32)

    def block(*dims):
        return pl.BlockSpec(dims, lambda i: (0,) * len(dims))

    rows, cosine, sine, outgoing = pl.pallas_call(
        functools.partial(rows_kernel, slot_count, outer > 0),
        grid=(1,),
        out_shape=(
            shape((tok, EXT)),
            shape((tok, 128), jnp.float32),
            shape((tok, 128), jnp.float32),
            shape((size * slot_count, ROW)),
        ),
        in_specs=[smem, smem, block(ROW, tok), block(1, LAT), block(1, tok), block(1, 128)],
        out_specs=[
            block(tok, EXT),
            block(tok, 128),
            block(tok, 128),
            block(size * slot_count, ROW),
        ],
        compiler_params=alone,
        name="rows",
    )(
        mine_info,
        lengths,
        *in_hbm(kv_latent.T, latent_gain[None, :], page_ranks.T, frequency),
    )

    queries = pl.pallas_call(
        query_kernel,
        out_shape=[shape((tok, h * (NOPE + ROPE))) for h in CHUNK_HEADS] * QUAD,
        grid=(1,),
        in_specs=[smem, block(*q_heads.shape), block(tok, 128), block(tok, 128)],
        out_specs=[block(tok, h * (NOPE + ROPE)) for h in CHUNK_HEADS] * QUAD,
        compiler_params=params,
        cost_estimate=pl.CostEstimate(
            flops=0, bytes_accessed=4 * q_heads.size, transcendentals=0
        ),
        name="queries",
    )(quarter_info, *in_hbm(q_heads, tie(cosine, pair_rows if outer else got), sine))

    phases = Phases()
    line = [pair_rows] if outer else []
    side = []
    half = width // CHUNKS
    halves = []
    moved = [[queries[j]] + [None] * (QUAD - 1) for j in range(CHUNKS)]
    parts = {"r": tie(rows, pair_rows if outer else got)}
    for name in [name for phase in PHASES for name in phase + ("|",)]:
        kind, late = name[0], name[-1]
        if kind == "|":
            phases.now.append(queries[0])
            phases.turn()
        elif kind == "z" and outer:
            line.append(phases.send(late, around, line[-1], 4))
        elif kind == "y" and outer:
            step = int(name[1])
            if step < outer - 1:
                side.append(phases.send(late, inner_swap, line[step]))
            else:
                halves.append(phases.send(late, inner_swap, line[step][:, :half]))
        elif kind == "w" and outer:
            halves.append(phases.send(late, around, side[-1][:, half:], 4))
        elif kind == "k":
            swapped = phases.send(late, quad_swap, parts["r"], 2)
            both_groups = jnp.concatenate([parts["r"], swapped], axis=0)
        elif kind == "b":
            behind = phases.send(late, from_behind, both_groups, 2, False)
        elif kind == "f":
            far_behind = phases.send(late, from_behind, both_groups, 4, True)
        elif kind == "p":
            own_rows = jnp.concatenate([both_groups, behind, far_behind], axis=0)
            other_rows = phases.send(late, quad_swap, own_rows, 1)
        elif kind == "q":
            j, r = int(name[1]), int(name[2])
            moved[j][r] = phases.send(late, quad_swap, queries[r * CHUNKS + j], r)

    def weights_for(j):
        if not outer:
            return [(gathered, FIRST_HEAD[j] // 2)]
        return [(piece, FIRST_HEAD[j] // 2) for piece in line + side] + [(halves[j], 0)]

    window = (REACH + 2) * tok
    resident = pl.BlockSpec(memory_space=VMEM)
    keys = pl.pallas_call(
        keys_kernel,
        out_shape=(
            shape((2, window, LAT)),
            shape((2, window, 128)),
            shape((2, window, 128)),
            shape((2, 2 * tok, window), jnp.float32),
        ),
        in_specs=[smem, resident, resident],
        out_specs=[resident] * 4,
        compiler_params=params,
        cost_estimate=pl.CostEstimate(flops=0, bytes_accessed=8 << 20, transcendentals=0),
        name="keys",
    )(mine_info, own_rows, other_rows)

    def attend(j, first, steps):
        heads = 2 * steps
        pieces_of_weight = [piece for piece, begin in weights_for(j)]
        flops = 2 * heads * 2 * (window * LAT * 256 + 2 * tok * window * (NOPE + ROPE + VDIM))
        return pl.pallas_call(
            functools.partial(attend_kernel, outer),
            grid=(steps,),
            out_shape=[shape((tok, heads * VDIM))] * QUAD,
            in_specs=[smem] + [resident] * 4
            + [
                pl.BlockSpec((piece.shape[0], 512), lambda i, begin=begin: (0, begin + first + i))
                for piece, begin in weights_for(j)
            ]
            + [pl.BlockSpec((tok, 256), lambda i: (0, first + i))] * QUAD
            + [pl.BlockSpec((tok, 128), lambda i: (0, CHUNK_HEADS[j] + first + i))] * QUAD,
            out_specs=[pl.BlockSpec((tok, 256), lambda i: (0, i))] * QUAD,
            scratch_shapes=[VMEM((LAT, 512), jnp.bfloat16)],
            compiler_params=params,
            cost_estimate=pl.CostEstimate(
                flops=flops,
                bytes_accessed=heads << 20,
                transcendentals=heads * 4 * tok * window,
            ),
            name="attend",
        )(mine_info, *keys, *pieces_of_weight, *moved[j], *moved[j])

    held = outgoing.reshape(1, size, slot_count, ROW)
    exchanged = []

    def exchange(*others):
        half_of = held.shape[1] // 2
        moving = tie(held[:, half_of:], *others)
        exchanged.append(pair_swap(moving, 1 << len(exchanged)))
        return jnp.concatenate([held[:, :half_of], exchanged[-1]], axis=0)

    if outer:
        held = exchange(*line[outer - 1 :])
        held = exchange(halves[0])
    results = []
    for call in CALLS:
        last = len(results) + 1 == len(CALLS)
        if results:
            mine_info = tie(mine_info, *halves[1:], *exchanged[len(results) : len(results) + 1])
        mine_info = tie(mine_info, *(results[0][2:] if last else []))
        pieces = attend(*call)
        mine_info = tie(mine_info, pieces[0])
        if outer and not last:
            held = exchange(pieces[0])
        sent = list(pieces)
        for r in (2, 3, 1):
            before = ([sent[2]] if r == 1 else [results[-1][r]]) if last else []
            sent[r] = quad_swap(tie(pieces[r], *before), r)
        results.append(sent)
    pieces = [one[r] for r in range(QUAD) for one in results]
    if outer:
        decode_cache = pl.pallas_call(
            sort_kernel,
            out_shape=shape((size * slot_count, ROW)),
            in_specs=[smem, anywhere],
            out_specs=anywhere,
            scratch_shapes=[pltpu.SemaphoreType.DMA((size,))],
            compiler_params=params,
            name="sort",
        )(mine_info, held.reshape(size, slot_count, ROW))
    else:
        outgoing = tie(outgoing, results[-1][0]).reshape(size, slot_count, ROW)
        arrived = lax.all_to_all(outgoing, "ctx", split_axis=0, concat_axis=0, tiled=True)
        decode_cache = arrived.reshape(size * slot_count, ROW)
    attn_out = pl.pallas_call(
        gather_kernel,
        out_shape=shape((tok, H * VDIM)),
        in_specs=[smem] + [anywhere] * len(pieces),
        out_specs=anywhere,
        scratch_shapes=[pltpu.SemaphoreType.DMA((len(pieces),))],
        compiler_params=params,
        name="place",
    )(tie(quarter_info, decode_cache), *pieces)
    return (attn_out, decode_cache)


def solution(mesh):
    return jax.shard_map(
        body,
        mesh=mesh,
        in_specs=(
            P(("groups", "ctx"), None),
            P(("groups", "ctx"), None),
            P(),
            P("ctx", None),
            P(("groups", "ctx"), None),
            P("groups"),
        ),
        out_specs=(P(("groups", "ctx"), None), P(("groups", "ctx"), None)),
        check_vma=False,
    )
```

```python
import functools
import math

import jax
import jax.numpy as jnp
import numpy as np
from jax import lax
from jax.experimental import pallas as pl
from jax.experimental.pallas import tpu as pltpu
from jax.sharding import PartitionSpec as P

H = 64
NOPE = 128
ROPE = 64
VDIM = 128
LAT = 512
REACH = 3
QUAD = 4
HQ = H // QUAD
CHUNK_HEADS = (8, 8)
PHASES = (
    ("z", "y0", "k", "q02", "b~", "f~"),
    ("z", "y1", "q03", "q01"),
    ("z", "y2", "p", "q12"),
    ("y3", "w", "q13~", "q11"),
)
CHUNKS = len(CHUNK_HEADS)
FIRST_HEAD = tuple(sum(CHUNK_HEADS[:j]) for j in range(CHUNKS))
ROW = LAT + ROPE
EXT = 640
VMEM_LIMIT = 20 * 1024 * 1024
CALLS = ((0, 0, 4), (1, 0, 2), (1, 2, 2))
SMEM = pltpu.SMEM
VMEM = pltpu.VMEM


def rows_kernel(
    slot_count,
    relative,
    info,
    lengths,
    kv,
    gain,
    ranks,
    freq,
    rows_out,
    cos_out,
    sin_out,
    outgoing_out,
):
    tok = kv.shape[1]
    base = info[0] * tok
    spots = base + lax.broadcasted_iota(jnp.int32, (tok, 128), 0)
    lane = lax.broadcasted_iota(jnp.int32, (tok, 128), 1)
    begin = jnp.int32(0)
    own_start = jnp.zeros((tok, 128), jnp.int32)
    for r in range(lengths.shape[0]):
        own_start = jnp.where(spots >= begin, begin, own_start)
        begin = begin + lengths[r]
    offset = spots - own_start
    angles = offset.astype(jnp.float32) * freq[...]
    cosine = jnp.cos(angles)
    sine = jnp.where((lane & 32) == 0, -jnp.sin(angles), jnp.sin(angles))
    cos_out[...] = cosine
    sin_out[...] = sine
    raw = kv[...].astype(jnp.float32).T
    latent = raw[:, :LAT]
    mean = jnp.sum(latent * latent, axis=1, keepdims=True) * (1.0 / LAT)
    latent = latent * lax.rsqrt(mean + 1e-06) * gain[...]
    key = raw[:, LAT:]
    swapped = jnp.concatenate([key[:, ROPE // 2 :], key[:, : ROPE // 2]], axis=1)
    turned = key * cosine[:, :ROPE] + swapped * sine[:, :ROPE]
    high = (offset >> 8).astype(jnp.float32)
    low = (offset & 255).astype(jnp.float32)
    meta = jnp.where(lane == 0, high, jnp.where(lane == 1, low, 0.0))
    tail = jnp.concatenate([turned, meta[:, :ROPE]], axis=1)
    rows_out[:, :LAT] = latent.astype(jnp.bfloat16)
    rows_out[:, LAT:] = tail.astype(jnp.bfloat16)

    block = ranks[...]
    if relative:
        away = block ^ info[0]
        block = ((away & 1) << 3) | ((away & 2) << 1) | ((away & 4) >> 1) | (away >> 3)
    rank_row = jnp.broadcast_to(block, (tok, tok)).astype(jnp.float32)
    rank_col = rank_row.T
    earlier = lax.broadcasted_iota(jnp.int32, (tok, tok), 0) < lax.broadcasted_iota(
        jnp.int32, (tok, tok), 1
    )
    same = jnp.where((rank_col == rank_row) & earlier, 1.0, 0.0)
    slot = jnp.sum(same, axis=0, keepdims=True)
    target = (rank_row[:1] * slot_count + slot).astype(jnp.int32)
    spots_out = lax.broadcasted_iota(jnp.int32, (outgoing_out.shape[0], tok), 0)
    selector = jnp.where(spots_out == target, 1.0, 0.0).astype(jnp.bfloat16)
    picked = jnp.dot(selector, rows_out[:, :ROW], preferred_element_type=jnp.float32)
    outgoing_out[...] = picked.astype(jnp.bfloat16)


def query_kernel(info, query, cosine, sine, *outs):
    tok = query.shape[0]
    lane = lax.broadcasted_iota(jnp.int32, (tok, 128), 1)
    low_half = lane < 64
    first_quarter = (lane & 32) == 0
    cos_table = cosine[...]
    sin_table = sine[...]
    for r in range(QUAD):
        first = (info[0] ^ r) * (HQ * (NOPE + ROPE))
        for pair in range(HQ // 2):
            j = max(j for j in range(CHUNKS) if FIRST_HEAD[j] <= 2 * pair)
            out = outs[r * CHUNKS + j]
            at = pair - FIRST_HEAD[j] // 2
            rope_at = CHUNK_HEADS[j] * NOPE + at * 128
            begin = pl.multiple_of(first + pair * 2 * (NOPE + ROPE), 128)
            both = query[:, pl.ds(begin, 2 * (NOPE + ROPE))]
            mid = both[:, 128:256].astype(jnp.float32)
            end = both[:, 256:384].astype(jnp.float32)
            turned = jnp.where(low_half, mid, end)
            odd_nope = pltpu.roll(jnp.where(low_half, end, mid), 64, 1)
            swapped = jnp.where(
                first_quarter, pltpu.roll(turned, 96, 1), pltpu.roll(turned, 32, 1)
            )
            turned = turned * cos_table + swapped * sin_table
            out[:, at * 256 : at * 256 + 128] = both[:, :128]
            out[:, at * 256 + 128 : at * 256 + 256] = odd_nope.astype(jnp.bfloat16)
            out[:, rope_at : rope_at + 128] = turned.astype(jnp.bfloat16)


def pair_kernel(info, w_up, got, out, sem):
    rows, width = got.shape
    begin = pl.multiple_of(info[0] * width, 128)
    copies = [
        pltpu.make_async_copy(w_up.at[:, pl.ds(begin, width)], out.at[pl.ds(0, rows)], sem.at[0]),
        pltpu.make_async_copy(got, out.at[pl.ds(rows, rows)], sem.at[1]),
    ]
    for copy in copies:
        copy.start()
    for copy in copies:
        copy.wait()


def keys_kernel(info, own, other, latent, rope_even, rope_odd, bias):
    tok = own.shape[0] // 6
    mine = info[0]
    partner = mine ^ 1
    has_last = (mine & 1) == 1
    starts = [mine, partner, mine - 2, partner - 2, (mine >> 1) * 2 - 3]
    blank = jnp.zeros((tok, ROPE), jnp.bfloat16)
    lane = lax.broadcasted_iota(jnp.int32, (tok, tok), 1)
    row = lax.broadcasted_iota(jnp.int32, (tok, tok), 0)
    for g in range(2):
        mine_of, other_of = [
            [ref[(2 * n + g) * tok : (2 * n + g + 1) * tok] for n in range(3)]
            for ref in (own, other)
        ]
        pieces = [
            mine_of[0],
            other_of[0],
            mine_of[1],
            other_of[1],
            jnp.where(has_last, mine_of[2], other_of[2]),
        ]
        for b, piece in enumerate(pieces):
            here = slice(b * tok, (b + 1) * tok)
            latent[g, here] = piece[:, :LAT]
            turned = piece[:, LAT : LAT + ROPE]
            rope_even[g, here] = jnp.concatenate([turned, blank], axis=1)
            rope_odd[g, here] = jnp.concatenate([blank, turned], axis=1)
        for half in range(2):
            meta = pieces[half][:, LAT:].astype(jnp.float32)
            offset = (meta[:, ROPE : ROPE + 1] * 256.0 + meta[:, ROPE + 1 : ROPE + 2]).astype(
                jnp.int32
            )
            spots = starts[half] * tok + row
            lowest = jnp.maximum(spots - offset, (starts[half] - REACH) * tok)
            for b in range(REACH + 2):
                keys = starts[b] * tok + lane
                allowed = (keys >= lowest) & (keys <= spots)
                bias[g, half * tok : (half + 1) * tok, b * tok : (b + 1) * tok] = jnp.where(
                    allowed, 0.0, -1e30
                )


def attend_kernel(outer, info, latent, rope_even, rope_odd, bias, *refs):
    pieces_count = 2 * outer if outer else 1
    pieces_of_weight, refs = refs[:pieces_count], refs[pieces_count:]
    nope = refs[0:QUAD]
    rope = refs[QUAD : 2 * QUAD]
    outs = refs[2 * QUAD : 3 * QUAD]
    held = refs[3 * QUAD]
    tok = nope[0].shape[0]
    mine = info[0]
    scale = (NOPE + ROPE) ** (-0.5) * math.log2(math.e)

    if outer:
        weight = held
        for i, piece in enumerate(pieces_of_weight):
            side, behind = i // outer, i % outer
            chip = ((mine >> 2) + outer - behind) % outer * 2 + (((mine >> 1) & 1) ^ side)
            rows = piece.shape[0] // 2
            for core in range(2):
                begin = pl.multiple_of(chip * 2 * rows + ((mine & 1) ^ core) * rows, rows)
                held[pl.ds(begin, rows)] = piece[core * rows : (core + 1) * rows]
    else:
        weight = pieces_of_weight[0]

    def expand(g):
        wide = jnp.dot(latent[g], weight[...], preferred_element_type=jnp.float32)
        return wide.astype(jnp.bfloat16)

    def score(g, b, expanded):
        at = slice(b * 128, (b + 1) * 128)
        key_rope = (rope_even, rope_odd)[b][g]
        key = jnp.concatenate([expanded[:, b * 256 : b * 256 + 128], key_rope], axis=1)
        query = jnp.concatenate(
            [
                jnp.concatenate([nope[2 * g][:, at], rope[2 * g][...]], axis=1),
                jnp.concatenate([nope[2 * g + 1][:, at], rope[2 * g + 1][...]], axis=1),
            ],
            axis=0,
        )
        return lax.dot_general(
            query, key, (((1,), (1,)), ((), ())), preferred_element_type=jnp.float32
        )

    def weigh(g, scores):
        scores = scores * scale + bias[g]
        largest = jnp.max(scores, axis=1, keepdims=True)
        expo = jnp.exp2(scores - largest)
        return expo.astype(jnp.bfloat16), jnp.sum(expo, axis=1, keepdims=True)

    def mix(g, b, expanded, weights, total):
        at = slice(b * 128, (b + 1) * 128)
        value = expanded[:, b * 256 + 128 : b * 256 + 256]
        mixed = jnp.dot(weights, value, preferred_element_type=jnp.float32)
        mixed = (mixed / total).astype(jnp.bfloat16)
        outs[2 * g][:, at] = mixed[:tok]
        outs[2 * g + 1][:, at] = mixed[tok:]

    first = expand(0)
    scores = score(0, 0, first)
    second = expand(1)
    weighed = weigh(0, scores)
    scores = score(0, 1, first)
    mix(0, 0, first, *weighed)
    weighed = weigh(0, scores)
    scores = score(1, 0, second)
    mix(0, 1, first, *weighed)
    weighed = weigh(1, scores)
    scores = score(1, 1, second)
    mix(1, 0, second, *weighed)
    weighed = weigh(1, scores)
    mix(1, 1, second, *weighed)


def sort_kernel(info, relative, out, sem):
    rows = relative.shape[1]
    copies = []
    for d in range(relative.shape[0]):
        begin = pl.multiple_of((info[0] ^ d) * rows, rows)
        copies.append(
            pltpu.make_async_copy(relative.at[d], out.at[pl.ds(begin, rows)], sem.at[d])
        )
    for copy in copies:
        copy.start()
    for copy in copies:
        copy.wait()


def gather_kernel(info, *refs):
    pieces, out, sems = refs[:-2], refs[-2], refs[-1]
    copies = []
    for i, piece in enumerate(pieces):
        r, (j, first, steps) = i // len(CALLS), CALLS[i % len(CALLS)]
        begin = ((info[0] ^ r) * HQ + FIRST_HEAD[j] + 2 * first) * VDIM
        begin = pl.multiple_of(begin, 128)
        copies.append(
            pltpu.make_async_copy(piece, out.at[:, pl.ds(begin, piece.shape[1])], sems.at[i])
        )
    for copy in copies:
        copy.start()
    for copy in copies:
        copy.wait()


def tie(array, *others):
    return lax.optimization_barrier((array,) + others)[0]


class Phases:
    def __init__(self):
        self.before, self.before_late, self.now, self.late = [], [], [], []

    def turn(self):
        self.before = self.now + self.before_late
        self.before_late, self.now, self.late = self.late, [], []

    def send(self, late, permute, array, *args):
        arrived = permute(tie(array, *self.before) if self.before else array, *args)
        if late != "-":
            (self.late if late == "~" else self.now).append(arrived)
        return arrived


def shape(dims, kind=jnp.bfloat16):
    return jax.ShapeDtypeStruct(dims, kind)


def in_hbm(*arrays):
    return [pltpu.with_memory_space_constraint(array, pltpu.HBM) for array in arrays]


def body(q_heads, kv_latent, latent_gain, w_up, page_ranks, lengths):
    tok = q_heads.shape[0]
    size = lax.axis_size("ctx")
    groups = lax.axis_size("groups")
    mine = lax.axis_index("ctx")
    quarter = lax.axis_index("groups") * 2 + mine % 2
    slot_count = max(2, 2 * tok // size)
    smem = pl.BlockSpec(memory_space=SMEM)
    params = pltpu.CompilerParams(vmem_limit_bytes=VMEM_LIMIT)
    alone = pltpu.CompilerParams(vmem_limit_bytes=3 * VMEM_LIMIT)

    def quad_swap(array, r):
        dx, dc = r // 2, r % 2
        pairs = [
            (g * size + i, (g ^ dx) * size + (i ^ dc)) for g in range(groups) for i in range(size)
        ]
        return lax.ppermute(array, ("groups", "ctx"), pairs)

    def around(array, by):
        return lax.ppermute(array, "ctx", [(i, (i + by) % size) for i in range(size)])

    def inner_swap(array):
        return lax.ppermute(array, "ctx", [(i, i ^ 2) for i in range(size)])

    def pair_swap(array, distance):
        return lax.ppermute(array, "ctx", [(i, i ^ distance) for i in range(size)])

    def from_behind(array, by, odd_only):
        first = 1 if odd_only else 0
        step = 2 if odd_only else 1
        pairs = [(i, i + by) for i in range(first, size - by, step)]
        return lax.ppermute(array, "ctx", pairs)

    width = HQ * (NOPE + VDIM)
    quarter_info = quarter[None].astype(jnp.int32)
    anywhere = pl.BlockSpec(memory_space=pl.ANY)
    give = lax.dynamic_slice_in_dim(w_up, (quarter ^ 1) * width, width, 1)
    give, lengths = lax.optimization_barrier((give, lengths))
    got = quad_swap(give, 1)
    outer = 4 if size == 16 else 0
    if outer:
        pair_rows = pl.pallas_call(
            pair_kernel,
            out_shape=shape((2 * w_up.shape[0], width)),
            in_specs=[smem, pl.BlockSpec(memory_space=pltpu.HBM), anywhere],
            out_specs=anywhere,
            scratch_shapes=[pltpu.SemaphoreType.DMA((2,))],
            compiler_params=params,
            name="pair",
        )(quarter_info, *in_hbm(w_up), got)
    else:
        keep = lax.dynamic_slice_in_dim(w_up, quarter * width, width, 1)
        even = mine % 2 == 0
        both = jnp.concatenate(
            [jnp.where(even, keep, got), jnp.where(even, got, keep)], axis=0
        )
        same_core = [list(range(c, size, 2)) for c in range(2)]
        gathered = lax.all_gather(both, "ctx", axis=0, tiled=True, axis_index_groups=same_core)

    frequency = np.exp(-np.arange(ROPE // 2) * (2.0 * math.log(10000.0) / ROPE))
    frequency = jnp.asarray(np.tile(frequency, 4)[None, :], jnp.float32)
    mine_info = mine[None].astype(jnp.int32)

    def block(*dims):
        return pl.BlockSpec(dims, lambda i: (0,) * len(dims))

    rows, cosine, sine, outgoing = pl.pallas_call(
        functools.partial(rows_kernel, slot_count, outer > 0),
        grid=(1,),
        out_shape=(
            shape((tok, EXT)),
            shape((tok, 128), jnp.float32),
            shape((tok, 128), jnp.float32),
            shape((size * slot_count, ROW)),
        ),
        in_specs=[smem, smem, block(ROW, tok), block(1, LAT), block(1, tok), block(1, 128)],
        out_specs=[
            block(tok, EXT),
            block(tok, 128),
            block(tok, 128),
            block(size * slot_count, ROW),
        ],
        compiler_params=alone,
        name="rows",
    )(
        mine_info,
        lengths,
        *in_hbm(kv_latent.T, latent_gain[None, :], page_ranks.T, frequency),
    )

    queries = pl.pallas_call(
        query_kernel,
        out_shape=[shape((tok, h * (NOPE + ROPE))) for h in CHUNK_HEADS] * QUAD,
        grid=(1,),
        in_specs=[smem, block(*q_heads.shape), block(tok, 128), block(tok, 128)],
        out_specs=[block(tok, h * (NOPE + ROPE)) for h in CHUNK_HEADS] * QUAD,
        compiler_params=params,
        cost_estimate=pl.CostEstimate(
            flops=0, bytes_accessed=4 * q_heads.size, transcendentals=0
        ),
        name="queries",
    )(quarter_info, *in_hbm(q_heads, tie(cosine, pair_rows if outer else got), sine))

    held = outgoing.reshape(1, size, slot_count, ROW)
    exchanged = []

    def exchange(*others):
        half_of = held.shape[1] // 2
        moving = tie(held[:, half_of:], *others)
        exchanged.append(pair_swap(moving, 1 << len(exchanged)))
        return jnp.concatenate([held[:, :half_of], exchanged[-1]], axis=0)

    phases = Phases()
    line = [pair_rows] if outer else []
    side = []
    half = width // CHUNKS
    halves = []
    moved = [[queries[j]] + [None] * (QUAD - 1) for j in range(CHUNKS)]
    parts = {"r": tie(rows, pair_rows if outer else got)}
    for name in [name for phase in PHASES for name in phase + ("|",)]:
        kind, late = name[0], name[-1]
        if kind == "|":
            phases.now.append(queries[0])
            phases.turn()
        elif kind == "z" and outer:
            line.append(phases.send(late, around, line[-1], 4))
        elif kind == "y" and outer:
            step = int(name[1])
            if step < outer - 1:
                side.append(phases.send(late, inner_swap, line[step]))
            else:
                halves.append(phases.send(late, inner_swap, line[step][:, :half]))
        elif kind == "w" and outer:
            halves.append(phases.send(late, around, side[-1][:, half:], 4))
        elif kind == "k":
            swapped = phases.send(late, quad_swap, parts["r"], 2)
            both_groups = jnp.concatenate([parts["r"], swapped], axis=0)
        elif kind == "b":
            behind = phases.send(late, from_behind, both_groups, 2, False)
        elif kind == "f":
            far_behind = phases.send(late, from_behind, both_groups, 4, True)
        elif kind == "p":
            if outer:
                held = exchange(line[1])
                both_groups = tie(both_groups, exchanged[0])
            own_rows = jnp.concatenate([both_groups, behind, far_behind], axis=0)
            other_rows = phases.send(late, quad_swap, own_rows, 1)
        elif kind == "q":
            j, r = int(name[1]), int(name[2])
            if outer and name[1:3] == "13":
                held = exchange(line[2])
            moved[j][r] = phases.send(
                late, quad_swap, tie(queries[r * CHUNKS + j], *exchanged[1:]), r
            )

    def weights_for(j):
        if not outer:
            return [(gathered, FIRST_HEAD[j] // 2)]
        return [(piece, FIRST_HEAD[j] // 2) for piece in line + side] + [(halves[j], 0)]

    window = (REACH + 2) * tok
    resident = pl.BlockSpec(memory_space=VMEM)
    keys = pl.pallas_call(
        keys_kernel,
        out_shape=(
            shape((2, window, LAT)),
            shape((2, window, 128)),
            shape((2, window, 128)),
            shape((2, 2 * tok, window), jnp.float32),
        ),
        in_specs=[smem, resident, resident],
        out_specs=[resident] * 4,
        compiler_params=params,
        cost_estimate=pl.CostEstimate(flops=0, bytes_accessed=8 << 20, transcendentals=0),
        name="keys",
    )(mine_info, own_rows, other_rows)

    def attend(j, first, steps):
        heads = 2 * steps
        pieces_of_weight = [piece for piece, begin in weights_for(j)]
        flops = 2 * heads * 2 * (window * LAT * 256 + 2 * tok * window * (NOPE + ROPE + VDIM))
        return pl.pallas_call(
            functools.partial(attend_kernel, outer),
            grid=(steps,),
            out_shape=[shape((tok, heads * VDIM))] * QUAD,
            in_specs=[smem] + [resident] * 4
            + [
                pl.BlockSpec((piece.shape[0], 512), lambda i, begin=begin: (0, begin + first + i))
                for piece, begin in weights_for(j)
            ]
            + [pl.BlockSpec((tok, 256), lambda i: (0, first + i))] * QUAD
            + [pl.BlockSpec((tok, 128), lambda i: (0, CHUNK_HEADS[j] + first + i))] * QUAD,
            out_specs=[pl.BlockSpec((tok, 256), lambda i: (0, i))] * QUAD,
            scratch_shapes=[VMEM((LAT, 512), jnp.bfloat16)],
            compiler_params=params,
            cost_estimate=pl.CostEstimate(
                flops=flops,
                bytes_accessed=heads << 20,
                transcendentals=heads * 4 * tok * window,
            ),
            name="attend",
        )(mine_info, *keys, *pieces_of_weight, *moved[j], *moved[j])

    results = []
    for call in CALLS:
        last = len(results) + 1 == len(CALLS)
        if results:
            mine_info = tie(mine_info, *halves[1:], *exchanged[len(results) : len(results) + 1])
        mine_info = tie(mine_info, *(results[0][2:3] if last else []))
        pieces = attend(*call)
        mine_info = tie(mine_info, pieces[0])
        before = results[-1][2:] if last else []
        if outer and not last:
            held = exchange(pieces[0])
        results.append(
            [pieces[0], quad_swap(tie(pieces[1], *before), 1)]
            + [quad_swap(pieces[r], r) for r in (2, 3)]
        )
    pieces = [one[r] for r in range(QUAD) for one in results]
    if outer:
        decode_cache = pl.pallas_call(
            sort_kernel,
            out_shape=shape((size * slot_count, ROW)),
            in_specs=[smem, anywhere],
            out_specs=anywhere,
            scratch_shapes=[pltpu.SemaphoreType.DMA((size,))],
            compiler_params=params,
            name="sort",
        )(mine_info, held.reshape(size, slot_count, ROW))
    else:
        outgoing = tie(outgoing, results[-1][0]).reshape(size, slot_count, ROW)
        arrived = lax.all_to_all(outgoing, "ctx", split_axis=0, concat_axis=0, tiled=True)
        decode_cache = arrived.reshape(size * slot_count, ROW)
    attn_out = pl.pallas_call(
        gather_kernel,
        out_shape=shape((tok, H * VDIM)),
        in_specs=[smem] + [anywhere] * len(pieces),
        out_specs=anywhere,
        scratch_shapes=[pltpu.SemaphoreType.DMA((len(pieces),))],
        compiler_params=params,
        name="place",
    )(tie(quarter_info, decode_cache), *pieces)
    return (attn_out, decode_cache)


def solution(mesh):
    return jax.shard_map(
        body,
        mesh=mesh,
        in_specs=(
            P(("groups", "ctx"), None),
            P(("groups", "ctx"), None),
            P(),
            P("ctx", None),
            P(("groups", "ctx"), None),
            P("groups"),
        ),
        out_specs=(P(("groups", "ctx"), None), P(("groups", "ctx"), None)),
        check_vma=False,
    )
```

```python
import functools
import math

import jax
import jax.numpy as jnp
import numpy as np
from jax import lax
from jax.experimental import pallas as pl
from jax.experimental.pallas import tpu as pltpu
from jax.sharding import PartitionSpec as P

H = 64
NOPE = 128
ROPE = 64
VDIM = 128
LAT = 512
REACH = 3
QUAD = 4
HQ = H // QUAD
CHUNK_HEADS = (8, 8)
PHASES = (
    ("z", "y0", "k", "q02", "b~", "f~"),
    ("z", "y1", "q03", "q01", "e-"),
    ("z", "y2", "p", "q12"),
    ("y3", "w", "q13~", "q11", "e-", "e-", "e-"),
)
CHUNKS = len(CHUNK_HEADS)
FIRST_HEAD = tuple(sum(CHUNK_HEADS[:j]) for j in range(CHUNKS))
ROW = LAT + ROPE
EXT = 640
VMEM_LIMIT = 20 * 1024 * 1024
CALLS = ((0, 0, 4), (1, 0, 3), (1, 3, 1))
SMEM = pltpu.SMEM
VMEM = pltpu.VMEM


def rows_kernel(
    slot_count,
    relative,
    info,
    lengths,
    kv,
    gain,
    ranks,
    freq,
    rows_out,
    cos_out,
    sin_out,
    outgoing_out,
):
    tok = kv.shape[1]
    base = info[0] * tok
    spots = base + lax.broadcasted_iota(jnp.int32, (tok, 128), 0)
    lane = lax.broadcasted_iota(jnp.int32, (tok, 128), 1)
    begin = jnp.int32(0)
    own_start = jnp.zeros((tok, 128), jnp.int32)
    for r in range(lengths.shape[0]):
        own_start = jnp.where(spots >= begin, begin, own_start)
        begin = begin + lengths[r]
    offset = spots - own_start
    angles = offset.astype(jnp.float32) * freq[...]
    cosine = jnp.cos(angles)
    sine = jnp.where((lane & 32) == 0, -jnp.sin(angles), jnp.sin(angles))
    cos_out[...] = cosine
    sin_out[...] = sine
    raw = kv[...].astype(jnp.float32).T
    latent = raw[:, :LAT]
    mean = jnp.sum(latent * latent, axis=1, keepdims=True) * (1.0 / LAT)
    latent = latent * lax.rsqrt(mean + 1e-06) * gain[...]
    key = raw[:, LAT:]
    swapped = jnp.concatenate([key[:, ROPE // 2 :], key[:, : ROPE // 2]], axis=1)
    turned = key * cosine[:, :ROPE] + swapped * sine[:, :ROPE]
    high = (offset >> 8).astype(jnp.float32)
    low = (offset & 255).astype(jnp.float32)
    meta = jnp.where(lane == 0, high, jnp.where(lane == 1, low, 0.0))
    tail = jnp.concatenate([turned, meta[:, :ROPE]], axis=1)
    rows_out[:, :LAT] = latent.astype(jnp.bfloat16)
    rows_out[:, LAT:] = tail.astype(jnp.bfloat16)

    block = ranks[...]
    if relative:
        away = block ^ info[0]
        block = ((away & 1) << 3) | ((away & 2) << 1) | ((away & 4) >> 1) | (away >> 3)
    rank_row = jnp.broadcast_to(block, (tok, tok)).astype(jnp.float32)
    rank_col = rank_row.T
    earlier = lax.broadcasted_iota(jnp.int32, (tok, tok), 0) < lax.broadcasted_iota(
        jnp.int32, (tok, tok), 1
    )
    same = jnp.where((rank_col == rank_row) & earlier, 1.0, 0.0)
    slot = jnp.sum(same, axis=0, keepdims=True)
    target = (rank_row[:1] * slot_count + slot).astype(jnp.int32)
    spots_out = lax.broadcasted_iota(jnp.int32, (outgoing_out.shape[0], tok), 0)
    selector = jnp.where(spots_out == target, 1.0, 0.0).astype(jnp.bfloat16)
    picked = jnp.dot(selector, rows_out[:, :ROW], preferred_element_type=jnp.float32)
    outgoing_out[...] = picked.astype(jnp.bfloat16)


def query_kernel(info, query, cosine, sine, *outs):
    tok = query.shape[0]
    lane = lax.broadcasted_iota(jnp.int32, (tok, 128), 1)
    low_half = lane < 64
    first_quarter = (lane & 32) == 0
    cos_table = cosine[...]
    sin_table = sine[...]
    for r in range(QUAD):
        first = (info[0] ^ r) * (HQ * (NOPE + ROPE))
        for pair in range(HQ // 2):
            j = max(j for j in range(CHUNKS) if FIRST_HEAD[j] <= 2 * pair)
            out = outs[r * CHUNKS + j]
            at = pair - FIRST_HEAD[j] // 2
            rope_at = CHUNK_HEADS[j] * NOPE + at * 128
            begin = pl.multiple_of(first + pair * 2 * (NOPE + ROPE), 128)
            both = query[:, pl.ds(begin, 2 * (NOPE + ROPE))]
            mid = both[:, 128:256].astype(jnp.float32)
            end = both[:, 256:384].astype(jnp.float32)
            turned = jnp.where(low_half, mid, end)
            odd_nope = pltpu.roll(jnp.where(low_half, end, mid), 64, 1)
            swapped = jnp.where(
                first_quarter, pltpu.roll(turned, 96, 1), pltpu.roll(turned, 32, 1)
            )
            turned = turned * cos_table + swapped * sin_table
            out[:, at * 256 : at * 256 + 128] = both[:, :128]
            out[:, at * 256 + 128 : at * 256 + 256] = odd_nope.astype(jnp.bfloat16)
            out[:, rope_at : rope_at + 128] = turned.astype(jnp.bfloat16)


def pair_kernel(info, w_up, got, out, sem):
    rows, width = got.shape
    begin = pl.multiple_of(info[0] * width, 128)
    copies = [
        pltpu.make_async_copy(w_up.at[:, pl.ds(begin, width)], out.at[pl.ds(0, rows)], sem.at[0]),
        pltpu.make_async_copy(got, out.at[pl.ds(rows, rows)], sem.at[1]),
    ]
    for copy in copies:
        copy.start()
    for copy in copies:
        copy.wait()


def keys_kernel(info, own, other, latent, rope_even, rope_odd, bias):
    tok = own.shape[0] // 6
    mine = info[0]
    partner = mine ^ 1
    has_last = (mine & 1) == 1
    starts = [mine, partner, mine - 2, partner - 2, (mine >> 1) * 2 - 3]
    blank = jnp.zeros((tok, ROPE), jnp.bfloat16)
    lane = lax.broadcasted_iota(jnp.int32, (tok, tok), 1)
    row = lax.broadcasted_iota(jnp.int32, (tok, tok), 0)
    for g in range(2):
        mine_of, other_of = [
            [ref[(2 * n + g) * tok : (2 * n + g + 1) * tok] for n in range(3)]
            for ref in (own, other)
        ]
        pieces = [
            mine_of[0],
            other_of[0],
            mine_of[1],
            other_of[1],
            jnp.where(has_last, mine_of[2], other_of[2]),
        ]
        for b, piece in enumerate(pieces):
            here = slice(b * tok, (b + 1) * tok)
            latent[g, here] = piece[:, :LAT]
            turned = piece[:, LAT : LAT + ROPE]
            rope_even[g, here] = jnp.concatenate([turned, blank], axis=1)
            rope_odd[g, here] = jnp.concatenate([blank, turned], axis=1)
        for half in range(2):
            meta = pieces[half][:, LAT:].astype(jnp.float32)
            offset = (meta[:, ROPE : ROPE + 1] * 256.0 + meta[:, ROPE + 1 : ROPE + 2]).astype(
                jnp.int32
            )
            spots = starts[half] * tok + row
            lowest = jnp.maximum(spots - offset, (starts[half] - REACH) * tok)
            for b in range(REACH + 2):
                keys = starts[b] * tok + lane
                allowed = (keys >= lowest) & (keys <= spots)
                bias[g, half * tok : (half + 1) * tok, b * tok : (b + 1) * tok] = jnp.where(
                    allowed, 0.0, -1e30
                )


def attend_kernel(outer, info, latent, rope_even, rope_odd, bias, *refs):
    pieces_count = 2 * outer if outer else 1
    pieces_of_weight, refs = refs[:pieces_count], refs[pieces_count:]
    nope = refs[0:QUAD]
    rope = refs[QUAD : 2 * QUAD]
    outs = refs[2 * QUAD : 3 * QUAD]
    held = refs[3 * QUAD]
    tok = nope[0].shape[0]
    mine = info[0]
    scale = (NOPE + ROPE) ** (-0.5) * math.log2(math.e)

    if outer:
        weight = held
        for i, piece in enumerate(pieces_of_weight):
            side, behind = i // outer, i % outer
            chip = ((mine >> 2) + outer - behind) % outer * 2 + (((mine >> 1) & 1) ^ side)
            rows = piece.shape[0] // 2
            for core in range(2):
                begin = pl.multiple_of(chip * 2 * rows + ((mine & 1) ^ core) * rows, rows)
                held[pl.ds(begin, rows)] = piece[core * rows : (core + 1) * rows]
    else:
        weight = pieces_of_weight[0]

    def expand(g):
        wide = jnp.dot(latent[g], weight[...], preferred_element_type=jnp.float32)
        return wide.astype(jnp.bfloat16)

    def score(g, b, expanded):
        at = slice(b * 128, (b + 1) * 128)
        key_rope = (rope_even, rope_odd)[b][g]
        key = jnp.concatenate([expanded[:, b * 256 : b * 256 + 128], key_rope], axis=1)
        query = jnp.concatenate(
            [
                jnp.concatenate([nope[2 * g][:, at], rope[2 * g][...]], axis=1),
                jnp.concatenate([nope[2 * g + 1][:, at], rope[2 * g + 1][...]], axis=1),
            ],
            axis=0,
        )
        return lax.dot_general(
            query, key, (((1,), (1,)), ((), ())), preferred_element_type=jnp.float32
        )

    def weigh(g, scores):
        scores = scores * scale + bias[g]
        largest = jnp.max(scores, axis=1, keepdims=True)
        expo = jnp.exp2(scores - largest)
        return expo.astype(jnp.bfloat16), jnp.sum(expo, axis=1, keepdims=True)

    def mix(g, b, expanded, weights, total):
        at = slice(b * 128, (b + 1) * 128)
        value = expanded[:, b * 256 + 128 : b * 256 + 256]
        mixed = jnp.dot(weights, value, preferred_element_type=jnp.float32)
        mixed = (mixed / total).astype(jnp.bfloat16)
        outs[2 * g][:, at] = mixed[:tok]
        outs[2 * g + 1][:, at] = mixed[tok:]

    first = expand(0)
    scores = score(0, 0, first)
    second = expand(1)
    weighed = weigh(0, scores)
    scores = score(0, 1, first)
    mix(0, 0, first, *weighed)
    weighed = weigh(0, scores)
    scores = score(1, 0, second)
    mix(0, 1, first, *weighed)
    weighed = weigh(1, scores)
    scores = score(1, 1, second)
    mix(1, 0, second, *weighed)
    weighed = weigh(1, scores)
    mix(1, 1, second, *weighed)


def sort_kernel(info, relative, out, sem):
    rows = relative.shape[1]
    copies = []
    for d in range(relative.shape[0]):
        begin = pl.multiple_of((info[0] ^ d) * rows, rows)
        copies.append(
            pltpu.make_async_copy(relative.at[d], out.at[pl.ds(begin, rows)], sem.at[d])
        )
    for copy in copies:
        copy.start()
    for copy in copies:
        copy.wait()


def gather_kernel(info, *refs):
    pieces, out, sems = refs[:-2], refs[-2], refs[-1]
    copies = []
    for i, piece in enumerate(pieces):
        r, (j, first, steps) = i // len(CALLS), CALLS[i % len(CALLS)]
        begin = ((info[0] ^ r) * HQ + FIRST_HEAD[j] + 2 * first) * VDIM
        begin = pl.multiple_of(begin, 128)
        copies.append(
            pltpu.make_async_copy(piece, out.at[:, pl.ds(begin, piece.shape[1])], sems.at[i])
        )
    for copy in copies:
        copy.start()
    for copy in copies:
        copy.wait()


def tie(array, *others):
    return lax.optimization_barrier((array,) + others)[0]


class Phases:
    def __init__(self):
        self.before, self.before_late, self.now, self.late = [], [], [], []

    def turn(self):
        self.before = self.now + self.before_late
        self.before_late, self.now, self.late = self.late, [], []

    def send(self, late, permute, array, *args):
        arrived = permute(tie(array, *self.before) if self.before else array, *args)
        if late != "-":
            (self.late if late == "~" else self.now).append(arrived)
        return arrived


def shape(dims, kind=jnp.bfloat16):
    return jax.ShapeDtypeStruct(dims, kind)


def in_hbm(*arrays):
    return [pltpu.with_memory_space_constraint(array, pltpu.HBM) for array in arrays]


def body(q_heads, kv_latent, latent_gain, w_up, page_ranks, lengths):
    tok = q_heads.shape[0]
    size = lax.axis_size("ctx")
    groups = lax.axis_size("groups")
    mine = lax.axis_index("ctx")
    quarter = lax.axis_index("groups") * 2 + mine % 2
    slot_count = max(2, 2 * tok // size)
    smem = pl.BlockSpec(memory_space=SMEM)
    params = pltpu.CompilerParams(vmem_limit_bytes=VMEM_LIMIT)
    alone = pltpu.CompilerParams(vmem_limit_bytes=3 * VMEM_LIMIT)

    def quad_swap(array, r):
        dx, dc = r // 2, r % 2
        pairs = [
            (g * size + i, (g ^ dx) * size + (i ^ dc)) for g in range(groups) for i in range(size)
        ]
        return lax.ppermute(array, ("groups", "ctx"), pairs)

    def around(array, by):
        return lax.ppermute(array, "ctx", [(i, (i + by) % size) for i in range(size)])

    def inner_swap(array):
        return lax.ppermute(array, "ctx", [(i, i ^ 2) for i in range(size)])

    def pair_swap(array, distance):
        return lax.ppermute(array, "ctx", [(i, i ^ distance) for i in range(size)])

    def from_behind(array, by, odd_only):
        first = 1 if odd_only else 0
        step = 2 if odd_only else 1
        pairs = [(i, i + by) for i in range(first, size - by, step)]
        return lax.ppermute(array, "ctx", pairs)

    width = HQ * (NOPE + VDIM)
    quarter_info = quarter[None].astype(jnp.int32)
    anywhere = pl.BlockSpec(memory_space=pl.ANY)
    give = lax.dynamic_slice_in_dim(w_up, (quarter ^ 1) * width, width, 1)
    give, lengths = lax.optimization_barrier((give, lengths))
    got = quad_swap(give, 1)
    outer = 4 if size == 16 else 0
    if outer:
        pair_rows = pl.pallas_call(
            pair_kernel,
            out_shape=shape((2 * w_up.shape[0], width)),
            in_specs=[smem, pl.BlockSpec(memory_space=pltpu.HBM), anywhere],
            out_specs=anywhere,
            scratch_shapes=[pltpu.SemaphoreType.DMA((2,))],
            compiler_params=params,
            name="pair",
        )(quarter_info, *in_hbm(w_up), got)
    else:
        keep = lax.dynamic_slice_in_dim(w_up, quarter * width, width, 1)
        even = mine % 2 == 0
        both = jnp.concatenate(
            [jnp.where(even, keep, got), jnp.where(even, got, keep)], axis=0
        )
        same_core = [list(range(c, size, 2)) for c in range(2)]
        gathered = lax.all_gather(both, "ctx", axis=0, tiled=True, axis_index_groups=same_core)

    frequency = np.exp(-np.arange(ROPE // 2) * (2.0 * math.log(10000.0) / ROPE))
    frequency = jnp.asarray(np.tile(frequency, 4)[None, :], jnp.float32)
    mine_info = mine[None].astype(jnp.int32)

    def block(*dims):
        return pl.BlockSpec(dims, lambda i: (0,) * len(dims))

    rows, cosine, sine, outgoing = pl.pallas_call(
        functools.partial(rows_kernel, slot_count, outer > 0),
        grid=(1,),
        out_shape=(
            shape((tok, EXT)),
            shape((tok, 128), jnp.float32),
            shape((tok, 128), jnp.float32),
            shape((size * slot_count, ROW)),
        ),
        in_specs=[smem, smem, block(ROW, tok), block(1, LAT), block(1, tok), block(1, 128)],
        out_specs=[
            block(tok, EXT),
            block(tok, 128),
            block(tok, 128),
            block(size * slot_count, ROW),
        ],
        compiler_params=alone,
        name="rows",
    )(
        mine_info,
        lengths,
        *in_hbm(kv_latent.T, latent_gain[None, :], page_ranks.T, frequency),
    )

    queries = pl.pallas_call(
        query_kernel,
        out_shape=[shape((tok, h * (NOPE + ROPE))) for h in CHUNK_HEADS] * QUAD,
        grid=(1,),
        in_specs=[smem, block(*q_heads.shape), block(tok, 128), block(tok, 128)],
        out_specs=[block(tok, h * (NOPE + ROPE)) for h in CHUNK_HEADS] * QUAD,
        compiler_params=params,
        cost_estimate=pl.CostEstimate(
            flops=0, bytes_accessed=4 * q_heads.size, transcendentals=0
        ),
        name="queries",
    )(quarter_info, *in_hbm(q_heads, tie(cosine, pair_rows if outer else got), sine))

    phases = Phases()
    line = [pair_rows] if outer else []
    side = []
    half = width // CHUNKS
    halves = []
    moved = [[queries[j]] + [None] * (QUAD - 1) for j in range(CHUNKS)]
    held = outgoing.reshape(1, size, slot_count, ROW)
    exchanged = []
    parts = {"r": tie(rows, pair_rows if outer else got)}
    for name in [name for phase in PHASES for name in phase + ("|",)]:
        kind, late = name[0], name[-1]
        if kind == "|":
            phases.now.append(queries[0])
            phases.turn()
        elif kind == "z" and outer:
            line.append(phases.send(late, around, line[-1], 4))
        elif kind == "y" and outer:
            step = int(name[1])
            if step < outer - 1:
                side.append(phases.send(late, inner_swap, line[step]))
            else:
                halves.append(phases.send(late, inner_swap, line[step][:, :half]))
        elif kind == "w" and outer:
            halves.append(phases.send(late, around, side[-1][:, half:], 4))
        elif kind == "k":
            swapped = phases.send(late, quad_swap, parts["r"], 2)
            both_groups = jnp.concatenate([parts["r"], swapped], axis=0)
        elif kind == "b":
            behind = phases.send(late, from_behind, both_groups, 2, False)
        elif kind == "f":
            far_behind = phases.send(late, from_behind, both_groups, 4, True)
        elif kind == "p":
            own_rows = jnp.concatenate([both_groups, behind, far_behind], axis=0)
            other_rows = phases.send(late, quad_swap, own_rows, 1)
        elif kind == "e" and outer:
            half_of = held.shape[1] // 2
            distance = 1 << len(exchanged)
            exchanged.append(phases.send(late, pair_swap, held[:, half_of:], distance))
            held = jnp.concatenate([held[:, :half_of], exchanged[-1]], axis=0)
        elif kind == "q":
            j, r = int(name[1]), int(name[2])
            moved[j][r] = phases.send(late, quad_swap, queries[r * CHUNKS + j], r)

    def weights_for(j):
        if not outer:
            return [(gathered, FIRST_HEAD[j] // 2)]
        return [(piece, FIRST_HEAD[j] // 2) for piece in line + side] + [(halves[j], 0)]

    window = (REACH + 2) * tok
    resident = pl.BlockSpec(memory_space=VMEM)
    keys = pl.pallas_call(
        keys_kernel,
        out_shape=(
            shape((2, window, LAT)),
            shape((2, window, 128)),
            shape((2, window, 128)),
            shape((2, 2 * tok, window), jnp.float32),
        ),
        in_specs=[smem, resident, resident],
        out_specs=[resident] * 4,
        compiler_params=params,
        cost_estimate=pl.CostEstimate(flops=0, bytes_accessed=8 << 20, transcendentals=0),
        name="keys",
    )(mine_info, own_rows, other_rows)

    def attend(j, first, steps):
        heads = 2 * steps
        pieces_of_weight = [piece for piece, begin in weights_for(j)]
        flops = 2 * heads * 2 * (window * LAT * 256 + 2 * tok * window * (NOPE + ROPE + VDIM))
        return pl.pallas_call(
            functools.partial(attend_kernel, outer),
            grid=(steps,),
            out_shape=[shape((tok, heads * VDIM))] * QUAD,
            in_specs=[smem] + [resident] * 4
            + [
                pl.BlockSpec((piece.shape[0], 512), lambda i, begin=begin: (0, begin + first + i))
                for piece, begin in weights_for(j)
            ]
            + [pl.BlockSpec((tok, 256), lambda i: (0, first + i))] * QUAD
            + [pl.BlockSpec((tok, 128), lambda i: (0, CHUNK_HEADS[j] + first + i))] * QUAD,
            out_specs=[pl.BlockSpec((tok, 256), lambda i: (0, i))] * QUAD,
            scratch_shapes=[VMEM((LAT, 512), jnp.bfloat16)],
            compiler_params=params,
            cost_estimate=pl.CostEstimate(
                flops=flops,
                bytes_accessed=heads << 20,
                transcendentals=heads * 4 * tok * window,
            ),
            name="attend",
        )(mine_info, *keys, *pieces_of_weight, *moved[j], *moved[j])

    results = []
    for call in CALLS:
        last = len(results) + 1 == len(CALLS)
        mine_info = tie(mine_info, *exchanged[len(results) : len(results) + 1])
        mine_info = tie(mine_info, *(results[0][2:3] if last else []))
        pieces = attend(*call)
        mine_info = tie(mine_info, pieces[0])
        before = results[-1][2:] if last else []
        results.append(
            [pieces[0], quad_swap(tie(pieces[1], *before), 1)]
            + [quad_swap(pieces[r], r) for r in (2, 3)]
        )
    pieces = [one[r] for r in range(QUAD) for one in results]
    if outer:
        decode_cache = pl.pallas_call(
            sort_kernel,
            out_shape=shape((size * slot_count, ROW)),
            in_specs=[smem, anywhere],
            out_specs=anywhere,
            scratch_shapes=[pltpu.SemaphoreType.DMA((size,))],
            compiler_params=params,
            name="sort",
        )(mine_info, held.reshape(size, slot_count, ROW))
    else:
        outgoing = tie(outgoing, results[-1][0]).reshape(size, slot_count, ROW)
        arrived = lax.all_to_all(outgoing, "ctx", split_axis=0, concat_axis=0, tiled=True)
        decode_cache = arrived.reshape(size * slot_count, ROW)
    attn_out = pl.pallas_call(
        gather_kernel,
        out_shape=shape((tok, H * VDIM)),
        in_specs=[smem] + [anywhere] * len(pieces),
        out_specs=anywhere,
        scratch_shapes=[pltpu.SemaphoreType.DMA((len(pieces),))],
        compiler_params=params,
        name="place",
    )(quarter_info, *pieces)
    return (attn_out, decode_cache)


def solution(mesh):
    return jax.shard_map(
        body,
        mesh=mesh,
        in_specs=(
            P(("groups", "ctx"), None),
            P(("groups", "ctx"), None),
            P(),
            P("ctx", None),
            P(("groups", "ctx"), None),
            P("groups"),
        ),
        out_specs=(P(("groups", "ctx"), None), P(("groups", "ctx"), None)),
        check_vma=False,
    )
```
